32 devices in a mesh: gz: 4 (over y, core), gy: 8 (over z, x).
Axes of the slice: x: 2, y: 2, z: 4, core: 2. Of those that a mesh axis runs over, the one named last changes fastest.
Arguments:
- density: float32 [32, 64, 512], P(None, 'gy', 'gz'), may hold values from 0.5 to 2
- diffusion: float32 [3], replicated, may hold values from 800 to 3000
- centers: float32 [16, 3], replicated, may hold values from -1 to 1
- sharpness: float32 [16], replicated, may hold values from 1 to 8
- affine: float32 [16, 3, 3], replicated, may hold values from -6 to 6
- offsets: float32 [16, 3], replicated, may hold values from -6 to 6
Outputs:
- density_next: float32 [32, 64, 512], P(None, 'gy', 'gz')
The draws below stay inside these ranges and needn't reach their ends.
All inputs are finite; a program needn't handle non-finite values.
Results may differ from the reference program's by a relative error of at most 0.00065.
Values sent between devices are 32-bit elements; how exact they have to be, the bound alone decides.
No kernel may reach another device: no remote copies, remote signals or barrier semaphores. Data moves between devices by JAX's collectives and lax.ppermute only.
A program may use at most 64 MiB of HBM per device.

```python
import math
import jax
import jax.numpy as jnp
from jax import lax

NX = 32
COMPONENTS = 16
NY = 64
NZ = 512


def draw_density(key, part):
    rough_part = jax.random.uniform(key, (NX, NY, NZ), jnp.float32)
    return 0.5 + rough_part


def centred(own_key, shape, scale, limit, held_as=jnp.bfloat16):
    return jnp.clip(scale * jax.random.normal(own_key, shape, jnp.float32), -limit, limit).astype(held_as)


def setup_inputs(seed: int = 0) -> dict:
    seeds = jax.random.split(jax.random.key(seed), 7)
    return {
        "density": draw_density(jax.random.fold_in(seeds[6], 71), 0),
        "diffusion": jnp.clip(jnp.exp(jax.random.uniform(seeds[1], (3,), jnp.float32, math.log(800.0), math.log(3000.0))), 800.0, 3000.0),
        "centers": jnp.clip(jax.random.uniform(seeds[2], (COMPONENTS, 3), jnp.float32, -1.0, 1.0), -1.0, 1.0),
        "sharpness": jnp.clip(jnp.exp(jax.random.uniform(seeds[3], (COMPONENTS,), jnp.float32, math.log(1.0), math.log(8.0))), 1.0, 8.0),
        "affine": centred(seeds[4], (COMPONENTS, 3, 3), 1.0, 6.0, jnp.float32),
        "offsets": centred(seeds[5], (COMPONENTS, 3), 1.0, 6.0, jnp.float32),
    }


DRIFT_LIMIT = 1200.0


def axis_coord(positions, line_total):
    return (2.0 * positions.astype(jnp.float32) + 1.0) / line_total - 1.0


def bump_factor(coords, centers, sharpness, column):
    return jnp.exp(-sharpness[:, None] * (coords[None, :] - centers[:, column:column + 1]) ** 2)


def field_drift(component, x_index, y_index, z_index, mixture, totals):
    centers, sharpness, affine, offsets = mixture
    x_coord = axis_coord(x_index, totals[0])
    y_coord = axis_coord(y_index, totals[1])
    z_coord = axis_coord(z_index, totals[2])
    x_factor = bump_factor(x_coord, centers, sharpness, 0)
    y_factor = bump_factor(y_coord, centers, sharpness, 1)
    z_factor = bump_factor(z_coord, centers, sharpness, 2)
    matrix = affine[:, component, :]
    shift_term = offsets[:, component]
    left_part = jnp.concatenate([x_factor * (matrix[:, 0:1] * x_coord[None, :] + shift_term[:, None]),
                                 x_factor * matrix[:, 1:2], x_factor * matrix[:, 2:3]], axis=0)
    yz_plane = y_factor[:, :, None] * z_factor[:, None, :]
    right_part = jnp.concatenate([yz_plane, yz_plane * y_coord[None, :, None],
                                  yz_plane * z_coord[None, None, :]], axis=0)
    right_part = right_part.reshape(right_part.shape[0], -1)
    raw_drift = jnp.dot(left_part.T, right_part, precision=lax.Precision.HIGHEST,
                        preferred_element_type=jnp.float32)
    return DRIFT_LIMIT * jnp.tanh(raw_drift.reshape(x_coord.shape[0], y_coord.shape[0], z_coord.shape[0]))


def transport(framed_part, drift_part, diffuse, line_axis):
    length = framed_part.shape[line_axis] - 2
    centre = lax.slice_in_dim(framed_part, 1, length + 1, axis=line_axis)
    onward = lax.slice_in_dim(framed_part, 2, length + 2, axis=line_axis)
    backward = lax.slice_in_dim(framed_part, 0, length, axis=line_axis)
    drift_on = lax.slice_in_dim(drift_part, 2, length + 2, axis=line_axis)
    drift_back = lax.slice_in_dim(drift_part, 0, length, axis=line_axis)
    return diffuse * (onward - 2.0 * centre + backward) - 0.5 * (drift_on * onward - drift_back * backward)


def implicit_rows(drift_part, diffuse, line_axis, at_start, at_end):
    length = drift_part.shape[line_axis] - 2
    drift_on = lax.slice_in_dim(drift_part, 2, length + 2, axis=line_axis)
    drift_back = lax.slice_in_dim(drift_part, 0, length, axis=line_axis)
    pivots = 1.0 + 2.0 * diffuse
    sub_diag = jnp.where(at_start, 0.0, (-diffuse - 0.5 * drift_back) / pivots)
    super_diag = jnp.where(at_end, 0.0, (-diffuse + 0.5 * drift_on) / pivots)
    return sub_diag, super_diag


def edge_masks(positions, line_total, line_axis):
    layout = [1, 1, 1]
    layout[line_axis] = positions.shape[0]
    return (positions == 0).reshape(layout), (positions == line_total - 1).reshape(layout)


def shifted(values, stride, line_axis, onward):
    line_dim = line_axis % values.ndim
    length = values.shape[line_dim]
    if stride >= length:
        return jnp.zeros_like(values)
    layout = list(values.shape)
    layout[line_dim] = stride
    padding = jnp.zeros(layout, values.dtype)
    if onward:
        return jnp.concatenate([lax.slice_in_dim(values, stride, length, axis=line_dim), padding], axis=line_dim)
    return jnp.concatenate([padding, lax.slice_in_dim(values, 0, length - stride, axis=line_dim)], axis=line_dim)


def eliminate(row_set, below_set, above_set):
    sub_diag, super_diag, source = row_set
    pivots = 1.0 - sub_diag * below_set[1] - super_diag * above_set[0]
    return (-sub_diag * below_set[0] / pivots, -super_diag * above_set[1] / pivots,
            (source - sub_diag * below_set[2] - super_diag * above_set[2]) / pivots)


def reduce_lines(sub_diag, super_diag, source, line_axis):
    length = sub_diag.shape[line_axis]
    row_set = (sub_diag, super_diag, source)
    stride = 1
    while stride < length:
        below_set = tuple(shifted(member, stride, line_axis, False) for member in row_set)
        above_set = tuple(shifted(member, stride, line_axis, True) for member in row_set)
        row_set = eliminate(row_set, below_set, above_set)
        stride = stride * 2
    return row_set[2]


def reference(density, diffusion, centers, sharpness, affine, offsets):
    size_x, size_y, size_z = density.shape
    totals = (size_x, size_y, size_z)
    mixture = (centers, sharpness, affine, offsets)
    x_index = jnp.arange(size_x, dtype=jnp.int32)
    y_index = jnp.arange(size_y, dtype=jnp.int32)
    z_index = jnp.arange(size_z, dtype=jnp.int32)
    drift_x = field_drift(0, jnp.arange(-1, size_x + 1, dtype=jnp.int32), y_index, z_index, mixture, totals)
    drift_y = field_drift(1, x_index, jnp.arange(-1, size_y + 1, dtype=jnp.int32), z_index, mixture, totals)
    drift_z = field_drift(2, x_index, y_index, jnp.arange(-1, size_z + 1, dtype=jnp.int32), mixture, totals)
    flux_y = transport(jnp.pad(density, ((0, 0), (1, 1), (0, 0))), drift_y, diffusion[1], 1)
    flux_z = transport(jnp.pad(density, ((0, 0), (0, 0), (1, 1))), drift_z, diffusion[2], 2)
    start_x, end_x = edge_masks(x_index, size_x, 0)
    sub_x, super_x = implicit_rows(drift_x, diffusion[0], 0, start_x, end_x)
    first_section = reduce_lines(sub_x, super_x, (density + flux_y + flux_z) / (1.0 + 2.0 * diffusion[0]), -3)
    start_y, end_y = edge_masks(y_index, size_y, 1)
    sub_y, super_y = implicit_rows(drift_y, diffusion[1], 1, start_y, end_y)
    second_section = reduce_lines(sub_y, super_y, (first_section - flux_y) / (1.0 + 2.0 * diffusion[1]), -2)
    start_z, end_z = edge_masks(z_index, size_z, 2)
    sub_z, super_z = implicit_rows(drift_z, diffusion[2], 2, start_z, end_z)
    return reduce_lines(sub_z, super_z, (second_section - flux_z) / (1.0 + 2.0 * diffusion[2]), -1)
```

```python
import functools

import jax
import jax.numpy as jnp
from jax import lax
from jax.experimental import pallas as pl
from jax.experimental.pallas import tpu as pltpu
from jax.sharding import PartitionSpec as P

HALF_LIMIT = 600.0
LANES = 128
ROWS = 8
VMEM_LIMIT = 48 * 1024 * 1024


def iota(shape, axis):
    return lax.broadcasted_iota(jnp.int32, shape, axis)


def coordinate(positions, line_total):
    return (2.0 * positions.astype(jnp.float32) + 1.0) / line_total - 1.0


def roll(values, shift, axis):
    return pltpu.roll(values, shift % values.shape[axis], axis)


def matmul(left, right):
    return jnp.dot(
        left, right, precision=lax.Precision.HIGHEST, preferred_element_type=jnp.float32
    )


def lane_params(par):
    maps = par.shape[0]
    lane = iota((maps, LANES), 1)
    pick = ((lane % maps == iota((maps, LANES), 0)) & (lane < 6 * maps)).astype(jnp.float32)
    rows = lax.dot_general(
        par,
        pick,
        (((0,), (0,)), ((), ())),
        precision=lax.Precision.HIGHEST,
        preferred_element_type=jnp.float32,
    )
    group = iota((1, LANES), 1) // (2 * maps)
    first_term = (iota((1, LANES), 1) // maps) % 2 == 0

    def by_component(column, step):
        return jnp.where(
            group == 0,
            rows[column : column + 1],
            jnp.where(
                group == 1,
                rows[column + step : column + step + 1],
                rows[column + 2 * step : column + 2 * step + 1],
            ),
        )

    return {
        "sharpness": rows[3:4],
        "center_x": rows[0:1],
        "center_y": rows[1:2],
        "slope_x": jnp.where(first_term, by_component(4, 3), 0.0),
        "slope_y": jnp.where(first_term, by_component(5, 3), 0.0),
        "rest": jnp.where(first_term, by_component(13, 1), by_component(6, 3)),
    }


def side_factors(params, coord, center, slope):
    bump = jnp.exp(-params["sharpness"] * (coord - params[center]) ** 2)
    return bump, coord * params[slope]


def z_matrix(par, z_start, size_z, total_z):
    maps = par.shape[0]
    tall = jnp.concatenate([par[:, 2:4]] * (LANES // maps), axis=0)
    lane = iota((LANES, 2 * LANES), 1)
    position = jnp.where(
        lane < LANES, z_start + lane, jnp.where(lane == LANES, z_start + size_z, z_start - 1)
    )
    coord = coordinate(position, total_z)
    row = iota((LANES, 2 * LANES), 0)
    bump = jnp.exp(-tall[:, 1:2] * (coord - tall[:, 0:1]) ** 2)
    return jnp.where((row // maps) % 2 == 0, bump, bump * coord)


def component_part(values, maps, component):
    return jnp.where(iota(values.shape, 0) // (2 * maps) == component, values, 0.0)


def half_drift(left, right):
    return HALF_LIMIT * jnp.tanh(matmul(left, right))


def pack_rows(first, last):
    f2, l2 = first[:, LANES:], last[:, LANES:]
    lane = iota(f2.shape, 1)
    extra = jnp.where(
        lane == 0,
        f2,
        jnp.where(
            lane == 1, roll(f2, 2, 1), jnp.where(lane == 2, roll(l2, 2, 1), roll(l2, 4, 1))
        ),
    )
    return jnp.concatenate([first[:, :LANES], last[:, :LANES], extra], axis=0)


def unpack_rows(message, size_x):
    extra = message[2 * size_x :]
    lane = iota(extra.shape, 1)
    by_two, by_four = roll(extra, -2, 1), roll(extra, -4, 1)
    f2 = jnp.where(lane == LANES - 1, by_two, extra)
    l2 = jnp.where(lane == LANES - 1, by_four, by_two)
    return (
        jnp.concatenate([message[:size_x], f2], axis=1),
        jnp.concatenate([message[size_x : 2 * size_x], l2], axis=1),
    )


def merge_coefs(low, high):
    inverse = 1.0 / (1.0 - low[3] * high[0])
    onward, back = low[1] * inverse, high[2] * inverse
    return (
        low[0] + onward * high[0] * low[2],
        onward * high[1],
        back * low[2],
        high[3] + back * low[3] * high[1],
    )


def merge_values(low, high, low_values, high_values):
    inverse = 1.0 / (1.0 - low[3] * high[0])
    return (
        low_values[0] + low[1] * inverse * (high_values[0] + high[0] * low_values[1]),
        high_values[1] + high[2] * inverse * (low_values[1] + low[3] * high_values[0]),
    )


def chain(coefs, values, below, above):
    count = len(coefs)
    held, slope = below, None
    befores, firsts = [], []
    for j in range(count):
        a_first, c_first, a_last, c_last = coefs[j]
        r_first, r_last = values[j]
        befores.append((held, slope))
        if slope is None:
            first, first_slope = r_first + a_first * held, c_first
            held, slope = r_last + a_last * held, c_last
        else:
            inverse = 1.0 / (1.0 - a_first * slope)
            first = (r_first + a_first * held) * inverse
            first_slope = c_first * inverse
            held, slope = (
                r_last + a_last * (held + slope * first),
                c_last + a_last * slope * first_slope,
            )
        firsts.append((first, first_slope))
    seen_above = [None] * count
    seen_below = [None] * count
    upper = above
    for j in reversed(range(count)):
        seen_above[j] = upper
        upper = firsts[j][0] + firsts[j][1] * upper
        held, slope = befores[j]
        seen_below[j] = held if slope is None else held + slope * upper
    return seen_below, seen_above


def solve_x(up, down, source, pivot):
    size = source.shape[0]
    half = size // 2
    low_g, low_c, high_g, high_c = {}, {}, {}, {}
    g = c = None
    for i in range(half):
        if i == 0:
            weight = 1.0 / pivot
            c = down[1] * weight
            g = source[0] * weight
        else:
            weight = 1.0 / (pivot - up[i - 1] * c)
            g = (source[i] + up[i - 1] * g) * weight
            c = down[i + 1] * weight
        low_g[i], low_c[i] = g, c
    for i in reversed(range(half, size)):
        if i == size - 1:
            weight = 1.0 / pivot
            c = up[i - 1] * weight
            g = source[i] * weight
        else:
            weight = 1.0 / (pivot - down[i + 1] * c)
            g = (source[i] + down[i + 1] * g) * weight
            c = up[i - 1] * weight
        high_g[i], high_c[i] = g, c
    out = [None] * size
    inverse = 1.0 / (1.0 - low_c[half - 1] * high_c[half])
    out[half - 1] = (low_g[half - 1] + low_c[half - 1] * high_g[half]) * inverse
    out[half] = high_g[half] + high_c[half] * out[half - 1]
    for i in reversed(range(half - 1)):
        out[i] = low_g[i] + low_c[i] * out[i + 1]
    for i in range(half + 1, size):
        out[i] = high_g[i] + high_c[i] * out[i - 1]
    return out


def start_kernel(
    extent_y, extent_z, diffusion, par_ref, density, message, base, from_below, from_above, solved
):
    size_x, size_y, size_z = density.shape
    total_y, total_z = size_y * extent_y, size_z * extent_z
    y_start = lax.axis_index("gy") * size_y
    z_start = lax.axis_index("gz") * size_z
    maps = par_ref.shape[0]
    par = par_ref[...]
    params = lane_params(par)
    x_coord = coordinate(iota((size_x, LANES), 0), size_x)
    x_bump, x_part = side_factors(params, x_coord, "center_x", "slope_x")
    y_row = iota((size_y, LANES), 0)

    def y_factors(position):
        bump, part = side_factors(params, coordinate(position, total_y), "center_y", "slope_y")
        return bump, part + params["rest"]

    y_bump, y_part = y_factors(y_start + y_row)
    out_bump, out_part = y_factors(jnp.where(y_row == 0, y_start + size_y, y_start - 1))
    z_values = z_matrix(par, z_start, size_z, total_z)
    parts = [component_part(z_values, maps, c) for c in range(3)]
    d0, d1, d2 = diffusion[0], diffusion[1], diffusion[2]

    def rows_by_x(bump, part):
        return jnp.concatenate(
            [
                (x_bump[i : i + 1] * bump) * (x_part[i : i + 1] + part)
                for i in range(size_x)
            ],
            axis=0,
        )

    right = jnp.concatenate([parts[0], parts[1][:, :LANES], parts[2][:, :LANES]], axis=1)
    drifts = half_drift(rows_by_x(y_bump, y_part), right)
    out_drift = half_drift(rows_by_x(out_bump, out_part), parts[0][:, :LANES])

    def block(columns):
        return drifts[:, columns * LANES : (columns + 1) * LANES].reshape(size_x, size_y, LANES)

    drift_x, plane_drift, drift_y, drift_z = block(0), block(1), block(2), block(3)
    out_drift = out_drift.reshape(size_x, size_y, LANES)
    rho = density[...]
    zero = jnp.zeros((1, size_y, LANES), jnp.float32)
    up, down = (d0 + drift_x) * rho, (d0 - drift_x) * rho
    total = (
        jnp.concatenate([zero, up[:-1]], axis=0)
        + jnp.concatenate([down[1:], zero], axis=0)
        - (2.0 * (d0 + d1 + d2)) * rho
    )
    sublane = iota((size_x, size_y, LANES), 1)
    lane = iota((size_x, size_y, LANES), 2)
    up, down = roll((d1 + drift_y) * rho, 1, 1), roll((d1 - drift_y) * rho, -1, 1)
    at_low, at_high = sublane == 0, sublane == size_y - 1
    row_source = jnp.where(at_low, up, jnp.where(at_high, down, 0.0))
    total = total + jnp.where(at_low, 0.0, up) + jnp.where(at_high, 0.0, down)
    up, down = roll((d2 + drift_z) * rho, 1, 2), roll((d2 - drift_z) * rho, -1, 2)
    at_low, at_high = lane == 0, lane == size_z - 1
    plane_source = jnp.where(at_low, up, jnp.where(at_high, down, 0.0))
    total = total + jnp.where(at_low, 0.0, up) + jnp.where(at_high, 0.0, down)

    source = jnp.concatenate([total, row_source, plane_source], axis=1)
    drift = jnp.concatenate([drift_x, out_drift, plane_drift], axis=1)
    ups, downs = d0 + drift, d0 - drift
    answers = solve_x(ups, downs, source, 1.0 + 2.0 * d0)
    for i in range(size_x):
        solved[i] = answers[i]

    def rows_by_y(position):
        row = iota((1, LANES), 0)
        bump, part = y_factors(row + position)
        return (x_bump * bump) * (x_part + part)

    left = jnp.concatenate([rows_by_y(y_start + j) for j in range(-1, size_y + 1)], axis=0)
    line_drift = half_drift(left, parts[1]).reshape(size_y + 2, size_x, 2 * LANES)
    pivot = 1.0 + 2.0 * d1
    at_start = y_start == 0
    at_end = y_start + size_y == total_y
    g = a = c = None
    gs, as_, cs = [], [], []
    for j in range(size_y):
        value = jnp.concatenate([solved[:, j, :], solved[:, 2 * size_y + j, :]], axis=1)
        lower = d1 + line_drift[j]
        upper = d1 - line_drift[j + 2]
        if j == 0:
            lower = jnp.where(at_start, 0.0, lower)
        if j == size_y - 1:
            upper = jnp.where(at_end, 0.0, upper)
        if j == 0:
            weight = 1.0 / pivot
            g, a = value * weight, lower * weight
        else:
            weight = 1.0 / (pivot - lower * c)
            g, a = (value + lower * g) * weight, lower * a * weight
        c = upper * weight
        gs.append(g)
        as_.append(a)
        cs.append(c)
    base[size_y - 1], from_below[size_y - 1], from_above[size_y - 1] = g, a, c
    r_last = g
    for j in reversed(range(size_y - 1)):
        g, a, c = gs[j] + cs[j] * g, as_[j] + cs[j] * a, cs[j] * c
        base[j], from_below[j], from_above[j] = g, a, c
    pushed_up = solved[:, size_y, :] / (d1 + line_drift[size_y][:, :LANES])
    pushed_down = solved[:, 2 * size_y - 1, :] / (d1 - line_drift[1][:, :LANES])
    blank = jnp.zeros_like(pushed_up)
    message[...] = pack_rows(
        g + jnp.concatenate([pushed_down, blank], axis=1),
        r_last + jnp.concatenate([pushed_up, blank], axis=1),
    )


def line_kernel(extent_y, extent_z, size_x, size_y, size_z, diffusion, par_ref, coefs, drifts):
    total_y, total_z = size_y * extent_y, size_z * extent_z
    z_start = lax.axis_index("gz") * size_z
    maps = par_ref.shape[0]
    par = par_ref[...]
    params = lane_params(par)
    x_coord = coordinate(iota((size_x, LANES), 0), size_x)
    x_bump, x_part = side_factors(params, x_coord, "center_x", "slope_x")
    right = component_part(z_matrix(par, z_start, size_z, total_z), maps, 1)
    d1 = diffusion[1]
    pivot = 1.0 + 2.0 * d1

    @pl.loop(0, extent_y)
    def _(number):
        rows = []
        for j in range(size_y):
            position = iota((1, LANES), 0) + (number * size_y + j)
            bump, part = side_factors(
                params, coordinate(position, total_y), "center_y", "slope_y"
            )
            rows.append((x_bump * bump) * (x_part + (part + params["rest"])))
        drift = half_drift(jnp.concatenate(rows, axis=0), right)
        drifts[pl.ds(number * size_y + 1, size_y)] = drift.reshape(size_y, size_x, 2 * LANES)

    drifts[0] = jnp.full((size_x, 2 * LANES), -d1, jnp.float32)
    drifts[total_y + 1] = jnp.full((size_x, 2 * LANES), d1, jnp.float32)

    @pl.loop(0, extent_y)
    def _(number):
        start = number * size_y
        weight = 1.0 / pivot
        a_first = (d1 + drifts[start]) * weight
        c_first = (d1 - drifts[start + 2]) * weight
        a_last, c_last = a_first, c_first
        for j in range(1, size_y):
            lower = d1 + drifts[start + j]
            upper = d1 - drifts[start + j + 2]
            weight = 1.0 / (pivot - lower * c_last)
            step, c_last = lower * weight, upper * weight
            a_last = step * a_last
            a_first = a_first + c_first * a_last
            c_first = c_first * c_last
        coefs[number, 0] = a_first
        coefs[number, 1] = c_first
        coefs[number, 2] = a_last
        coefs[number, 3] = c_last


def z_coef_kernel(
    extent_y, extent_z, size_x, size_y, size_z, diffusion, par_ref, steps, ends, pushes, packed
):
    total_y, total_z = size_y * extent_y, size_z * extent_z
    y_start = lax.axis_index("gy") * size_y
    z_start = lax.axis_index("gz") * size_z
    maps = par_ref.shape[0]
    par = par_ref[...]
    params = lane_params(par)
    x_coord = coordinate(iota((size_x, LANES), 0), size_x)
    x_bump, x_part = side_factors(params, x_coord, "center_x", "slope_x")
    right = component_part(z_matrix(par, z_start, size_z, total_z), maps, 2)
    d2 = diffusion[2]
    scale = 1.0 / (1.0 + 2.0 * d2)
    rows = []
    for j in range(size_y):
        position = iota((1, LANES), 0) + (y_start + j)
        bump, part = side_factors(params, coordinate(position, total_y), "center_y", "slope_y")
        rows.append((x_bump * bump) * (x_part + (part + params["rest"])))
    drift = half_drift(jnp.concatenate(rows, axis=0), right)
    inner, outer = drift[:, :LANES], drift[:, LANES:]
    lane = iota(inner.shape, 1)
    low, high = lane == 0, lane == size_z - 1
    before, after = roll(inner, 1, 1), roll(inner, -1, 1)
    pushes[...] = (1.0 / jnp.where(low, d2 + before, d2 - after)).reshape(pushes.shape)
    before = jnp.where(low, roll(outer, 1, 1), before)
    after = jnp.where(high, roll(outer, -1, 1), after)
    below = jnp.where(low & (z_start == 0), 0.0, (d2 + before) * scale)
    above = jnp.where(high & (z_start + size_z == total_z), 0.0, (d2 - after) * scale)
    stride, level = 1, 0
    while stride < size_z:
        low, high = lane < stride, lane >= size_z - stride
        low_a = jnp.where(low, 1.0, roll(below, stride, 1))
        low_c = jnp.where(low, 0.0, roll(above, stride, 1))
        high_a = jnp.where(high, 0.0, roll(below, -stride, 1))
        high_c = jnp.where(high, 1.0, roll(above, -stride, 1))
        inverse = 1.0 / (1.0 - below * low_c - above * high_a)
        below, above = below * inverse, above * inverse
        factor = scale if level == 0 else 1.0
        steps[level, 0] = (inverse * factor).reshape(pushes.shape)
        steps[level, 1] = jnp.where(low, 0.0, below * factor).reshape(pushes.shape)
        steps[level, 2] = jnp.where(high, 0.0, above * factor).reshape(pushes.shape)
        below, above = below * low_a, above * high_c
        stride, level = stride * 2, level + 1
    ends[0] = below.reshape(pushes.shape)
    ends[1] = above.reshape(pushes.shape)
    packed[...] = pack_ends(
        [ends[0, j] for j in range(size_y)], 1, size_y
    ) + pack_ends([ends[1, j] for j in range(size_y)], 2, size_y)


def pack_ends(rows, slot, size_y):
    shape = rows[0].shape
    lane = iota(shape, 1)
    out = jnp.zeros(shape, jnp.float32)
    for j in range(size_y):
        first = slot * 2 * size_y + j
        last = first + size_y
        out = jnp.where(lane == first, roll(rows[j], first, 1), out)
        out = jnp.where(lane == last, roll(rows[j], last - (LANES - 1), 1), out)
    return out


def gather_members(refs, own, count):
    held = [ref[...] for ref in refs]
    return [
        functools.reduce(
            lambda acc, s: jnp.where((own ^ s) == j, held[s], acc), range(1, count), held[0]
        )
        for j in range(count)
    ]


def merge_kernel(stride, radix, size_x, coefs, *refs):
    received, message = refs[:radix], refs[radix]
    digit = lax.rem(lax.div(lax.axis_index("gy"), stride), radix)
    first = lax.div(lax.axis_index("gy"), stride) - digit
    values = [unpack_rows(m, size_x) for m in gather_members(received, digit, radix)]
    group = [tuple(coefs[first + j, q] for q in range(4)) for j in range(radix)]
    merged, total = group[0], values[0]
    for j in range(1, radix):
        total = merge_values(merged, group[j], total, values[j])
        merged = merge_coefs(merged, group[j])
    message[...] = pack_rows(*total)


def group_kernel(radix, coefs, merged):
    @pl.loop(0, merged.shape[0])
    def _(number):
        total = tuple(coefs[number * radix, q] for q in range(4))
        for j in range(1, radix):
            total = merge_coefs(total, tuple(coefs[number * radix + j, q] for q in range(4)))
        for q in range(4):
            merged[number, q] = total[q]


def middle_kernel(levels, size_x, *refs):
    refs = list(refs)
    steps, pushes, packed, base, from_below, from_above = refs[:6]
    refs = refs[6:]
    inputs = []
    for stride, radix in levels:
        inputs.append((refs[0], refs[1 : 1 + radix]))
        refs = refs[1 + radix :]
    message, doubled, seen = refs
    size_y = base.shape[0]
    below = above = jnp.zeros((size_x, 2 * LANES), jnp.float32)
    for (stride, radix), (coefs, received) in zip(reversed(levels), reversed(inputs)):
        digit = lax.rem(lax.div(lax.axis_index("gy"), stride), radix)
        first = lax.div(lax.axis_index("gy"), stride) - digit
        values = [unpack_rows(m, size_x) for m in gather_members(received, digit, radix)]
        group = [tuple(coefs[first + j, q] for q in range(4)) for j in range(radix)]
        lows, highs = chain(group, values, below, above)
        for j in range(radix):
            seen[j, 0] = lows[j]
            seen[j, 1] = highs[j]
        below, above = seen[digit, 0], seen[digit, 1]
    inner, outer = [], []
    for j in range(size_y):
        value = base[j] + from_below[j] * below + from_above[j] * above
        inner.append(value[:, :LANES])
        outer.append(value[:, LANES:] * pushes[j])
    values = jnp.stack(inner)
    stride, level = 1, 0
    while stride < LANES:
        values = (
            steps[level, 0] * values
            + steps[level, 1] * roll(values, stride, 2)
            + steps[level, 2] * roll(values, -stride, 2)
        )
        stride, level = stride * 2, level + 1
    doubled[...] = values
    lane = iota(inner[0].shape, 1)
    rows = []
    for j in range(size_y):
        rows.append(
            values[j]
            + jnp.where(
                lane == 0,
                roll(outer[j], 1, 1),
                jnp.where(lane == LANES - 1, roll(outer[j], -1, 1), 0.0),
            )
        )
    message[...] = pack_ends(rows, 0, size_y) + packed[...]


def merge_z(low, high):
    inverse = 1.0 / (1.0 - low[5] * high[2])
    onward, back = low[4] * inverse, high[3] * inverse
    return (
        low[0] + onward * (high[0] + high[2] * low[1]),
        high[1] + back * (low[1] + low[5] * high[0]),
        low[2] + onward * high[2] * low[3],
        back * low[3],
        onward * high[4],
        high[5] + back * low[5] * high[4],
    )


def unpack_ends(message, size_y):
    return tuple(message if s == 0 else roll(message, -s * size_y, 1) for s in range(6))


def merge_z_kernel(stride, radix, size_y, *refs):
    received, message = refs[:radix], refs[radix]
    digit = lax.rem(lax.div(lax.axis_index("gz"), stride), radix)
    members = [unpack_ends(m, size_y) for m in gather_members(received, digit, radix)]
    total = functools.reduce(merge_z, members)
    lane = iota(total[0].shape, 1)
    out = jnp.zeros(total[0].shape, jnp.float32)
    for s in range(6):
        shifted = total[s] if s == 0 else roll(total[s], s * size_y, 1)
        out = jnp.where(lane // size_y == s, shifted, out)
    message[...] = out


def end_kernel(levels, density, doubled, ends, *refs):
    refs = list(refs)
    inputs = []
    for stride, radix in levels:
        inputs.append(refs[:radix])
        refs = refs[radix:]
    out, seen = refs
    size_x, size_y, _ = density.shape
    below = above = jnp.zeros((size_x, LANES), jnp.float32)
    for (stride, radix), received in zip(reversed(levels), reversed(inputs)):
        digit = lax.rem(lax.div(lax.axis_index("gz"), stride), radix)
        members = [unpack_ends(m, size_y) for m in gather_members(received, digit, radix)]
        lows, highs = chain(
            [(m[2], m[4], m[3], m[5]) for m in members],
            [(m[0], m[1]) for m in members],
            below,
            above,
        )
        for j in range(radix):
            seen[j, 0] = lows[j]
            seen[j, 1] = highs[j]
        below, above = seen[digit, 0], seen[digit, 1]
    for j in range(size_y):
        out[:, j, :] = (
            density[:, j, :]
            + doubled[j]
            + ends[0, j] * below[:, j : j + 1]
            + ends[1, j] * above[:, j : j + 1]
        )


def radices(extent):
    rounds, stride = [], 1
    while stride < extent:
        left = extent // stride
        power = left.bit_length() - 1
        radix = 4 if left % 4 == 0 and power % 2 == 0 else 2
        rounds.append((stride, radix))
        stride *= radix
    return rounds


def exchange(message, axis, stride, radix):
    devices = range(lax.axis_size(axis))
    return [message] + [
        lax.ppermute(message, axis, [(i, i ^ (s * stride)) for i in devices])
        for s in range(1, radix)
    ]


def body(density, diffusion, centers, sharpness, affine, offsets):
    size_x, size_y, size_z = density.shape
    extent_y, extent_z = lax.axis_size("gy"), lax.axis_size("gz")
    sizes = (extent_y, extent_z, size_x, size_y, size_z)
    maps = centers.shape[0]
    wide = (size_y, size_x, 2 * LANES)
    narrow = (size_y, size_x, LANES)
    float32 = jnp.float32

    def shape(*dims):
        return jax.ShapeDtypeStruct(dims, float32)

    vmem = pl.BlockSpec(memory_space=pltpu.VMEM)
    smem = pl.BlockSpec(memory_space=pltpu.SMEM)

    def call(kernel, inputs, outputs, in_specs=None, scratch=(), flops=10**6):
        return pl.pallas_call(
            kernel,
            out_shape=outputs,
            in_specs=in_specs or [vmem] * len(inputs),
            out_specs=jax.tree.map(lambda _: vmem, outputs),
            scratch_shapes=list(scratch),
            compiler_params=pltpu.CompilerParams(vmem_limit_bytes=VMEM_LIMIT),
            cost_estimate=pl.CostEstimate(flops=flops, bytes_accessed=10**6, transcendentals=0),
        )(*inputs)

    par = jnp.concatenate(
        [centers, sharpness[:, None], affine.reshape(maps, 9), offsets], axis=1
    )
    message, base, from_below, from_above = call(
        functools.partial(start_kernel, extent_y, extent_z),
        (diffusion, par, density),
        (shape(3 * size_x, LANES), shape(*wide), shape(*wide), shape(*wide)),
        [smem, vmem, vmem],
        [pltpu.VMEM((size_x, 3 * size_y, LANES), float32)],
    )
    total_y = extent_y * size_y
    coefs = call(
        functools.partial(line_kernel, *sizes),
        (diffusion, par),
        shape(extent_y, 4, size_x, 2 * LANES),
        [smem, vmem],
        [pltpu.VMEM((total_y + 2, size_x, 2 * LANES), float32)],
    )
    doublings = size_z.bit_length() - 1
    steps, ends, pushes, packed = call(
        functools.partial(z_coef_kernel, *sizes),
        (diffusion, par),
        (shape(doublings, 3, *narrow), shape(2, *narrow), shape(*narrow), shape(size_x, LANES)),
        [smem, vmem],
    )
    y_levels, z_levels = radices(extent_y), radices(extent_z)
    line_inputs = []
    for number, (stride, radix) in enumerate(y_levels):
        received = exchange(message, "gy", stride, radix)
        line_inputs += [coefs] + received
        if number + 1 < len(y_levels):
            message = call(
                functools.partial(merge_kernel, stride, radix, size_x),
                [coefs] + received,
                shape(3 * size_x, LANES),
            )
            coefs = call(
                functools.partial(group_kernel, radix),
                [coefs],
                shape(extent_y // (stride * radix), 4, size_x, 2 * LANES),
            )
    message, doubled = call(
        functools.partial(middle_kernel, y_levels, size_x),
        [steps, pushes, packed, base, from_below, from_above] + line_inputs,
        (shape(size_x, LANES), shape(*narrow)),
        scratch=[pltpu.VMEM((4, 2, size_x, 2 * LANES), float32)],
    )
    end_inputs = []
    for number, (stride, radix) in enumerate(z_levels):
        received = exchange(message, "gz", stride, radix)
        end_inputs += received
        if number + 1 < len(z_levels):
            message = call(
                functools.partial(merge_z_kernel, stride, radix, size_y),
                received,
                shape(size_x, LANES),
            )
    return call(
        functools.partial(end_kernel, z_levels),
        [density, doubled, ends] + end_inputs,
        shape(size_x, size_y, size_z),
        scratch=[pltpu.VMEM((4, 2, size_x, LANES), float32)],
    )


def solution(mesh):
    placed = (P(None, "gy", "gz"), P(), P(), P(), P(), P())
    return jax.shard_map(
        body, mesh=mesh, in_specs=placed, out_specs=P(None, "gy", "gz"), check_vma=False
    )
```

```python
import functools

import jax
import jax.numpy as jnp
from jax import lax
from jax.experimental import pallas as pl
from jax.experimental.pallas import tpu as pltpu
from jax.sharding import PartitionSpec as P

HALF_LIMIT = 600.0
LANES = 128
ROWS = 8
VMEM_LIMIT = 48 * 1024 * 1024


def iota(shape, axis):
    return lax.broadcasted_iota(jnp.int32, shape, axis)


def coordinate(positions, line_total):
    return (2.0 * positions.astype(jnp.float32) + 1.0) / line_total - 1.0


def roll(values, shift, axis):
    return pltpu.roll(values, shift % values.shape[axis], axis)


def matmul(left, right):
    return lax.dot_general(
        left,
        right,
        (((1,), (1,)), ((), ())),
        precision=lax.Precision.HIGHEST,
        preferred_element_type=jnp.float32,
    )


def half_drift(left, right):
    return HALF_LIMIT * jnp.tanh(matmul(left, right))


SHARPNESS, CENTER, SLOPE, OFFSET, DIFFUSION, PREPARED = 0, 1, 4, 7, 8, 16


def component_of(maps):
    return iota((1, LANES), 1) // (2 * maps)


def first_term(maps):
    return (iota((1, LANES), 1) // maps) % 2 == 0


def bump(params, coord, axis):
    center = params[CENTER + axis : CENTER + axis + 1]
    return jnp.exp(-params[SHARPNESS : SHARPNESS + 1] * (coord - center) ** 2)


def slope(params, coord, axis):
    return coord * params[SLOPE + axis : SLOPE + axis + 1]


def x_factors(params, maps, size_x):
    coord = coordinate(iota((size_x, LANES), 0), size_x)
    return bump(params, coord, 0), jnp.where(first_term(maps), slope(params, coord, 0), 0.0)


def y_factors(params, maps, position, total_y):
    coord = coordinate(position, total_y)
    part = slope(params, coord, 1) + params[OFFSET : OFFSET + 1]
    return bump(params, coord, 1), jnp.where(
        first_term(maps), part, params[SLOPE + 2 : SLOPE + 3]
    )


def z_rows(params, maps, position, total_z):
    coord = coordinate(position, total_z)
    return bump(params, coord, 2) * jnp.where(first_term(maps), 1.0, coord)


def inner_z_rows(params, maps, z_start, size_z, total_z):
    return z_rows(params, maps, z_start + iota((size_z, LANES), 0), total_z)


def outer_z_rows(params, maps, z_start, size_z, total_z):
    row = iota((size_z, LANES), 0)
    return z_rows(
        params, maps, jnp.where(row == 0, z_start + size_z, z_start - 1), total_z
    )


def only(rows, maps, component):
    return jnp.where(component_of(maps) == component, rows, 0.0)


def y_rows(params, maps, position, total_y):
    coord = coordinate(position, total_y)
    part = slope(params, coord, 1) + params[OFFSET : OFFSET + 1]
    return bump(params, coord, 1) * jnp.where(first_term(maps), part, 1.0)


def xz_rows(params, maps, size_x, z_start, size_z, total_z):
    row = iota((2 * size_x, LANES), 0)
    x_coord = coordinate(row // 2, size_x)
    z_coord = coordinate(jnp.where(row % 2 == 0, z_start - 1, z_start + size_z), total_z)
    part = slope(params, x_coord, 0) + slope(params, z_coord, 2)
    both = bump(params, x_coord, 0) * bump(params, z_coord, 2)
    both = both * jnp.where(first_term(maps), 1.0, part)
    return jnp.concatenate(
        [both, jnp.zeros((LANES - 2 * size_x, LANES), jnp.float32)], axis=0
    )


def with_extra(main, row):
    return jnp.concatenate([main, jnp.broadcast_to(row, (ROWS, LANES))], axis=0)


def pack_planes(planes):
    lane = iota(planes[0].shape, 1)
    out = jnp.zeros(planes[0].shape, jnp.float32)
    for i, plane in enumerate(planes):
        out = jnp.where(lane // 2 == i, roll(plane, 2 * i + 1, 1), out)
    return out


def merge_coefs(low, high):
    inverse = 1.0 / (1.0 - low[3] * high[0])
    onward, back = low[1] * inverse, high[2] * inverse
    return (
        low[0] + onward * high[0] * low[2],
        onward * high[1],
        back * low[2],
        high[3] + back * low[3] * high[1],
    )


def merge_values(low, high, low_values, high_values):
    inverse = 1.0 / (1.0 - low[3] * high[0])
    return (
        low_values[0] + low[1] * inverse * (high_values[0] + high[0] * low_values[1]),
        high_values[1] + high[2] * inverse * (low_values[1] + low[3] * high_values[0]),
    )


def chain(coefs, values, below, above):
    count = len(coefs)
    held, slope = below, None
    befores, firsts = [], []
    for j in range(count):
        a_first, c_first, a_last, c_last = coefs[j]
        r_first, r_last = values[j]
        befores.append((held, slope))
        if slope is None:
            first, first_slope = r_first + a_first * held, c_first
            held, slope = r_last + a_last * held, c_last
        else:
            inverse = 1.0 / (1.0 - a_first * slope)
            first = (r_first + a_first * held) * inverse
            first_slope = c_first * inverse
            held, slope = (
                r_last + a_last * (held + slope * first),
                c_last + a_last * slope * first_slope,
            )
        firsts.append((first, first_slope))
    seen_above = [None] * count
    seen_below = [None] * count
    upper = above
    for j in reversed(range(count)):
        seen_above[j] = upper
        upper = firsts[j][0] + firsts[j][1] * upper
        held, slope = befores[j]
        seen_below[j] = held if slope is None else held + slope * upper
    return seen_below, seen_above


def solve_x(up, down, source, pivot):
    size = source.shape[0]
    half = size // 2
    low_g, low_c, high_g, high_c = {}, {}, {}, {}
    g = c = None
    for i in range(half):
        if i == 0:
            weight = 1.0 / pivot
            c = down[1] * weight
            g = source[0] * weight
        else:
            weight = 1.0 / (pivot - up[i - 1] * c)
            g = (source[i] + up[i - 1] * g) * weight
            c = down[i + 1] * weight
        low_g[i], low_c[i] = g, c
    for i in reversed(range(half, size)):
        if i == size - 1:
            weight = 1.0 / pivot
            c = up[i - 1] * weight
            g = source[i] * weight
        else:
            weight = 1.0 / (pivot - down[i + 1] * c)
            g = (source[i] + down[i + 1] * g) * weight
            c = up[i - 1] * weight
        high_g[i], high_c[i] = g, c
    out = [None] * size
    inverse = 1.0 / (1.0 - low_c[half - 1] * high_c[half])
    out[half - 1] = (low_g[half - 1] + low_c[half - 1] * high_g[half]) * inverse
    out[half] = high_g[half] + high_c[half] * out[half - 1]
    for i in reversed(range(half - 1)):
        out[i] = low_g[i] + low_c[i] * out[i + 1]
    for i in range(half + 1, size):
        out[i] = high_g[i] + high_c[i] * out[i - 1]
    return out


def start_kernel(
    extent_y,
    extent_z,
    density_hbm,
    diffusion_hbm,
    centers_hbm,
    sharpness_hbm,
    affine_hbm,
    offsets_hbm,
    message,
    base,
    from_below,
    from_above,
    drift_z_out,
    prepared,
    solved,
    drift_y_held,
    density,
    diffusion,
    centers,
    sharpness,
    affine,
    offsets,
    staged,
    semaphores,
):
    copies = [
        pltpu.make_async_copy(source, target, semaphores.at[number])
        for number, (source, target) in enumerate(
            [
                (diffusion_hbm, diffusion),
                (centers_hbm, centers),
                (sharpness_hbm, sharpness),
                (affine_hbm, affine),
                (offsets_hbm, offsets),
                (density_hbm, density),
            ]
        )
    ]
    for copy in copies:
        copy.start()
    size_x, size_y, size_z = density.shape
    total_y, total_z = size_y * extent_y, size_z * extent_z
    y_start = lax.axis_index("gy") * size_y
    z_start = lax.axis_index("gz") * size_z
    maps = centers.shape[1]
    for copy in copies[:-1]:
        copy.wait()

    staged[...] = jnp.zeros(staged.shape, jnp.float32)
    staged[0:1, :maps] = sharpness[...]
    staged[1:4, :maps] = centers[...]
    for c in range(3):
        staged[4 + 3 * c : 7 + 3 * c, :maps] = affine[c]
    staged[13:16, :maps] = offsets[...]
    rows = staged[...]
    width = maps
    while width < LANES:
        rows = rows + roll(rows, width, 1)
        width = 2 * width
    component = component_of(maps)
    rows = jnp.where(component < 3, rows, 0.0)

    def by_component(first, step):
        return jnp.where(
            component == 0,
            rows[first : first + 1],
            jnp.where(
                component == 1,
                rows[first + step : first + step + 1],
                rows[first + 2 * step : first + 2 * step + 1],
            ),
        )

    weights = [jnp.broadcast_to(diffusion[:, c : c + 1], (1, LANES)) for c in range(3)]
    params = jnp.concatenate(
        [rows[0:4]]
        + [by_component(4 + j, 3) for j in range(3)]
        + [by_component(13, 1)]
        + weights
        + [jnp.zeros((PREPARED - DIFFUSION - 3, LANES), jnp.float32)],
        axis=0,
    )
    prepared[...] = params
    d0, d1, d2 = weights

    x_bump, x_part = x_factors(params, maps, size_x)
    y_row = iota((size_y, LANES), 0)
    y_bump, y_part = y_factors(params, maps, y_start + y_row, total_y)
    out_bump, out_part = y_factors(
        params, maps, jnp.where(y_row == 0, y_start + size_y, y_start - 1), total_y
    )
    inner = inner_z_rows(params, maps, z_start, size_z, total_z)
    outer = outer_z_rows(params, maps, z_start, size_z, total_z)
    inner = [only(inner, maps, c) for c in range(3)]
    outer = only(outer, maps, 0)

    def rows_by_x(bumps, part):
        return jnp.concatenate(
            [(x_bump[i : i + 1] * bumps) * (x_part[i : i + 1] + part) for i in range(size_x)],
            axis=0,
        )

    right = jnp.concatenate([inner[0], outer, inner[1], inner[2]], axis=0)
    drifts = half_drift(rows_by_x(y_bump, y_part), right)
    out_drift = half_drift(rows_by_x(out_bump, out_part), inner[0])

    def block(number):
        columns = drifts[:, number * LANES : (number + 1) * LANES]
        return columns.reshape(size_x, size_y, LANES)

    drift_x, plane_drift, drift_y, drift_z = block(0), block(1), block(2), block(3)
    out_drift = out_drift.reshape(size_x, size_y, LANES)
    drift_y_held[...] = drift_y
    drift_z_out[...] = drift_z
    copies[-1].wait()
    rho = density[...]
    zero = jnp.zeros((1, size_y, LANES), jnp.float32)
    up, down = (d0 + drift_x) * rho, (d0 - drift_x) * rho
    total = (
        jnp.concatenate([zero, up[:-1]], axis=0)
        + jnp.concatenate([down[1:], zero], axis=0)
        - (2.0 * (d0 + d1 + d2)) * rho
    )
    sublane = iota((size_x, size_y, LANES), 1)
    lane = iota((size_x, size_y, LANES), 2)
    up, down = roll((d1 + drift_y) * rho, 1, 1), roll((d1 - drift_y) * rho, -1, 1)
    at_low, at_high = sublane == 0, sublane == size_y - 1
    row_source = jnp.where(at_low, up, jnp.where(at_high, down, 0.0))
    total = total + jnp.where(at_low, 0.0, up) + jnp.where(at_high, 0.0, down)
    up, down = roll((d2 + drift_z) * rho, 1, 2), roll((d2 - drift_z) * rho, -1, 2)
    at_low, at_high = lane == 0, lane == size_z - 1
    plane_source = jnp.where(at_low, up, jnp.where(at_high, down, 0.0))
    total = total + jnp.where(at_low, 0.0, up) + jnp.where(at_high, 0.0, down)

    source = jnp.concatenate([total, row_source, plane_source], axis=1)
    drift = jnp.concatenate([drift_x, out_drift, plane_drift], axis=1)
    answers = solve_x(d0 + drift, d0 - drift, source, 1.0 + 2.0 * d0)
    for i in range(size_x):
        solved[i] = answers[i][: 2 * size_y]
    planes = pack_planes([answer[2 * size_y :] for answer in answers])

    row = iota((1, LANES), 0)
    out_rows = []
    for position in (y_start - 1, y_start + size_y):
        bumps, part = y_factors(params, maps, row + position, total_y)
        out_rows.append((x_bump * bumps) * (x_part + part))
    ends = half_drift(jnp.concatenate(out_rows, axis=0), inner[1])
    position = y_start - 1 + iota((2 * ROWS, LANES), 0)
    extra = half_drift(
        y_rows(params, maps, position, total_y),
        only(xz_rows(params, maps, size_x, z_start, size_z, total_z), maps, 1),
    )
    line_drift = (
        [ends[:size_x]]
        + [drift_y_held[:, j, :] for j in range(size_y)]
        + [ends[size_x:]]
    )
    line_drift = [with_extra(line_drift[j], extra[j : j + 1]) for j in range(size_y + 2)]
    pivot = 1.0 + 2.0 * d1
    at_start = y_start == 0
    at_end = y_start + size_y == total_y
    g = a = c = None
    gs, as_, cs = [], [], []
    for j in range(size_y):
        value = with_extra(solved[:, j, :], planes[j : j + 1])
        lower = d1 + line_drift[j]
        upper = d1 - line_drift[j + 2]
        if j == 0:
            lower = jnp.where(at_start, 0.0, lower)
        if j == size_y - 1:
            upper = jnp.where(at_end, 0.0, upper)
        if j == 0:
            weight = 1.0 / pivot
            g, a = value * weight, lower * weight
        else:
            weight = 1.0 / (pivot - lower * c)
            g, a = (value + lower * g) * weight, lower * a * weight
        c = upper * weight
        gs.append(g)
        as_.append(a)
        cs.append(c)
    base[size_y - 1], from_below[size_y - 1], from_above[size_y - 1] = g, a, c
    r_last = g
    for j in reversed(range(size_y - 1)):
        g, a, c = gs[j] + cs[j] * g, as_[j] + cs[j] * a, cs[j] * c
        base[j], from_below[j], from_above[j] = g, a, c
    pushed_up = solved[:, size_y, :] / (d1 + line_drift[size_y][:size_x])
    pushed_down = solved[:, 2 * size_y - 1, :] / (d1 - line_drift[1][:size_x])
    blank = jnp.zeros((1, LANES), jnp.float32)
    width = size_x + ROWS
    message[:width] = g + with_extra(pushed_down, blank)
    message[width:] = r_last + with_extra(pushed_up, blank)


def line_coefs(params, maps, sizes, start, count, store):
    extent_y, extent_z, size_x, size_y, size_z = sizes
    total_y, total_z = size_y * extent_y, size_z * extent_z
    z_start = lax.axis_index("gz") * size_z
    d1 = params[DIFFUSION + 1 : DIFFUSION + 2]
    x_bump, x_part = x_factors(params, maps, size_x)
    inner = only(inner_z_rows(params, maps, z_start, size_z, total_z), maps, 1)
    planes = only(xz_rows(params, maps, size_x, z_start, size_z, total_z), maps, 1)
    whole = count == extent_y
    offsets = list(range(size_y)) if whole else list(range(-1, size_y + 1))
    left, left_extra = [], []
    for j in offsets:
        for b in range(count):
            position = iota((1, LANES), 0) + ((start + b) * size_y + j)
            bumps, part = y_factors(params, maps, position, total_y)
            left.append((x_bump * bumps) * (x_part + part))
        block = iota((max(count, ROWS), LANES), 0)
        left_extra.append(
            y_rows(params, maps, (start + block) * size_y + j, total_y)
        )
    depth = left_extra[0].shape[0]
    main = half_drift(jnp.concatenate(left, axis=0), inner)
    main = main.reshape(len(offsets), count, size_x, LANES)
    main = [main[j] for j in range(len(offsets))]
    extra = half_drift(jnp.concatenate(left_extra, axis=0), planes)
    extra = [extra[j * depth : (j + 1) * depth] for j in range(len(offsets))]
    if whole:
        main = (
            [jnp.concatenate([main[-1][:1], main[-1][:-1]], axis=0)]
            + main
            + [jnp.concatenate([main[0][1:], main[0][-1:]], axis=0)]
        )
        extra = [roll(extra[-1], 1, 0)] + extra + [roll(extra[0], -1, 0)]
    numbers = start + iota((depth, LANES), 0)
    pivot = 1.0 + 2.0 * d1
    at_start, at_end = numbers == 0, numbers == extent_y - 1

    def scan(drifts, starts, ends):
        a_first = c_first = a_last = c_last = None
        for j in range(size_y):
            lower, upper = d1 + drifts[j], d1 - drifts[j + 2]
            if j == 0:
                lower = starts(lower)
            if j == size_y - 1:
                upper = ends(upper)
            if j == 0:
                weight = 1.0 / pivot
                a_first, c_first = lower * weight, upper * weight
                a_last, c_last = a_first, c_first
            else:
                weight = 1.0 / (pivot - lower * c_last)
                step, c_last = lower * weight, upper * weight
                a_last = step * a_last
                a_first = a_first + c_first * a_last
                c_first = c_first * c_last
        return a_first, c_first, a_last, c_last

    def masked(values, number):
        return jnp.concatenate(
            [
                jnp.where(start + b == number, 0.0, values[b])[None]
                for b in range(count)
            ],
            axis=0,
        )

    main = scan(main, lambda v: masked(v, 0), lambda v: masked(v, extent_y - 1))
    extra = scan(
        extra,
        lambda v: jnp.where(at_start, 0.0, v),
        lambda v: jnp.where(at_end, 0.0, v),
    )
    for b in range(count):
        for q in range(4):
            store(b, q, with_extra(main[q][b], extra[q][b : b + 1]))


def near_kernel(sizes, maps, stride, radix, prepared, coefs):
    digit = lax.rem(lax.div(lax.axis_index("gy"), stride), radix)
    start = lax.div(lax.axis_index("gy"), stride) - digit

    def store(b, q, value):
        coefs[b, q] = value

    line_coefs(prepared[...], maps, sizes, start, radix, store)


def far_kernel(sizes, maps, levels, prepared, *outputs):
    held = {}

    def store(b, q, value):
        held[b, q] = value

    extent_y = sizes[0]
    line_coefs(prepared[...], maps, sizes, 0, extent_y, store)
    groups = [tuple(held[b, q] for q in range(4)) for b in range(extent_y)]
    for (_, radix), coefs in zip(levels, outputs):
        groups = [
            functools.reduce(merge_coefs, groups[g : g + radix])
            for g in range(0, len(groups), radix)
        ]
        for number, group in enumerate(groups):
            for q in range(4):
                coefs[number, q] = group[q]


def z_coef_kernel(sizes, maps, prepared, drift_z, steps, ends, pushes, packed):
    extent_y, extent_z, size_x, size_y, size_z = sizes
    total_y, total_z = size_y * extent_y, size_z * extent_z
    y_start = lax.axis_index("gy") * size_y
    z_start = lax.axis_index("gz") * size_z
    params = prepared[...]
    d2 = params[DIFFUSION + 2 : DIFFUSION + 3]
    scale = 1.0 / (1.0 + 2.0 * d2)
    lane = iota((size_y, LANES), 1)
    divisors = []
    for i in range(size_x):
        plane = drift_z[i]
        divisors.append(
            1.0 / jnp.where(lane == 0, d2 + roll(plane, 1, 1), d2 - roll(plane, -1, 1))
        )
    pushes[...] = pack_planes(divisors)
    x_bump, x_part = x_factors(params, maps, size_x)
    outer = only(outer_z_rows(params, maps, z_start, size_z, total_z), maps, 2)
    rows = []
    for j in range(size_y):
        position = iota((1, LANES), 0) + (y_start + j)
        bumps, part = y_factors(params, maps, position, total_y)
        rows.append((x_bump * bumps) * (x_part + part))
    outer = half_drift(jnp.concatenate(rows, axis=0), outer)
    inner = jnp.concatenate([drift_z[:, j, :] for j in range(size_y)], axis=0)
    lane = iota(inner.shape, 1)
    low, high = lane == 0, lane == size_z - 1
    before = jnp.where(low, roll(outer, 1, 1), roll(inner, 1, 1))
    after = jnp.where(high, roll(outer, -1, 1), roll(inner, -1, 1))
    below = jnp.where(low & (z_start == 0), 0.0, (d2 + before) * scale)
    above = jnp.where(high & (z_start + size_z == total_z), 0.0, (d2 - after) * scale)
    shape = (size_y, size_x, LANES)
    stride, level = 1, 0
    while stride < size_z:
        low, high = lane < stride, lane >= size_z - stride
        low_a = jnp.where(low, 1.0, roll(below, stride, 1))
        low_c = jnp.where(low, 0.0, roll(above, stride, 1))
        high_a = jnp.where(high, 0.0, roll(below, -stride, 1))
        high_c = jnp.where(high, 1.0, roll(above, -stride, 1))
        inverse = 1.0 / (1.0 - below * low_c - above * high_a)
        below, above = below * inverse, above * inverse
        factor = scale if level == 0 else 1.0
        steps[level, 0] = (inverse * factor).reshape(shape)
        steps[level, 1] = jnp.where(low, 0.0, below * factor).reshape(shape)
        steps[level, 2] = jnp.where(high, 0.0, above * factor).reshape(shape)
        below, above = below * low_a, above * high_c
        stride, level = stride * 2, level + 1
    below, above = below.reshape(shape), above.reshape(shape)
    ends[0] = below
    ends[1] = above
    packed[...] = pack_ends([below[j] for j in range(size_y)], 1, size_y) + pack_ends(
        [above[j] for j in range(size_y)], 2, size_y
    )


def pack_ends(rows, slot, size_y):
    shape = rows[0].shape
    lane = iota(shape, 1)
    out = jnp.zeros(shape, jnp.float32)
    for j in range(size_y):
        first = slot * 2 * size_y + j
        last = first + size_y
        out = jnp.where(lane == first, roll(rows[j], first, 1), out)
        out = jnp.where(lane == last, roll(rows[j], last - (LANES - 1), 1), out)
    return out


def gather_members(refs, own, count):
    held = [ref[...] for ref in refs]
    return [
        functools.reduce(
            lambda acc, s: jnp.where((own ^ s) == j, held[s], acc), range(1, count), held[0]
        )
        for j in range(count)
    ]


def split_message(message):
    width = message.shape[0] // 2
    return message[:width], message[width:]


def merge_kernel(stride, radix, local, coefs, *refs):
    received, message = refs[:radix], refs[radix]
    digit = lax.rem(lax.div(lax.axis_index("gy"), stride), radix)
    first = 0 if local else lax.div(lax.axis_index("gy"), stride) - digit
    values = [split_message(m) for m in gather_members(received, digit, radix)]
    group = [tuple(coefs[first + j, q] for q in range(4)) for j in range(radix)]
    merged, total = group[0], values[0]
    for j in range(1, radix):
        total = merge_values(merged, group[j], total, values[j])
        merged = merge_coefs(merged, group[j])
    message[...] = jnp.concatenate(total, axis=0)


def middle_kernel(levels, *refs):
    refs = list(refs)
    steps, pushes, packed, base, from_below, from_above = refs[:6]
    refs = refs[6:]
    inputs = []
    for stride, radix in levels:
        inputs.append((refs[0], refs[1 : 1 + radix]))
        refs = refs[1 + radix :]
    message, doubled, seen, turned = refs
    size_y, width = base.shape[:2]
    size_x = width - ROWS
    below = above = jnp.zeros((width, LANES), jnp.float32)
    for number in reversed(range(len(levels))):
        (stride, radix), (coefs, received) = levels[number], inputs[number]
        digit = lax.rem(lax.div(lax.axis_index("gy"), stride), radix)
        first = 0 if number == 0 else lax.div(lax.axis_index("gy"), stride) - digit
        values = [split_message(m) for m in gather_members(received, digit, radix)]
        group = [tuple(coefs[first + j, q] for q in range(4)) for j in range(radix)]
        lows, highs = chain(group, values, below, above)
        for j in range(radix):
            seen[j, 0] = lows[j]
            seen[j, 1] = highs[j]
        below, above = seen[digit, 0], seen[digit, 1]
    inner, outer = [], []
    for j in range(size_y):
        value = base[j] + from_below[j] * below + from_above[j] * above
        inner.append(value[:size_x])
        outer.append(value[size_x : size_x + 1])
    turned[...] = jnp.transpose(jnp.concatenate(outer, axis=0) * pushes[...])
    values = jnp.stack(inner)
    stride, level = 1, 0
    while stride < LANES:
        values = (
            steps[level, 0] * values
            + steps[level, 1] * roll(values, stride, 2)
            + steps[level, 2] * roll(values, -stride, 2)
        )
        stride, level = stride * 2, level + 1
    doubled[...] = values
    ends = pack_ends([values[j] for j in range(size_y)], 0, size_y) + packed[...]
    message[...] = ends
    message[:, :size_y] = ends[:, :size_y] + turned[pl.ds(0, size_x, stride=2), :]
    message[:, size_y : 2 * size_y] = (
        ends[:, size_y : 2 * size_y] + turned[pl.ds(1, size_x, stride=2), :]
    )


def merge_z(low, high):
    inverse = 1.0 / (1.0 - low[5] * high[2])
    onward, back = low[4] * inverse, high[3] * inverse
    return (
        low[0] + onward * (high[0] + high[2] * low[1]),
        high[1] + back * (low[1] + low[5] * high[0]),
        low[2] + onward * high[2] * low[3],
        back * low[3],
        onward * high[4],
        high[5] + back * low[5] * high[4],
    )


def unpack_ends(message, size_y):
    return tuple(message if s == 0 else roll(message, -s * size_y, 1) for s in range(6))


def merge_z_kernel(stride, radix, size_y, *refs):
    received, message = refs[:radix], refs[radix]
    digit = lax.rem(lax.div(lax.axis_index("gz"), stride), radix)
    members = [unpack_ends(m, size_y) for m in gather_members(received, digit, radix)]
    total = functools.reduce(merge_z, members)
    lane = iota(total[0].shape, 1)
    out = jnp.zeros(total[0].shape, jnp.float32)
    for s in range(6):
        shifted = total[s] if s == 0 else roll(total[s], s * size_y, 1)
        out = jnp.where(lane // size_y == s, shifted, out)
    message[...] = out


def end_kernel(levels, density, doubled, ends, *refs):
    refs = list(refs)
    inputs = []
    for stride, radix in levels:
        inputs.append(refs[:radix])
        refs = refs[radix:]
    out, seen = refs
    size_x, size_y, _ = density.shape
    below = above = jnp.zeros((size_x, LANES), jnp.float32)
    for (stride, radix), received in zip(reversed(levels), reversed(inputs)):
        digit = lax.rem(lax.div(lax.axis_index("gz"), stride), radix)
        members = [unpack_ends(m, size_y) for m in gather_members(received, digit, radix)]
        lows, highs = chain(
            [(m[2], m[4], m[3], m[5]) for m in members],
            [(m[0], m[1]) for m in members],
            below,
            above,
        )
        for j in range(radix):
            seen[j, 0] = lows[j]
            seen[j, 1] = highs[j]
        below, above = seen[digit, 0], seen[digit, 1]
    for j in range(size_y):
        out[:, j, :] = (
            density[:, j, :]
            + doubled[j]
            + ends[0, j] * below[:, j : j + 1]
            + ends[1, j] * above[:, j : j + 1]
        )


def radices(extent):
    rounds, stride = [], 1
    while stride < extent:
        left = extent // stride
        power = left.bit_length() - 1
        radix = 4 if left % 4 == 0 and power % 2 == 0 else 2
        rounds.append((stride, radix))
        stride *= radix
    return rounds


def exchange(message, axis, stride, radix):
    devices = range(lax.axis_size(axis))
    return [message] + [
        lax.ppermute(message, axis, [(i, i ^ (s * stride)) for i in devices])
        for s in range(1, radix)
    ]


def body(density, diffusion, centers, sharpness, affine, offsets):
    size_x, size_y, size_z = density.shape
    extent_y, extent_z = lax.axis_size("gy"), lax.axis_size("gz")
    sizes = (extent_y, extent_z, size_x, size_y, size_z)
    maps = centers.shape[0]
    width = size_x + ROWS
    wide = (size_y, width, LANES)
    narrow = (size_y, size_x, LANES)
    float32 = jnp.float32
    y_levels, z_levels = radices(extent_y), radices(extent_z)

    def shape(*dims):
        return jax.ShapeDtypeStruct(dims, float32)

    vmem = pl.BlockSpec(memory_space=pltpu.VMEM)
    hbm = pl.BlockSpec(memory_space=pltpu.HBM)

    def call(kernel, inputs, outputs, in_specs=None, scratch=(), flops=10**6):
        return pl.pallas_call(
            kernel,
            out_shape=outputs,
            in_specs=in_specs or [vmem] * len(inputs),
            out_specs=jax.tree.map(lambda _: vmem, outputs),
            scratch_shapes=list(scratch),
            compiler_params=pltpu.CompilerParams(vmem_limit_bytes=VMEM_LIMIT),
            cost_estimate=pl.CostEstimate(flops=flops, bytes_accessed=10**6, transcendentals=0),
        )(*inputs)

    raw = (
        density,
        diffusion.reshape(1, 3),
        centers.T,
        sharpness.reshape(1, maps),
        affine.transpose(1, 2, 0),
        offsets.T,
    )
    message, base, from_below, from_above, drift_z, prepared = call(
        functools.partial(start_kernel, extent_y, extent_z),
        raw,
        (
            shape(2 * width, LANES),
            shape(*wide),
            shape(*wide),
            shape(*wide),
            shape(size_x, size_y, LANES),
            shape(PREPARED, LANES),
        ),
        [hbm] * len(raw),
        [
            pltpu.VMEM((size_x, 2 * size_y, LANES), float32),
            pltpu.VMEM((size_x, size_y, LANES), float32),
        ]
        + [pltpu.VMEM(array.shape, float32) for array in raw]
        + [pltpu.VMEM((PREPARED, LANES), float32), pltpu.SemaphoreType.DMA((len(raw),))],
    )
    stride, radix = y_levels[0]
    near = call(
        functools.partial(near_kernel, sizes, maps, stride, radix),
        [prepared],
        shape(radix, 4, width, LANES),
    )
    far, count = [], extent_y
    for _, radix in y_levels[:-1]:
        count = count // radix
        far.append(shape(count, 4, width, LANES))
    if far:
        far = call(functools.partial(far_kernel, sizes, maps, y_levels[:-1]), [prepared], far)
    coefs = [near] + list(far)
    doublings = size_z.bit_length() - 1
    steps, ends, pushes, packed = call(
        functools.partial(z_coef_kernel, sizes, maps),
        (prepared, drift_z),
        (
            shape(doublings, 3, *narrow),
            shape(2, *narrow),
            shape(size_y, LANES),
            shape(size_x, LANES),
        ),
    )
    line_inputs = []
    for number, (stride, radix) in enumerate(y_levels):
        received = exchange(message, "gy", stride, radix)
        line_inputs += [coefs[number]] + received
        if number + 1 < len(y_levels):
            message = call(
                functools.partial(merge_kernel, stride, radix, number == 0),
                [coefs[number]] + received,
                shape(2 * width, LANES),
            )
    message, doubled = call(
        functools.partial(middle_kernel, y_levels),
        [steps, pushes, packed, base, from_below, from_above] + line_inputs,
        (shape(size_x, LANES), shape(*narrow)),
        scratch=[
            pltpu.VMEM((4, 2, width, LANES), float32),
            pltpu.VMEM((LANES, size_y), float32),
        ],
    )
    end_inputs = []
    for number, (stride, radix) in enumerate(z_levels):
        received = exchange(message, "gz", stride, radix)
        end_inputs += received
        if number + 1 < len(z_levels):
            message = call(
                functools.partial(merge_z_kernel, stride, radix, size_y),
                received,
                shape(size_x, LANES),
            )
    return call(
        functools.partial(end_kernel, z_levels),
        [density, doubled, ends] + end_inputs,
        shape(size_x, size_y, size_z),
        scratch=[pltpu.VMEM((4, 2, size_x, LANES), float32)],
    )


def solution(mesh):
    placed = (P(None, "gy", "gz"), P(), P(), P(), P(), P())
    return jax.shard_map(
        body, mesh=mesh, in_specs=placed, out_specs=P(None, "gy", "gz"), check_vma=False
    )
```

```python
import functools

import jax
import jax.numpy as jnp
from jax import lax
from jax.experimental import pallas as pl
from jax.experimental.pallas import tpu as pltpu
from jax.sharding import PartitionSpec as P

HALF_LIMIT = 600.0
LANES = 128
ROWS = 8
VMEM_LIMIT = 48 * 1024 * 1024


def iota(shape, axis):
    return lax.broadcasted_iota(jnp.int32, shape, axis)


def coordinate(positions, line_total):
    return (2.0 * positions.astype(jnp.float32) + 1.0) / line_total - 1.0


def roll(values, shift, axis):
    return pltpu.roll(values, shift % values.shape[axis], axis)


def matmul(left, right):
    return lax.dot_general(
        left,
        right,
        (((1,), (1,)), ((), ())),
        precision=lax.Precision.HIGHEST,
        preferred_element_type=jnp.float32,
    )


def half_drift(left, right):
    return HALF_LIMIT * jnp.tanh(matmul(left, right))


SHARPNESS, CENTER, SLOPE, OFFSET, DIFFUSION, PREPARED = 0, 1, 4, 7, 8, 16


def component_of(maps):
    return iota((1, LANES), 1) // (2 * maps)


def first_term(maps):
    return (iota((1, LANES), 1) // maps) % 2 == 0


def bump(params, coord, axis):
    center = params[CENTER + axis : CENTER + axis + 1]
    return jnp.exp(-params[SHARPNESS : SHARPNESS + 1] * (coord - center) ** 2)


def slope(params, coord, axis):
    return coord * params[SLOPE + axis : SLOPE + axis + 1]


def x_factors(params, maps, size_x):
    coord = coordinate(iota((size_x, LANES), 0), size_x)
    return bump(params, coord, 0), jnp.where(first_term(maps), slope(params, coord, 0), 0.0)


def y_factors(params, maps, position, total_y):
    coord = coordinate(position, total_y)
    part = slope(params, coord, 1) + params[OFFSET : OFFSET + 1]
    return bump(params, coord, 1), jnp.where(
        first_term(maps), part, params[SLOPE + 2 : SLOPE + 3]
    )


def z_rows(params, maps, position, total_z):
    coord = coordinate(position, total_z)
    return bump(params, coord, 2) * jnp.where(first_term(maps), 1.0, coord)


def inner_z_rows(params, maps, z_start, size_z, total_z):
    return z_rows(params, maps, z_start + iota((size_z, LANES), 0), total_z)


def outer_z_rows(params, maps, z_start, size_z, total_z):
    row = iota((size_z, LANES), 0)
    return z_rows(
        params, maps, jnp.where(row == 0, z_start + size_z, z_start - 1), total_z
    )


def only(rows, maps, component):
    return jnp.where(component_of(maps) == component, rows, 0.0)


def y_rows(params, maps, position, total_y):
    coord = coordinate(position, total_y)
    part = slope(params, coord, 1) + params[OFFSET : OFFSET + 1]
    return bump(params, coord, 1) * jnp.where(first_term(maps), part, 1.0)


def xz_rows(params, maps, size_x, z_start, size_z, total_z):
    row = iota((2 * size_x, LANES), 0)
    x_coord = coordinate(row // 2, size_x)
    z_coord = coordinate(jnp.where(row % 2 == 0, z_start - 1, z_start + size_z), total_z)
    part = slope(params, x_coord, 0) + slope(params, z_coord, 2)
    both = bump(params, x_coord, 0) * bump(params, z_coord, 2)
    both = both * jnp.where(first_term(maps), 1.0, part)
    return jnp.concatenate(
        [both, jnp.zeros((LANES - 2 * size_x, LANES), jnp.float32)], axis=0
    )


def with_extra(main, row):
    return jnp.concatenate([main, jnp.broadcast_to(row, (ROWS, LANES))], axis=0)


def pack_planes(planes):
    lane = iota(planes[0].shape, 1)
    out = jnp.zeros(planes[0].shape, jnp.float32)
    for i, plane in enumerate(planes):
        out = jnp.where(lane // 2 == i, roll(plane, 2 * i + 1, 1), out)
    return out


def merge_coefs(low, high):
    inverse = 1.0 / (1.0 - low[3] * high[0])
    onward, back = low[1] * inverse, high[2] * inverse
    return (
        low[0] + onward * high[0] * low[2],
        onward * high[1],
        back * low[2],
        high[3] + back * low[3] * high[1],
    )


def merge_values(low, high, low_values, high_values):
    inverse = 1.0 / (1.0 - low[3] * high[0])
    return (
        low_values[0] + low[1] * inverse * (high_values[0] + high[0] * low_values[1]),
        high_values[1] + high[2] * inverse * (low_values[1] + low[3] * high_values[0]),
    )


def chain(coefs, values, below, above):
    count = len(coefs)
    held, slope = below, None
    befores, firsts = [], []
    for j in range(count):
        a_first, c_first, a_last, c_last = coefs[j]
        r_first, r_last = values[j]
        befores.append((held, slope))
        if slope is None:
            first, first_slope = r_first + a_first * held, c_first
            held, slope = r_last + a_last * held, c_last
        else:
            inverse = 1.0 / (1.0 - a_first * slope)
            first = (r_first + a_first * held) * inverse
            first_slope = c_first * inverse
            held, slope = (
                r_last + a_last * (held + slope * first),
                c_last + a_last * slope * first_slope,
            )
        firsts.append((first, first_slope))
    seen_above = [None] * count
    seen_below = [None] * count
    upper = above
    for j in reversed(range(count)):
        seen_above[j] = upper
        upper = firsts[j][0] + firsts[j][1] * upper
        held, slope = befores[j]
        seen_below[j] = held if slope is None else held + slope * upper
    return seen_below, seen_above


def solve_x(up, down, source, pivot):
    size = source.shape[0]
    half = size // 2
    low_g, low_c, high_g, high_c = {}, {}, {}, {}
    g = c = None
    for i in range(half):
        if i == 0:
            weight = 1.0 / pivot
            c = down[1] * weight
            g = source[0] * weight
        else:
            weight = 1.0 / (pivot - up[i - 1] * c)
            g = (source[i] + up[i - 1] * g) * weight
            c = down[i + 1] * weight
        low_g[i], low_c[i] = g, c
    for i in reversed(range(half, size)):
        if i == size - 1:
            weight = 1.0 / pivot
            c = up[i - 1] * weight
            g = source[i] * weight
        else:
            weight = 1.0 / (pivot - down[i + 1] * c)
            g = (source[i] + down[i + 1] * g) * weight
            c = up[i - 1] * weight
        high_g[i], high_c[i] = g, c
    out = [None] * size
    inverse = 1.0 / (1.0 - low_c[half - 1] * high_c[half])
    out[half - 1] = (low_g[half - 1] + low_c[half - 1] * high_g[half]) * inverse
    out[half] = high_g[half] + high_c[half] * out[half - 1]
    for i in reversed(range(half - 1)):
        out[i] = low_g[i] + low_c[i] * out[i + 1]
    for i in range(half + 1, size):
        out[i] = high_g[i] + high_c[i] * out[i - 1]
    return out


def start_kernel(
    extent_y,
    extent_z,
    density_hbm,
    diffusion_hbm,
    centers_hbm,
    sharpness_hbm,
    affine_hbm,
    offsets_hbm,
    message,
    base,
    from_below,
    from_above,
    drift_z_out,
    prepared,
    solved,
    drift_y_held,
    density,
    diffusion,
    centers,
    sharpness,
    affine,
    offsets,
    staged,
    semaphores,
):
    copies = [
        pltpu.make_async_copy(source, target, semaphores.at[number])
        for number, (source, target) in enumerate(
            [
                (diffusion_hbm, diffusion),
                (centers_hbm, centers),
                (sharpness_hbm, sharpness),
                (affine_hbm, affine),
                (offsets_hbm, offsets),
                (density_hbm, density),
            ]
        )
    ]
    for copy in copies:
        copy.start()
    size_x, size_y, size_z = density.shape
    total_y, total_z = size_y * extent_y, size_z * extent_z
    y_start = lax.axis_index("gy") * size_y
    z_start = lax.axis_index("gz") * size_z
    maps = centers.shape[1]
    for copy in copies[:-1]:
        copy.wait()

    staged[...] = jnp.zeros(staged.shape, jnp.float32)
    staged[0:1, :maps] = sharpness[...]
    staged[1:4, :maps] = centers[...]
    for c in range(3):
        staged[4 + 3 * c : 7 + 3 * c, :maps] = affine[c]
    staged[13:16, :maps] = offsets[...]
    rows = staged[...]
    width = maps
    while width < LANES:
        rows = rows + roll(rows, width, 1)
        width = 2 * width
    component = component_of(maps)
    rows = jnp.where(component < 3, rows, 0.0)

    def by_component(first, step):
        return jnp.where(
            component == 0,
            rows[first : first + 1],
            jnp.where(
                component == 1,
                rows[first + step : first + step + 1],
                rows[first + 2 * step : first + 2 * step + 1],
            ),
        )

    weights = [jnp.broadcast_to(diffusion[:, c : c + 1], (1, LANES)) for c in range(3)]
    params = jnp.concatenate(
        [rows[0:4]]
        + [by_component(4 + j, 3) for j in range(3)]
        + [by_component(13, 1)]
        + weights
        + [jnp.zeros((PREPARED - DIFFUSION - 3, LANES), jnp.float32)],
        axis=0,
    )
    prepared[...] = params
    d0, d1, d2 = weights

    x_bump, x_part = x_factors(params, maps, size_x)
    y_row = iota((size_y, LANES), 0)
    y_bump, y_part = y_factors(params, maps, y_start + y_row, total_y)
    out_bump, out_part = y_factors(
        params, maps, jnp.where(y_row == 0, y_start + size_y, y_start - 1), total_y
    )
    inner = inner_z_rows(params, maps, z_start, size_z, total_z)
    outer = outer_z_rows(params, maps, z_start, size_z, total_z)
    inner = [only(inner, maps, c) for c in range(3)]
    outer = only(outer, maps, 0)

    def rows_by_x(bumps, part):
        return jnp.concatenate(
            [(x_bump[i : i + 1] * bumps) * (x_part[i : i + 1] + part) for i in range(size_x)],
            axis=0,
        )

    right = jnp.concatenate([inner[0], outer, inner[1], inner[2]], axis=0)
    drifts = half_drift(rows_by_x(y_bump, y_part), right)
    out_drift = half_drift(rows_by_x(out_bump, out_part), inner[0])

    def block(number):
        columns = drifts[:, number * LANES : (number + 1) * LANES]
        return columns.reshape(size_x, size_y, LANES)

    drift_x, plane_drift, drift_y, drift_z = block(0), block(1), block(2), block(3)
    out_drift = out_drift.reshape(size_x, size_y, LANES)
    drift_y_held[...] = drift_y
    drift_z_out[...] = drift_z
    copies[-1].wait()
    rho = density[...]
    zero = jnp.zeros((1, size_y, LANES), jnp.float32)
    up, down = (d0 + drift_x) * rho, (d0 - drift_x) * rho
    total = (
        jnp.concatenate([zero, up[:-1]], axis=0)
        + jnp.concatenate([down[1:], zero], axis=0)
        - (2.0 * (d0 + d1 + d2)) * rho
    )
    sublane = iota((size_x, size_y, LANES), 1)
    lane = iota((size_x, size_y, LANES), 2)
    up, down = roll((d1 + drift_y) * rho, 1, 1), roll((d1 - drift_y) * rho, -1, 1)
    at_low, at_high = sublane == 0, sublane == size_y - 1
    row_source = jnp.where(at_low, up, jnp.where(at_high, down, 0.0))
    total = total + jnp.where(at_low, 0.0, up) + jnp.where(at_high, 0.0, down)
    up, down = roll((d2 + drift_z) * rho, 1, 2), roll((d2 - drift_z) * rho, -1, 2)
    at_low, at_high = lane == 0, lane == size_z - 1
    plane_source = jnp.where(at_low, up, jnp.where(at_high, down, 0.0))
    total = total + jnp.where(at_low, 0.0, up) + jnp.where(at_high, 0.0, down)

    source = jnp.concatenate([total, row_source, plane_source], axis=1)
    drift = jnp.concatenate([drift_x, out_drift, plane_drift], axis=1)
    answers = solve_x(d0 + drift, d0 - drift, source, 1.0 + 2.0 * d0)
    for i in range(size_x):
        solved[i] = answers[i][: 2 * size_y]
    planes = pack_planes([answer[2 * size_y :] for answer in answers])

    row = iota((1, LANES), 0)
    out_rows = []
    for position in (y_start - 1, y_start + size_y):
        bumps, part = y_factors(params, maps, row + position, total_y)
        out_rows.append((x_bump * bumps) * (x_part + part))
    ends = half_drift(jnp.concatenate(out_rows, axis=0), inner[1])
    position = y_start - 1 + iota((2 * ROWS, LANES), 0)
    extra = half_drift(
        y_rows(params, maps, position, total_y),
        only(xz_rows(params, maps, size_x, z_start, size_z, total_z), maps, 1),
    )
    line_drift = (
        [ends[:size_x]]
        + [drift_y_held[:, j, :] for j in range(size_y)]
        + [ends[size_x:]]
    )
    line_drift = [with_extra(line_drift[j], extra[j : j + 1]) for j in range(size_y + 2)]
    pivot = 1.0 + 2.0 * d1
    at_start = y_start == 0
    at_end = y_start + size_y == total_y
    g = a = c = None
    gs, as_, cs = [], [], []
    for j in range(size_y):
        value = with_extra(solved[:, j, :], planes[j : j + 1])
        lower = d1 + line_drift[j]
        upper = d1 - line_drift[j + 2]
        if j == 0:
            lower = jnp.where(at_start, 0.0, lower)
        if j == size_y - 1:
            upper = jnp.where(at_end, 0.0, upper)
        if j == 0:
            weight = 1.0 / pivot
            g, a = value * weight, lower * weight
        else:
            weight = 1.0 / (pivot - lower * c)
            g, a = (value + lower * g) * weight, lower * a * weight
        c = upper * weight
        gs.append(g)
        as_.append(a)
        cs.append(c)
    base[size_y - 1], from_below[size_y - 1], from_above[size_y - 1] = g, a, c
    r_last = g
    for j in reversed(range(size_y - 1)):
        g, a, c = gs[j] + cs[j] * g, as_[j] + cs[j] * a, cs[j] * c
        base[j], from_below[j], from_above[j] = g, a, c
    pushed_up = solved[:, size_y, :] / (d1 + line_drift[size_y][:size_x])
    pushed_down = solved[:, 2 * size_y - 1, :] / (d1 - line_drift[1][:size_x])
    blank = jnp.zeros((1, LANES), jnp.float32)
    width = size_x + ROWS
    message[:width] = g + with_extra(pushed_down, blank)
    message[width:] = r_last + with_extra(pushed_up, blank)


def line_coefs(params, maps, sizes, start, count, store):
    extent_y, extent_z, size_x, size_y, size_z = sizes
    total_y, total_z = size_y * extent_y, size_z * extent_z
    z_start = lax.axis_index("gz") * size_z
    d1 = params[DIFFUSION + 1 : DIFFUSION + 2]
    x_bump, x_part = x_factors(params, maps, size_x)
    inner = only(inner_z_rows(params, maps, z_start, size_z, total_z), maps, 1)
    planes = only(xz_rows(params, maps, size_x, z_start, size_z, total_z), maps, 1)
    whole = count == extent_y
    offsets = list(range(size_y)) if whole else list(range(-1, size_y + 1))
    left, left_extra = [], []
    for j in offsets:
        for b in range(count):
            position = iota((1, LANES), 0) + ((start + b) * size_y + j)
            bumps, part = y_factors(params, maps, position, total_y)
            left.append((x_bump * bumps) * (x_part + part))
        block = iota((max(count, ROWS), LANES), 0)
        left_extra.append(
            y_rows(params, maps, (start + block) * size_y + j, total_y)
        )
    depth = left_extra[0].shape[0]
    main = half_drift(jnp.concatenate(left, axis=0), inner)
    main = main.reshape(len(offsets), count, size_x, LANES)
    main = [main[j] for j in range(len(offsets))]
    extra = half_drift(jnp.concatenate(left_extra, axis=0), planes)
    extra = [extra[j * depth : (j + 1) * depth] for j in range(len(offsets))]
    if whole:
        main = (
            [jnp.concatenate([main[-1][:1], main[-1][:-1]], axis=0)]
            + main
            + [jnp.concatenate([main[0][1:], main[0][-1:]], axis=0)]
        )
        extra = [roll(extra[-1], 1, 0)] + extra + [roll(extra[0], -1, 0)]
    numbers = start + iota((depth, LANES), 0)
    pivot = 1.0 + 2.0 * d1
    at_start, at_end = numbers == 0, numbers == extent_y - 1

    def scan(drifts, starts, ends):
        a_first = c_first = a_last = c_last = None
        for j in range(size_y):
            lower, upper = d1 + drifts[j], d1 - drifts[j + 2]
            if j == 0:
                lower = starts(lower)
            if j == size_y - 1:
                upper = ends(upper)
            if j == 0:
                weight = 1.0 / pivot
                a_first, c_first = lower * weight, upper * weight
                a_last, c_last = a_first, c_first
            else:
                weight = 1.0 / (pivot - lower * c_last)
                step, c_last = lower * weight, upper * weight
                a_last = step * a_last
                a_first = a_first + c_first * a_last
                c_first = c_first * c_last
        return a_first, c_first, a_last, c_last

    def masked(values, number):
        return jnp.concatenate(
            [
                jnp.where(start + b == number, 0.0, values[b])[None]
                for b in range(count)
            ],
            axis=0,
        )

    main = scan(main, lambda v: masked(v, 0), lambda v: masked(v, extent_y - 1))
    extra = scan(
        extra,
        lambda v: jnp.where(at_start, 0.0, v),
        lambda v: jnp.where(at_end, 0.0, v),
    )
    for b in range(count):
        for q in range(4):
            store(b, q, with_extra(main[q][b], extra[q][b : b + 1]))


def near_kernel(sizes, maps, stride, radix, prepared, coefs):
    digit = lax.rem(lax.div(lax.axis_index("gy"), stride), radix)
    start = lax.div(lax.axis_index("gy"), stride) - digit

    def store(b, q, value):
        coefs[b, q] = value

    line_coefs(prepared[...], maps, sizes, start, radix, store)


def far_kernel(sizes, maps, levels, prepared, *outputs):
    held = {}

    def store(b, q, value):
        held[b, q] = value

    extent_y = sizes[0]
    line_coefs(prepared[...], maps, sizes, 0, extent_y, store)
    groups = [tuple(held[b, q] for q in range(4)) for b in range(extent_y)]
    for (_, radix), coefs in zip(levels, outputs):
        groups = [
            functools.reduce(merge_coefs, groups[g : g + radix])
            for g in range(0, len(groups), radix)
        ]
        for number, group in enumerate(groups):
            for q in range(4):
                coefs[number, q] = group[q]


def z_coef_kernel(sizes, maps, prepared, drift_z, steps, ends, pushes, packed):
    extent_y, extent_z, size_x, size_y, size_z = sizes
    total_y, total_z = size_y * extent_y, size_z * extent_z
    y_start = lax.axis_index("gy") * size_y
    z_start = lax.axis_index("gz") * size_z
    params = prepared[...]
    d2 = params[DIFFUSION + 2 : DIFFUSION + 3]
    scale = 1.0 / (1.0 + 2.0 * d2)
    lane = iota((size_y, LANES), 1)
    divisors = []
    for i in range(size_x):
        plane = drift_z[i]
        divisors.append(
            1.0 / jnp.where(lane == 0, d2 + roll(plane, 1, 1), d2 - roll(plane, -1, 1))
        )
    pushes[...] = pack_planes(divisors)
    x_bump, x_part = x_factors(params, maps, size_x)
    outer = only(outer_z_rows(params, maps, z_start, size_z, total_z), maps, 2)
    rows = []
    for j in range(size_y):
        position = iota((1, LANES), 0) + (y_start + j)
        bumps, part = y_factors(params, maps, position, total_y)
        rows.append((x_bump * bumps) * (x_part + part))
    outer = half_drift(jnp.concatenate(rows, axis=0), outer)
    inner = jnp.concatenate([drift_z[:, j, :] for j in range(size_y)], axis=0)
    lane = iota(inner.shape, 1)
    low, high = lane == 0, lane == size_z - 1
    before = jnp.where(low, roll(outer, 1, 1), roll(inner, 1, 1))
    after = jnp.where(high, roll(outer, -1, 1), roll(inner, -1, 1))
    below = jnp.where(low & (z_start == 0), 0.0, (d2 + before) * scale)
    above = jnp.where(high & (z_start + size_z == total_z), 0.0, (d2 - after) * scale)
    shape = (size_y, size_x, LANES)
    stride, level = 1, 0
    while stride < size_z:
        low, high = lane < stride, lane >= size_z - stride
        low_a = jnp.where(low, 1.0, roll(below, stride, 1))
        low_c = jnp.where(low, 0.0, roll(above, stride, 1))
        high_a = jnp.where(high, 0.0, roll(below, -stride, 1))
        high_c = jnp.where(high, 1.0, roll(above, -stride, 1))
        inverse = 1.0 / (1.0 - below * low_c - above * high_a)
        below, above = below * inverse, above * inverse
        factor = scale if level == 0 else 1.0
        steps[level, 0] = (inverse * factor).reshape(shape)
        steps[level, 1] = jnp.where(low, 0.0, below * factor).reshape(shape)
        steps[level, 2] = jnp.where(high, 0.0, above * factor).reshape(shape)
        below, above = below * low_a, above * high_c
        stride, level = stride * 2, level + 1
    below, above = below.reshape(shape), above.reshape(shape)
    ends[0] = below
    ends[1] = above
    packed[...] = pack_ends([below[j] for j in range(size_y)], 1, size_y) + pack_ends(
        [above[j] for j in range(size_y)], 2, size_y
    )


def pack_ends(rows, slot, size_y):
    shape = rows[0].shape
    lane = iota(shape, 1)
    out = jnp.zeros(shape, jnp.float32)
    for j in range(size_y):
        first = slot * 2 * size_y + j
        last = first + size_y
        out = jnp.where(lane == first, roll(rows[j], first, 1), out)
        out = jnp.where(lane == last, roll(rows[j], last - (LANES - 1), 1), out)
    return out


def gather_members(refs, own, count):
    held = [ref[...] for ref in refs]
    return [
        functools.reduce(
            lambda acc, s: jnp.where((own ^ s) == j, held[s], acc), range(1, count), held[0]
        )
        for j in range(count)
    ]


def split_message(message):
    width = message.shape[0] // 2
    return message[:width], message[width:]


def merge_kernel(stride, radix, local, coefs, *refs):
    received, message = refs[:radix], refs[radix]
    digit = lax.rem(lax.div(lax.axis_index("gy"), stride), radix)
    first = 0 if local else lax.div(lax.axis_index("gy"), stride) - digit
    values = [split_message(m) for m in gather_members(received, digit, radix)]
    group = [tuple(coefs[first + j, q] for q in range(4)) for j in range(radix)]
    merged, total = group[0], values[0]
    for j in range(1, radix):
        total = merge_values(merged, group[j], total, values[j])
        merged = merge_coefs(merged, group[j])
    message[...] = jnp.concatenate(total, axis=0)


def middle_kernel(levels, *refs):
    refs = list(refs)
    steps, pushes, packed, base, from_below, from_above = refs[:6]
    refs = refs[6:]
    inputs = []
    for stride, radix in levels:
        inputs.append((refs[0], refs[1 : 1 + radix]))
        refs = refs[1 + radix :]
    message, doubled, seen, turned = refs
    size_y, width = base.shape[:2]
    size_x = width - ROWS
    below = above = jnp.zeros((width, LANES), jnp.float32)
    for number in reversed(range(len(levels))):
        (stride, radix), (coefs, received) = levels[number], inputs[number]
        digit = lax.rem(lax.div(lax.axis_index("gy"), stride), radix)
        first = 0 if number == 0 else lax.div(lax.axis_index("gy"), stride) - digit
        values = [split_message(m) for m in gather_members(received, digit, radix)]
        group = [tuple(coefs[first + j, q] for q in range(4)) for j in range(radix)]
        lows, highs = chain(group, values, below, above)
        for j in range(radix):
            seen[j, 0] = lows[j]
            seen[j, 1] = highs[j]
        below, above = seen[digit, 0], seen[digit, 1]
    inner, outer = [], []
    for j in range(size_y):
        value = base[j] + from_below[j] * below + from_above[j] * above
        inner.append(value[:size_x])
        outer.append(value[size_x : size_x + 1])
    turned[...] = jnp.transpose(jnp.concatenate(outer, axis=0) * pushes[...])
    values = jnp.stack(inner)
    stride, level = 1, 0
    while stride < LANES:
        values = (
            steps[level, 0] * values
            + steps[level, 1] * roll(values, stride, 2)
            + steps[level, 2] * roll(values, -stride, 2)
        )
        stride, level = stride * 2, level + 1
    doubled[...] = values
    ends = pack_ends([values[j] for j in range(size_y)], 0, size_y) + packed[...]
    message[...] = ends
    message[:, :size_y] = ends[:, :size_y] + turned[pl.ds(0, size_x, stride=2), :]
    message[:, size_y : 2 * size_y] = (
        ends[:, size_y : 2 * size_y] + turned[pl.ds(1, size_x, stride=2), :]
    )


def merge_z(low, high):
    inverse = 1.0 / (1.0 - low[5] * high[2])
    onward, back = low[4] * inverse, high[3] * inverse
    return (
        low[0] + onward * (high[0] + high[2] * low[1]),
        high[1] + back * (low[1] + low[5] * high[0]),
        low[2] + onward * high[2] * low[3],
        back * low[3],
        onward * high[4],
        high[5] + back * low[5] * high[4],
    )


def unpack_ends(message, size_y):
    return tuple(message if s == 0 else roll(message, -s * size_y, 1) for s in range(6))


def merge_z_kernel(stride, radix, size_y, *refs):
    received, message = refs[:radix], refs[radix]
    digit = lax.rem(lax.div(lax.axis_index("gz"), stride), radix)
    members = [unpack_ends(m, size_y) for m in gather_members(received, digit, radix)]
    total = functools.reduce(merge_z, members)
    lane = iota(total[0].shape, 1)
    out = jnp.zeros(total[0].shape, jnp.float32)
    for s in range(6):
        shifted = total[s] if s == 0 else roll(total[s], s * size_y, 1)
        out = jnp.where(lane // size_y == s, shifted, out)
    message[...] = out


def end_kernel(levels, density, doubled, ends, *refs):
    refs = list(refs)
    inputs = []
    for stride, radix in levels:
        inputs.append(refs[:radix])
        refs = refs[radix:]
    out, seen = refs
    size_x, size_y, _ = density.shape
    below = above = jnp.zeros((size_x, LANES), jnp.float32)
    for (stride, radix), received in zip(reversed(levels), reversed(inputs)):
        digit = lax.rem(lax.div(lax.axis_index("gz"), stride), radix)
        members = [unpack_ends(m, size_y) for m in gather_members(received, digit, radix)]
        lows, highs = chain(
            [(m[2], m[4], m[3], m[5]) for m in members],
            [(m[0], m[1]) for m in members],
            below,
            above,
        )
        for j in range(radix):
            seen[j, 0] = lows[j]
            seen[j, 1] = highs[j]
        below, above = seen[digit, 0], seen[digit, 1]
    for j in range(size_y):
        out[:, j, :] = (
            density[:, j, :]
            + doubled[j]
            + ends[0, j] * below[:, j : j + 1]
            + ends[1, j] * above[:, j : j + 1]
        )


def radices(extent):
    rounds, stride = [], 1
    while stride < extent:
        left = extent // stride
        power = left.bit_length() - 1
        radix = 4 if left % 4 == 0 and power % 2 == 0 else 2
        rounds.append((stride, radix))
        stride *= radix
    return rounds


def exchange(message, axis, stride, radix):
    devices = range(lax.axis_size(axis))
    return [message] + [
        lax.ppermute(message, axis, [(i, i ^ (s * stride)) for i in devices])
        for s in range(1, radix)
    ]


def body(density, diffusion, centers, sharpness, affine, offsets):
    size_x, size_y, size_z = density.shape
    extent_y, extent_z = lax.axis_size("gy"), lax.axis_size("gz")
    sizes = (extent_y, extent_z, size_x, size_y, size_z)
    maps = centers.shape[0]
    width = size_x + ROWS
    wide = (size_y, width, LANES)
    narrow = (size_y, size_x, LANES)
    float32 = jnp.float32
    y_levels, z_levels = radices(extent_y), radices(extent_z)

    def shape(*dims):
        return jax.ShapeDtypeStruct(dims, float32)

    vmem = pl.BlockSpec(memory_space=pltpu.VMEM)
    hbm = pl.BlockSpec(memory_space=pltpu.HBM)

    def call(kernel, inputs, outputs, in_specs=None, scratch=(), flops=10**6):
        return pl.pallas_call(
            kernel,
            out_shape=outputs,
            in_specs=in_specs or [vmem] * len(inputs),
            out_specs=jax.tree.map(lambda _: vmem, outputs),
            scratch_shapes=list(scratch),
            compiler_params=pltpu.CompilerParams(vmem_limit_bytes=VMEM_LIMIT),
            cost_estimate=pl.CostEstimate(flops=flops, bytes_accessed=10**6, transcendentals=0),
        )(*inputs)

    raw = (
        density,
        diffusion.reshape(1, 3),
        centers.T,
        sharpness.reshape(1, maps),
        affine.transpose(1, 2, 0),
        offsets.T,
    )
    raw = tuple(pltpu.with_memory_space_constraint(array, pltpu.HBM) for array in raw)
    message, base, from_below, from_above, drift_z, prepared = call(
        functools.partial(start_kernel, extent_y, extent_z),
        raw,
        (
            shape(2 * width, LANES),
            shape(*wide),
            shape(*wide),
            shape(*wide),
            shape(size_x, size_y, LANES),
            shape(PREPARED, LANES),
        ),
        [hbm] * len(raw),
        [
            pltpu.VMEM((size_x, 2 * size_y, LANES), float32),
            pltpu.VMEM((size_x, size_y, LANES), float32),
        ]
        + [pltpu.VMEM(array.shape, float32) for array in raw]
        + [pltpu.VMEM((PREPARED, LANES), float32), pltpu.SemaphoreType.DMA((len(raw),))],
    )
    stride, radix = y_levels[0]
    near = call(
        functools.partial(near_kernel, sizes, maps, stride, radix),
        [prepared],
        shape(radix, 4, width, LANES),
    )
    far, count = [], extent_y
    for _, radix in y_levels[:-1]:
        count = count // radix
        far.append(shape(count, 4, width, LANES))
    if far:
        far = call(functools.partial(far_kernel, sizes, maps, y_levels[:-1]), [prepared], far)
    coefs = [near] + list(far)
    doublings = size_z.bit_length() - 1
    steps, ends, pushes, packed = call(
        functools.partial(z_coef_kernel, sizes, maps),
        (prepared, drift_z),
        (
            shape(doublings, 3, *narrow),
            shape(2, *narrow),
            shape(size_y, LANES),
            shape(size_x, LANES),
        ),
    )
    line_inputs = []
    for number, (stride, radix) in enumerate(y_levels):
        received = exchange(message, "gy", stride, radix)
        line_inputs += [coefs[number]] + received
        if number + 1 < len(y_levels):
            message = call(
                functools.partial(merge_kernel, stride, radix, number == 0),
                [coefs[number]] + received,
                shape(2 * width, LANES),
            )
    message, doubled = call(
        functools.partial(middle_kernel, y_levels),
        [steps, pushes, packed, base, from_below, from_above] + line_inputs,
        (shape(size_x, LANES), shape(*narrow)),
        scratch=[
            pltpu.VMEM((4, 2, width, LANES), float32),
            pltpu.VMEM((LANES, size_y), float32),
        ],
    )
    end_inputs = []
    for number, (stride, radix) in enumerate(z_levels):
        received = exchange(message, "gz", stride, radix)
        end_inputs += received
        if number + 1 < len(z_levels):
            message = call(
                functools.partial(merge_z_kernel, stride, radix, size_y),
                received,
                shape(size_x, LANES),
            )
    return call(
        functools.partial(end_kernel, z_levels),
        [density, doubled, ends] + end_inputs,
        shape(size_x, size_y, size_z),
        scratch=[pltpu.VMEM((4, 2, size_x, LANES), float32)],
    )


def solution(mesh):
    placed = (P(None, "gy", "gz"), P(), P(), P(), P(), P())
    return jax.shard_map(
        body, mesh=mesh, in_specs=placed, out_specs=P(None, "gy", "gz"), check_vma=False
    )
```

```python
import functools

import jax
import jax.numpy as jnp
from jax import lax
from jax.experimental import pallas as pl
from jax.experimental.pallas import tpu as pltpu
from jax.sharding import PartitionSpec as P

HALF_LIMIT = 600.0
LANES = 128
ROWS = 8
VMEM_LIMIT = 48 * 1024 * 1024


def iota(shape, axis):
    return lax.broadcasted_iota(jnp.int32, shape, axis)


def coordinate(positions, line_total):
    return (2.0 * positions.astype(jnp.float32) + 1.0) / line_total - 1.0


def roll(values, shift, axis):
    return pltpu.roll(values, shift % values.shape[axis], axis)


def matmul(left, right):
    low, high = split(left), split(right)
    columns = right.shape[0]
    both = lax.dot_general(
        jnp.concatenate(low, axis=1),
        jnp.concatenate([jnp.concatenate([part, part], axis=1) for part in high], axis=0),
        (((1,), (1,)), ((), ())),
        preferred_element_type=jnp.float32,
    )
    return both[:, :columns] + both[:, columns:]


def split(values):
    upper = values.astype(jnp.bfloat16)
    return upper, (values - upper.astype(jnp.float32)).astype(jnp.bfloat16)


def half_drift(left, right):
    return HALF_LIMIT * jnp.tanh(matmul(left, right))


SHARPNESS, CENTER, SLOPE, OFFSET, DIFFUSION, PREPARED = 0, 1, 4, 7, 8, 16


def component_of(maps):
    return iota((1, LANES), 1) // (2 * maps)


def first_term(maps):
    return (iota((1, LANES), 1) // maps) % 2 == 0


def bump(params, coord, axis):
    center = params[CENTER + axis : CENTER + axis + 1]
    return jnp.exp(-params[SHARPNESS : SHARPNESS + 1] * (coord - center) ** 2)


def slope(params, coord, axis):
    return coord * params[SLOPE + axis : SLOPE + axis + 1]


def x_factors(params, maps, size_x):
    coord = coordinate(iota((size_x, LANES), 0), size_x)
    return bump(params, coord, 0), jnp.where(first_term(maps), slope(params, coord, 0), 0.0)


def y_factors(params, maps, position, total_y):
    coord = coordinate(position, total_y)
    part = slope(params, coord, 1) + params[OFFSET : OFFSET + 1]
    return bump(params, coord, 1), jnp.where(
        first_term(maps), part, params[SLOPE + 2 : SLOPE + 3]
    )


def z_rows(params, maps, position, total_z):
    coord = coordinate(position, total_z)
    return bump(params, coord, 2) * jnp.where(first_term(maps), 1.0, coord)


def inner_z_rows(params, maps, z_start, size_z, total_z):
    return z_rows(params, maps, z_start + iota((size_z, LANES), 0), total_z)


def outer_z_rows(params, maps, z_start, size_z, total_z):
    row = iota((size_z, LANES), 0)
    return z_rows(
        params, maps, jnp.where(row == 0, z_start + size_z, z_start - 1), total_z
    )


def only(rows, maps, component):
    return jnp.where(component_of(maps) == component, rows, 0.0)


def y_rows(params, maps, position, total_y):
    coord = coordinate(position, total_y)
    part = slope(params, coord, 1) + params[OFFSET : OFFSET + 1]
    return bump(params, coord, 1) * jnp.where(first_term(maps), part, 1.0)


def xz_rows(params, maps, size_x, z_start, size_z, total_z):
    row = iota((2 * size_x, LANES), 0)
    x_coord = coordinate(row // 2, size_x)
    z_coord = coordinate(jnp.where(row % 2 == 0, z_start - 1, z_start + size_z), total_z)
    part = slope(params, x_coord, 0) + slope(params, z_coord, 2)
    both = bump(params, x_coord, 0) * bump(params, z_coord, 2)
    both = both * jnp.where(first_term(maps), 1.0, part)
    return jnp.concatenate(
        [both, jnp.zeros((LANES - 2 * size_x, LANES), jnp.float32)], axis=0
    )


def with_extra(main, row):
    return jnp.concatenate([main, jnp.broadcast_to(row, (ROWS, LANES))], axis=0)


def pack_planes(planes):
    lane = iota(planes[0].shape, 1)
    out = jnp.zeros(planes[0].shape, jnp.float32)
    for i, plane in enumerate(planes):
        out = jnp.where(lane // 2 == i, roll(plane, 2 * i + 1, 1), out)
    return out


def merge_coefs(low, high):
    inverse = 1.0 / (1.0 - low[3] * high[0])
    onward, back = low[1] * inverse, high[2] * inverse
    return (
        low[0] + onward * high[0] * low[2],
        onward * high[1],
        back * low[2],
        high[3] + back * low[3] * high[1],
    )


def merge_values(low, high, low_values, high_values):
    inverse = 1.0 / (1.0 - low[3] * high[0])
    return (
        low_values[0] + low[1] * inverse * (high_values[0] + high[0] * low_values[1]),
        high_values[1] + high[2] * inverse * (low_values[1] + low[3] * high_values[0]),
    )


def chain(coefs, values, below, above):
    count = len(coefs)
    held, slope = below, None
    befores, firsts = [], []
    for j in range(count):
        a_first, c_first, a_last, c_last = coefs[j]
        r_first, r_last = values[j]
        befores.append((held, slope))
        if slope is None:
            first, first_slope = r_first + a_first * held, c_first
            held, slope = r_last + a_last * held, c_last
        else:
            inverse = 1.0 / (1.0 - a_first * slope)
            first = (r_first + a_first * held) * inverse
            first_slope = c_first * inverse
            held, slope = (
                r_last + a_last * (held + slope * first),
                c_last + a_last * slope * first_slope,
            )
        firsts.append((first, first_slope))
    seen_above = [None] * count
    seen_below = [None] * count
    upper = above
    for j in reversed(range(count)):
        seen_above[j] = upper
        upper = firsts[j][0] + firsts[j][1] * upper
        held, slope = befores[j]
        seen_below[j] = held if slope is None else held + slope * upper
    return seen_below, seen_above


def solve_x(up, down, source, pivot):
    size = source.shape[0]
    half = size // 2
    low_g, low_c, high_g, high_c = {}, {}, {}, {}
    g = c = None
    for i in range(half):
        if i == 0:
            weight = 1.0 / pivot
            c = down[1] * weight
            g = source[0] * weight
        else:
            weight = 1.0 / (pivot - up[i - 1] * c)
            g = (source[i] + up[i - 1] * g) * weight
            c = down[i + 1] * weight
        low_g[i], low_c[i] = g, c
    for i in reversed(range(half, size)):
        if i == size - 1:
            weight = 1.0 / pivot
            c = up[i - 1] * weight
            g = source[i] * weight
        else:
            weight = 1.0 / (pivot - down[i + 1] * c)
            g = (source[i] + down[i + 1] * g) * weight
            c = up[i - 1] * weight
        high_g[i], high_c[i] = g, c
    out = [None] * size
    inverse = 1.0 / (1.0 - low_c[half - 1] * high_c[half])
    out[half - 1] = (low_g[half - 1] + low_c[half - 1] * high_g[half]) * inverse
    out[half] = high_g[half] + high_c[half] * out[half - 1]
    for i in reversed(range(half - 1)):
        out[i] = low_g[i] + low_c[i] * out[i + 1]
    for i in range(half + 1, size):
        out[i] = high_g[i] + high_c[i] * out[i - 1]
    return out


def start_kernel(
    extent_y,
    extent_z,
    density_hbm,
    diffusion_hbm,
    centers_hbm,
    sharpness_hbm,
    affine_hbm,
    offsets_hbm,
    message,
    base,
    from_below,
    from_above,
    drift_z_out,
    prepared,
    solved,
    drift_y_held,
    density,
    diffusion,
    centers,
    sharpness,
    affine,
    offsets,
    staged,
    semaphores,
):
    copies = [
        pltpu.make_async_copy(source, target, semaphores.at[number])
        for number, (source, target) in enumerate(
            [
                (diffusion_hbm, diffusion),
                (centers_hbm, centers),
                (sharpness_hbm, sharpness),
                (affine_hbm, affine),
                (offsets_hbm, offsets),
                (density_hbm, density),
            ]
        )
    ]
    for copy in copies:
        copy.start()
    size_x, size_y, size_z = density.shape
    total_y, total_z = size_y * extent_y, size_z * extent_z
    y_start = lax.axis_index("gy") * size_y
    z_start = lax.axis_index("gz") * size_z
    maps = centers.shape[1]
    for copy in copies[:-1]:
        copy.wait()

    staged[...] = jnp.zeros(staged.shape, jnp.float32)
    staged[0:1, :maps] = sharpness[...]
    staged[1:4, :maps] = centers[...]
    for c in range(3):
        staged[4 + 3 * c : 7 + 3 * c, :maps] = affine[c]
    staged[13:16, :maps] = offsets[...]
    rows = staged[...]
    width = maps
    while width < LANES:
        rows = rows + roll(rows, width, 1)
        width = 2 * width
    component = component_of(maps)
    rows = jnp.where(component < 3, rows, 0.0)

    def by_component(first, step):
        return jnp.where(
            component == 0,
            rows[first : first + 1],
            jnp.where(
                component == 1,
                rows[first + step : first + step + 1],
                rows[first + 2 * step : first + 2 * step + 1],
            ),
        )

    weights = [jnp.broadcast_to(diffusion[:, c : c + 1], (1, LANES)) for c in range(3)]
    params = jnp.concatenate(
        [rows[0:4]]
        + [by_component(4 + j, 3) for j in range(3)]
        + [by_component(13, 1)]
        + weights
        + [jnp.zeros((PREPARED - DIFFUSION - 3, LANES), jnp.float32)],
        axis=0,
    )
    prepared[...] = params
    d0, d1, d2 = weights

    x_bump, x_part = x_factors(params, maps, size_x)
    y_row = iota((size_y, LANES), 0)
    y_bump, y_part = y_factors(params, maps, y_start + y_row, total_y)
    out_bump, out_part = y_factors(
        params, maps, jnp.where(y_row == 0, y_start + size_y, y_start - 1), total_y
    )
    inner = inner_z_rows(params, maps, z_start, size_z, total_z)
    outer = outer_z_rows(params, maps, z_start, size_z, total_z)
    inner = [only(inner, maps, c) for c in range(3)]
    outer = only(outer, maps, 0)

    def rows_by_x(bumps, part):
        return jnp.concatenate(
            [(x_bump[i : i + 1] * bumps) * (x_part[i : i + 1] + part) for i in range(size_x)],
            axis=0,
        )

    right = jnp.concatenate([inner[0], outer, inner[1], inner[2]], axis=0)
    drifts = half_drift(rows_by_x(y_bump, y_part), right)
    out_drift = half_drift(rows_by_x(out_bump, out_part), inner[0])

    def block(number):
        columns = drifts[:, number * LANES : (number + 1) * LANES]
        return columns.reshape(size_x, size_y, LANES)

    drift_x, plane_drift, drift_y, drift_z = block(0), block(1), block(2), block(3)
    out_drift = out_drift.reshape(size_x, size_y, LANES)
    drift_y_held[...] = drift_y
    drift_z_out[...] = drift_z
    copies[-1].wait()
    rho = density[...]
    zero = jnp.zeros((1, size_y, LANES), jnp.float32)
    up, down = (d0 + drift_x) * rho, (d0 - drift_x) * rho
    total = (
        jnp.concatenate([zero, up[:-1]], axis=0)
        + jnp.concatenate([down[1:], zero], axis=0)
        - (2.0 * (d0 + d1 + d2)) * rho
    )
    sublane = iota((size_x, size_y, LANES), 1)
    lane = iota((size_x, size_y, LANES), 2)
    up, down = roll((d1 + drift_y) * rho, 1, 1), roll((d1 - drift_y) * rho, -1, 1)
    at_low, at_high = sublane == 0, sublane == size_y - 1
    row_source = jnp.where(at_low, up, jnp.where(at_high, down, 0.0))
    total = total + jnp.where(at_low, 0.0, up) + jnp.where(at_high, 0.0, down)
    up, down = roll((d2 + drift_z) * rho, 1, 2), roll((d2 - drift_z) * rho, -1, 2)
    at_low, at_high = lane == 0, lane == size_z - 1
    plane_source = jnp.where(at_low, up, jnp.where(at_high, down, 0.0))
    total = total + jnp.where(at_low, 0.0, up) + jnp.where(at_high, 0.0, down)

    source = jnp.concatenate([total, row_source, plane_source], axis=1)
    drift = jnp.concatenate([drift_x, out_drift, plane_drift], axis=1)
    answers = solve_x(d0 + drift, d0 - drift, source, 1.0 + 2.0 * d0)
    for i in range(size_x):
        solved[i] = answers[i][: 2 * size_y]
    planes = pack_planes([answer[2 * size_y :] for answer in answers])

    row = iota((1, LANES), 0)
    out_rows = []
    for position in (y_start - 1, y_start + size_y):
        bumps, part = y_factors(params, maps, row + position, total_y)
        out_rows.append((x_bump * bumps) * (x_part + part))
    ends = half_drift(jnp.concatenate(out_rows, axis=0), inner[1])
    position = y_start - 1 + iota((2 * ROWS, LANES), 0)
    extra = half_drift(
        y_rows(params, maps, position, total_y),
        only(xz_rows(params, maps, size_x, z_start, size_z, total_z), maps, 1),
    )
    line_drift = (
        [ends[:size_x]]
        + [drift_y_held[:, j, :] for j in range(size_y)]
        + [ends[size_x:]]
    )
    line_drift = [with_extra(line_drift[j], extra[j : j + 1]) for j in range(size_y + 2)]
    pivot = 1.0 + 2.0 * d1
    at_start = y_start == 0
    at_end = y_start + size_y == total_y
    g = a = c = None
    gs, as_, cs = [], [], []
    for j in range(size_y):
        value = with_extra(solved[:, j, :], planes[j : j + 1])
        lower = d1 + line_drift[j]
        upper = d1 - line_drift[j + 2]
        if j == 0:
            lower = jnp.where(at_start, 0.0, lower)
        if j == size_y - 1:
            upper = jnp.where(at_end, 0.0, upper)
        if j == 0:
            weight = 1.0 / pivot
            g, a = value * weight, lower * weight
        else:
            weight = 1.0 / (pivot - lower * c)
            g, a = (value + lower * g) * weight, lower * a * weight
        c = upper * weight
        gs.append(g)
        as_.append(a)
        cs.append(c)
    base[size_y - 1], from_below[size_y - 1], from_above[size_y - 1] = g, a, c
    r_last = g
    for j in reversed(range(size_y - 1)):
        g, a, c = gs[j] + cs[j] * g, as_[j] + cs[j] * a, cs[j] * c
        base[j], from_below[j], from_above[j] = g, a, c
    pushed_up = solved[:, size_y, :] / (d1 + line_drift[size_y][:size_x])
    pushed_down = solved[:, 2 * size_y - 1, :] / (d1 - line_drift[1][:size_x])
    blank = jnp.zeros((1, LANES), jnp.float32)
    width = size_x + ROWS
    message[:width] = g + with_extra(pushed_down, blank)
    message[width:] = r_last + with_extra(pushed_up, blank)


def line_coefs(params, maps, sizes, start, count, store):
    extent_y, extent_z, size_x, size_y, size_z = sizes
    total_y, total_z = size_y * extent_y, size_z * extent_z
    z_start = lax.axis_index("gz") * size_z
    d1 = params[DIFFUSION + 1 : DIFFUSION + 2]
    x_bump, x_part = x_factors(params, maps, size_x)
    inner = only(inner_z_rows(params, maps, z_start, size_z, total_z), maps, 1)
    planes = only(xz_rows(params, maps, size_x, z_start, size_z, total_z), maps, 1)
    whole = count == extent_y
    offsets = list(range(size_y)) if whole else list(range(-1, size_y + 1))
    left, left_extra = [], []
    for j in offsets:
        for b in range(count):
            position = iota((1, LANES), 0) + ((start + b) * size_y + j)
            bumps, part = y_factors(params, maps, position, total_y)
            left.append((x_bump * bumps) * (x_part + part))
        block = iota((max(count, ROWS), LANES), 0)
        left_extra.append(
            y_rows(params, maps, (start + block) * size_y + j, total_y)
        )
    depth = left_extra[0].shape[0]
    main = half_drift(jnp.concatenate(left, axis=0), inner)
    main = main.reshape(len(offsets), count, size_x, LANES)
    main = [main[j] for j in range(len(offsets))]
    extra = half_drift(jnp.concatenate(left_extra, axis=0), planes)
    extra = [extra[j * depth : (j + 1) * depth] for j in range(len(offsets))]
    if whole:
        main = (
            [jnp.concatenate([main[-1][:1], main[-1][:-1]], axis=0)]
            + main
            + [jnp.concatenate([main[0][1:], main[0][-1:]], axis=0)]
        )
        extra = [roll(extra[-1], 1, 0)] + extra + [roll(extra[0], -1, 0)]
    numbers = start + iota((depth, LANES), 0)
    pivot = 1.0 + 2.0 * d1
    at_start, at_end = numbers == 0, numbers == extent_y - 1

    def scan(drifts, starts, ends):
        a_first = c_first = a_last = c_last = None
        for j in range(size_y):
            lower, upper = d1 + drifts[j], d1 - drifts[j + 2]
            if j == 0:
                lower = starts(lower)
            if j == size_y - 1:
                upper = ends(upper)
            if j == 0:
                weight = 1.0 / pivot
                a_first, c_first = lower * weight, upper * weight
                a_last, c_last = a_first, c_first
            else:
                weight = 1.0 / (pivot - lower * c_last)
                step, c_last = lower * weight, upper * weight
                a_last = step * a_last
                a_first = a_first + c_first * a_last
                c_first = c_first * c_last
        return a_first, c_first, a_last, c_last

    def masked(values, number):
        return jnp.concatenate(
            [
                jnp.where(start + b == number, 0.0, values[b])[None]
                for b in range(count)
            ],
            axis=0,
        )

    main = scan(main, lambda v: masked(v, 0), lambda v: masked(v, extent_y - 1))
    extra = scan(
        extra,
        lambda v: jnp.where(at_start, 0.0, v),
        lambda v: jnp.where(at_end, 0.0, v),
    )
    for b in range(count):
        for q in range(4):
            store(b, q, with_extra(main[q][b], extra[q][b : b + 1]))


def near_kernel(sizes, maps, stride, radix, prepared, coefs):
    digit = lax.rem(lax.div(lax.axis_index("gy"), stride), radix)
    start = lax.div(lax.axis_index("gy"), stride) - digit

    def store(b, q, value):
        coefs[b, q] = value

    line_coefs(prepared[...], maps, sizes, start, radix, store)


def far_kernel(sizes, maps, levels, prepared, *outputs):
    held = {}

    def store(b, q, value):
        held[b, q] = value

    extent_y = sizes[0]
    line_coefs(prepared[...], maps, sizes, 0, extent_y, store)
    groups = [tuple(held[b, q] for q in range(4)) for b in range(extent_y)]
    for (_, radix), coefs in zip(levels, outputs):
        groups = [
            functools.reduce(merge_coefs, groups[g : g + radix])
            for g in range(0, len(groups), radix)
        ]
        for number, group in enumerate(groups):
            for q in range(4):
                coefs[number, q] = group[q]


def z_coef_kernel(sizes, maps, prepared, drift_z, steps, ends, pushes, packed):
    extent_y, extent_z, size_x, size_y, size_z = sizes
    total_y, total_z = size_y * extent_y, size_z * extent_z
    y_start = lax.axis_index("gy") * size_y
    z_start = lax.axis_index("gz") * size_z
    params = prepared[...]
    d2 = params[DIFFUSION + 2 : DIFFUSION + 3]
    scale = 1.0 / (1.0 + 2.0 * d2)
    lane = iota((size_y, LANES), 1)
    divisors = []
    for i in range(size_x):
        plane = drift_z[i]
        divisors.append(
            1.0 / jnp.where(lane == 0, d2 + roll(plane, 1, 1), d2 - roll(plane, -1, 1))
        )
    pushes[...] = pack_planes(divisors)
    x_bump, x_part = x_factors(params, maps, size_x)
    outer = only(outer_z_rows(params, maps, z_start, size_z, total_z), maps, 2)
    rows = []
    for j in range(size_y):
        position = iota((1, LANES), 0) + (y_start + j)
        bumps, part = y_factors(params, maps, position, total_y)
        rows.append((x_bump * bumps) * (x_part + part))
    outer = half_drift(jnp.concatenate(rows, axis=0), outer)
    inner = jnp.concatenate([drift_z[:, j, :] for j in range(size_y)], axis=0)
    lane = iota(inner.shape, 1)
    low, high = lane == 0, lane == size_z - 1
    before = jnp.where(low, roll(outer, 1, 1), roll(inner, 1, 1))
    after = jnp.where(high, roll(outer, -1, 1), roll(inner, -1, 1))
    below = jnp.where(low & (z_start == 0), 0.0, (d2 + before) * scale)
    above = jnp.where(high & (z_start + size_z == total_z), 0.0, (d2 - after) * scale)
    shape = (size_y, size_x, LANES)
    stride, level = 1, 0
    while stride < size_z:
        low, high = lane < stride, lane >= size_z - stride
        low_a = jnp.where(low, 1.0, roll(below, stride, 1))
        low_c = jnp.where(low, 0.0, roll(above, stride, 1))
        high_a = jnp.where(high, 0.0, roll(below, -stride, 1))
        high_c = jnp.where(high, 1.0, roll(above, -stride, 1))
        inverse = 1.0 / (1.0 - below * low_c - above * high_a)
        below, above = below * inverse, above * inverse
        factor = scale if level == 0 else 1.0
        steps[level, 0] = (inverse * factor).reshape(shape)
        steps[level, 1] = jnp.where(low, 0.0, below * factor).reshape(shape)
        steps[level, 2] = jnp.where(high, 0.0, above * factor).reshape(shape)
        below, above = below * low_a, above * high_c
        stride, level = stride * 2, level + 1
    below, above = below.reshape(shape), above.reshape(shape)
    ends[0] = below
    ends[1] = above
    packed[...] = pack_ends([below[j] for j in range(size_y)], 1, size_y) + pack_ends(
        [above[j] for j in range(size_y)], 2, size_y
    )


def pack_ends(rows, slot, size_y):
    shape = rows[0].shape
    lane = iota(shape, 1)
    out = jnp.zeros(shape, jnp.float32)
    for j in range(size_y):
        first = slot * 2 * size_y + j
        last = first + size_y
        out = jnp.where(lane == first, roll(rows[j], first, 1), out)
        out = jnp.where(lane == last, roll(rows[j], last - (LANES - 1), 1), out)
    return out


def gather_members(refs, own, count):
    held = [ref[...] for ref in refs]
    return [
        functools.reduce(
            lambda acc, s: jnp.where((own ^ s) == j, held[s], acc), range(1, count), held[0]
        )
        for j in range(count)
    ]


def split_message(message):
    width = message.shape[0] // 2
    return message[:width], message[width:]


def merge_kernel(stride, radix, local, coefs, *refs):
    received, message = refs[:radix], refs[radix]
    digit = lax.rem(lax.div(lax.axis_index("gy"), stride), radix)
    first = 0 if local else lax.div(lax.axis_index("gy"), stride) - digit
    values = [split_message(m) for m in gather_members(received, digit, radix)]
    group = [tuple(coefs[first + j, q] for q in range(4)) for j in range(radix)]
    merged, total = group[0], values[0]
    for j in range(1, radix):
        total = merge_values(merged, group[j], total, values[j])
        merged = merge_coefs(merged, group[j])
    message[...] = jnp.concatenate(total, axis=0)


def middle_kernel(levels, *refs):
    refs = list(refs)
    steps, pushes, packed, base, from_below, from_above = refs[:6]
    refs = refs[6:]
    inputs = []
    for stride, radix in levels:
        inputs.append((refs[0], refs[1 : 1 + radix]))
        refs = refs[1 + radix :]
    message, doubled, seen, turned = refs
    size_y, width = base.shape[:2]
    size_x = width - ROWS
    below = above = jnp.zeros((width, LANES), jnp.float32)
    for number in reversed(range(len(levels))):
        (stride, radix), (coefs, received) = levels[number], inputs[number]
        digit = lax.rem(lax.div(lax.axis_index("gy"), stride), radix)
        first = 0 if number == 0 else lax.div(lax.axis_index("gy"), stride) - digit
        values = [split_message(m) for m in gather_members(received, digit, radix)]
        group = [tuple(coefs[first + j, q] for q in range(4)) for j in range(radix)]
        lows, highs = chain(group, values, below, above)
        for j in range(radix):
            seen[j, 0] = lows[j]
            seen[j, 1] = highs[j]
        below, above = seen[digit, 0], seen[digit, 1]
    inner, outer = [], []
    for j in range(size_y):
        value = base[j] + from_below[j] * below + from_above[j] * above
        inner.append(value[:size_x])
        outer.append(value[size_x : size_x + 1])
    turned[...] = jnp.transpose(jnp.concatenate(outer, axis=0) * pushes[...])
    values = jnp.stack(inner)
    stride, level = 1, 0
    while stride < LANES:
        values = (
            steps[level, 0] * values
            + steps[level, 1] * roll(values, stride, 2)
            + steps[level, 2] * roll(values, -stride, 2)
        )
        stride, level = stride * 2, level + 1
    doubled[...] = values
    ends = pack_ends([values[j] for j in range(size_y)], 0, size_y) + packed[...]
    message[...] = ends
    message[:, :size_y] = ends[:, :size_y] + turned[pl.ds(0, size_x, stride=2), :]
    message[:, size_y : 2 * size_y] = (
        ends[:, size_y : 2 * size_y] + turned[pl.ds(1, size_x, stride=2), :]
    )


def merge_z(low, high):
    inverse = 1.0 / (1.0 - low[5] * high[2])
    onward, back = low[4] * inverse, high[3] * inverse
    return (
        low[0] + onward * (high[0] + high[2] * low[1]),
        high[1] + back * (low[1] + low[5] * high[0]),
        low[2] + onward * high[2] * low[3],
        back * low[3],
        onward * high[4],
        high[5] + back * low[5] * high[4],
    )


def unpack_ends(message, size_y):
    return tuple(message if s == 0 else roll(message, -s * size_y, 1) for s in range(6))


def merge_z_kernel(stride, radix, size_y, *refs):
    received, message = refs[:radix], refs[radix]
    digit = lax.rem(lax.div(lax.axis_index("gz"), stride), radix)
    members = [unpack_ends(m, size_y) for m in gather_members(received, digit, radix)]
    total = functools.reduce(merge_z, members)
    lane = iota(total[0].shape, 1)
    out = jnp.zeros(total[0].shape, jnp.float32)
    for s in range(6):
        shifted = total[s] if s == 0 else roll(total[s], s * size_y, 1)
        out = jnp.where(lane // size_y == s, shifted, out)
    message[...] = out


def end_kernel(levels, density, doubled, ends, *refs):
    refs = list(refs)
    inputs = []
    for stride, radix in levels:
        inputs.append(refs[:radix])
        refs = refs[radix:]
    out, seen = refs
    size_x, size_y, _ = density.shape
    below = above = jnp.zeros((size_x, LANES), jnp.float32)
    for (stride, radix), received in zip(reversed(levels), reversed(inputs)):
        digit = lax.rem(lax.div(lax.axis_index("gz"), stride), radix)
        members = [unpack_ends(m, size_y) for m in gather_members(received, digit, radix)]
        lows, highs = chain(
            [(m[2], m[4], m[3], m[5]) for m in members],
            [(m[0], m[1]) for m in members],
            below,
            above,
        )
        for j in range(radix):
            seen[j, 0] = lows[j]
            seen[j, 1] = highs[j]
        below, above = seen[digit, 0], seen[digit, 1]
    for j in range(size_y):
        out[:, j, :] = (
            density[:, j, :]
            + doubled[j]
            + ends[0, j] * below[:, j : j + 1]
            + ends[1, j] * above[:, j : j + 1]
        )


def radices(extent):
    rounds, stride = [], 1
    while stride < extent:
        left = extent // stride
        power = left.bit_length() - 1
        radix = 4 if left % 4 == 0 and power % 2 == 0 else 2
        rounds.append((stride, radix))
        stride *= radix
    return rounds


def exchange(message, axis, stride, radix):
    devices = range(lax.axis_size(axis))
    return [message] + [
        lax.ppermute(message, axis, [(i, i ^ (s * stride)) for i in devices])
        for s in range(1, radix)
    ]


def body(density, diffusion, centers, sharpness, affine, offsets):
    size_x, size_y, size_z = density.shape
    extent_y, extent_z = lax.axis_size("gy"), lax.axis_size("gz")
    sizes = (extent_y, extent_z, size_x, size_y, size_z)
    maps = centers.shape[0]
    width = size_x + ROWS
    wide = (size_y, width, LANES)
    narrow = (size_y, size_x, LANES)
    float32 = jnp.float32
    y_levels, z_levels = radices(extent_y), radices(extent_z)

    def shape(*dims):
        return jax.ShapeDtypeStruct(dims, float32)

    vmem = pl.BlockSpec(memory_space=pltpu.VMEM)
    hbm = pl.BlockSpec(memory_space=pltpu.HBM)

    def call(kernel, inputs, outputs, in_specs=None, scratch=(), flops=10**6):
        return pl.pallas_call(
            kernel,
            out_shape=outputs,
            in_specs=in_specs or [vmem] * len(inputs),
            out_specs=jax.tree.map(lambda _: vmem, outputs),
            scratch_shapes=list(scratch),
            compiler_params=pltpu.CompilerParams(vmem_limit_bytes=VMEM_LIMIT),
            cost_estimate=pl.CostEstimate(flops=flops, bytes_accessed=10**6, transcendentals=0),
        )(*inputs)

    raw = (
        density,
        diffusion.reshape(1, 3),
        centers.T,
        sharpness.reshape(1, maps),
        affine.transpose(1, 2, 0),
        offsets.T,
    )
    raw = tuple(pltpu.with_memory_space_constraint(array, pltpu.HBM) for array in raw)
    message, base, from_below, from_above, drift_z, prepared = call(
        functools.partial(start_kernel, extent_y, extent_z),
        raw,
        (
            shape(2 * width, LANES),
            shape(*wide),
            shape(*wide),
            shape(*wide),
            shape(size_x, size_y, LANES),
            shape(PREPARED, LANES),
        ),
        [hbm] * len(raw),
        [
            pltpu.VMEM((size_x, 2 * size_y, LANES), float32),
            pltpu.VMEM((size_x, size_y, LANES), float32),
        ]
        + [pltpu.VMEM(array.shape, float32) for array in raw]
        + [pltpu.VMEM((PREPARED, LANES), float32), pltpu.SemaphoreType.DMA((len(raw),))],
    )
    stride, radix = y_levels[0]
    near = call(
        functools.partial(near_kernel, sizes, maps, stride, radix),
        [prepared],
        shape(radix, 4, width, LANES),
    )
    far, count = [], extent_y
    for _, radix in y_levels[:-1]:
        count = count // radix
        far.append(shape(count, 4, width, LANES))
    if far:
        far = call(functools.partial(far_kernel, sizes, maps, y_levels[:-1]), [prepared], far)
    coefs = [near] + list(far)
    doublings = size_z.bit_length() - 1
    steps, ends, pushes, packed = call(
        functools.partial(z_coef_kernel, sizes, maps),
        (prepared, drift_z),
        (
            shape(doublings, 3, *narrow),
            shape(2, *narrow),
            shape(size_y, LANES),
            shape(size_x, LANES),
        ),
    )
    line_inputs = []
    for number, (stride, radix) in enumerate(y_levels):
        received = exchange(message, "gy", stride, radix)
        line_inputs += [coefs[number]] + received
        if number + 1 < len(y_levels):
            message = call(
                functools.partial(merge_kernel, stride, radix, number == 0),
                [coefs[number]] + received,
                shape(2 * width, LANES),
            )
    message, doubled = call(
        functools.partial(middle_kernel, y_levels),
        [steps, pushes, packed, base, from_below, from_above] + line_inputs,
        (shape(size_x, LANES), shape(*narrow)),
        scratch=[
            pltpu.VMEM((4, 2, width, LANES), float32),
            pltpu.VMEM((LANES, size_y), float32),
        ],
    )
    end_inputs = []
    for number, (stride, radix) in enumerate(z_levels):
        received = exchange(message, "gz", stride, radix)
        end_inputs += received
        if number + 1 < len(z_levels):
            message = call(
                functools.partial(merge_z_kernel, stride, radix, size_y),
                received,
                shape(size_x, LANES),
            )
    return call(
        functools.partial(end_kernel, z_levels),
        [density, doubled, ends] + end_inputs,
        shape(size_x, size_y, size_z),
        scratch=[pltpu.VMEM((4, 2, size_x, LANES), float32)],
    )


def solution(mesh):
    placed = (P(None, "gy", "gz"), P(), P(), P(), P(), P())
    return jax.shard_map(
        body, mesh=mesh, in_specs=placed, out_specs=P(None, "gy", "gz"), check_vma=False
    )
```

```python
import functools

import jax
import jax.numpy as jnp
from jax import lax
from jax.experimental import pallas as pl
from jax.experimental.pallas import tpu as pltpu
from jax.sharding import PartitionSpec as P

HALF_LIMIT = 600.0
LANES = 128
ROWS = 8
VMEM_LIMIT = 48 * 1024 * 1024


def iota(shape, axis):
    return lax.broadcasted_iota(jnp.int32, shape, axis)


def coordinate(positions, line_total):
    return (2.0 * positions.astype(jnp.float32) + 1.0) / line_total - 1.0


def roll(values, shift, axis):
    return pltpu.roll(values, shift % values.shape[axis], axis)


def matmul(left, right):
    low, high = split(left), split(right)
    columns = right.shape[0]
    both = lax.dot_general(
        jnp.concatenate(low, axis=1),
        jnp.concatenate([jnp.concatenate([part, part], axis=1) for part in high], axis=0),
        (((1,), (1,)), ((), ())),
        preferred_element_type=jnp.float32,
    )
    return both[:, :columns] + both[:, columns:]


def split(values):
    upper = values.astype(jnp.bfloat16)
    return upper, (values - upper.astype(jnp.float32)).astype(jnp.bfloat16)


def half_drift(left, right):
    return HALF_LIMIT * jnp.tanh(matmul(left, right))


SHARPNESS, CENTER, SLOPE, OFFSET, DIFFUSION, PREPARED = 0, 1, 4, 7, 8, 16


def component_of(maps):
    return iota((1, LANES), 1) // (2 * maps)


def first_term(maps):
    return (iota((1, LANES), 1) // maps) % 2 == 0


def bump(params, coord, axis):
    center = params[CENTER + axis : CENTER + axis + 1]
    return jnp.exp(-params[SHARPNESS : SHARPNESS + 1] * (coord - center) ** 2)


def slope(params, coord, axis):
    return coord * params[SLOPE + axis : SLOPE + axis + 1]


def x_factors(params, maps, size_x):
    coord = coordinate(iota((size_x, LANES), 0), size_x)
    return bump(params, coord, 0), jnp.where(first_term(maps), slope(params, coord, 0), 0.0)


def y_factors(params, maps, position, total_y):
    coord = coordinate(position, total_y)
    part = slope(params, coord, 1) + params[OFFSET : OFFSET + 1]
    return bump(params, coord, 1), jnp.where(
        first_term(maps), part, params[SLOPE + 2 : SLOPE + 3]
    )


def z_rows(params, maps, position, total_z):
    coord = coordinate(position, total_z)
    return bump(params, coord, 2) * jnp.where(first_term(maps), 1.0, coord)


def inner_z_rows(params, maps, z_start, size_z, total_z):
    return z_rows(params, maps, z_start + iota((size_z, LANES), 0), total_z)


def outer_z_rows(params, maps, z_start, size_z, total_z):
    row = iota((size_z, LANES), 0)
    return z_rows(
        params, maps, jnp.where(row == 0, z_start + size_z, z_start - 1), total_z
    )


def only(rows, maps, component):
    return jnp.where(component_of(maps) == component, rows, 0.0)


def y_rows(params, maps, position, total_y):
    coord = coordinate(position, total_y)
    part = slope(params, coord, 1) + params[OFFSET : OFFSET + 1]
    return bump(params, coord, 1) * jnp.where(first_term(maps), part, 1.0)


def xz_rows(params, maps, size_x, z_start, size_z, total_z):
    row = iota((2 * size_x, LANES), 0)
    x_coord = coordinate(row % size_x, size_x)
    z_coord = coordinate(jnp.where(row < size_x, z_start - 1, z_start + size_z), total_z)
    part = slope(params, x_coord, 0) + slope(params, z_coord, 2)
    both = bump(params, x_coord, 0) * bump(params, z_coord, 2)
    both = both * jnp.where(first_term(maps), 1.0, part)
    return jnp.concatenate(
        [both, jnp.zeros((LANES - 2 * size_x, LANES), jnp.float32)], axis=0
    )


def with_extra(main, row):
    return jnp.concatenate([main, jnp.broadcast_to(row, (ROWS, LANES))], axis=0)


def pack_planes(planes):
    lane = iota(planes[0].shape, 1)
    first = last = jnp.zeros(planes[0].shape, jnp.float32)
    for i, plane in enumerate(planes):
        turned = roll(plane, i + 1, 1)
        first = jnp.where(lane == i, turned, first)
        last = jnp.where(lane == i + 1, turned, last)
    return first + roll(last, len(planes) - 1, 1)


def lines_of(planes, size_x, side):
    group = LANES // size_x
    place = iota((1, LANES), 1) // size_x
    turned = [roll(planes, (q - side) * size_x, 1) for q in range(group)]
    rows = []
    for first in range(0, planes.shape[0], group):
        row = turned[0][first : first + 1]
        for q in range(1, group):
            row = jnp.where(place == q, turned[q][first + q : first + q + 1], row)
        rows.append(row)
    return jnp.concatenate(rows, axis=1)


def to_lines(rows, size_x):
    group = LANES // size_x
    return jnp.concatenate(
        [
            jnp.transpose(jnp.concatenate(rows[first : first + group], axis=0))
            for first in range(0, len(rows), group)
        ],
        axis=1,
    )


def turn(values, stride):
    stride = stride % values.shape[0]
    if stride % ROWS == 0:
        return jnp.concatenate([values[-stride:], values[:-stride]], axis=0)
    return roll(values, stride, 0)


def merge_coefs(low, high):
    inverse = 1.0 / (1.0 - low[3] * high[0])
    onward, back = low[1] * inverse, high[2] * inverse
    return (
        low[0] + onward * high[0] * low[2],
        onward * high[1],
        back * low[2],
        high[3] + back * low[3] * high[1],
    )


def merge_values(low, high, low_values, high_values):
    inverse = 1.0 / (1.0 - low[3] * high[0])
    return (
        low_values[0] + low[1] * inverse * (high_values[0] + high[0] * low_values[1]),
        high_values[1] + high[2] * inverse * (low_values[1] + low[3] * high_values[0]),
    )


def chain(coefs, values, below, above):
    count = len(coefs)
    held, slope = below, None
    befores, firsts = [], []
    for j in range(count):
        a_first, c_first, a_last, c_last = coefs[j]
        r_first, r_last = values[j]
        befores.append((held, slope))
        if slope is None:
            first, first_slope = r_first + a_first * held, c_first
            held, slope = r_last + a_last * held, c_last
        else:
            inverse = 1.0 / (1.0 - a_first * slope)
            first = (r_first + a_first * held) * inverse
            first_slope = c_first * inverse
            held, slope = (
                r_last + a_last * (held + slope * first),
                c_last + a_last * slope * first_slope,
            )
        firsts.append((first, first_slope))
    seen_above = [None] * count
    seen_below = [None] * count
    upper = above
    for j in reversed(range(count)):
        seen_above[j] = upper
        upper = firsts[j][0] + firsts[j][1] * upper
        held, slope = befores[j]
        seen_below[j] = held if slope is None else held + slope * upper
    return seen_below, seen_above


def solve_x(up, down, source, pivot):
    size = source.shape[0]
    half = size // 2
    low_g, low_c, high_g, high_c = {}, {}, {}, {}
    g = c = None
    for i in range(half):
        if i == 0:
            weight = 1.0 / pivot
            c = down[1] * weight
            g = source[0] * weight
        else:
            weight = 1.0 / (pivot - up[i - 1] * c)
            g = (source[i] + up[i - 1] * g) * weight
            c = down[i + 1] * weight
        low_g[i], low_c[i] = g, c
    for i in reversed(range(half, size)):
        if i == size - 1:
            weight = 1.0 / pivot
            c = up[i - 1] * weight
            g = source[i] * weight
        else:
            weight = 1.0 / (pivot - down[i + 1] * c)
            g = (source[i] + down[i + 1] * g) * weight
            c = up[i - 1] * weight
        high_g[i], high_c[i] = g, c
    out = [None] * size
    inverse = 1.0 / (1.0 - low_c[half - 1] * high_c[half])
    out[half - 1] = (low_g[half - 1] + low_c[half - 1] * high_g[half]) * inverse
    out[half] = high_g[half] + high_c[half] * out[half - 1]
    for i in reversed(range(half - 1)):
        out[i] = low_g[i] + low_c[i] * out[i + 1]
    for i in range(half + 1, size):
        out[i] = high_g[i] + high_c[i] * out[i - 1]
    return out


def start_kernel(
    extent_y,
    extent_z,
    density_hbm,
    diffusion_hbm,
    centers_hbm,
    sharpness_hbm,
    affine_hbm,
    offsets_hbm,
    message,
    line_values,
    line_drifts,
    drift_z_out,
    prepared,
    solved,
    drift_y_held,
    density,
    diffusion,
    centers,
    sharpness,
    affine,
    offsets,
    staged,
    semaphores,
):
    copies = [
        pltpu.make_async_copy(source, target, semaphores.at[number])
        for number, (source, target) in enumerate(
            [
                (diffusion_hbm, diffusion),
                (centers_hbm, centers),
                (sharpness_hbm, sharpness),
                (affine_hbm, affine),
                (offsets_hbm, offsets),
                (density_hbm, density),
            ]
        )
    ]
    for copy in copies:
        copy.start()
    size_x, size_y, size_z = density.shape
    total_y, total_z = size_y * extent_y, size_z * extent_z
    y_start = lax.axis_index("gy") * size_y
    z_start = lax.axis_index("gz") * size_z
    maps = centers.shape[1]
    for copy in copies[:-1]:
        copy.wait()

    staged[...] = jnp.zeros(staged.shape, jnp.float32)
    staged[0:1, :maps] = sharpness[...]
    staged[1:4, :maps] = centers[...]
    for c in range(3):
        staged[4 + 3 * c : 7 + 3 * c, :maps] = affine[c]
    staged[13:16, :maps] = offsets[...]
    rows = staged[...]
    width = maps
    while width < LANES:
        rows = rows + roll(rows, width, 1)
        width = 2 * width
    component = component_of(maps)
    rows = jnp.where(component < 3, rows, 0.0)

    def by_component(first, step):
        return jnp.where(
            component == 0,
            rows[first : first + 1],
            jnp.where(
                component == 1,
                rows[first + step : first + step + 1],
                rows[first + 2 * step : first + 2 * step + 1],
            ),
        )

    weights = [jnp.broadcast_to(diffusion[:, c : c + 1], (1, LANES)) for c in range(3)]
    params = jnp.concatenate(
        [rows[0:4]]
        + [by_component(4 + j, 3) for j in range(3)]
        + [by_component(13, 1)]
        + weights
        + [jnp.zeros((PREPARED - DIFFUSION - 3, LANES), jnp.float32)],
        axis=0,
    )
    prepared[...] = params
    d0, d1, d2 = weights

    x_bump, x_part = x_factors(params, maps, size_x)
    y_row = iota((size_y, LANES), 0)
    y_bump, y_part = y_factors(params, maps, y_start + y_row, total_y)
    out_bump, out_part = y_factors(
        params, maps, jnp.where(y_row == 0, y_start + size_y, y_start - 1), total_y
    )
    inner = inner_z_rows(params, maps, z_start, size_z, total_z)
    outer = outer_z_rows(params, maps, z_start, size_z, total_z)
    inner = [only(inner, maps, c) for c in range(3)]
    outer = only(outer, maps, 0)

    def rows_by_x(bumps, part):
        return jnp.concatenate(
            [(x_bump[i : i + 1] * bumps) * (x_part[i : i + 1] + part) for i in range(size_x)],
            axis=0,
        )

    right = jnp.concatenate([inner[0], outer, inner[1], inner[2]], axis=0)
    drifts = half_drift(rows_by_x(y_bump, y_part), right)
    out_drift = half_drift(rows_by_x(out_bump, out_part), inner[0])

    def block(number):
        columns = drifts[:, number * LANES : (number + 1) * LANES]
        return columns.reshape(size_x, size_y, LANES)

    drift_x, plane_drift, drift_y, drift_z = block(0), block(1), block(2), block(3)
    out_drift = out_drift.reshape(size_x, size_y, LANES)
    drift_y_held[...] = drift_y
    drift_z_out[...] = drift_z
    copies[-1].wait()
    rho = density[...]
    zero = jnp.zeros((1, size_y, LANES), jnp.float32)
    up, down = (d0 + drift_x) * rho, (d0 - drift_x) * rho
    total = (
        jnp.concatenate([zero, up[:-1]], axis=0)
        + jnp.concatenate([down[1:], zero], axis=0)
        - (2.0 * (d0 + d1 + d2)) * rho
    )
    sublane = iota((size_x, size_y, LANES), 1)
    lane = iota((size_x, size_y, LANES), 2)
    up, down = roll((d1 + drift_y) * rho, 1, 1), roll((d1 - drift_y) * rho, -1, 1)
    at_low, at_high = sublane == 0, sublane == size_y - 1
    row_source = jnp.where(at_low, up, jnp.where(at_high, down, 0.0))
    total = total + jnp.where(at_low, 0.0, up) + jnp.where(at_high, 0.0, down)
    up, down = roll((d2 + drift_z) * rho, 1, 2), roll((d2 - drift_z) * rho, -1, 2)
    at_low, at_high = lane == 0, lane == size_z - 1
    plane_source = jnp.where(at_low, up, jnp.where(at_high, down, 0.0))
    total = total + jnp.where(at_low, 0.0, up) + jnp.where(at_high, 0.0, down)

    source = jnp.concatenate([total, row_source, plane_source], axis=1)
    drift = jnp.concatenate([drift_x, out_drift, plane_drift], axis=1)
    answers = solve_x(d0 + drift, d0 - drift, source, 1.0 + 2.0 * d0)
    for i in range(size_x):
        solved[i] = answers[i][: 2 * size_y]
    planes = pack_planes([answer[2 * size_y :] for answer in answers])

    row = iota((1, LANES), 0)
    out_rows = []
    for position in (y_start - 1, y_start + size_y):
        bumps, part = y_factors(params, maps, row + position, total_y)
        out_rows.append((x_bump * bumps) * (x_part + part))
    ends = half_drift(jnp.concatenate(out_rows, axis=0), inner[1])
    position = y_start - 1 + iota((2 * ROWS, LANES), 0)
    extra = half_drift(
        y_rows(params, maps, position, total_y),
        only(xz_rows(params, maps, size_x, z_start, size_z, total_z), maps, 1),
    )
    line_drift = (
        [ends[:size_x]]
        + [drift_y_held[:, j, :] for j in range(size_y)]
        + [ends[size_x:]]
    )
    line_drift = [with_extra(line_drift[j], extra[j : j + 1]) for j in range(size_y + 2)]
    values = [with_extra(solved[:, j, :], planes[j : j + 1]) for j in range(size_y)]
    for j in range(size_y):
        line_values[j] = values[j]
    for j in range(size_y + 2):
        line_drifts[j] = line_drift[j]
    pivot = 1.0 + 2.0 * d1
    g = c = None
    gs, cs = [], []
    for j in range(size_y):
        lower, upper = line_factors(line_drift, j, size_y, d1, y_start, total_y)
        weight = 1.0 / (pivot if j == 0 else pivot - lower * c)
        g = (values[j] if j == 0 else values[j] + lower * g) * weight
        c = upper * weight
        gs.append(g)
        cs.append(c)
    r_first = r_last = g
    for j in reversed(range(size_y - 1)):
        r_first = gs[j] + cs[j] * r_first
    pushed_up = solved[:, size_y, :] / (d1 + line_drift[size_y][:size_x])
    pushed_down = solved[:, 2 * size_y - 1, :] / (d1 - line_drift[1][:size_x])
    blank = jnp.zeros((1, LANES), jnp.float32)
    width = size_x + ROWS
    message[:width] = r_first + with_extra(pushed_down, blank)
    message[width:] = r_last + with_extra(pushed_up, blank)


def line_factors(line_drift, j, size_y, d1, y_start, total_y):
    lower, upper = d1 + line_drift[j], d1 - line_drift[j + 2]
    if j == 0:
        lower = jnp.where(y_start == 0, 0.0, lower)
    if j == size_y - 1:
        upper = jnp.where(y_start + size_y == total_y, 0.0, upper)
    return lower, upper


def line_coefs(params, maps, sizes, start, count, store):
    extent_y, extent_z, size_x, size_y, size_z = sizes
    total_y, total_z = size_y * extent_y, size_z * extent_z
    z_start = lax.axis_index("gz") * size_z
    d1 = params[DIFFUSION + 1 : DIFFUSION + 2]
    x_bump, x_part = x_factors(params, maps, size_x)
    inner = only(inner_z_rows(params, maps, z_start, size_z, total_z), maps, 1)
    planes = only(xz_rows(params, maps, size_x, z_start, size_z, total_z), maps, 1)
    whole = count == extent_y
    offsets = list(range(size_y)) if whole else list(range(-1, size_y + 1))
    left, left_extra = [], []
    for j in offsets:
        for b in range(count):
            position = iota((1, LANES), 0) + ((start + b) * size_y + j)
            bumps, part = y_factors(params, maps, position, total_y)
            left.append((x_bump * bumps) * (x_part + part))
        block = iota((max(count, ROWS), LANES), 0)
        left_extra.append(
            y_rows(params, maps, (start + block) * size_y + j, total_y)
        )
    depth = left_extra[0].shape[0]
    main = half_drift(jnp.concatenate(left, axis=0), inner)
    main = main.reshape(len(offsets), count, size_x, LANES)
    main = [main[j] for j in range(len(offsets))]
    extra = half_drift(jnp.concatenate(left_extra, axis=0), planes)
    extra = [extra[j * depth : (j + 1) * depth] for j in range(len(offsets))]
    if whole:
        main = (
            [jnp.concatenate([main[-1][:1], main[-1][:-1]], axis=0)]
            + main
            + [jnp.concatenate([main[0][1:], main[0][-1:]], axis=0)]
        )
        extra = [roll(extra[-1], 1, 0)] + extra + [roll(extra[0], -1, 0)]
    numbers = start + iota((depth, LANES), 0)
    pivot = 1.0 + 2.0 * d1
    at_start, at_end = numbers == 0, numbers == extent_y - 1

    def scan(drifts, starts, ends):
        a_first = c_first = a_last = c_last = None
        for j in range(size_y):
            lower, upper = d1 + drifts[j], d1 - drifts[j + 2]
            if j == 0:
                lower = starts(lower)
            if j == size_y - 1:
                upper = ends(upper)
            if j == 0:
                weight = 1.0 / pivot
                a_first, c_first = lower * weight, upper * weight
                a_last, c_last = a_first, c_first
            else:
                weight = 1.0 / (pivot - lower * c_last)
                step, c_last = lower * weight, upper * weight
                a_last = step * a_last
                a_first = a_first + c_first * a_last
                c_first = c_first * c_last
        return a_first, c_first, a_last, c_last

    def masked(values, number):
        return jnp.concatenate(
            [
                jnp.where(start + b == number, 0.0, values[b])[None]
                for b in range(count)
            ],
            axis=0,
        )

    main = scan(main, lambda v: masked(v, 0), lambda v: masked(v, extent_y - 1))
    extra = scan(
        extra,
        lambda v: jnp.where(at_start, 0.0, v),
        lambda v: jnp.where(at_end, 0.0, v),
    )
    for b in range(count):
        for q in range(4):
            store(b, q, with_extra(main[q][b], extra[q][b : b + 1]))


def near_kernel(
    sizes,
    maps,
    stride,
    radix,
    prepared,
    line_values,
    line_drifts,
    coefs,
    base,
    from_below,
    from_above,
):
    digit = lax.rem(lax.div(lax.axis_index("gy"), stride), radix)
    start = lax.div(lax.axis_index("gy"), stride) - digit
    params = prepared[...]

    def store(b, q, value):
        coefs[b, q] = value

    line_coefs(params, maps, sizes, start, radix, store)
    extent_y, _, _, size_y, _ = sizes
    d1 = params[DIFFUSION + 1 : DIFFUSION + 2]
    pivot = 1.0 + 2.0 * d1
    y_start = lax.axis_index("gy") * size_y
    g = a = c = None
    gs, as_, cs = [], [], []
    for j in range(size_y):
        lower, upper = line_factors(line_drifts, j, size_y, d1, y_start, size_y * extent_y)
        if j == 0:
            weight = 1.0 / pivot
            g, a = line_values[j] * weight, lower * weight
        else:
            weight = 1.0 / (pivot - lower * c)
            g, a = (line_values[j] + lower * g) * weight, lower * a * weight
        c = upper * weight
        gs.append(g)
        as_.append(a)
        cs.append(c)
    base[size_y - 1], from_below[size_y - 1], from_above[size_y - 1] = g, a, c
    for j in reversed(range(size_y - 1)):
        g, a, c = gs[j] + cs[j] * g, as_[j] + cs[j] * a, cs[j] * c
        base[j], from_below[j], from_above[j] = g, a, c


def far_kernel(sizes, maps, levels, prepared, *outputs):
    held = {}

    def store(b, q, value):
        held[b, q] = value

    extent_y = sizes[0]
    line_coefs(prepared[...], maps, sizes, 0, extent_y, store)
    groups = [tuple(held[b, q] for q in range(4)) for b in range(extent_y)]
    for (_, radix), coefs in zip(levels, outputs):
        groups = [
            functools.reduce(merge_coefs, groups[g : g + radix])
            for g in range(0, len(groups), radix)
        ]
        for number, group in enumerate(groups):
            for q in range(4):
                coefs[number, q] = group[q]


def z_coef_kernel(sizes, maps, prepared, drift_z, steps, ends, pushes, packed):
    extent_y, extent_z, size_x, size_y, size_z = sizes
    total_y, total_z = size_y * extent_y, size_z * extent_z
    y_start = lax.axis_index("gy") * size_y
    z_start = lax.axis_index("gz") * size_z
    params = prepared[...]
    d2 = params[DIFFUSION + 2 : DIFFUSION + 3]
    lane = iota((size_y, LANES), 1)
    divisors = []
    for i in range(size_x):
        plane = drift_z[i]
        divisors.append(
            1.0 / jnp.where(lane == 0, d2 + roll(plane, 1, 1), d2 - roll(plane, -1, 1))
        )
    pushes[...] = pack_planes(divisors)
    x_bump, x_part = x_factors(params, maps, size_x)
    outer = only(outer_z_rows(params, maps, z_start, size_z, total_z), maps, 2)
    rows = []
    for j in range(size_y):
        position = iota((1, LANES), 0) + (y_start + j)
        bumps, part = y_factors(params, maps, position, total_y)
        rows.append((x_bump * bumps) * (x_part + part))
    outer = half_drift(jnp.concatenate(rows, axis=0), outer)
    outer = to_lines([outer[j * size_x : (j + 1) * size_x] for j in range(size_y)], size_x)
    inner = to_lines([drift_z[:, j, :] for j in range(size_y)], size_x)
    d2 = jnp.concatenate([d2] * (inner.shape[1] // LANES), axis=1)
    scale = 1.0 / (1.0 + 2.0 * d2)
    row = iota(inner.shape, 0)
    low, high = row == 0, row == size_z - 1
    before = jnp.where(low, outer[size_z - 1 :], turn(inner, 1))
    after = jnp.where(high, outer[:1], turn(inner, -1))
    below = jnp.where(low & (z_start == 0), 0.0, (d2 + before) * scale)
    above = jnp.where(high & (z_start + size_z == total_z), 0.0, (d2 - after) * scale)
    stride, level = 1, 0
    while stride < size_z:
        low, high = row < stride, row >= size_z - stride
        low_a = jnp.where(low, 1.0, turn(below, stride))
        low_c = jnp.where(low, 0.0, turn(above, stride))
        high_a = jnp.where(high, 0.0, turn(below, -stride))
        high_c = jnp.where(high, 1.0, turn(above, -stride))
        inverse = 1.0 / (1.0 - below * low_c - above * high_a)
        below, above = below * inverse, above * inverse
        factor = scale if level == 0 else 1.0
        steps[level, 0] = inverse * factor
        steps[level, 1] = jnp.where(low, 0.0, below * factor)
        steps[level, 2] = jnp.where(high, 0.0, above * factor)
        below, above = below * low_a, above * high_c
        stride, level = stride * 2, level + 1
    ends[0] = below
    ends[1] = above
    packed[...] = jnp.concatenate(
        [
            jnp.zeros((2, inner.shape[1]), jnp.float32),
            below[:1],
            below[size_z - 1 :],
            above[:1],
            above[size_z - 1 :],
            jnp.zeros((2, inner.shape[1]), jnp.float32),
        ],
        axis=0,
    )


def gather_members(refs, own, count):
    held = [ref[...] for ref in refs]
    return [
        functools.reduce(
            lambda acc, s: jnp.where((own ^ s) == j, held[s], acc), range(1, count), held[0]
        )
        for j in range(count)
    ]


def split_message(message):
    width = message.shape[0] // 2
    return message[:width], message[width:]


def merge_kernel(stride, radix, local, coefs, *refs):
    received, message = refs[:radix], refs[-1]
    digit = lax.rem(lax.div(lax.axis_index("gy"), stride), radix)
    first = 0 if local else lax.div(lax.axis_index("gy"), stride) - digit
    values = [split_message(m) for m in gather_members(received, digit, radix)]
    group = [tuple(coefs[first + j, q] for q in range(4)) for j in range(radix)]
    merged, total = group[0], values[0]
    for j in range(1, radix):
        total = merge_values(merged, group[j], total, values[j])
        merged = merge_coefs(merged, group[j])
    message[...] = jnp.concatenate(total, axis=0)


def middle_kernel(levels, *refs):
    refs = list(refs)
    steps, pushes, packed, base, from_below, from_above = refs[:6]
    refs = refs[6:]
    inputs = []
    for stride, radix in levels:
        inputs.append((refs[0], refs[1 : 1 + radix]))
        refs = refs[1 + radix :]
    message, doubled, seen = refs
    size_y, width = base.shape[:2]
    size_x = width - ROWS
    below = above = jnp.zeros((width, LANES), jnp.float32)
    for number in reversed(range(len(levels))):
        (stride, radix), (coefs, received) = levels[number], inputs[number]
        digit = lax.rem(lax.div(lax.axis_index("gy"), stride), radix)
        first = 0 if number == 0 else lax.div(lax.axis_index("gy"), stride) - digit
        values = [split_message(m) for m in gather_members(received, digit, radix)]
        group = [tuple(coefs[first + j, q] for q in range(4)) for j in range(radix)]
        lows, highs = chain(group, values, below, above)
        for j in range(radix):
            seen[j, 0] = lows[j]
            seen[j, 1] = highs[j]
        below, above = seen[digit, 0], seen[digit, 1]
    inner, outer = [], []
    for j in range(size_y):
        value = base[j] + from_below[j] * below + from_above[j] * above
        inner.append(value[:size_x])
        outer.append(value[size_x : size_x + 1])
    pushed = jnp.concatenate(outer, axis=0) * pushes[...]
    values = to_lines(inner, size_x)
    stride, level = 1, 0
    while stride < values.shape[0]:
        values = (
            steps[level, 0] * values
            + steps[level, 1] * turn(values, stride)
            + steps[level, 2] * turn(values, -stride)
        )
        stride, level = stride * 2, level + 1
    doubled[...] = values
    message[...] = packed[...]
    message[0:1] = values[:1] + lines_of(pushed, size_x, 0)
    message[1:2] = values[-1:] + lines_of(pushed, size_x, 1)


def merge_z(low, high):
    inverse = 1.0 / (1.0 - low[5] * high[2])
    onward, back = low[4] * inverse, high[3] * inverse
    return (
        low[0] + onward * (high[0] + high[2] * low[1]),
        high[1] + back * (low[1] + low[5] * high[0]),
        low[2] + onward * high[2] * low[3],
        back * low[3],
        onward * high[4],
        high[5] + back * low[5] * high[4],
    )


def unpack_ends(message):
    return tuple(message[s : s + 1] for s in range(6))


def merge_z_kernel(stride, radix, *refs):
    received, message = refs[:radix], refs[radix]
    digit = lax.rem(lax.div(lax.axis_index("gz"), stride), radix)
    members = [unpack_ends(m) for m in gather_members(received, digit, radix)]
    total = functools.reduce(merge_z, members)
    message[...] = jnp.concatenate(total + total[:2], axis=0)


def end_kernel(levels, density, doubled, ends, *refs):
    refs = list(refs)
    inputs = []
    for stride, radix in levels:
        inputs.append(refs[:radix])
        refs = refs[radix:]
    out, seen = refs
    size_x, size_y, _ = density.shape
    below = above = jnp.zeros((1, doubled.shape[1]), jnp.float32)
    for (stride, radix), received in zip(reversed(levels), reversed(inputs)):
        digit = lax.rem(lax.div(lax.axis_index("gz"), stride), radix)
        members = [unpack_ends(m) for m in gather_members(received, digit, radix)]
        lows, highs = chain(
            [(m[2], m[4], m[3], m[5]) for m in members],
            [(m[0], m[1]) for m in members],
            below,
            above,
        )
        for j in range(radix):
            seen[j, 0:1] = lows[j]
            seen[j, 1:2] = highs[j]
        below, above = seen[digit, 0:1], seen[digit, 1:2]
    values = doubled[...] + ends[0] * below + ends[1] * above
    group = LANES // size_x
    for first in range(0, size_y, group):
        tile = first // group
        lines = jnp.transpose(values[:, tile * LANES : (tile + 1) * LANES])
        for q in range(group):
            out[:, first + q, :] = (
                density[:, first + q, :] + lines[q * size_x : (q + 1) * size_x]
            )


def radices(extent):
    rounds, stride = [], 1
    while stride < extent:
        radix = 4 if (extent // stride) % 4 == 0 else 2
        rounds.append((stride, radix))
        stride *= radix
    return rounds


def exchange(message, axis, stride, radix):
    devices = range(lax.axis_size(axis))
    return [message] + [
        lax.ppermute(message, axis, [(i, i ^ (s * stride)) for i in devices])
        for s in range(1, radix)
    ]


def body(density, diffusion, centers, sharpness, affine, offsets):
    size_x, size_y, size_z = density.shape
    extent_y, extent_z = lax.axis_size("gy"), lax.axis_size("gz")
    sizes = (extent_y, extent_z, size_x, size_y, size_z)
    maps = centers.shape[0]
    width = size_x + ROWS
    wide = (size_y, width, LANES)
    narrow = (size_z, size_y * size_x)
    float32 = jnp.float32
    y_levels, z_levels = radices(extent_y), radices(extent_z)

    def shape(*dims):
        return jax.ShapeDtypeStruct(dims, float32)

    vmem = pl.BlockSpec(memory_space=pltpu.VMEM)
    hbm = pl.BlockSpec(memory_space=pltpu.HBM)

    def call(kernel, inputs, outputs, in_specs=None, scratch=(), flops=10**6):
        return pl.pallas_call(
            kernel,
            out_shape=outputs,
            in_specs=in_specs or [vmem] * len(inputs),
            out_specs=jax.tree.map(lambda _: vmem, outputs),
            scratch_shapes=list(scratch),
            compiler_params=pltpu.CompilerParams(vmem_limit_bytes=VMEM_LIMIT),
            cost_estimate=pl.CostEstimate(flops=flops, bytes_accessed=10**6, transcendentals=0),
        )(*inputs)

    raw = (
        density,
        diffusion.reshape(1, 3),
        centers.T,
        sharpness.reshape(1, maps),
        affine.transpose(1, 2, 0),
        offsets.T,
    )
    raw = tuple(pltpu.with_memory_space_constraint(array, pltpu.HBM) for array in raw)
    message, line_values, line_drifts, drift_z, prepared = call(
        functools.partial(start_kernel, extent_y, extent_z),
        raw,
        (
            shape(2 * width, LANES),
            shape(*wide),
            shape(size_y + 2, width, LANES),
            shape(size_x, size_y, LANES),
            shape(PREPARED, LANES),
        ),
        [hbm] * len(raw),
        [
            pltpu.VMEM((size_x, 2 * size_y, LANES), float32),
            pltpu.VMEM((size_x, size_y, LANES), float32),
        ]
        + [pltpu.VMEM(array.shape, float32) for array in raw]
        + [pltpu.VMEM((PREPARED, LANES), float32), pltpu.SemaphoreType.DMA((len(raw),))],
    )
    stride, radix = y_levels[0]
    near, base, from_below, from_above = call(
        functools.partial(near_kernel, sizes, maps, stride, radix),
        [prepared, line_values, line_drifts],
        (shape(radix, 4, width, LANES), shape(*wide), shape(*wide), shape(*wide)),
    )
    far, count = [], extent_y
    for _, radix in y_levels[:-1]:
        count = count // radix
        far.append(shape(count, 4, width, LANES))
    if far:
        far = call(functools.partial(far_kernel, sizes, maps, y_levels[:-1]), [prepared], far)
    coefs = [near] + list(far)
    doublings = size_z.bit_length() - 1
    steps, ends, pushes, packed = call(
        functools.partial(z_coef_kernel, sizes, maps),
        (prepared, drift_z),
        (
            shape(doublings, 3, *narrow),
            shape(2, *narrow),
            shape(size_y, LANES),
            shape(ROWS, size_y * size_x),
        ),
    )
    line_inputs = []
    for number, (stride, radix) in enumerate(y_levels):
        received = exchange(message, "gy", stride, radix)
        line_inputs += [coefs[number]] + received
        if number + 1 < len(y_levels):
            message = call(
                functools.partial(merge_kernel, stride, radix, number == 0),
                [coefs[number]] + received + ([packed] if number == 0 else []),
                shape(2 * width, LANES),
            )
    message, doubled = call(
        functools.partial(middle_kernel, y_levels),
        [steps, pushes, packed, base, from_below, from_above] + line_inputs,
        (shape(ROWS, size_y * size_x), shape(*narrow)),
        scratch=[pltpu.VMEM((4, 2, width, LANES), float32)],
    )
    end_inputs = []
    for number, (stride, radix) in enumerate(z_levels):
        received = exchange(message, "gz", stride, radix)
        end_inputs += received
        if number + 1 < len(z_levels):
            message = call(
                functools.partial(merge_z_kernel, stride, radix),
                received,
                shape(ROWS, size_y * size_x),
            )
    return call(
        functools.partial(end_kernel, z_levels),
        [density, doubled, ends] + end_inputs,
        shape(size_x, size_y, size_z),
        scratch=[pltpu.VMEM((4, ROWS, size_y * size_x), float32)],
    )


def solution(mesh):
    placed = (P(None, "gy", "gz"), P(), P(), P(), P(), P())
    return jax.shard_map(
        body, mesh=mesh, in_specs=placed, out_specs=P(None, "gy", "gz"), check_vma=False
    )
```

```python
import functools

import jax
import jax.numpy as jnp
from jax import lax
from jax.experimental import pallas as pl
from jax.experimental.pallas import tpu as pltpu
from jax.sharding import PartitionSpec as P

HALF_LIMIT = 600.0
LANES = 128
ROWS = 8
VMEM_LIMIT = 48 * 1024 * 1024


def iota(shape, axis):
    return lax.broadcasted_iota(jnp.int32, shape, axis)


def coordinate(positions, line_total):
    return (2.0 * positions.astype(jnp.float32) + 1.0) / line_total - 1.0


def roll(values, shift, axis):
    return pltpu.roll(values, shift % values.shape[axis], axis)


def matmul(left, right):
    low, high = split(left), split(right)
    columns = right.shape[0]
    both = lax.dot_general(
        jnp.concatenate(low, axis=1),
        jnp.concatenate([jnp.concatenate([part, part], axis=1) for part in high], axis=0),
        (((1,), (1,)), ((), ())),
        preferred_element_type=jnp.float32,
    )
    return both[:, :columns] + both[:, columns:]


def split(values):
    upper = values.astype(jnp.bfloat16)
    return upper, (values - upper.astype(jnp.float32)).astype(jnp.bfloat16)


def half_drift(left, right):
    return HALF_LIMIT * jnp.tanh(matmul(left, right))


SHARPNESS, CENTER, SLOPE, OFFSET, DIFFUSION, PREPARED = 0, 1, 4, 7, 8, 16


def component_of(maps):
    return iota((1, LANES), 1) // (2 * maps)


def first_term(maps):
    return (iota((1, LANES), 1) // maps) % 2 == 0


def bump(params, coord, axis):
    center = params[CENTER + axis : CENTER + axis + 1]
    return jnp.exp(-params[SHARPNESS : SHARPNESS + 1] * (coord - center) ** 2)


def slope(params, coord, axis):
    return coord * params[SLOPE + axis : SLOPE + axis + 1]


def x_factors(params, maps, size_x):
    coord = coordinate(iota((size_x, LANES), 0), size_x)
    return bump(params, coord, 0), jnp.where(first_term(maps), slope(params, coord, 0), 0.0)


def y_factors(params, maps, position, total_y):
    coord = coordinate(position, total_y)
    part = slope(params, coord, 1) + params[OFFSET : OFFSET + 1]
    return bump(params, coord, 1), jnp.where(
        first_term(maps), part, params[SLOPE + 2 : SLOPE + 3]
    )


def z_rows(params, maps, position, total_z):
    coord = coordinate(position, total_z)
    return bump(params, coord, 2) * jnp.where(first_term(maps), 1.0, coord)


def inner_z_rows(params, maps, z_start, size_z, total_z):
    return z_rows(params, maps, z_start + iota((size_z, LANES), 0), total_z)


def outer_z_rows(params, maps, z_start, size_z, total_z):
    row = iota((size_z, LANES), 0)
    return z_rows(
        params, maps, jnp.where(row == 0, z_start + size_z, z_start - 1), total_z
    )


def only(rows, maps, component):
    return jnp.where(component_of(maps) == component, rows, 0.0)


def y_rows(params, maps, position, total_y):
    coord = coordinate(position, total_y)
    part = slope(params, coord, 1) + params[OFFSET : OFFSET + 1]
    return bump(params, coord, 1) * jnp.where(first_term(maps), part, 1.0)


def xz_rows(params, maps, size_x, z_start, size_z, total_z):
    row = iota((2 * size_x, LANES), 0)
    x_coord = coordinate(row % size_x, size_x)
    z_coord = coordinate(jnp.where(row < size_x, z_start - 1, z_start + size_z), total_z)
    part = slope(params, x_coord, 0) + slope(params, z_coord, 2)
    both = bump(params, x_coord, 0) * bump(params, z_coord, 2)
    both = both * jnp.where(first_term(maps), 1.0, part)
    return jnp.concatenate(
        [both, jnp.zeros((LANES - 2 * size_x, LANES), jnp.float32)], axis=0
    )


def with_extra(main, row):
    return jnp.concatenate([main, jnp.broadcast_to(row, (ROWS, LANES))], axis=0)


def pack_planes(planes):
    lane = iota(planes[0].shape, 1)
    first = last = jnp.zeros(planes[0].shape, jnp.float32)
    for i, plane in enumerate(planes):
        turned = roll(plane, i + 1, 1)
        first = jnp.where(lane == i, turned, first)
        last = jnp.where(lane == i + 1, turned, last)
    return first + roll(last, len(planes) - 1, 1)


def lines_of(planes, size_x, side):
    group = LANES // size_x
    place = iota((1, LANES), 1) // size_x
    turned = [roll(planes, (q - side) * size_x, 1) for q in range(group)]
    rows = []
    for first in range(0, planes.shape[0], group):
        row = turned[0][first : first + 1]
        for q in range(1, group):
            row = jnp.where(place == q, turned[q][first + q : first + q + 1], row)
        rows.append(row)
    return jnp.concatenate(rows, axis=1)


def to_lines(rows, size_x):
    group = LANES // size_x
    return jnp.concatenate(
        [
            jnp.transpose(jnp.concatenate(rows[first : first + group], axis=0))
            for first in range(0, len(rows), group)
        ],
        axis=1,
    )


def turn(values, stride):
    stride = stride % values.shape[0]
    if stride % ROWS == 0:
        return jnp.concatenate([values[-stride:], values[:-stride]], axis=0)
    return roll(values, stride, 0)


def merge_coefs(low, high):
    inverse = 1.0 / (1.0 - low[3] * high[0])
    onward, back = low[1] * inverse, high[2] * inverse
    return (
        low[0] + onward * high[0] * low[2],
        onward * high[1],
        back * low[2],
        high[3] + back * low[3] * high[1],
    )


def merge_values(low, high, low_values, high_values):
    inverse = 1.0 / (1.0 - low[3] * high[0])
    return (
        low_values[0] + low[1] * inverse * (high_values[0] + high[0] * low_values[1]),
        high_values[1] + high[2] * inverse * (low_values[1] + low[3] * high_values[0]),
    )


def chain(coefs, values, below, above):
    count = len(coefs)
    held, slope = below, None
    befores, firsts = [], []
    for j in range(count):
        a_first, c_first, a_last, c_last = coefs[j]
        r_first, r_last = values[j]
        befores.append((held, slope))
        if slope is None:
            first, first_slope = r_first + a_first * held, c_first
            held, slope = r_last + a_last * held, c_last
        else:
            inverse = 1.0 / (1.0 - a_first * slope)
            first = (r_first + a_first * held) * inverse
            first_slope = c_first * inverse
            held, slope = (
                r_last + a_last * (held + slope * first),
                c_last + a_last * slope * first_slope,
            )
        firsts.append((first, first_slope))
    seen_above = [None] * count
    seen_below = [None] * count
    upper = above
    for j in reversed(range(count)):
        seen_above[j] = upper
        upper = firsts[j][0] + firsts[j][1] * upper
        held, slope = befores[j]
        seen_below[j] = held if slope is None else held + slope * upper
    return seen_below, seen_above


def solve_x(up, down, source, pivot):
    size = source.shape[0]
    half = size // 2
    low_g, low_c, high_g, high_c = {}, {}, {}, {}
    g = c = None
    for i in range(half):
        if i == 0:
            weight = 1.0 / pivot
            c = down[1] * weight
            g = source[0] * weight
        else:
            weight = 1.0 / (pivot - up[i - 1] * c)
            g = (source[i] + up[i - 1] * g) * weight
            c = down[i + 1] * weight
        low_g[i], low_c[i] = g, c
    for i in reversed(range(half, size)):
        if i == size - 1:
            weight = 1.0 / pivot
            c = up[i - 1] * weight
            g = source[i] * weight
        else:
            weight = 1.0 / (pivot - down[i + 1] * c)
            g = (source[i] + down[i + 1] * g) * weight
            c = up[i - 1] * weight
        high_g[i], high_c[i] = g, c
    out = [None] * size
    inverse = 1.0 / (1.0 - low_c[half - 1] * high_c[half])
    out[half - 1] = (low_g[half - 1] + low_c[half - 1] * high_g[half]) * inverse
    out[half] = high_g[half] + high_c[half] * out[half - 1]
    for i in reversed(range(half - 1)):
        out[i] = low_g[i] + low_c[i] * out[i + 1]
    for i in range(half + 1, size):
        out[i] = high_g[i] + high_c[i] * out[i - 1]
    return out


def start_kernel(
    extent_y,
    extent_z,
    density_hbm,
    diffusion_hbm,
    centers_hbm,
    sharpness_hbm,
    affine_hbm,
    offsets_hbm,
    message,
    line_values,
    line_drifts,
    drift_z_out,
    prepared,
    solved,
    drift_y_held,
    density,
    diffusion,
    centers,
    sharpness,
    affine,
    offsets,
    staged,
    semaphores,
):
    copies = [
        pltpu.make_async_copy(source, target, semaphores.at[number])
        for number, (source, target) in enumerate(
            [
                (diffusion_hbm, diffusion),
                (centers_hbm, centers),
                (sharpness_hbm, sharpness),
                (affine_hbm, affine),
                (offsets_hbm, offsets),
                (density_hbm, density),
            ]
        )
    ]
    for copy in copies:
        copy.start()
    size_x, size_y, size_z = density.shape
    total_y, total_z = size_y * extent_y, size_z * extent_z
    y_start = lax.axis_index("gy") * size_y
    z_start = lax.axis_index("gz") * size_z
    maps = centers.shape[1]
    for copy in copies[:-1]:
        copy.wait()

    staged[...] = jnp.zeros(staged.shape, jnp.float32)
    staged[0:1, :maps] = sharpness[...]
    staged[1:4, :maps] = centers[...]
    for c in range(3):
        staged[4 + 3 * c : 7 + 3 * c, :maps] = affine[c]
    staged[13:16, :maps] = offsets[...]
    rows = staged[...]
    width = maps
    while width < LANES:
        rows = rows + roll(rows, width, 1)
        width = 2 * width
    component = component_of(maps)
    rows = jnp.where(component < 3, rows, 0.0)

    def by_component(first, step):
        return jnp.where(
            component == 0,
            rows[first : first + 1],
            jnp.where(
                component == 1,
                rows[first + step : first + step + 1],
                rows[first + 2 * step : first + 2 * step + 1],
            ),
        )

    weights = [jnp.broadcast_to(diffusion[:, c : c + 1], (1, LANES)) for c in range(3)]
    params = jnp.concatenate(
        [rows[0:4]]
        + [by_component(4 + j, 3) for j in range(3)]
        + [by_component(13, 1)]
        + weights
        + [jnp.zeros((PREPARED - DIFFUSION - 3, LANES), jnp.float32)],
        axis=0,
    )
    prepared[...] = params
    d0, d1, d2 = weights

    x_bump, x_part = x_factors(params, maps, size_x)
    y_row = iota((size_y, LANES), 0)
    y_bump, y_part = y_factors(params, maps, y_start + y_row, total_y)
    out_bump, out_part = y_factors(
        params, maps, jnp.where(y_row == 0, y_start + size_y, y_start - 1), total_y
    )
    inner = inner_z_rows(params, maps, z_start, size_z, total_z)
    outer = outer_z_rows(params, maps, z_start, size_z, total_z)
    inner = [only(inner, maps, c) for c in range(3)]
    outer = only(outer, maps, 0)

    def rows_by_x(bumps, part):
        return jnp.concatenate(
            [(x_bump[i : i + 1] * bumps) * (x_part[i : i + 1] + part) for i in range(size_x)],
            axis=0,
        )

    right = jnp.concatenate([inner[0], outer, inner[1], inner[2]], axis=0)
    drifts = half_drift(rows_by_x(y_bump, y_part), right)
    out_drift = half_drift(rows_by_x(out_bump, out_part), inner[0])

    def block(number):
        columns = drifts[:, number * LANES : (number + 1) * LANES]
        return columns.reshape(size_x, size_y, LANES)

    drift_x, plane_drift, drift_y, drift_z = block(0), block(1), block(2), block(3)
    out_drift = out_drift.reshape(size_x, size_y, LANES)
    drift_y_held[...] = drift_y
    drift_z_out[...] = drift_z
    copies[-1].wait()
    rho = density[...]
    zero = jnp.zeros((1, size_y, LANES), jnp.float32)
    up, down = (d0 + drift_x) * rho, (d0 - drift_x) * rho
    total = (
        jnp.concatenate([zero, up[:-1]], axis=0)
        + jnp.concatenate([down[1:], zero], axis=0)
        - (2.0 * (d0 + d1 + d2)) * rho
    )
    sublane = iota((size_x, size_y, LANES), 1)
    lane = iota((size_x, size_y, LANES), 2)
    up, down = roll((d1 + drift_y) * rho, 1, 1), roll((d1 - drift_y) * rho, -1, 1)
    at_low, at_high = sublane == 0, sublane == size_y - 1
    row_source = jnp.where(at_low, up, jnp.where(at_high, down, 0.0))
    total = total + jnp.where(at_low, 0.0, up) + jnp.where(at_high, 0.0, down)
    up, down = roll((d2 + drift_z) * rho, 1, 2), roll((d2 - drift_z) * rho, -1, 2)
    at_low, at_high = lane == 0, lane == size_z - 1
    plane_source = jnp.where(at_low, up, jnp.where(at_high, down, 0.0))
    total = total + jnp.where(at_low, 0.0, up) + jnp.where(at_high, 0.0, down)

    source = jnp.concatenate([total, row_source, plane_source], axis=1)
    drift = jnp.concatenate([drift_x, out_drift, plane_drift], axis=1)
    answers = solve_x(d0 + drift, d0 - drift, source, 1.0 + 2.0 * d0)
    for i in range(size_x):
        solved[i] = answers[i][: 2 * size_y]
    planes = pack_planes([answer[2 * size_y :] for answer in answers])

    row = iota((1, LANES), 0)
    out_rows = []
    for position in (y_start - 1, y_start + size_y):
        bumps, part = y_factors(params, maps, row + position, total_y)
        out_rows.append((x_bump * bumps) * (x_part + part))
    ends = half_drift(jnp.concatenate(out_rows, axis=0), inner[1])
    position = y_start - 1 + iota((2 * ROWS, LANES), 0)
    extra = half_drift(
        y_rows(params, maps, position, total_y),
        only(xz_rows(params, maps, size_x, z_start, size_z, total_z), maps, 1),
    )
    line_drift = (
        [ends[:size_x]]
        + [drift_y_held[:, j, :] for j in range(size_y)]
        + [ends[size_x:]]
    )
    line_drift = [with_extra(line_drift[j], extra[j : j + 1]) for j in range(size_y + 2)]
    values = [with_extra(solved[:, j, :], planes[j : j + 1]) for j in range(size_y)]
    for j in range(size_y):
        line_values[j] = values[j]
    for j in range(size_y + 2):
        line_drifts[j] = line_drift[j]
    pivot = 1.0 + 2.0 * d1
    g = c = None
    gs, cs = [], []
    for j in range(size_y):
        lower, upper = line_factors(line_drift, j, size_y, d1, y_start, total_y)
        weight = 1.0 / (pivot if j == 0 else pivot - lower * c)
        g = (values[j] if j == 0 else values[j] + lower * g) * weight
        c = upper * weight
        gs.append(g)
        cs.append(c)
    r_first = r_last = g
    for j in reversed(range(size_y - 1)):
        r_first = gs[j] + cs[j] * r_first
    pushed_up = solved[:, size_y, :] / (d1 + line_drift[size_y][:size_x])
    pushed_down = solved[:, 2 * size_y - 1, :] / (d1 - line_drift[1][:size_x])
    blank = jnp.zeros((1, LANES), jnp.float32)
    width = size_x + ROWS
    message[:width] = r_first + with_extra(pushed_down, blank)
    message[width:] = r_last + with_extra(pushed_up, blank)


def line_factors(line_drift, j, size_y, d1, y_start, total_y):
    lower, upper = d1 + line_drift[j], d1 - line_drift[j + 2]
    if j == 0:
        lower = jnp.where(y_start == 0, 0.0, lower)
    if j == size_y - 1:
        upper = jnp.where(y_start + size_y == total_y, 0.0, upper)
    return lower, upper


def line_coefs(params, maps, sizes, start, count, store):
    extent_y, extent_z, size_x, size_y, size_z = sizes
    total_y, total_z = size_y * extent_y, size_z * extent_z
    z_start = lax.axis_index("gz") * size_z
    d1 = params[DIFFUSION + 1 : DIFFUSION + 2]
    x_bump, x_part = x_factors(params, maps, size_x)
    inner = only(inner_z_rows(params, maps, z_start, size_z, total_z), maps, 1)
    planes = only(xz_rows(params, maps, size_x, z_start, size_z, total_z), maps, 1)
    whole = count == extent_y
    offsets = list(range(size_y)) if whole else list(range(-1, size_y + 1))
    left, left_extra = [], []
    for j in offsets:
        for b in range(count):
            position = iota((1, LANES), 0) + ((start + b) * size_y + j)
            bumps, part = y_factors(params, maps, position, total_y)
            left.append((x_bump * bumps) * (x_part + part))
        block = iota((max(count, ROWS), LANES), 0)
        left_extra.append(
            y_rows(params, maps, (start + block) * size_y + j, total_y)
        )
    depth = left_extra[0].shape[0]
    main = half_drift(jnp.concatenate(left, axis=0), inner)
    main = main.reshape(len(offsets), count, size_x, LANES)
    main = [main[j] for j in range(len(offsets))]
    extra = half_drift(jnp.concatenate(left_extra, axis=0), planes)
    extra = [extra[j * depth : (j + 1) * depth] for j in range(len(offsets))]
    if whole:
        main = (
            [jnp.concatenate([main[-1][:1], main[-1][:-1]], axis=0)]
            + main
            + [jnp.concatenate([main[0][1:], main[0][-1:]], axis=0)]
        )
        extra = [roll(extra[-1], 1, 0)] + extra + [roll(extra[0], -1, 0)]
    numbers = start + iota((depth, LANES), 0)
    pivot = 1.0 + 2.0 * d1
    at_start, at_end = numbers == 0, numbers == extent_y - 1

    def scan(drifts, starts, ends):
        a_first = c_first = a_last = c_last = None
        for j in range(size_y):
            lower, upper = d1 + drifts[j], d1 - drifts[j + 2]
            if j == 0:
                lower = starts(lower)
            if j == size_y - 1:
                upper = ends(upper)
            if j == 0:
                weight = 1.0 / pivot
                a_first, c_first = lower * weight, upper * weight
                a_last, c_last = a_first, c_first
            else:
                weight = 1.0 / (pivot - lower * c_last)
                step, c_last = lower * weight, upper * weight
                a_last = step * a_last
                a_first = a_first + c_first * a_last
                c_first = c_first * c_last
        return a_first, c_first, a_last, c_last

    def masked(values, number):
        return jnp.concatenate(
            [
                jnp.where(start + b == number, 0.0, values[b])[None]
                for b in range(count)
            ],
            axis=0,
        )

    main = scan(main, lambda v: masked(v, 0), lambda v: masked(v, extent_y - 1))
    extra = scan(
        extra,
        lambda v: jnp.where(at_start, 0.0, v),
        lambda v: jnp.where(at_end, 0.0, v),
    )
    for b in range(count):
        for q in range(4):
            store(b, q, with_extra(main[q][b], extra[q][b : b + 1]))


def near_kernel(
    sizes,
    maps,
    stride,
    radix,
    prepared,
    line_values,
    line_drifts,
    coefs,
    base,
    from_below,
    from_above,
):
    digit = lax.rem(lax.div(lax.axis_index("gy"), stride), radix)
    start = lax.div(lax.axis_index("gy"), stride) - digit
    params = prepared[...]

    def store(b, q, value):
        coefs[b, q] = value

    line_coefs(params, maps, sizes, start, radix, store)
    extent_y, _, _, size_y, _ = sizes
    d1 = params[DIFFUSION + 1 : DIFFUSION + 2]
    pivot = 1.0 + 2.0 * d1
    y_start = lax.axis_index("gy") * size_y
    g = a = c = None
    gs, as_, cs = [], [], []
    for j in range(size_y):
        lower, upper = line_factors(line_drifts, j, size_y, d1, y_start, size_y * extent_y)
        if j == 0:
            weight = 1.0 / pivot
            g, a = line_values[j] * weight, lower * weight
        else:
            weight = 1.0 / (pivot - lower * c)
            g, a = (line_values[j] + lower * g) * weight, lower * a * weight
        c = upper * weight
        gs.append(g)
        as_.append(a)
        cs.append(c)
    base[size_y - 1], from_below[size_y - 1], from_above[size_y - 1] = g, a, c
    for j in reversed(range(size_y - 1)):
        g, a, c = gs[j] + cs[j] * g, as_[j] + cs[j] * a, cs[j] * c
        base[j], from_below[j], from_above[j] = g, a, c


def far_kernel(sizes, maps, levels, prepared, *outputs):
    held = {}

    def store(b, q, value):
        held[b, q] = value

    extent_y = sizes[0]
    line_coefs(prepared[...], maps, sizes, 0, extent_y, store)
    groups = [tuple(held[b, q] for q in range(4)) for b in range(extent_y)]
    for (_, radix), coefs in zip(levels, outputs):
        groups = [
            functools.reduce(merge_coefs, groups[g : g + radix])
            for g in range(0, len(groups), radix)
        ]
        for number, group in enumerate(groups):
            for q in range(4):
                coefs[number, q] = group[q]


def z_coef_kernel(sizes, maps, prepared, drift_z, steps, ends, pushes, packed):
    extent_y, extent_z, size_x, size_y, size_z = sizes
    total_y, total_z = size_y * extent_y, size_z * extent_z
    y_start = lax.axis_index("gy") * size_y
    z_start = lax.axis_index("gz") * size_z
    params = prepared[...]
    d2 = params[DIFFUSION + 2 : DIFFUSION + 3]
    lane = iota((size_y, LANES), 1)
    divisors = []
    for i in range(size_x):
        plane = drift_z[i]
        divisors.append(
            1.0 / jnp.where(lane == 0, d2 + roll(plane, 1, 1), d2 - roll(plane, -1, 1))
        )
    pushes[...] = pack_planes(divisors)
    x_bump, x_part = x_factors(params, maps, size_x)
    outer = only(outer_z_rows(params, maps, z_start, size_z, total_z), maps, 2)
    rows = []
    for j in range(size_y):
        position = iota((1, LANES), 0) + (y_start + j)
        bumps, part = y_factors(params, maps, position, total_y)
        rows.append((x_bump * bumps) * (x_part + part))
    outer = half_drift(jnp.concatenate(rows, axis=0), outer)
    outer = to_lines([outer[j * size_x : (j + 1) * size_x] for j in range(size_y)], size_x)
    inner = to_lines([drift_z[:, j, :] for j in range(size_y)], size_x)
    d2 = jnp.concatenate([d2] * (inner.shape[1] // LANES), axis=1)
    scale = 1.0 / (1.0 + 2.0 * d2)
    row = iota(inner.shape, 0)
    low, high = row == 0, row == size_z - 1
    before = jnp.where(low, outer[size_z - 1 :], turn(inner, 1))
    after = jnp.where(high, outer[:1], turn(inner, -1))
    below = jnp.where(low & (z_start == 0), 0.0, (d2 + before) * scale)
    above = jnp.where(high & (z_start + size_z == total_z), 0.0, (d2 - after) * scale)
    stride, level = 1, 0
    while stride < size_z:
        low, high = row < stride, row >= size_z - stride
        low_a = jnp.where(low, 1.0, turn(below, stride))
        low_c = jnp.where(low, 0.0, turn(above, stride))
        high_a = jnp.where(high, 0.0, turn(below, -stride))
        high_c = jnp.where(high, 1.0, turn(above, -stride))
        inverse = 1.0 / (1.0 - below * low_c - above * high_a)
        below, above = below * inverse, above * inverse
        factor = scale if level == 0 else 1.0
        steps[level, 0] = inverse * factor
        steps[level, 1] = jnp.where(low, 0.0, below * factor)
        steps[level, 2] = jnp.where(high, 0.0, above * factor)
        below, above = below * low_a, above * high_c
        stride, level = stride * 2, level + 1
    ends[0] = below
    ends[1] = above
    packed[...] = jnp.concatenate(
        [
            jnp.zeros((2, inner.shape[1]), jnp.float32),
            below[:1],
            below[size_z - 1 :],
            above[:1],
            above[size_z - 1 :],
            jnp.zeros((2, inner.shape[1]), jnp.float32),
        ],
        axis=0,
    )


def gather_members(refs, own, count):
    held = [ref[...] for ref in refs]
    return [
        functools.reduce(
            lambda acc, s: jnp.where((own ^ s) == j, held[s], acc), range(1, count), held[0]
        )
        for j in range(count)
    ]


def split_message(message):
    width = message.shape[0] // 2
    return message[:width], message[width:]


def merge_kernel(stride, radix, local, facing, coefs, *refs):
    received, message = refs[:radix], refs[-1]
    digit = lax.rem(lax.div(lax.axis_index("gy"), stride), radix)
    first = 0 if local else lax.div(lax.axis_index("gy"), stride) - digit
    values = [split_message(m) for m in gather_members(received, digit, radix)]
    group = [tuple(coefs[first + j, q] for q in range(4)) for j in range(radix)]
    merged, total = group[0], values[0]
    for j in range(1, radix):
        total = merge_values(merged, group[j], total, values[j])
        merged = merge_coefs(merged, group[j])
    if facing:
        is_low = lax.axis_index("gy") < stride * radix
        message[...] = jnp.where(is_low, total[1], total[0])
    else:
        message[...] = jnp.concatenate(total, axis=0)


def middle_kernel(levels, *refs):
    refs = list(refs)
    steps, pushes, packed, base, from_below, from_above = refs[:6]
    refs = refs[6:]
    inputs = []
    for stride, radix in levels:
        inputs.append((refs[0], refs[1 : 1 + radix]))
        refs = refs[1 + radix :]
    message, doubled, seen = refs
    size_y, width = base.shape[:2]
    size_x = width - ROWS
    below = above = jnp.zeros((width, LANES), jnp.float32)
    for number in reversed(range(len(levels))):
        (stride, radix), (coefs, received) = levels[number], inputs[number]
        digit = lax.rem(lax.div(lax.axis_index("gy"), stride), radix)
        first = 0 if number == 0 else lax.div(lax.axis_index("gy"), stride) - digit
        members = gather_members(received, digit, radix)
        group = [tuple(coefs[first + j, q] for q in range(4)) for j in range(radix)]
        if members[0].shape[0] == width:
            c_last, a_first = group[0][3], group[1][0]
            inverse = 1.0 / (1.0 - c_last * a_first)
            below = jnp.where(digit == 0, 0.0, (members[0] + c_last * members[1]) * inverse)
            above = jnp.where(digit == 0, (members[1] + a_first * members[0]) * inverse, 0.0)
            continue
        values = [split_message(m) for m in members]
        lows, highs = chain(group, values, below, above)
        for j in range(radix):
            seen[j, 0] = lows[j]
            seen[j, 1] = highs[j]
        below, above = seen[digit, 0], seen[digit, 1]
    inner, outer = [], []
    for j in range(size_y):
        value = base[j] + from_below[j] * below + from_above[j] * above
        inner.append(value[:size_x])
        outer.append(value[size_x : size_x + 1])
    pushed = jnp.concatenate(outer, axis=0) * pushes[...]
    values = to_lines(inner, size_x)
    stride, level = 1, 0
    while stride < values.shape[0]:
        values = (
            steps[level, 0] * values
            + steps[level, 1] * turn(values, stride)
            + steps[level, 2] * turn(values, -stride)
        )
        stride, level = stride * 2, level + 1
    doubled[...] = values
    message[...] = packed[...]
    message[0:1] = values[:1] + lines_of(pushed, size_x, 0)
    message[1:2] = values[-1:] + lines_of(pushed, size_x, 1)


def merge_z(low, high):
    inverse = 1.0 / (1.0 - low[5] * high[2])
    onward, back = low[4] * inverse, high[3] * inverse
    return (
        low[0] + onward * (high[0] + high[2] * low[1]),
        high[1] + back * (low[1] + low[5] * high[0]),
        low[2] + onward * high[2] * low[3],
        back * low[3],
        onward * high[4],
        high[5] + back * low[5] * high[4],
    )


def unpack_ends(message):
    return tuple(message[s : s + 1] for s in range(6))


def merge_z_kernel(stride, radix, *refs):
    received, message = refs[:radix], refs[radix]
    digit = lax.rem(lax.div(lax.axis_index("gz"), stride), radix)
    members = [unpack_ends(m) for m in gather_members(received, digit, radix)]
    total = functools.reduce(merge_z, members)
    message[...] = jnp.concatenate(total + total[:2], axis=0)


def end_kernel(levels, density, doubled, ends, *refs):
    refs = list(refs)
    inputs = []
    for stride, radix in levels:
        inputs.append(refs[:radix])
        refs = refs[radix:]
    out, seen = refs
    size_x, size_y, _ = density.shape
    below = above = jnp.zeros((1, doubled.shape[1]), jnp.float32)
    for (stride, radix), received in zip(reversed(levels), reversed(inputs)):
        digit = lax.rem(lax.div(lax.axis_index("gz"), stride), radix)
        members = [unpack_ends(m) for m in gather_members(received, digit, radix)]
        lows, highs = chain(
            [(m[2], m[4], m[3], m[5]) for m in members],
            [(m[0], m[1]) for m in members],
            below,
            above,
        )
        for j in range(radix):
            seen[j, 0:1] = lows[j]
            seen[j, 1:2] = highs[j]
        below, above = seen[digit, 0:1], seen[digit, 1:2]
    values = doubled[...] + ends[0] * below + ends[1] * above
    group = LANES // size_x
    for first in range(0, size_y, group):
        tile = first // group
        lines = jnp.transpose(values[:, tile * LANES : (tile + 1) * LANES])
        for q in range(group):
            out[:, first + q, :] = (
                density[:, first + q, :] + lines[q * size_x : (q + 1) * size_x]
            )


def radices(extent):
    rounds, stride = [], 1
    while stride < extent:
        radix = 4 if (extent // stride) % 4 == 0 else 2
        rounds.append((stride, radix))
        stride *= radix
    return rounds


def exchange(message, axis, stride, radix):
    devices = range(lax.axis_size(axis))
    return [message] + [
        lax.ppermute(message, axis, [(i, i ^ (s * stride)) for i in devices])
        for s in range(1, radix)
    ]


def body(density, diffusion, centers, sharpness, affine, offsets):
    size_x, size_y, size_z = density.shape
    extent_y, extent_z = lax.axis_size("gy"), lax.axis_size("gz")
    sizes = (extent_y, extent_z, size_x, size_y, size_z)
    maps = centers.shape[0]
    width = size_x + ROWS
    wide = (size_y, width, LANES)
    narrow = (size_z, size_y * size_x)
    float32 = jnp.float32
    y_levels, z_levels = radices(extent_y), radices(extent_z)

    def shape(*dims):
        return jax.ShapeDtypeStruct(dims, float32)

    vmem = pl.BlockSpec(memory_space=pltpu.VMEM)
    hbm = pl.BlockSpec(memory_space=pltpu.HBM)

    def call(kernel, inputs, outputs, in_specs=None, scratch=(), flops=10**6):
        return pl.pallas_call(
            kernel,
            out_shape=outputs,
            in_specs=in_specs or [vmem] * len(inputs),
            out_specs=jax.tree.map(lambda _: vmem, outputs),
            scratch_shapes=list(scratch),
            compiler_params=pltpu.CompilerParams(vmem_limit_bytes=VMEM_LIMIT),
            cost_estimate=pl.CostEstimate(flops=flops, bytes_accessed=10**6, transcendentals=0),
        )(*inputs)

    raw = (
        density,
        diffusion.reshape(1, 3),
        centers.T,
        sharpness.reshape(1, maps),
        affine.transpose(1, 2, 0),
        offsets.T,
    )
    raw = tuple(pltpu.with_memory_space_constraint(array, pltpu.HBM) for array in raw)
    message, line_values, line_drifts, drift_z, prepared = call(
        functools.partial(start_kernel, extent_y, extent_z),
        raw,
        (
            shape(2 * width, LANES),
            shape(*wide),
            shape(size_y + 2, width, LANES),
            shape(size_x, size_y, LANES),
            shape(PREPARED, LANES),
        ),
        [hbm] * len(raw),
        [
            pltpu.VMEM((size_x, 2 * size_y, LANES), float32),
            pltpu.VMEM((size_x, size_y, LANES), float32),
        ]
        + [pltpu.VMEM(array.shape, float32) for array in raw]
        + [pltpu.VMEM((PREPARED, LANES), float32), pltpu.SemaphoreType.DMA((len(raw),))],
    )
    stride, radix = y_levels[0]
    near, base, from_below, from_above = call(
        functools.partial(near_kernel, sizes, maps, stride, radix),
        [prepared, line_values, line_drifts],
        (shape(radix, 4, width, LANES), shape(*wide), shape(*wide), shape(*wide)),
    )
    far, count = [], extent_y
    for _, radix in y_levels[:-1]:
        count = count // radix
        far.append(shape(count, 4, width, LANES))
    if far:
        far = call(functools.partial(far_kernel, sizes, maps, y_levels[:-1]), [prepared], far)
    coefs = [near] + list(far)
    doublings = size_z.bit_length() - 1
    steps, ends, pushes, packed = call(
        functools.partial(z_coef_kernel, sizes, maps),
        (prepared, drift_z),
        (
            shape(doublings, 3, *narrow),
            shape(2, *narrow),
            shape(size_y, LANES),
            shape(ROWS, size_y * size_x),
        ),
    )
    line_inputs = []
    for number, (stride, radix) in enumerate(y_levels):
        received = exchange(message, "gy", stride, radix)
        line_inputs += [coefs[number]] + received
        if number + 1 < len(y_levels):
            facing = number + 2 == len(y_levels) and y_levels[-1][1] == 2
            message = call(
                functools.partial(merge_kernel, stride, radix, number == 0, facing),
                [coefs[number]] + received + ([packed] if number == 0 else []),
                shape(width if facing else 2 * width, LANES),
            )
    message, doubled = call(
        functools.partial(middle_kernel, y_levels),
        [steps, pushes, packed, base, from_below, from_above] + line_inputs,
        (shape(ROWS, size_y * size_x), shape(*narrow)),
        scratch=[pltpu.VMEM((4, 2, width, LANES), float32)],
    )
    end_inputs = []
    for number, (stride, radix) in enumerate(z_levels):
        received = exchange(message, "gz", stride, radix)
        end_inputs += received
        if number + 1 < len(z_levels):
            message = call(
                functools.partial(merge_z_kernel, stride, radix),
                received,
                shape(ROWS, size_y * size_x),
            )
    return call(
        functools.partial(end_kernel, z_levels),
        [density, doubled, ends] + end_inputs,
        shape(size_x, size_y, size_z),
        scratch=[pltpu.VMEM((4, ROWS, size_y * size_x), float32)],
    )


def solution(mesh):
    placed = (P(None, "gy", "gz"), P(), P(), P(), P(), P())
    return jax.shard_map(
        body, mesh=mesh, in_specs=placed, out_specs=P(None, "gy", "gz"), check_vma=False
    )
```

```python
import functools

import jax
import jax.numpy as jnp
from jax import lax
from jax.experimental import pallas as pl
from jax.experimental.pallas import tpu as pltpu
from jax.sharding import PartitionSpec as P

HALF_LIMIT = 600.0
LANES = 128
ROWS = 8
ABOVE, BELOW = 127, 31
VMEM_LIMIT = 48 * 1024 * 1024


def iota(shape, axis):
    return lax.broadcasted_iota(jnp.int32, shape, axis)


def coordinate(positions, line_total):
    return (2.0 * positions.astype(jnp.float32) + 1.0) / line_total - 1.0


def roll(values, shift, axis):
    return pltpu.roll(values, shift % values.shape[axis], axis)


def matmul(left, right):
    low, high = split(left), split(right)
    columns = right.shape[0]
    both = lax.dot_general(
        jnp.concatenate(low, axis=1),
        jnp.concatenate([jnp.concatenate([part, part], axis=1) for part in high], axis=0),
        (((1,), (1,)), ((), ())),
        preferred_element_type=jnp.float32,
    )
    return both[:, :columns] + both[:, columns:]


def split(values):
    upper = values.astype(jnp.bfloat16)
    return upper, (values - upper.astype(jnp.float32)).astype(jnp.bfloat16)


def half_drift(left, right):
    return HALF_LIMIT * jnp.tanh(matmul(left, right))


SHARPNESS, CENTER, SLOPE, OFFSET, DIFFUSION, PREPARED = 0, 1, 4, 7, 8, 16


def component_of(maps):
    return iota((1, LANES), 1) // (2 * maps)


def first_term(maps):
    return (iota((1, LANES), 1) // maps) % 2 == 0


def bump(params, coord, axis):
    center = params[CENTER + axis : CENTER + axis + 1]
    return jnp.exp(-params[SHARPNESS : SHARPNESS + 1] * (coord - center) ** 2)


def slope(params, coord, axis):
    return coord * params[SLOPE + axis : SLOPE + axis + 1]


def x_factors(params, maps, size_x):
    coord = coordinate(iota((size_x, LANES), 0), size_x)
    return bump(params, coord, 0), jnp.where(first_term(maps), slope(params, coord, 0), 0.0)


def y_factors(params, maps, position, total_y):
    coord = coordinate(position, total_y)
    part = slope(params, coord, 1) + params[OFFSET : OFFSET + 1]
    return bump(params, coord, 1), jnp.where(
        first_term(maps), part, params[SLOPE + 2 : SLOPE + 3]
    )


def z_rows(params, maps, position, total_z):
    coord = coordinate(position, total_z)
    return bump(params, coord, 2) * jnp.where(first_term(maps), 1.0, coord)


def inner_z_rows(params, maps, z_start, size_z, total_z):
    return z_rows(params, maps, z_start + iota((size_z, LANES), 0), total_z)


def outer_z_rows(params, maps, z_start, size_z, total_z):
    row = iota((size_z, LANES), 0)
    return z_rows(
        params, maps, jnp.where(row == BELOW, z_start - 1, z_start + size_z), total_z
    )


def only(rows, maps, component):
    return jnp.where(component_of(maps) == component, rows, 0.0)


def y_rows(params, maps, position, total_y):
    coord = coordinate(position, total_y)
    part = slope(params, coord, 1) + params[OFFSET : OFFSET + 1]
    return bump(params, coord, 1) * jnp.where(first_term(maps), part, 1.0)


def xz_rows(params, maps, size_x, z_start, size_z, total_z):
    row = iota((BELOW + 1 + size_x, LANES), 0)
    x_coord = coordinate(jnp.where(row < size_x, row, row - BELOW - 1), size_x)
    z_coord = coordinate(jnp.where(row > BELOW, z_start - 1, z_start + size_z), total_z)
    part = slope(params, x_coord, 0) + slope(params, z_coord, 2)
    both = bump(params, x_coord, 0) * bump(params, z_coord, 2)
    both = both * jnp.where(first_term(maps), 1.0, part)
    return jnp.concatenate(
        [both, jnp.zeros((LANES - BELOW - 1 - size_x, LANES), jnp.float32)], axis=0
    )


def with_extra(main, row):
    return jnp.concatenate([main, jnp.broadcast_to(row, (ROWS, LANES))], axis=0)


def pack_planes(planes):
    turned = [roll(plane, i + 1, 1) for i, plane in enumerate(planes)]
    while len(turned) > 1:
        turned = [sum(turned[i : i + 2]) for i in range(0, len(turned), 2)]
    return turned[0]


def lines_of(planes, size_x, first_lane):
    group = LANES // size_x
    place = iota((1, LANES), 1) // size_x
    turned = [roll(planes, q * size_x - first_lane, 1) for q in range(group)]
    rows = []
    for first in range(0, planes.shape[0], group):
        row = turned[0][first : first + 1]
        for q in range(1, group):
            row = jnp.where(place == q, turned[q][first + q : first + q + 1], row)
        rows.append(row)
    return jnp.concatenate(rows, axis=1)


def to_lines(rows, size_x):
    group = LANES // size_x
    return jnp.concatenate(
        [
            jnp.transpose(jnp.concatenate(rows[first : first + group], axis=0))
            for first in range(0, len(rows), group)
        ],
        axis=1,
    )


def turn(values, stride):
    stride = stride % values.shape[0]
    if stride % ROWS == 0:
        return jnp.concatenate([values[-stride:], values[:-stride]], axis=0)
    return roll(values, stride, 0)


def merge_coefs(low, high):
    inverse = 1.0 / (1.0 - low[3] * high[0])
    onward, back = low[1] * inverse, high[2] * inverse
    return (
        low[0] + onward * high[0] * low[2],
        onward * high[1],
        back * low[2],
        high[3] + back * low[3] * high[1],
    )


def merge_values(low, high, low_values, high_values):
    inverse = 1.0 / (1.0 - low[3] * high[0])
    return (
        low_values[0] + low[1] * inverse * (high_values[0] + high[0] * low_values[1]),
        high_values[1] + high[2] * inverse * (low_values[1] + low[3] * high_values[0]),
    )


def merge(low, high, low_values, high_values):
    return merge_coefs(low, high), merge_values(low, high, low_values, high_values)


def meet(low, high, below, above):
    (_, _, a_last, c_last), (_, r_last) = low
    (a_first, c_first, _, _), (r_first, _) = high
    inverse = 1.0 / (1.0 - c_last * a_first)
    upper = r_first + c_first * above
    left = (r_last + a_last * below + c_last * upper) * inverse
    return left, upper + a_first * left


def chain(coefs, values, below, above):
    count = len(coefs)
    if count == 4:
        halves = [merge(coefs[j], coefs[j + 1], values[j], values[j + 1]) for j in (0, 2)]
        left, right = meet(halves[0], halves[1], below, above)
        seen = [
            meet((coefs[j], values[j]), (coefs[j + 1], values[j + 1]), low, high)
            for j, low, high in ((0, below, right), (2, left, above))
        ]
        return [below, seen[0][0], left, seen[1][0]], [seen[0][1], right, seen[1][1], above]
    held, slope = below, None
    befores, firsts = [], []
    for j in range(count):
        a_first, c_first, a_last, c_last = coefs[j]
        r_first, r_last = values[j]
        befores.append((held, slope))
        if slope is None:
            first, first_slope = r_first + a_first * held, c_first
            held, slope = r_last + a_last * held, c_last
        else:
            inverse = 1.0 / (1.0 - a_first * slope)
            first = (r_first + a_first * held) * inverse
            first_slope = c_first * inverse
            held, slope = (
                r_last + a_last * (held + slope * first),
                c_last + a_last * slope * first_slope,
            )
        firsts.append((first, first_slope))
    seen_above = [None] * count
    seen_below = [None] * count
    upper = above
    for j in reversed(range(count)):
        seen_above[j] = upper
        upper = firsts[j][0] + firsts[j][1] * upper
        held, slope = befores[j]
        seen_below[j] = held if slope is None else held + slope * upper
    return seen_below, seen_above


def solve_x(up, down, source, pivot):
    size = source.shape[0]
    half = size // 2
    low_g, low_c, high_g, high_c = {}, {}, {}, {}
    g = c = None
    for i in range(half):
        if i == 0:
            weight = 1.0 / pivot
            c = down[1] * weight
            g = source[0] * weight
        else:
            weight = 1.0 / (pivot - up[i - 1] * c)
            g = (source[i] + up[i - 1] * g) * weight
            c = down[i + 1] * weight
        low_g[i], low_c[i] = g, c
    for i in reversed(range(half, size)):
        if i == size - 1:
            weight = 1.0 / pivot
            c = up[i - 1] * weight
            g = source[i] * weight
        else:
            weight = 1.0 / (pivot - down[i + 1] * c)
            g = (source[i] + down[i + 1] * g) * weight
            c = up[i - 1] * weight
        high_g[i], high_c[i] = g, c
    out = [None] * size
    inverse = 1.0 / (1.0 - low_c[half - 1] * high_c[half])
    out[half - 1] = (low_g[half - 1] + low_c[half - 1] * high_g[half]) * inverse
    out[half] = high_g[half] + high_c[half] * out[half - 1]
    for i in reversed(range(half - 1)):
        out[i] = low_g[i] + low_c[i] * out[i + 1]
    for i in range(half + 1, size):
        out[i] = high_g[i] + high_c[i] * out[i - 1]
    return out


def start_kernel(
    extent_y,
    extent_z,
    density_hbm,
    diffusion_hbm,
    centers_hbm,
    sharpness_hbm,
    affine_hbm,
    offsets_hbm,
    message,
    line_values,
    line_drifts,
    drift_z_out,
    prepared,
    solved,
    drift_y_held,
    density,
    diffusion,
    centers,
    sharpness,
    affine,
    offsets,
    staged,
    semaphores,
):
    copies = [
        pltpu.make_async_copy(source, target, semaphores.at[number])
        for number, (source, target) in enumerate(
            [
                (diffusion_hbm, diffusion),
                (centers_hbm, centers),
                (sharpness_hbm, sharpness),
                (affine_hbm, affine),
                (offsets_hbm, offsets),
                (density_hbm, density),
            ]
        )
    ]
    for copy in copies:
        copy.start()
    size_x, size_y, size_z = density.shape
    total_y, total_z = size_y * extent_y, size_z * extent_z
    y_start = lax.axis_index("gy") * size_y
    z_start = lax.axis_index("gz") * size_z
    maps = centers.shape[1]
    for copy in copies[:-1]:
        copy.wait()

    staged[...] = jnp.zeros(staged.shape, jnp.float32)
    staged[0:1, :maps] = sharpness[...]
    staged[1:4, :maps] = centers[...]
    for c in range(3):
        staged[4 + 3 * c : 7 + 3 * c, :maps] = affine[c]
    staged[13:16, :maps] = offsets[...]
    rows = staged[...]
    width = maps
    while width < LANES:
        rows = rows + roll(rows, width, 1)
        width = 2 * width
    component = component_of(maps)
    rows = jnp.where(component < 3, rows, 0.0)

    def by_component(first, step):
        return jnp.where(
            component == 0,
            rows[first : first + 1],
            jnp.where(
                component == 1,
                rows[first + step : first + step + 1],
                rows[first + 2 * step : first + 2 * step + 1],
            ),
        )

    weights = [jnp.broadcast_to(diffusion[:, c : c + 1], (1, LANES)) for c in range(3)]
    params = jnp.concatenate(
        [rows[0:4]]
        + [by_component(4 + j, 3) for j in range(3)]
        + [by_component(13, 1)]
        + weights
        + [jnp.zeros((PREPARED - DIFFUSION - 3, LANES), jnp.float32)],
        axis=0,
    )
    prepared[...] = params
    d0, d1, d2 = weights

    x_bump, x_part = x_factors(params, maps, size_x)
    y_row = iota((size_y, LANES), 0)
    y_bump, y_part = y_factors(params, maps, y_start + y_row, total_y)
    out_bump, out_part = y_factors(
        params, maps, jnp.where(y_row == 0, y_start + size_y, y_start - 1), total_y
    )
    inner = inner_z_rows(params, maps, z_start, size_z, total_z)
    outer = outer_z_rows(params, maps, z_start, size_z, total_z)
    inner = [only(inner, maps, c) for c in range(3)]
    outer = only(outer, maps, 0)

    def rows_by_x(bumps, part):
        return jnp.concatenate(
            [(x_bump[i : i + 1] * bumps) * (x_part[i : i + 1] + part) for i in range(size_x)],
            axis=0,
        )

    right = jnp.concatenate([inner[0], outer, inner[1], inner[2]], axis=0)
    drifts = half_drift(rows_by_x(y_bump, y_part), right)
    out_drift = half_drift(rows_by_x(out_bump, out_part), inner[0])

    def block(number):
        columns = drifts[:, number * LANES : (number + 1) * LANES]
        return columns.reshape(size_x, size_y, LANES)

    drift_x, plane_drift, drift_y, drift_z = block(0), block(1), block(2), block(3)
    out_drift = out_drift.reshape(size_x, size_y, LANES)
    drift_y_held[...] = drift_y
    drift_z_out[...] = drift_z
    copies[-1].wait()
    rho = density[...]
    zero = jnp.zeros((1, size_y, LANES), jnp.float32)
    up, down = (d0 + drift_x) * rho, (d0 - drift_x) * rho
    total = (
        jnp.concatenate([zero, up[:-1]], axis=0)
        + jnp.concatenate([down[1:], zero], axis=0)
        - (2.0 * (d0 + d1 + d2)) * rho
    )
    sublane = iota((size_x, size_y, LANES), 1)
    lane = iota((size_x, size_y, LANES), 2)
    up, down = roll((d1 + drift_y) * rho, 1, 1), roll((d1 - drift_y) * rho, -1, 1)
    at_low, at_high = sublane == 0, sublane == size_y - 1
    row_source = jnp.where(at_low, up, jnp.where(at_high, down, 0.0))
    total = total + jnp.where(at_low, 0.0, up) + jnp.where(at_high, 0.0, down)
    up, down = (d2 + drift_z) * rho, (d2 - drift_z) * rho
    plane_source = jnp.where(
        lane == ABOVE, up, jnp.where(lane == BELOW, roll(down, BELOW, 2), 0.0)
    )
    up, down = roll(up, 1, 2), roll(down, -1, 2)
    at_low, at_high = lane == 0, lane == size_z - 1
    total = total + jnp.where(at_low, 0.0, up) + jnp.where(at_high, 0.0, down)

    source = jnp.concatenate([total, row_source, plane_source], axis=1)
    drift = jnp.concatenate([drift_x, out_drift, plane_drift], axis=1)
    answers = solve_x(d0 + drift, d0 - drift, source, 1.0 + 2.0 * d0)
    for i in range(size_x):
        solved[i] = answers[i][: 2 * size_y]
    planes = pack_planes([answer[2 * size_y :] for answer in answers])

    row = iota((1, LANES), 0)
    out_rows = []
    for position in (y_start - 1, y_start + size_y):
        bumps, part = y_factors(params, maps, row + position, total_y)
        out_rows.append((x_bump * bumps) * (x_part + part))
    ends = half_drift(jnp.concatenate(out_rows, axis=0), inner[1])
    position = y_start - 1 + iota((2 * ROWS, LANES), 0)
    extra = half_drift(
        y_rows(params, maps, position, total_y),
        only(xz_rows(params, maps, size_x, z_start, size_z, total_z), maps, 1),
    )
    line_drift = (
        [ends[:size_x]]
        + [drift_y_held[:, j, :] for j in range(size_y)]
        + [ends[size_x:]]
    )
    line_drift = [with_extra(line_drift[j], extra[j : j + 1]) for j in range(size_y + 2)]
    values = [with_extra(solved[:, j, :], planes[j : j + 1]) for j in range(size_y)]
    for j in range(size_y):
        line_values[j] = values[j]
    for j in range(size_y + 2):
        line_drifts[j] = line_drift[j]
    pivot = 1.0 + 2.0 * d1
    g = c = None
    gs, cs = [], []
    for j in range(size_y):
        lower, upper = line_factors(line_drift, j, size_y, d1, y_start, total_y)
        weight = 1.0 / (pivot if j == 0 else pivot - lower * c)
        g = (values[j] if j == 0 else values[j] + lower * g) * weight
        c = upper * weight
        gs.append(g)
        cs.append(c)
    r_first = r_last = g
    for j in reversed(range(size_y - 1)):
        r_first = gs[j] + cs[j] * r_first
    pushed_up = solved[:, size_y, :] / (d1 + line_drift[size_y][:size_x])
    pushed_down = solved[:, 2 * size_y - 1, :] / (d1 - line_drift[1][:size_x])
    blank = jnp.zeros((1, LANES), jnp.float32)
    message[...] = join_message(
        r_first + with_extra(pushed_down, blank), r_last + with_extra(pushed_up, blank)
    )


def line_factors(line_drift, j, size_y, d1, y_start, total_y):
    lower, upper = d1 + line_drift[j], d1 - line_drift[j + 2]
    if j == 0:
        lower = jnp.where(y_start == 0, 0.0, lower)
    if j == size_y - 1:
        upper = jnp.where(y_start + size_y == total_y, 0.0, upper)
    return lower, upper


def line_coefs(params, maps, sizes, start, count, store):
    extent_y, extent_z, size_x, size_y, size_z = sizes
    total_y, total_z = size_y * extent_y, size_z * extent_z
    z_start = lax.axis_index("gz") * size_z
    d1 = params[DIFFUSION + 1 : DIFFUSION + 2]
    x_bump, x_part = x_factors(params, maps, size_x)
    inner = only(inner_z_rows(params, maps, z_start, size_z, total_z), maps, 1)
    planes = only(xz_rows(params, maps, size_x, z_start, size_z, total_z), maps, 1)
    whole = count == extent_y
    offsets = list(range(size_y)) if whole else list(range(-1, size_y + 1))
    left, left_extra = [], []
    for j in offsets:
        for b in range(count):
            position = iota((1, LANES), 0) + ((start + b) * size_y + j)
            bumps, part = y_factors(params, maps, position, total_y)
            left.append((x_bump * bumps) * (x_part + part))
        block = iota((max(count, ROWS), LANES), 0)
        left_extra.append(
            y_rows(params, maps, (start + block) * size_y + j, total_y)
        )
    depth = left_extra[0].shape[0]
    main = half_drift(jnp.concatenate(left, axis=0), inner)
    main = main.reshape(len(offsets), count, size_x, LANES)
    main = [main[j] for j in range(len(offsets))]
    extra = half_drift(jnp.concatenate(left_extra, axis=0), planes)
    extra = [extra[j * depth : (j + 1) * depth] for j in range(len(offsets))]
    if whole:
        main = (
            [jnp.concatenate([main[-1][:1], main[-1][:-1]], axis=0)]
            + main
            + [jnp.concatenate([main[0][1:], main[0][-1:]], axis=0)]
        )
        extra = [roll(extra[-1], 1, 0)] + extra + [roll(extra[0], -1, 0)]
    numbers = start + iota((depth, LANES), 0)
    pivot = 1.0 + 2.0 * d1
    at_start, at_end = numbers == 0, numbers == extent_y - 1

    def scan(drifts, starts, ends):
        a_first = c_first = a_last = c_last = None
        for j in range(size_y):
            lower, upper = d1 + drifts[j], d1 - drifts[j + 2]
            if j == 0:
                lower = starts(lower)
            if j == size_y - 1:
                upper = ends(upper)
            if j == 0:
                weight = 1.0 / pivot
                a_first, c_first = lower * weight, upper * weight
                a_last, c_last = a_first, c_first
            else:
                weight = 1.0 / (pivot - lower * c_last)
                step, c_last = lower * weight, upper * weight
                a_last = step * a_last
                a_first = a_first + c_first * a_last
                c_first = c_first * c_last
        return a_first, c_first, a_last, c_last

    def masked(values, number):
        return jnp.concatenate(
            [
                jnp.where(start + b == number, 0.0, values[b])[None]
                for b in range(count)
            ],
            axis=0,
        )

    main = scan(main, lambda v: masked(v, 0), lambda v: masked(v, extent_y - 1))
    extra = scan(
        extra,
        lambda v: jnp.where(at_start, 0.0, v),
        lambda v: jnp.where(at_end, 0.0, v),
    )
    for b in range(count):
        for q in range(4):
            store(b, q, with_extra(main[q][b], extra[q][b : b + 1]))


def near_kernel(
    sizes,
    maps,
    stride,
    radix,
    prepared,
    line_values,
    line_drifts,
    coefs,
    base,
    from_below,
    from_above,
):
    digit = lax.rem(lax.div(lax.axis_index("gy"), stride), radix)
    start = lax.div(lax.axis_index("gy"), stride) - digit
    params = prepared[...]

    def store(b, q, value):
        coefs[b, q] = value

    line_coefs(params, maps, sizes, start, radix, store)
    extent_y, _, _, size_y, _ = sizes
    d1 = params[DIFFUSION + 1 : DIFFUSION + 2]
    pivot = 1.0 + 2.0 * d1
    y_start = lax.axis_index("gy") * size_y
    g = a = c = None
    gs, as_, cs = [], [], []
    for j in range(size_y):
        lower, upper = line_factors(line_drifts, j, size_y, d1, y_start, size_y * extent_y)
        if j == 0:
            weight = 1.0 / pivot
            g, a = line_values[j] * weight, lower * weight
        else:
            weight = 1.0 / (pivot - lower * c)
            g, a = (line_values[j] + lower * g) * weight, lower * a * weight
        c = upper * weight
        gs.append(g)
        as_.append(a)
        cs.append(c)
    base[size_y - 1], from_below[size_y - 1], from_above[size_y - 1] = g, a, c
    for j in reversed(range(size_y - 1)):
        g, a, c = gs[j] + cs[j] * g, as_[j] + cs[j] * a, cs[j] * c
        base[j], from_below[j], from_above[j] = g, a, c


def far_kernel(sizes, maps, levels, prepared, *outputs):
    held = {}

    def store(b, q, value):
        held[b, q] = value

    extent_y = sizes[0]
    line_coefs(prepared[...], maps, sizes, 0, extent_y, store)
    groups = [tuple(held[b, q] for q in range(4)) for b in range(extent_y)]
    for (_, radix), coefs in zip(levels, outputs):
        groups = [
            functools.reduce(merge_coefs, groups[g : g + radix])
            for g in range(0, len(groups), radix)
        ]
        for number, group in enumerate(groups):
            for q in range(4):
                coefs[number, q] = group[q]


def z_coef_kernel(sizes, maps, prepared, drift_z, steps, ends, pushes, packed):
    extent_y, extent_z, size_x, size_y, size_z = sizes
    total_y, total_z = size_y * extent_y, size_z * extent_z
    y_start = lax.axis_index("gy") * size_y
    z_start = lax.axis_index("gz") * size_z
    params = prepared[...]
    d2 = params[DIFFUSION + 2 : DIFFUSION + 3]
    lane = iota((size_y, LANES), 1)
    divisors = []
    for i in range(size_x):
        plane = drift_z[i]
        factor = jnp.where(lane == ABOVE, d2 + plane, d2 - roll(plane, BELOW, 1))
        divisors.append(
            jnp.where((lane == ABOVE) | (lane == BELOW), 1.0 / factor, 0.0)
        )
    pushes[...] = pack_planes(divisors)
    x_bump, x_part = x_factors(params, maps, size_x)
    outer = only(outer_z_rows(params, maps, z_start, size_z, total_z), maps, 2)
    rows = []
    for j in range(size_y):
        position = iota((1, LANES), 0) + (y_start + j)
        bumps, part = y_factors(params, maps, position, total_y)
        rows.append((x_bump * bumps) * (x_part + part))
    outer = half_drift(jnp.concatenate(rows, axis=0), outer)
    outer = to_lines([outer[j * size_x : (j + 1) * size_x] for j in range(size_y)], size_x)
    inner = to_lines([drift_z[:, j, :] for j in range(size_y)], size_x)
    d2 = jnp.concatenate([d2] * (inner.shape[1] // LANES), axis=1)
    scale = 1.0 / (1.0 + 2.0 * d2)
    row = iota(inner.shape, 0)
    low, high = row == 0, row == size_z - 1
    before = jnp.where(low, outer[BELOW : BELOW + 1], turn(inner, 1))
    after = jnp.where(high, outer[ABOVE : ABOVE + 1], turn(inner, -1))
    below = jnp.where(low & (z_start == 0), 0.0, (d2 + before) * scale)
    above = jnp.where(high & (z_start + size_z == total_z), 0.0, (d2 - after) * scale)
    stride, level = 1, 0
    while stride < size_z:
        low, high = row < stride, row >= size_z - stride
        low_a = jnp.where(low, 1.0, turn(below, stride))
        low_c = jnp.where(low, 0.0, turn(above, stride))
        high_a = jnp.where(high, 0.0, turn(below, -stride))
        high_c = jnp.where(high, 1.0, turn(above, -stride))
        inverse = 1.0 / (1.0 - below * low_c - above * high_a)
        below, above = below * inverse, above * inverse
        factor = scale if level == 0 else 1.0
        steps[level, 0] = inverse * factor
        steps[level, 1] = jnp.where(low, 0.0, below * factor)
        steps[level, 2] = jnp.where(high, 0.0, above * factor)
        below, above = below * low_a, above * high_c
        stride, level = stride * 2, level + 1
    ends[0] = below
    ends[1] = above
    packed[...] = jnp.concatenate(
        [
            jnp.zeros((2, inner.shape[1]), jnp.float32),
            below[:1],
            below[size_z - 1 :],
            above[:1],
            above[size_z - 1 :],
            jnp.zeros((2, inner.shape[1]), jnp.float32),
        ],
        axis=0,
    )


def gather_members(refs, own, count):
    held = [ref[...] for ref in refs]
    return [
        functools.reduce(
            lambda acc, s: jnp.where((own ^ s) == j, held[s], acc), range(1, count), held[0]
        )
        for j in range(count)
    ]


def join_message(first, last):
    size_x = first.shape[0] - ROWS
    extra = jnp.where(iota((ROWS, LANES), 0) == 0, first[size_x:], last[size_x:])
    return jnp.concatenate([first[:size_x], last[:size_x], extra], axis=0)


def split_message(message):
    size_x = (message.shape[0] - ROWS) // 2
    return (
        with_extra(message[:size_x], message[2 * size_x : 2 * size_x + 1]),
        with_extra(message[size_x : 2 * size_x], message[2 * size_x + 1 : 2 * size_x + 2]),
    )


def merge_kernel(stride, radix, local, facing, coefs, *refs):
    received, message = refs[:radix], refs[-1]
    digit = lax.rem(lax.div(lax.axis_index("gy"), stride), radix)
    first = 0 if local else lax.div(lax.axis_index("gy"), stride) - digit
    values = [split_message(m) for m in gather_members(received, digit, radix)]
    group = [tuple(coefs[first + j, q] for q in range(4)) for j in range(radix)]
    merged, total = group[0], values[0]
    for j in range(1, radix):
        total = merge_values(merged, group[j], total, values[j])
        merged = merge_coefs(merged, group[j])
    if facing:
        is_low = lax.axis_index("gy") < stride * radix
        message[...] = jnp.where(is_low, total[1], total[0])
    else:
        message[...] = join_message(*total)


def middle_kernel(levels, *refs):
    refs = list(refs)
    steps, pushes, packed, base, from_below, from_above = refs[:6]
    refs = refs[6:]
    inputs = []
    for stride, radix in levels:
        inputs.append((refs[0], refs[1 : 1 + radix]))
        refs = refs[1 + radix :]
    message, doubled, seen = refs
    size_y, width = base.shape[:2]
    size_x = width - ROWS
    below = above = jnp.zeros((width, LANES), jnp.float32)
    for number in reversed(range(len(levels))):
        (stride, radix), (coefs, received) = levels[number], inputs[number]
        digit = lax.rem(lax.div(lax.axis_index("gy"), stride), radix)
        first = 0 if number == 0 else lax.div(lax.axis_index("gy"), stride) - digit
        members = gather_members(received, digit, radix)
        group = [tuple(coefs[first + j, q] for q in range(4)) for j in range(radix)]
        if members[0].shape[0] == width:
            c_last, a_first = group[0][3], group[1][0]
            inverse = 1.0 / (1.0 - c_last * a_first)
            below = jnp.where(digit == 0, 0.0, (members[0] + c_last * members[1]) * inverse)
            above = jnp.where(digit == 0, (members[1] + a_first * members[0]) * inverse, 0.0)
            continue
        values = [split_message(m) for m in members]
        lows, highs = chain(group, values, below, above)
        for j in range(radix):
            seen[j, 0] = lows[j]
            seen[j, 1] = highs[j]
        below, above = seen[digit, 0], seen[digit, 1]
    inner, outer = [], []
    for j in range(size_y):
        value = base[j] + from_below[j] * below + from_above[j] * above
        inner.append(value[:size_x])
        outer.append(value[size_x : size_x + 1])
    pushed = jnp.concatenate(outer, axis=0) * pushes[...]
    values = to_lines(inner, size_x)
    stride, level = 1, 0
    while stride < values.shape[0]:
        values = (
            steps[level, 0] * values
            + steps[level, 1] * turn(values, stride)
            + steps[level, 2] * turn(values, -stride)
        )
        stride, level = stride * 2, level + 1
    doubled[...] = values
    message[...] = packed[...]
    message[0:1] = values[:1] + lines_of(pushed, size_x, BELOW + 1)
    message[1:2] = values[-1:] + lines_of(pushed, size_x, 0)


def merge_z(low, high):
    inverse = 1.0 / (1.0 - low[5] * high[2])
    onward, back = low[4] * inverse, high[3] * inverse
    return (
        low[0] + onward * (high[0] + high[2] * low[1]),
        high[1] + back * (low[1] + low[5] * high[0]),
        low[2] + onward * high[2] * low[3],
        back * low[3],
        onward * high[4],
        high[5] + back * low[5] * high[4],
    )


def unpack_ends(message):
    return tuple(message[s : s + 1] for s in range(6))


def merge_z_kernel(stride, radix, *refs):
    received, message = refs[:radix], refs[radix]
    digit = lax.rem(lax.div(lax.axis_index("gz"), stride), radix)
    members = [unpack_ends(m) for m in gather_members(received, digit, radix)]
    total = functools.reduce(merge_z, members)
    message[...] = jnp.concatenate(total + total[:2], axis=0)


def end_kernel(levels, density, doubled, ends, *refs):
    refs = list(refs)
    inputs = []
    for stride, radix in levels:
        inputs.append(refs[:radix])
        refs = refs[radix:]
    out, seen = refs
    size_x, size_y, _ = density.shape
    below = above = jnp.zeros((1, doubled.shape[1]), jnp.float32)
    for (stride, radix), received in zip(reversed(levels), reversed(inputs)):
        digit = lax.rem(lax.div(lax.axis_index("gz"), stride), radix)
        members = [unpack_ends(m) for m in gather_members(received, digit, radix)]
        lows, highs = chain(
            [(m[2], m[4], m[3], m[5]) for m in members],
            [(m[0], m[1]) for m in members],
            below,
            above,
        )
        for j in range(radix):
            seen[j, 0:1] = lows[j]
            seen[j, 1:2] = highs[j]
        below, above = seen[digit, 0:1], seen[digit, 1:2]
    values = doubled[...] + ends[0] * below + ends[1] * above
    group = LANES // size_x
    for first in range(0, size_y, group):
        tile = first // group
        lines = jnp.transpose(values[:, tile * LANES : (tile + 1) * LANES])
        for q in range(group):
            out[:, first + q, :] = (
                density[:, first + q, :] + lines[q * size_x : (q + 1) * size_x]
            )


def radices(extent):
    rounds, stride = [], 1
    while stride < extent:
        radix = 4 if (extent // stride) % 4 == 0 else 2
        rounds.append((stride, radix))
        stride *= radix
    return rounds


def exchange(message, axis, stride, radix):
    devices = range(lax.axis_size(axis))
    return [message] + [
        lax.ppermute(message, axis, [(i, i ^ (s * stride)) for i in devices])
        for s in range(1, radix)
    ]


def body(density, diffusion, centers, sharpness, affine, offsets):
    size_x, size_y, size_z = density.shape
    extent_y, extent_z = lax.axis_size("gy"), lax.axis_size("gz")
    sizes = (extent_y, extent_z, size_x, size_y, size_z)
    maps = centers.shape[0]
    width = size_x + ROWS
    wide = (size_y, width, LANES)
    narrow = (size_z, size_y * size_x)
    float32 = jnp.float32
    y_levels, z_levels = radices(extent_y), radices(extent_z)

    def shape(*dims):
        return jax.ShapeDtypeStruct(dims, float32)

    vmem = pl.BlockSpec(memory_space=pltpu.VMEM)
    hbm = pl.BlockSpec(memory_space=pltpu.HBM)

    def call(kernel, inputs, outputs, in_specs=None, scratch=(), flops=10**6):
        return pl.pallas_call(
            kernel,
            out_shape=outputs,
            in_specs=in_specs or [vmem] * len(inputs),
            out_specs=jax.tree.map(lambda _: vmem, outputs),
            scratch_shapes=list(scratch),
            compiler_params=pltpu.CompilerParams(vmem_limit_bytes=VMEM_LIMIT),
            cost_estimate=pl.CostEstimate(flops=flops, bytes_accessed=10**6, transcendentals=0),
        )(*inputs)

    raw = (
        density,
        diffusion.reshape(1, 3),
        centers.T,
        sharpness.reshape(1, maps),
        affine.transpose(1, 2, 0),
        offsets.T,
    )
    raw = tuple(pltpu.with_memory_space_constraint(array, pltpu.HBM) for array in raw)
    message, line_values, line_drifts, drift_z, prepared = call(
        functools.partial(start_kernel, extent_y, extent_z),
        raw,
        (
            shape(width + size_x, LANES),
            shape(*wide),
            shape(size_y + 2, width, LANES),
            shape(size_x, size_y, LANES),
            shape(PREPARED, LANES),
        ),
        [hbm] * len(raw),
        [
            pltpu.VMEM((size_x, 2 * size_y, LANES), float32),
            pltpu.VMEM((size_x, size_y, LANES), float32),
        ]
        + [pltpu.VMEM(array.shape, float32) for array in raw]
        + [pltpu.VMEM((PREPARED, LANES), float32), pltpu.SemaphoreType.DMA((len(raw),))],
    )
    stride, radix = y_levels[0]
    near, base, from_below, from_above = call(
        functools.partial(near_kernel, sizes, maps, stride, radix),
        [prepared, line_values, line_drifts],
        (shape(radix, 4, width, LANES), shape(*wide), shape(*wide), shape(*wide)),
    )
    far, count = [], extent_y
    for _, radix in y_levels[:-1]:
        count = count // radix
        far.append(shape(count, 4, width, LANES))
    if far:
        far = call(functools.partial(far_kernel, sizes, maps, y_levels[:-1]), [prepared], far)
    coefs = [near] + list(far)
    doublings = size_z.bit_length() - 1
    steps, ends, pushes, packed = call(
        functools.partial(z_coef_kernel, sizes, maps),
        (prepared, drift_z),
        (
            shape(doublings, 3, *narrow),
            shape(2, *narrow),
            shape(size_y, LANES),
            shape(ROWS, size_y * size_x),
        ),
    )
    line_inputs = []
    for number, (stride, radix) in enumerate(y_levels):
        received = exchange(message, "gy", stride, radix)
        line_inputs += [coefs[number]] + received
        if number + 1 < len(y_levels):
            facing = number + 2 == len(y_levels) and y_levels[-1][1] == 2
            message = call(
                functools.partial(merge_kernel, stride, radix, number == 0, facing),
                [coefs[number]] + received + ([packed] if number == 0 else []),
                shape(width if facing else width + size_x, LANES),
            )
    message, doubled = call(
        functools.partial(middle_kernel, y_levels),
        [steps, pushes, packed, base, from_below, from_above] + line_inputs,
        (shape(ROWS, size_y * size_x), shape(*narrow)),
        scratch=[pltpu.VMEM((4, 2, width, LANES), float32)],
    )
    end_inputs = []
    for number, (stride, radix) in enumerate(z_levels):
        received = exchange(message, "gz", stride, radix)
        end_inputs += received
        if number + 1 < len(z_levels):
            message = call(
                functools.partial(merge_z_kernel, stride, radix),
                received,
                shape(ROWS, size_y * size_x),
            )
    return call(
        functools.partial(end_kernel, z_levels),
        [density, doubled, ends] + end_inputs,
        shape(size_x, size_y, size_z),
        scratch=[pltpu.VMEM((4, ROWS, size_y * size_x), float32)],
    )


def solution(mesh):
    placed = (P(None, "gy", "gz"), P(), P(), P(), P(), P())
    return jax.shard_map(
        body, mesh=mesh, in_specs=placed, out_specs=P(None, "gy", "gz"), check_vma=False
    )
```

```python
import functools

import jax
import jax.numpy as jnp
from jax import lax
from jax.experimental import pallas as pl
from jax.experimental.pallas import tpu as pltpu
from jax.sharding import PartitionSpec as P

HALF_LIMIT = 600.0
LANES = 128
ROWS = 8
ABOVE, BELOW = 127, 31
VMEM_LIMIT = 48 * 1024 * 1024


def iota(shape, axis):
    return lax.broadcasted_iota(jnp.int32, shape, axis)


def coordinate(positions, line_total):
    return (2.0 * positions.astype(jnp.float32) + 1.0) / line_total - 1.0


def roll(values, shift, axis):
    return pltpu.roll(values, shift % values.shape[axis], axis)


def matmul(left, right):
    low, high = split(left), split(right)
    columns = right.shape[0]
    both = lax.dot_general(
        jnp.concatenate(low, axis=1),
        jnp.concatenate([jnp.concatenate([part, part], axis=1) for part in high], axis=0),
        (((1,), (1,)), ((), ())),
        preferred_element_type=jnp.float32,
    )
    return both[:, :columns] + both[:, columns:]


def split(values):
    upper = values.astype(jnp.bfloat16)
    return upper, (values - upper.astype(jnp.float32)).astype(jnp.bfloat16)


def half_drift(left, right):
    return HALF_LIMIT * jnp.tanh(matmul(left, right))


SHARPNESS, CENTER, SLOPE, OFFSET, DIFFUSION, PREPARED = 0, 1, 4, 7, 8, 16


def component_of(maps):
    return iota((1, LANES), 1) // (2 * maps)


def first_term(maps):
    return (iota((1, LANES), 1) // maps) % 2 == 0


def bump(params, coord, axis):
    center = params[CENTER + axis : CENTER + axis + 1]
    return jnp.exp(-params[SHARPNESS : SHARPNESS + 1] * (coord - center) ** 2)


def slope(params, coord, axis):
    return coord * params[SLOPE + axis : SLOPE + axis + 1]


def x_factors(params, maps, size_x):
    coord = coordinate(iota((size_x, LANES), 0), size_x)
    return bump(params, coord, 0), jnp.where(first_term(maps), slope(params, coord, 0), 0.0)


def y_factors(params, maps, position, total_y):
    coord = coordinate(position, total_y)
    part = slope(params, coord, 1) + params[OFFSET : OFFSET + 1]
    return bump(params, coord, 1), jnp.where(
        first_term(maps), part, params[SLOPE + 2 : SLOPE + 3]
    )


def z_rows(params, maps, position, total_z):
    coord = coordinate(position, total_z)
    return bump(params, coord, 2) * jnp.where(first_term(maps), 1.0, coord)


def inner_z_rows(params, maps, z_start, size_z, total_z):
    return z_rows(params, maps, z_start + iota((size_z, LANES), 0), total_z)


def outer_z_rows(params, maps, z_start, size_z, total_z):
    row = iota((size_z, LANES), 0)
    return z_rows(
        params, maps, jnp.where(row == BELOW, z_start - 1, z_start + size_z), total_z
    )


def only(rows, maps, component):
    return jnp.where(component_of(maps) == component, rows, 0.0)


def y_rows(params, maps, position, total_y):
    coord = coordinate(position, total_y)
    part = slope(params, coord, 1) + params[OFFSET : OFFSET + 1]
    return bump(params, coord, 1) * jnp.where(first_term(maps), part, 1.0)


def xz_rows(params, maps, size_x, z_start, size_z, total_z):
    row = iota((BELOW + 1 + size_x, LANES), 0)
    x_coord = coordinate(jnp.where(row < size_x, row, row - BELOW - 1), size_x)
    z_coord = coordinate(jnp.where(row > BELOW, z_start - 1, z_start + size_z), total_z)
    part = slope(params, x_coord, 0) + slope(params, z_coord, 2)
    both = bump(params, x_coord, 0) * bump(params, z_coord, 2)
    both = both * jnp.where(first_term(maps), 1.0, part)
    return jnp.concatenate(
        [both, jnp.zeros((LANES - BELOW - 1 - size_x, LANES), jnp.float32)], axis=0
    )


def with_extra(main, row):
    return jnp.concatenate([main, jnp.broadcast_to(row, (ROWS, LANES))], axis=0)


def pack_planes(planes):
    turned = [roll(plane, i + 1, 1) for i, plane in enumerate(planes)]
    while len(turned) > 1:
        turned = [sum(turned[i : i + 2]) for i in range(0, len(turned), 2)]
    return turned[0]


def lines_of(planes, size_x, first_lane):
    group = LANES // size_x
    place = iota((1, LANES), 1) // size_x
    turned = [roll(planes, q * size_x - first_lane, 1) for q in range(group)]
    rows = []
    for first in range(0, planes.shape[0], group):
        row = turned[0][first : first + 1]
        for q in range(1, group):
            row = jnp.where(place == q, turned[q][first + q : first + q + 1], row)
        rows.append(row)
    return jnp.concatenate(rows, axis=1)


def to_lines(rows, size_x):
    group = LANES // size_x
    return jnp.concatenate(
        [
            jnp.transpose(jnp.concatenate(rows[first : first + group], axis=0))
            for first in range(0, len(rows), group)
        ],
        axis=1,
    )


def turn(values, stride):
    stride = stride % values.shape[0]
    if stride % ROWS == 0:
        return jnp.concatenate([values[-stride:], values[:-stride]], axis=0)
    return roll(values, stride, 0)


def merge_coefs(low, high):
    inverse = 1.0 / (1.0 - low[3] * high[0])
    onward, back = low[1] * inverse, high[2] * inverse
    return (
        low[0] + onward * high[0] * low[2],
        onward * high[1],
        back * low[2],
        high[3] + back * low[3] * high[1],
    )


def merge_values(low, high, low_values, high_values):
    inverse = 1.0 / (1.0 - low[3] * high[0])
    return (
        low_values[0] + low[1] * inverse * (high_values[0] + high[0] * low_values[1]),
        high_values[1] + high[2] * inverse * (low_values[1] + low[3] * high_values[0]),
    )


def merge(low, high, low_values, high_values):
    return merge_coefs(low, high), merge_values(low, high, low_values, high_values)


def meet(low, high, below, above):
    (_, _, a_last, c_last), (_, r_last) = low
    (a_first, c_first, _, _), (r_first, _) = high
    inverse = 1.0 / (1.0 - c_last * a_first)
    upper = r_first + c_first * above
    left = (r_last + a_last * below + c_last * upper) * inverse
    return left, upper + a_first * left


def chain(coefs, values, below, above):
    count = len(coefs)
    if count == 4:
        halves = [merge(coefs[j], coefs[j + 1], values[j], values[j + 1]) for j in (0, 2)]
        left, right = meet(halves[0], halves[1], below, above)
        seen = [
            meet((coefs[j], values[j]), (coefs[j + 1], values[j + 1]), low, high)
            for j, low, high in ((0, below, right), (2, left, above))
        ]
        return [below, seen[0][0], left, seen[1][0]], [seen[0][1], right, seen[1][1], above]
    held, slope = below, None
    befores, firsts = [], []
    for j in range(count):
        a_first, c_first, a_last, c_last = coefs[j]
        r_first, r_last = values[j]
        befores.append((held, slope))
        if slope is None:
            first, first_slope = r_first + a_first * held, c_first
            held, slope = r_last + a_last * held, c_last
        else:
            inverse = 1.0 / (1.0 - a_first * slope)
            first = (r_first + a_first * held) * inverse
            first_slope = c_first * inverse
            held, slope = (
                r_last + a_last * (held + slope * first),
                c_last + a_last * slope * first_slope,
            )
        firsts.append((first, first_slope))
    seen_above = [None] * count
    seen_below = [None] * count
    upper = above
    for j in reversed(range(count)):
        seen_above[j] = upper
        upper = firsts[j][0] + firsts[j][1] * upper
        held, slope = befores[j]
        seen_below[j] = held if slope is None else held + slope * upper
    return seen_below, seen_above


def solve_x(up, down, source, pivot):
    size = source.shape[0]
    half = size // 2
    low_g, low_c, high_g, high_c = {}, {}, {}, {}
    g = c = None
    for i in range(half):
        if i == 0:
            weight = 1.0 / pivot
            c = down[1] * weight
            g = source[0] * weight
        else:
            weight = 1.0 / (pivot - up[i - 1] * c)
            g = (source[i] + up[i - 1] * g) * weight
            c = down[i + 1] * weight
        low_g[i], low_c[i] = g, c
    for i in reversed(range(half, size)):
        if i == size - 1:
            weight = 1.0 / pivot
            c = up[i - 1] * weight
            g = source[i] * weight
        else:
            weight = 1.0 / (pivot - down[i + 1] * c)
            g = (source[i] + down[i + 1] * g) * weight
            c = up[i - 1] * weight
        high_g[i], high_c[i] = g, c
    out = [None] * size
    inverse = 1.0 / (1.0 - low_c[half - 1] * high_c[half])
    out[half - 1] = (low_g[half - 1] + low_c[half - 1] * high_g[half]) * inverse
    out[half] = high_g[half] + high_c[half] * out[half - 1]
    for i in reversed(range(half - 1)):
        out[i] = low_g[i] + low_c[i] * out[i + 1]
    for i in range(half + 1, size):
        out[i] = high_g[i] + high_c[i] * out[i - 1]
    return out


def start_kernel(
    extent_y,
    extent_z,
    density_hbm,
    diffusion_hbm,
    centers_hbm,
    sharpness_hbm,
    affine_hbm,
    offsets_hbm,
    message,
    line_values,
    line_drifts,
    drift_z_out,
    prepared,
    solved,
    drift_y_held,
    density,
    diffusion,
    centers,
    sharpness,
    affine,
    offsets,
    staged,
    semaphores,
):
    copies = [
        pltpu.make_async_copy(source, target, semaphores.at[number])
        for number, (source, target) in enumerate(
            [
                (diffusion_hbm, diffusion),
                (centers_hbm, centers),
                (sharpness_hbm, sharpness),
                (affine_hbm, affine),
                (offsets_hbm, offsets),
                (density_hbm, density),
            ]
        )
    ]
    for copy in copies:
        copy.start()
    size_x, size_y, size_z = density.shape
    total_y, total_z = size_y * extent_y, size_z * extent_z
    y_start = lax.axis_index("gy") * size_y
    z_start = lax.axis_index("gz") * size_z
    maps = centers.shape[1]
    for copy in copies[:-1]:
        copy.wait()

    staged[...] = jnp.zeros(staged.shape, jnp.float32)
    staged[0:1, :maps] = sharpness[...]
    staged[1:4, :maps] = centers[...]
    for c in range(3):
        staged[4 + 3 * c : 7 + 3 * c, :maps] = affine[c]
    staged[13:16, :maps] = offsets[...]
    rows = staged[...]
    width = maps
    while width < LANES:
        rows = rows + roll(rows, width, 1)
        width = 2 * width
    component = component_of(maps)
    rows = jnp.where(component < 3, rows, 0.0)

    def by_component(first, step):
        return jnp.where(
            component == 0,
            rows[first : first + 1],
            jnp.where(
                component == 1,
                rows[first + step : first + step + 1],
                rows[first + 2 * step : first + 2 * step + 1],
            ),
        )

    weights = [jnp.broadcast_to(diffusion[:, c : c + 1], (1, LANES)) for c in range(3)]
    params = jnp.concatenate(
        [rows[0:4]]
        + [by_component(4 + j, 3) for j in range(3)]
        + [by_component(13, 1)]
        + weights
        + [jnp.zeros((PREPARED - DIFFUSION - 3, LANES), jnp.float32)],
        axis=0,
    )
    prepared[...] = params
    d0, d1, d2 = weights

    x_bump, x_part = x_factors(params, maps, size_x)
    y_row = iota((size_y, LANES), 0)
    y_bump, y_part = y_factors(params, maps, y_start + y_row, total_y)
    out_bump, out_part = y_factors(
        params, maps, jnp.where(y_row == 0, y_start + size_y, y_start - 1), total_y
    )
    inner = inner_z_rows(params, maps, z_start, size_z, total_z)
    outer = outer_z_rows(params, maps, z_start, size_z, total_z)
    inner = [only(inner, maps, c) for c in range(3)]
    outer = only(outer, maps, 0)

    def rows_by_x(bumps, part):
        return jnp.concatenate(
            [(x_bump[i : i + 1] * bumps) * (x_part[i : i + 1] + part) for i in range(size_x)],
            axis=0,
        )

    right = jnp.concatenate([inner[0], outer, inner[1], inner[2]], axis=0)
    drifts = half_drift(rows_by_x(y_bump, y_part), right)
    out_drift = half_drift(rows_by_x(out_bump, out_part), inner[0])

    def block(number):
        columns = drifts[:, number * LANES : (number + 1) * LANES]
        return columns.reshape(size_x, size_y, LANES)

    drift_x, plane_drift, drift_y, drift_z = block(0), block(1), block(2), block(3)
    out_drift = out_drift.reshape(size_x, size_y, LANES)
    drift_y_held[...] = drift_y
    drift_z_out[...] = drift_z
    copies[-1].wait()
    rho = density[...]
    zero = jnp.zeros((1, size_y, LANES), jnp.float32)
    up, down = (d0 + drift_x) * rho, (d0 - drift_x) * rho
    total = (
        jnp.concatenate([zero, up[:-1]], axis=0)
        + jnp.concatenate([down[1:], zero], axis=0)
        - (2.0 * (d0 + d1 + d2)) * rho
    )
    sublane = iota((size_x, size_y, LANES), 1)
    lane = iota((size_x, size_y, LANES), 2)
    up, down = roll((d1 + drift_y) * rho, 1, 1), roll((d1 - drift_y) * rho, -1, 1)
    at_low, at_high = sublane == 0, sublane == size_y - 1
    row_source = jnp.where(at_low, up, jnp.where(at_high, down, 0.0))
    total = total + jnp.where(at_low, 0.0, up) + jnp.where(at_high, 0.0, down)
    up, down = (d2 + drift_z) * rho, (d2 - drift_z) * rho
    plane_source = jnp.where(
        lane == ABOVE, up, jnp.where(lane == BELOW, roll(down, BELOW, 2), 0.0)
    )
    up, down = roll(up, 1, 2), roll(down, -1, 2)
    at_low, at_high = lane == 0, lane == size_z - 1
    total = total + jnp.where(at_low, 0.0, up) + jnp.where(at_high, 0.0, down)

    source = jnp.concatenate([total, row_source, plane_source], axis=1)
    drift = jnp.concatenate([drift_x, out_drift, plane_drift], axis=1)
    answers = solve_x(d0 + drift, d0 - drift, source, 1.0 + 2.0 * d0)
    for i in range(size_x):
        solved[i] = answers[i][: 2 * size_y]
    planes = pack_planes([answer[2 * size_y :] for answer in answers])

    row = iota((1, LANES), 0)
    out_rows = []
    for position in (y_start - 1, y_start + size_y):
        bumps, part = y_factors(params, maps, row + position, total_y)
        out_rows.append((x_bump * bumps) * (x_part + part))
    ends = half_drift(jnp.concatenate(out_rows, axis=0), inner[1])
    position = y_start - 1 + iota((2 * ROWS, LANES), 0)
    extra = half_drift(
        y_rows(params, maps, position, total_y),
        only(xz_rows(params, maps, size_x, z_start, size_z, total_z), maps, 1),
    )
    line_drift = (
        [ends[:size_x]]
        + [drift_y_held[:, j, :] for j in range(size_y)]
        + [ends[size_x:]]
    )
    line_drift = [with_extra(line_drift[j], extra[j : j + 1]) for j in range(size_y + 2)]
    values = [with_extra(solved[:, j, :], planes[j : j + 1]) for j in range(size_y)]
    for j in range(size_y):
        line_values[j] = values[j]
    for j in range(size_y + 2):
        line_drifts[j] = line_drift[j]
    pivot = 1.0 + 2.0 * d1
    g = c = None
    gs, cs = [], []
    for j in range(size_y):
        lower, upper = line_factors(line_drift, j, size_y, d1, y_start, total_y)
        weight = 1.0 / (pivot if j == 0 else pivot - lower * c)
        g = (values[j] if j == 0 else values[j] + lower * g) * weight
        c = upper * weight
        gs.append(g)
        cs.append(c)
    r_first = r_last = g
    for j in reversed(range(size_y - 1)):
        r_first = gs[j] + cs[j] * r_first
    pushed_up = solved[:, size_y, :] / (d1 + line_drift[size_y][:size_x])
    pushed_down = solved[:, 2 * size_y - 1, :] / (d1 - line_drift[1][:size_x])
    blank = jnp.zeros((1, LANES), jnp.float32)
    message[...] = join_message(
        r_first + with_extra(pushed_down, blank), r_last + with_extra(pushed_up, blank)
    )


def line_factors(line_drift, j, size_y, d1, y_start, total_y):
    lower, upper = d1 + line_drift[j], d1 - line_drift[j + 2]
    if j == 0:
        lower = jnp.where(y_start == 0, 0.0, lower)
    if j == size_y - 1:
        upper = jnp.where(y_start + size_y == total_y, 0.0, upper)
    return lower, upper


def line_coefs(params, maps, sizes, start, count, store):
    extent_y, extent_z, size_x, size_y, size_z = sizes
    total_y, total_z = size_y * extent_y, size_z * extent_z
    z_start = lax.axis_index("gz") * size_z
    d1 = params[DIFFUSION + 1 : DIFFUSION + 2]
    x_bump, x_part = x_factors(params, maps, size_x)
    inner = only(inner_z_rows(params, maps, z_start, size_z, total_z), maps, 1)
    planes = only(xz_rows(params, maps, size_x, z_start, size_z, total_z), maps, 1)
    whole = count == extent_y
    offsets = list(range(size_y)) if whole else list(range(-1, size_y + 1))
    left, left_extra = [], []
    for j in offsets:
        for b in range(count):
            position = iota((1, LANES), 0) + ((start + b) * size_y + j)
            bumps, part = y_factors(params, maps, position, total_y)
            left.append((x_bump * bumps) * (x_part + part))
        block = iota((max(count, ROWS), LANES), 0)
        left_extra.append(
            y_rows(params, maps, (start + block) * size_y + j, total_y)
        )
    depth = left_extra[0].shape[0]
    main = half_drift(jnp.concatenate(left, axis=0), inner)
    main = main.reshape(len(offsets), count, size_x, LANES)
    main = [main[j] for j in range(len(offsets))]
    extra = half_drift(jnp.concatenate(left_extra, axis=0), planes)
    extra = [extra[j * depth : (j + 1) * depth] for j in range(len(offsets))]
    if whole:
        main = (
            [jnp.concatenate([main[-1][:1], main[-1][:-1]], axis=0)]
            + main
            + [jnp.concatenate([main[0][1:], main[0][-1:]], axis=0)]
        )
        extra = [roll(extra[-1], 1, 0)] + extra + [roll(extra[0], -1, 0)]
    numbers = start + iota((depth, LANES), 0)
    pivot = 1.0 + 2.0 * d1
    at_start, at_end = numbers == 0, numbers == extent_y - 1

    def scan(drifts, starts, ends):
        a_first = c_first = a_last = c_last = None
        for j in range(size_y):
            lower, upper = d1 + drifts[j], d1 - drifts[j + 2]
            if j == 0:
                lower = starts(lower)
            if j == size_y - 1:
                upper = ends(upper)
            if j == 0:
                weight = 1.0 / pivot
                a_first, c_first = lower * weight, upper * weight
                a_last, c_last = a_first, c_first
            else:
                weight = 1.0 / (pivot - lower * c_last)
                step, c_last = lower * weight, upper * weight
                a_last = step * a_last
                a_first = a_first + c_first * a_last
                c_first = c_first * c_last
        return a_first, c_first, a_last, c_last

    def masked(values, number):
        return jnp.concatenate(
            [
                jnp.where(start + b == number, 0.0, values[b])[None]
                for b in range(count)
            ],
            axis=0,
        )

    main = scan(main, lambda v: masked(v, 0), lambda v: masked(v, extent_y - 1))
    extra = scan(
        extra,
        lambda v: jnp.where(at_start, 0.0, v),
        lambda v: jnp.where(at_end, 0.0, v),
    )
    for b in range(count):
        for q in range(4):
            store(b, q, with_extra(main[q][b], extra[q][b : b + 1]))


def near_kernel(
    sizes,
    maps,
    stride,
    radix,
    prepared,
    line_values,
    line_drifts,
    coefs,
    base,
    from_below,
    from_above,
):
    digit = lax.rem(lax.div(lax.axis_index("gy"), stride), radix)
    start = lax.div(lax.axis_index("gy"), stride) - digit
    params = prepared[...]

    def store(b, q, value):
        coefs[b, q] = value

    line_coefs(params, maps, sizes, start, radix, store)
    extent_y, _, _, size_y, _ = sizes
    d1 = params[DIFFUSION + 1 : DIFFUSION + 2]
    pivot = 1.0 + 2.0 * d1
    y_start = lax.axis_index("gy") * size_y
    g = a = c = None
    gs, as_, cs = [], [], []
    for j in range(size_y):
        lower, upper = line_factors(line_drifts, j, size_y, d1, y_start, size_y * extent_y)
        if j == 0:
            weight = 1.0 / pivot
            g, a = line_values[j] * weight, lower * weight
        else:
            weight = 1.0 / (pivot - lower * c)
            g, a = (line_values[j] + lower * g) * weight, lower * a * weight
        c = upper * weight
        gs.append(g)
        as_.append(a)
        cs.append(c)
    base[size_y - 1], from_below[size_y - 1], from_above[size_y - 1] = g, a, c
    for j in reversed(range(size_y - 1)):
        g, a, c = gs[j] + cs[j] * g, as_[j] + cs[j] * a, cs[j] * c
        base[j], from_below[j], from_above[j] = g, a, c


def far_kernel(sizes, maps, levels, prepared, *outputs):
    held = {}

    def store(b, q, value):
        held[b, q] = value

    extent_y = sizes[0]
    line_coefs(prepared[...], maps, sizes, 0, extent_y, store)
    groups = [tuple(held[b, q] for q in range(4)) for b in range(extent_y)]
    for (_, radix), coefs in zip(levels, outputs):
        groups = [
            functools.reduce(merge_coefs, groups[g : g + radix])
            for g in range(0, len(groups), radix)
        ]
        for number, group in enumerate(groups):
            for q in range(4):
                coefs[number, q] = group[q]


def double_coefs(below, above, scale, steps=None):
    size_z = below.shape[0]
    row = iota(below.shape, 0)
    stride, level = 1, 0
    while stride < size_z:
        low, high = row < stride, row >= size_z - stride
        low_a = jnp.where(low, 1.0, turn(below, stride))
        low_c = jnp.where(low, 0.0, turn(above, stride))
        high_a = jnp.where(high, 0.0, turn(below, -stride))
        high_c = jnp.where(high, 1.0, turn(above, -stride))
        inverse = 1.0 / (1.0 - below * low_c - above * high_a)
        below, above = below * inverse, above * inverse
        if steps is not None:
            factor = scale if level == 0 else 1.0
            steps[level, 0] = inverse * factor
            steps[level, 1] = jnp.where(low, 0.0, below * factor)
            steps[level, 2] = jnp.where(high, 0.0, above * factor)
        below, above = below * low_a, above * high_c
        stride, level = stride * 2, level + 1
    return below, above


def z_coef_kernel(sizes, maps, prepared, drift_z, steps, ends, pushes, packed, weights):
    extent_y, extent_z, size_x, size_y, size_z = sizes
    total_y, total_z = size_y * extent_y, size_z * extent_z
    y_start = lax.axis_index("gy") * size_y
    z_start = lax.axis_index("gz") * size_z
    params = prepared[...]
    d2 = params[DIFFUSION + 2 : DIFFUSION + 3]
    lane = iota((size_y, LANES), 1)
    divisors = []
    for i in range(size_x):
        plane = drift_z[i]
        factor = jnp.where(lane == ABOVE, d2 + plane, d2 - roll(plane, BELOW, 1))
        divisors.append(
            jnp.where((lane == ABOVE) | (lane == BELOW), 1.0 / factor, 0.0)
        )
    pushes[...] = pack_planes(divisors)
    x_bump, x_part = x_factors(params, maps, size_x)
    outer = only(outer_z_rows(params, maps, z_start, size_z, total_z), maps, 2)
    rows = []
    for j in range(size_y):
        position = iota((1, LANES), 0) + (y_start + j)
        bumps, part = y_factors(params, maps, position, total_y)
        rows.append((x_bump * bumps) * (x_part + part))
    outer = half_drift(jnp.concatenate(rows, axis=0), outer)
    outer = to_lines([outer[j * size_x : (j + 1) * size_x] for j in range(size_y)], size_x)
    inner = to_lines([drift_z[:, j, :] for j in range(size_y)], size_x)
    d2 = jnp.concatenate([d2] * (inner.shape[1] // LANES), axis=1)
    scale = 1.0 / (1.0 + 2.0 * d2)
    row = iota(inner.shape, 0)
    low, high = row == 0, row == size_z - 1
    before = jnp.where(low, outer[BELOW : BELOW + 1], turn(inner, 1))
    after = jnp.where(high, outer[ABOVE : ABOVE + 1], turn(inner, -1))
    below = jnp.where(low & (z_start == 0), 0.0, (d2 + before) * scale)
    above = jnp.where(high & (z_start + size_z == total_z), 0.0, (d2 - after) * scale)
    turned_below = jnp.where(low, 1.0, turn(above, 1))
    turned_above = jnp.where(high, 1.0, turn(below, -1))
    below, above = double_coefs(below, above, scale, steps)
    turned_below, turned_above = double_coefs(turned_below, turned_above, scale)
    weights[0] = turned_below * scale
    weights[1] = turned_above * scale
    ends[0] = below
    ends[1] = above
    packed[...] = jnp.concatenate(
        [
            jnp.zeros((2, inner.shape[1]), jnp.float32),
            below[:1],
            below[size_z - 1 :],
            above[:1],
            above[size_z - 1 :],
            jnp.zeros((2, inner.shape[1]), jnp.float32),
        ],
        axis=0,
    )


def gather_members(refs, own, count):
    held = [ref[...] for ref in refs]
    return [
        functools.reduce(
            lambda acc, s: jnp.where((own ^ s) == j, held[s], acc), range(1, count), held[0]
        )
        for j in range(count)
    ]


def join_message(first, last):
    size_x = first.shape[0] - ROWS
    extra = jnp.where(iota((ROWS, LANES), 0) == 0, first[size_x:], last[size_x:])
    return jnp.concatenate([first[:size_x], last[:size_x], extra], axis=0)


def split_message(message):
    size_x = (message.shape[0] - ROWS) // 2
    return (
        with_extra(message[:size_x], message[2 * size_x : 2 * size_x + 1]),
        with_extra(message[size_x : 2 * size_x], message[2 * size_x + 1 : 2 * size_x + 2]),
    )


def merge_kernel(stride, radix, local, facing, coefs, *refs):
    received, message = refs[:radix], refs[-1]
    digit = lax.rem(lax.div(lax.axis_index("gy"), stride), radix)
    first = 0 if local else lax.div(lax.axis_index("gy"), stride) - digit
    values = [split_message(m) for m in gather_members(received, digit, radix)]
    group = [tuple(coefs[first + j, q] for q in range(4)) for j in range(radix)]
    merged, total = group[0], values[0]
    for j in range(1, radix):
        total = merge_values(merged, group[j], total, values[j])
        merged = merge_coefs(merged, group[j])
    if facing:
        is_low = lax.axis_index("gy") < stride * radix
        message[...] = jnp.where(is_low, total[1], total[0])
    else:
        message[...] = join_message(*total)


def middle_kernel(levels, *refs):
    refs = list(refs)
    weights, pushes, packed, base, from_below, from_above = refs[:6]
    refs = refs[6:]
    inputs = []
    for stride, radix in levels:
        inputs.append((refs[0], refs[1 : 1 + radix]))
        refs = refs[1 + radix :]
    message, sources, seen = refs
    size_y, width = base.shape[:2]
    size_x = width - ROWS
    below = above = jnp.zeros((width, LANES), jnp.float32)
    for number in reversed(range(len(levels))):
        (stride, radix), (coefs, received) = levels[number], inputs[number]
        digit = lax.rem(lax.div(lax.axis_index("gy"), stride), radix)
        first = 0 if number == 0 else lax.div(lax.axis_index("gy"), stride) - digit
        members = gather_members(received, digit, radix)
        group = [tuple(coefs[first + j, q] for q in range(4)) for j in range(radix)]
        if members[0].shape[0] == width:
            c_last, a_first = group[0][3], group[1][0]
            inverse = 1.0 / (1.0 - c_last * a_first)
            below = jnp.where(digit == 0, 0.0, (members[0] + c_last * members[1]) * inverse)
            above = jnp.where(digit == 0, (members[1] + a_first * members[0]) * inverse, 0.0)
            continue
        values = [split_message(m) for m in members]
        lows, highs = chain(group, values, below, above)
        for j in range(radix):
            seen[j, 0] = lows[j]
            seen[j, 1] = highs[j]
        below, above = seen[digit, 0], seen[digit, 1]
    inner, outer = [], []
    for j in range(size_y):
        value = base[j] + from_below[j] * below + from_above[j] * above
        inner.append(value[:size_x])
        outer.append(value[size_x : size_x + 1])
    pushed = jnp.concatenate(outer, axis=0) * pushes[...]
    values = to_lines(inner, size_x)
    sources[...] = values
    message[...] = packed[...]
    message[0:1] = total_of(weights[0] * values) + lines_of(pushed, size_x, BELOW + 1)
    message[1:2] = total_of(weights[1] * values) + lines_of(pushed, size_x, 0)


def total_of(values):
    return jnp.sum(values, axis=0, keepdims=True)


def double_kernel(steps, sources, doubled):
    values = sources[...]
    stride, level = 1, 0
    while stride < values.shape[0]:
        values = (
            steps[level, 0] * values
            + steps[level, 1] * turn(values, stride)
            + steps[level, 2] * turn(values, -stride)
        )
        stride, level = stride * 2, level + 1
    doubled[...] = values


def merge_z(low, high):
    inverse = 1.0 / (1.0 - low[5] * high[2])
    onward, back = low[4] * inverse, high[3] * inverse
    return (
        low[0] + onward * (high[0] + high[2] * low[1]),
        high[1] + back * (low[1] + low[5] * high[0]),
        low[2] + onward * high[2] * low[3],
        back * low[3],
        onward * high[4],
        high[5] + back * low[5] * high[4],
    )


def unpack_ends(message):
    return tuple(message[s : s + 1] for s in range(6))


def merge_z_kernel(stride, radix, *refs):
    received, message = refs[:radix], refs[radix]
    digit = lax.rem(lax.div(lax.axis_index("gz"), stride), radix)
    members = [unpack_ends(m) for m in gather_members(received, digit, radix)]
    total = functools.reduce(merge_z, members)
    message[...] = jnp.concatenate(total + total[:2], axis=0)


def end_kernel(levels, density, doubled, ends, *refs):
    refs = list(refs)
    inputs = []
    for stride, radix in levels:
        inputs.append(refs[:radix])
        refs = refs[radix:]
    out, seen = refs
    size_x, size_y, _ = density.shape
    below = above = jnp.zeros((1, doubled.shape[1]), jnp.float32)
    for (stride, radix), received in zip(reversed(levels), reversed(inputs)):
        digit = lax.rem(lax.div(lax.axis_index("gz"), stride), radix)
        members = [unpack_ends(m) for m in gather_members(received, digit, radix)]
        lows, highs = chain(
            [(m[2], m[4], m[3], m[5]) for m in members],
            [(m[0], m[1]) for m in members],
            below,
            above,
        )
        for j in range(radix):
            seen[j, 0:1] = lows[j]
            seen[j, 1:2] = highs[j]
        below, above = seen[digit, 0:1], seen[digit, 1:2]
    values = doubled[...] + ends[0] * below + ends[1] * above
    group = LANES // size_x
    for first in range(0, size_y, group):
        tile = first // group
        lines = jnp.transpose(values[:, tile * LANES : (tile + 1) * LANES])
        for q in range(group):
            out[:, first + q, :] = (
                density[:, first + q, :] + lines[q * size_x : (q + 1) * size_x]
            )


def radices(extent):
    rounds, stride = [], 1
    while stride < extent:
        radix = 4 if (extent // stride) % 4 == 0 else 2
        rounds.append((stride, radix))
        stride *= radix
    return rounds


def exchange(message, axis, stride, radix):
    devices = range(lax.axis_size(axis))
    return [message] + [
        lax.ppermute(message, axis, [(i, i ^ (s * stride)) for i in devices])
        for s in range(1, radix)
    ]


def body(density, diffusion, centers, sharpness, affine, offsets):
    size_x, size_y, size_z = density.shape
    extent_y, extent_z = lax.axis_size("gy"), lax.axis_size("gz")
    sizes = (extent_y, extent_z, size_x, size_y, size_z)
    maps = centers.shape[0]
    width = size_x + ROWS
    wide = (size_y, width, LANES)
    narrow = (size_z, size_y * size_x)
    float32 = jnp.float32
    y_levels, z_levels = radices(extent_y), radices(extent_z)

    def shape(*dims):
        return jax.ShapeDtypeStruct(dims, float32)

    vmem = pl.BlockSpec(memory_space=pltpu.VMEM)
    hbm = pl.BlockSpec(memory_space=pltpu.HBM)

    def call(kernel, inputs, outputs, in_specs=None, scratch=(), flops=10**6):
        return pl.pallas_call(
            kernel,
            out_shape=outputs,
            in_specs=in_specs or [vmem] * len(inputs),
            out_specs=jax.tree.map(lambda _: vmem, outputs),
            scratch_shapes=list(scratch),
            compiler_params=pltpu.CompilerParams(vmem_limit_bytes=VMEM_LIMIT),
            cost_estimate=pl.CostEstimate(flops=flops, bytes_accessed=10**6, transcendentals=0),
        )(*inputs)

    raw = (
        density,
        diffusion.reshape(1, 3),
        centers.T,
        sharpness.reshape(1, maps),
        affine.transpose(1, 2, 0),
        offsets.T,
    )
    raw = tuple(pltpu.with_memory_space_constraint(array, pltpu.HBM) for array in raw)
    message, line_values, line_drifts, drift_z, prepared = call(
        functools.partial(start_kernel, extent_y, extent_z),
        raw,
        (
            shape(width + size_x, LANES),
            shape(*wide),
            shape(size_y + 2, width, LANES),
            shape(size_x, size_y, LANES),
            shape(PREPARED, LANES),
        ),
        [hbm] * len(raw),
        [
            pltpu.VMEM((size_x, 2 * size_y, LANES), float32),
            pltpu.VMEM((size_x, size_y, LANES), float32),
        ]
        + [pltpu.VMEM(array.shape, float32) for array in raw]
        + [pltpu.VMEM((PREPARED, LANES), float32), pltpu.SemaphoreType.DMA((len(raw),))],
    )
    stride, radix = y_levels[0]
    near, base, from_below, from_above = call(
        functools.partial(near_kernel, sizes, maps, stride, radix),
        [prepared, line_values, line_drifts],
        (shape(radix, 4, width, LANES), shape(*wide), shape(*wide), shape(*wide)),
    )
    far, count = [], extent_y
    for _, radix in y_levels[:-1]:
        count = count // radix
        far.append(shape(count, 4, width, LANES))
    if far:
        far = call(functools.partial(far_kernel, sizes, maps, y_levels[:-1]), [prepared], far)
    coefs = [near] + list(far)
    doublings = size_z.bit_length() - 1
    steps, ends, pushes, packed, weights = call(
        functools.partial(z_coef_kernel, sizes, maps),
        (prepared, drift_z),
        (
            shape(doublings, 3, *narrow),
            shape(2, *narrow),
            shape(size_y, LANES),
            shape(ROWS, size_y * size_x),
            shape(2, *narrow),
        ),
    )
    line_inputs = []
    for number, (stride, radix) in enumerate(y_levels):
        received = exchange(message, "gy", stride, radix)
        line_inputs += [coefs[number]] + received
        if number + 1 < len(y_levels):
            facing = number + 2 == len(y_levels) and y_levels[-1][1] == 2
            message = call(
                functools.partial(merge_kernel, stride, radix, number == 0, facing),
                [coefs[number]] + received + ([packed] if number == 0 else []),
                shape(width if facing else width + size_x, LANES),
            )
    message, sources = call(
        functools.partial(middle_kernel, y_levels),
        [weights, pushes, packed, base, from_below, from_above] + line_inputs,
        (shape(ROWS, size_y * size_x), shape(*narrow)),
        scratch=[pltpu.VMEM((4, 2, width, LANES), float32)],
    )
    doubled = call(double_kernel, [steps, sources], shape(*narrow))
    end_inputs = []
    for number, (stride, radix) in enumerate(z_levels):
        received = exchange(message, "gz", stride, radix)
        end_inputs += received
        if number + 1 < len(z_levels):
            message = call(
                functools.partial(merge_z_kernel, stride, radix),
                received,
                shape(ROWS, size_y * size_x),
            )
    return call(
        functools.partial(end_kernel, z_levels),
        [density, doubled, ends] + end_inputs,
        shape(size_x, size_y, size_z),
        scratch=[pltpu.VMEM((4, ROWS, size_y * size_x), float32)],
    )


def solution(mesh):
    placed = (P(None, "gy", "gz"), P(), P(), P(), P(), P())
    return jax.shard_map(
        body, mesh=mesh, in_specs=placed, out_specs=P(None, "gy", "gz"), check_vma=False
    )
```

```python
import functools

import jax
import jax.numpy as jnp
from jax import lax
from jax.experimental import pallas as pl
from jax.experimental.pallas import tpu as pltpu
from jax.sharding import PartitionSpec as P

HALF_LIMIT = 600.0
LANES = 128
ROWS = 8
ABOVE, BELOW = 127, 31
VMEM_LIMIT = 48 * 1024 * 1024


def iota(shape, axis):
    return lax.broadcasted_iota(jnp.int32, shape, axis)


def coordinate(positions, line_total):
    return (2.0 * positions.astype(jnp.float32) + 1.0) * (1.0 / line_total) - 1.0


def roll(values, shift, axis):
    return pltpu.roll(values, shift % values.shape[axis], axis)


def matmul(left, right):
    low, high = split(left), split(right)
    columns = right.shape[0]
    both = lax.dot_general(
        jnp.concatenate(low, axis=1),
        jnp.concatenate([jnp.concatenate([part, part], axis=1) for part in high], axis=0),
        (((1,), (1,)), ((), ())),
        preferred_element_type=jnp.float32,
    )
    return both[:, :columns] + both[:, columns:]


def split(values):
    upper = values.astype(jnp.bfloat16)
    return upper, (values - upper.astype(jnp.float32)).astype(jnp.bfloat16)


def half_drift(left, right):
    return HALF_LIMIT * jnp.tanh(matmul(left, right))


SHARPNESS, CENTER, SLOPE, OFFSET, DIFFUSION, PREPARED = 0, 1, 4, 7, 8, 16


def component_of(maps):
    return iota((1, LANES), 1) // (2 * maps)


def first_term(maps):
    return (iota((1, LANES), 1) // maps) % 2 == 0


def bump(params, coord, axis):
    center = params[CENTER + axis : CENTER + axis + 1]
    return jnp.exp(-params[SHARPNESS : SHARPNESS + 1] * (coord - center) ** 2)


def slope(params, coord, axis):
    return coord * params[SLOPE + axis : SLOPE + axis + 1]


def x_factors(params, maps, size_x):
    coord = coordinate(iota((size_x, LANES), 0), size_x)
    return bump(params, coord, 0), jnp.where(first_term(maps), slope(params, coord, 0), 0.0)


def y_factors(params, maps, position, total_y):
    coord = coordinate(position, total_y)
    part = slope(params, coord, 1) + params[OFFSET : OFFSET + 1]
    return bump(params, coord, 1), jnp.where(
        first_term(maps), part, params[SLOPE + 2 : SLOPE + 3]
    )


def z_rows(params, maps, position, total_z):
    coord = coordinate(position, total_z)
    return bump(params, coord, 2) * jnp.where(first_term(maps), 1.0, coord)


def inner_z_rows(params, maps, z_start, size_z, total_z):
    return z_rows(params, maps, z_start + iota((size_z, LANES), 0), total_z)


def outer_positions(z_start, size_z):
    return jnp.where(iota((ROWS, LANES), 0) == 0, z_start - 1, z_start + size_z)


def outer_z_rows(params, maps, z_start, size_z, total_z):
    rows = z_rows(params, maps, outer_positions(z_start, size_z), total_z)
    return jnp.where(iota((size_z, LANES), 0) == BELOW, rows[:1], rows[1:2])


def only(rows, maps, component):
    return jnp.where(component_of(maps) == component, rows, 0.0)


def y_rows(params, maps, position, total_y):
    coord = coordinate(position, total_y)
    part = slope(params, coord, 1) + params[OFFSET : OFFSET + 1]
    return bump(params, coord, 1) * jnp.where(first_term(maps), part, 1.0)


def xz_rows(params, maps, size_x, z_start, size_z, total_z):
    x_coord = coordinate(iota((size_x, LANES), 0), size_x)
    z_coord = coordinate(outer_positions(z_start, size_z), total_z)
    x_bump, z_bump = bump(params, x_coord, 0), bump(params, z_coord, 2)
    x_part, z_part = slope(params, x_coord, 0), slope(params, z_coord, 2)
    rows = [
        (x_bump * z_bump[i : i + 1])
        * jnp.where(first_term(maps), 1.0, x_part + z_part[i : i + 1])
        for i in (1, 0)
    ]
    blank = jnp.zeros((BELOW + 1 - size_x, LANES), jnp.float32)
    rest = jnp.zeros((LANES - BELOW - 1 - size_x, LANES), jnp.float32)
    parts = [rows[0], blank, rows[1], rest] if size_x <= BELOW else [rows[0], rows[1], rest]
    return jnp.concatenate(parts, axis=0)


def with_extra(main, row):
    return jnp.concatenate([main, jnp.broadcast_to(row, (ROWS, LANES))], axis=0)


def pack_planes(planes):
    turned = [roll(plane, i + 1, 1) for i, plane in enumerate(planes)]
    while len(turned) > 1:
        turned = [sum(turned[i : i + 2]) for i in range(0, len(turned), 2)]
    return turned[0]


def lines_of(planes, size_x, first_lane):
    group = LANES // size_x
    place = iota((1, LANES), 1) // size_x
    turned = [roll(planes, q * size_x - first_lane, 1) for q in range(group)]
    rows = []
    for first in range(0, planes.shape[0], group):
        row = turned[0][first : first + 1]
        for q in range(1, group):
            row = jnp.where(place == q, turned[q][first + q : first + q + 1], row)
        rows.append(row)
    return jnp.concatenate(rows, axis=1)


def to_lines(rows, size_x):
    group = LANES // size_x
    return jnp.concatenate(
        [
            jnp.transpose(jnp.concatenate(rows[first : first + group], axis=0))
            for first in range(0, len(rows), group)
        ],
        axis=1,
    )


def turn(values, stride):
    stride = stride % values.shape[0]
    if stride % ROWS == 0:
        return jnp.concatenate([values[-stride:], values[:-stride]], axis=0)
    return roll(values, stride, 0)


def merge_coefs(low, high):
    inverse = 1.0 / (1.0 - low[3] * high[0])
    onward, back = low[1] * inverse, high[2] * inverse
    return (
        low[0] + onward * high[0] * low[2],
        onward * high[1],
        back * low[2],
        high[3] + back * low[3] * high[1],
    )


def merge_values(low, high, low_values, high_values):
    inverse = 1.0 / (1.0 - low[3] * high[0])
    return (
        low_values[0] + low[1] * inverse * (high_values[0] + high[0] * low_values[1]),
        high_values[1] + high[2] * inverse * (low_values[1] + low[3] * high_values[0]),
    )


def merge(low, high, low_values, high_values):
    return merge_coefs(low, high), merge_values(low, high, low_values, high_values)


def meet(low, high, below, above):
    (_, _, a_last, c_last), (_, r_last) = low
    (a_first, c_first, _, _), (r_first, _) = high
    inverse = 1.0 / (1.0 - c_last * a_first)
    upper = r_first + c_first * above
    left = (r_last + a_last * below + c_last * upper) * inverse
    return left, upper + a_first * left


def chain(coefs, values, below, above):
    count = len(coefs)
    if count == 4:
        halves = [merge(coefs[j], coefs[j + 1], values[j], values[j + 1]) for j in (0, 2)]
        left, right = meet(halves[0], halves[1], below, above)
        seen = [
            meet((coefs[j], values[j]), (coefs[j + 1], values[j + 1]), low, high)
            for j, low, high in ((0, below, right), (2, left, above))
        ]
        return [below, seen[0][0], left, seen[1][0]], [seen[0][1], right, seen[1][1], above]
    held, slope = below, None
    befores, firsts = [], []
    for j in range(count):
        a_first, c_first, a_last, c_last = coefs[j]
        r_first, r_last = values[j]
        befores.append((held, slope))
        if slope is None:
            first, first_slope = r_first + a_first * held, c_first
            held, slope = r_last + a_last * held, c_last
        else:
            inverse = 1.0 / (1.0 - a_first * slope)
            first = (r_first + a_first * held) * inverse
            first_slope = c_first * inverse
            held, slope = (
                r_last + a_last * (held + slope * first),
                c_last + a_last * slope * first_slope,
            )
        firsts.append((first, first_slope))
    seen_above = [None] * count
    seen_below = [None] * count
    upper = above
    for j in reversed(range(count)):
        seen_above[j] = upper
        upper = firsts[j][0] + firsts[j][1] * upper
        held, slope = befores[j]
        seen_below[j] = held if slope is None else held + slope * upper
    return seen_below, seen_above


def solve_x(up, down, source, pivot):
    size = source.shape[0]
    half = size // 2
    low_g, low_c, high_g, high_c = {}, {}, {}, {}
    g = c = None
    for i in range(half):
        if i == 0:
            weight = 1.0 / pivot
            c = down[1] * weight
            g = source[0] * weight
        else:
            weight = 1.0 / (pivot - up[i - 1] * c)
            g = (source[i] + up[i - 1] * g) * weight
            c = down[i + 1] * weight
        low_g[i], low_c[i] = g, c
    for i in reversed(range(half, size)):
        if i == size - 1:
            weight = 1.0 / pivot
            c = up[i - 1] * weight
            g = source[i] * weight
        else:
            weight = 1.0 / (pivot - down[i + 1] * c)
            g = (source[i] + down[i + 1] * g) * weight
            c = up[i - 1] * weight
        high_g[i], high_c[i] = g, c
    out = [None] * size
    inverse = 1.0 / (1.0 - low_c[half - 1] * high_c[half])
    out[half - 1] = (low_g[half - 1] + low_c[half - 1] * high_g[half]) * inverse
    out[half] = high_g[half] + high_c[half] * out[half - 1]
    for i in reversed(range(half - 1)):
        out[i] = low_g[i] + low_c[i] * out[i + 1]
    for i in range(half + 1, size):
        out[i] = high_g[i] + high_c[i] * out[i - 1]
    return out


def start_kernel(
    extent_y,
    extent_z,
    density_hbm,
    diffusion_hbm,
    centers_hbm,
    sharpness_hbm,
    affine_hbm,
    offsets_hbm,
    message,
    line_values,
    line_drifts,
    drift_z_out,
    prepared,
    solved,
    drift_y_held,
    density,
    diffusion,
    centers,
    sharpness,
    affine,
    offsets,
    staged,
    semaphores,
):
    copies = [
        pltpu.make_async_copy(source, target, semaphores.at[number])
        for number, (source, target) in enumerate(
            [
                (diffusion_hbm, diffusion),
                (centers_hbm, centers),
                (sharpness_hbm, sharpness),
                (affine_hbm, affine),
                (offsets_hbm, offsets),
                (density_hbm, density),
            ]
        )
    ]
    for copy in copies:
        copy.start()
    size_x, size_y, size_z = density.shape
    total_y, total_z = size_y * extent_y, size_z * extent_z
    y_start = lax.axis_index("gy") * size_y
    z_start = lax.axis_index("gz") * size_z
    maps = centers.shape[1]
    for copy in copies[:-1]:
        copy.wait()

    staged[...] = jnp.zeros(staged.shape, jnp.float32)
    staged[0:1, :maps] = sharpness[...]
    staged[1:4, :maps] = centers[...]
    for c in range(3):
        staged[4 + 3 * c : 7 + 3 * c, :maps] = affine[c]
    staged[13:16, :maps] = offsets[...]
    rows = staged[...]
    width = maps
    while width < LANES:
        rows = rows + roll(rows, width, 1)
        width = 2 * width
    component = component_of(maps)
    rows = jnp.where(component < 3, rows, 0.0)

    def by_component(first, step):
        return jnp.where(
            component == 0,
            rows[first : first + 1],
            jnp.where(
                component == 1,
                rows[first + step : first + step + 1],
                rows[first + 2 * step : first + 2 * step + 1],
            ),
        )

    weights = [jnp.broadcast_to(diffusion[:, c : c + 1], (1, LANES)) for c in range(3)]
    params = jnp.concatenate(
        [rows[0:4]]
        + [by_component(4 + j, 3) for j in range(3)]
        + [by_component(13, 1)]
        + weights
        + [jnp.zeros((PREPARED - DIFFUSION - 3, LANES), jnp.float32)],
        axis=0,
    )
    prepared[...] = params
    d0, d1, d2 = weights

    x_bump, x_part = x_factors(params, maps, size_x)
    y_row = iota((size_y, LANES), 0)
    y_bump, y_part = y_factors(params, maps, y_start + y_row, total_y)
    out_bump, out_part = y_factors(
        params, maps, jnp.where(y_row == 0, y_start + size_y, y_start - 1), total_y
    )
    inner = inner_z_rows(params, maps, z_start, size_z, total_z)
    outer = outer_z_rows(params, maps, z_start, size_z, total_z)
    inner = [only(inner, maps, c) for c in range(3)]
    outer = only(outer, maps, 0)

    def rows_by_x(bumps, part):
        return jnp.concatenate(
            [(x_bump[i : i + 1] * bumps) * (x_part[i : i + 1] + part) for i in range(size_x)],
            axis=0,
        )

    right = jnp.concatenate([inner[0], outer, inner[1], inner[2]], axis=0)
    drifts = half_drift(rows_by_x(y_bump, y_part), right)
    out_drift = half_drift(rows_by_x(out_bump, out_part), inner[0])

    def block(number):
        columns = drifts[:, number * LANES : (number + 1) * LANES]
        return columns.reshape(size_x, size_y, LANES)

    drift_x, plane_drift, drift_y, drift_z = block(0), block(1), block(2), block(3)
    out_drift = out_drift.reshape(size_x, size_y, LANES)
    drift_y_held[...] = drift_y
    drift_z_out[...] = drift_z
    copies[-1].wait()
    rho = density[...]
    zero = jnp.zeros((1, size_y, LANES), jnp.float32)
    up, down = (d0 + drift_x) * rho, (d0 - drift_x) * rho
    total = (
        jnp.concatenate([zero, up[:-1]], axis=0)
        + jnp.concatenate([down[1:], zero], axis=0)
        - (2.0 * (d0 + d1 + d2)) * rho
    )
    sublane = iota((size_x, size_y, LANES), 1)
    lane = iota((size_x, size_y, LANES), 2)
    up, down = roll((d1 + drift_y) * rho, 1, 1), roll((d1 - drift_y) * rho, -1, 1)
    at_low, at_high = sublane == 0, sublane == size_y - 1
    row_source = jnp.where(at_low, up, jnp.where(at_high, down, 0.0))
    total = total + jnp.where(at_low, 0.0, up) + jnp.where(at_high, 0.0, down)
    up, down = (d2 + drift_z) * rho, (d2 - drift_z) * rho
    plane_source = jnp.where(
        lane == ABOVE, up, jnp.where(lane == BELOW, roll(down, BELOW, 2), 0.0)
    )
    up, down = roll(up, 1, 2), roll(down, -1, 2)
    at_low, at_high = lane == 0, lane == size_z - 1
    total = total + jnp.where(at_low, 0.0, up) + jnp.where(at_high, 0.0, down)

    source = jnp.concatenate([total, row_source, plane_source], axis=1)
    drift = jnp.concatenate([drift_x, out_drift, plane_drift], axis=1)
    answers = solve_x(d0 + drift, d0 - drift, source, 1.0 + 2.0 * d0)
    for i in range(size_x):
        solved[i] = answers[i][: 2 * size_y]
    planes = pack_planes([answer[2 * size_y :] for answer in answers])

    out_rows = [
        (x_bump * out_bump[j : j + 1]) * (x_part + out_part[j : j + 1])
        for j in (size_y - 1, 0)
    ]
    ends = half_drift(jnp.concatenate(out_rows, axis=0), inner[1])
    position = y_start - 1 + iota((2 * ROWS, LANES), 0)
    extra = half_drift(
        y_rows(params, maps, position, total_y),
        only(xz_rows(params, maps, size_x, z_start, size_z, total_z), maps, 1),
    )
    line_drift = (
        [ends[:size_x]]
        + [drift_y_held[:, j, :] for j in range(size_y)]
        + [ends[size_x:]]
    )
    line_drift = [with_extra(line_drift[j], extra[j : j + 1]) for j in range(size_y + 2)]
    values = [with_extra(solved[:, j, :], planes[j : j + 1]) for j in range(size_y)]
    for j in range(size_y):
        line_values[j] = values[j]
    for j in range(size_y + 2):
        line_drifts[j] = line_drift[j]
    pivot = 1.0 + 2.0 * d1
    g = c = None
    gs, cs = [], []
    for j in range(size_y):
        lower, upper = line_factors(line_drift, j, size_y, d1, y_start, total_y)
        weight = 1.0 / (pivot if j == 0 else pivot - lower * c)
        g = (values[j] if j == 0 else values[j] + lower * g) * weight
        c = upper * weight
        gs.append(g)
        cs.append(c)
    r_first = r_last = g
    for j in reversed(range(size_y - 1)):
        r_first = gs[j] + cs[j] * r_first
    pushed_up = solved[:, size_y, :] / (d1 + line_drift[size_y][:size_x])
    pushed_down = solved[:, 2 * size_y - 1, :] / (d1 - line_drift[1][:size_x])
    blank = jnp.zeros((1, LANES), jnp.float32)
    message[...] = join_message(
        r_first + with_extra(pushed_down, blank), r_last + with_extra(pushed_up, blank)
    )


def line_factors(line_drift, j, size_y, d1, y_start, total_y):
    lower, upper = d1 + line_drift[j], d1 - line_drift[j + 2]
    if j == 0:
        lower = jnp.where(y_start == 0, 0.0, lower)
    if j == size_y - 1:
        upper = jnp.where(y_start + size_y == total_y, 0.0, upper)
    return lower, upper


def line_coefs(params, maps, sizes, start, count, store):
    extent_y, extent_z, size_x, size_y, size_z = sizes
    total_y, total_z = size_y * extent_y, size_z * extent_z
    z_start = lax.axis_index("gz") * size_z
    d1 = params[DIFFUSION + 1 : DIFFUSION + 2]
    x_bump, x_part = x_factors(params, maps, size_x)
    inner = only(inner_z_rows(params, maps, z_start, size_z, total_z), maps, 1)
    planes = only(xz_rows(params, maps, size_x, z_start, size_z, total_z), maps, 1)
    whole = count == extent_y
    offsets = list(range(size_y)) if whole else list(range(-1, size_y + 1))
    left, left_extra = [], []
    for j in offsets:
        for b in range(count):
            position = iota((1, LANES), 0) + ((start + b) * size_y + j)
            bumps, part = y_factors(params, maps, position, total_y)
            left.append((x_bump * bumps) * (x_part + part))
        block = iota((max(count, ROWS), LANES), 0)
        left_extra.append(
            y_rows(params, maps, (start + block) * size_y + j, total_y)
        )
    depth = left_extra[0].shape[0]
    main = half_drift(jnp.concatenate(left, axis=0), inner)
    main = main.reshape(len(offsets), count, size_x, LANES)
    main = [main[j] for j in range(len(offsets))]
    extra = half_drift(jnp.concatenate(left_extra, axis=0), planes)
    extra = [extra[j * depth : (j + 1) * depth] for j in range(len(offsets))]
    if whole:
        main = (
            [jnp.concatenate([main[-1][:1], main[-1][:-1]], axis=0)]
            + main
            + [jnp.concatenate([main[0][1:], main[0][-1:]], axis=0)]
        )
        extra = [roll(extra[-1], 1, 0)] + extra + [roll(extra[0], -1, 0)]
    numbers = start + iota((depth, LANES), 0)
    pivot = 1.0 + 2.0 * d1
    at_start, at_end = numbers == 0, numbers == extent_y - 1

    def scan(drifts, starts, ends):
        a_first = c_first = a_last = c_last = None
        for j in range(size_y):
            lower, upper = d1 + drifts[j], d1 - drifts[j + 2]
            if j == 0:
                lower = starts(lower)
            if j == size_y - 1:
                upper = ends(upper)
            if j == 0:
                weight = 1.0 / pivot
                a_first, c_first = lower * weight, upper * weight
                a_last, c_last = a_first, c_first
            else:
                weight = 1.0 / (pivot - lower * c_last)
                step, c_last = lower * weight, upper * weight
                a_last = step * a_last
                a_first = a_first + c_first * a_last
                c_first = c_first * c_last
        return a_first, c_first, a_last, c_last

    def masked(values, number):
        return jnp.concatenate(
            [
                jnp.where(start + b == number, 0.0, values[b])[None]
                for b in range(count)
            ],
            axis=0,
        )

    main = scan(main, lambda v: masked(v, 0), lambda v: masked(v, extent_y - 1))
    extra = scan(
        extra,
        lambda v: jnp.where(at_start, 0.0, v),
        lambda v: jnp.where(at_end, 0.0, v),
    )
    for b in range(count):
        for q in range(4):
            store(b, q, with_extra(main[q][b], extra[q][b : b + 1]))


def near_kernel(
    sizes,
    maps,
    stride,
    radix,
    prepared,
    line_values,
    line_drifts,
    coefs,
    base,
    from_below,
    from_above,
):
    digit = lax.rem(lax.div(lax.axis_index("gy"), stride), radix)
    start = lax.div(lax.axis_index("gy"), stride) - digit
    params = prepared[...]

    def store(b, q, value):
        coefs[b, q] = value

    line_coefs(params, maps, sizes, start, radix, store)
    extent_y, _, _, size_y, _ = sizes
    d1 = params[DIFFUSION + 1 : DIFFUSION + 2]
    pivot = 1.0 + 2.0 * d1
    y_start = lax.axis_index("gy") * size_y
    g = a = c = None
    gs, as_, cs = [], [], []
    for j in range(size_y):
        lower, upper = line_factors(line_drifts, j, size_y, d1, y_start, size_y * extent_y)
        if j == 0:
            weight = 1.0 / pivot
            g, a = line_values[j] * weight, lower * weight
        else:
            weight = 1.0 / (pivot - lower * c)
            g, a = (line_values[j] + lower * g) * weight, lower * a * weight
        c = upper * weight
        gs.append(g)
        as_.append(a)
        cs.append(c)
    base[size_y - 1], from_below[size_y - 1], from_above[size_y - 1] = g, a, c
    for j in reversed(range(size_y - 1)):
        g, a, c = gs[j] + cs[j] * g, as_[j] + cs[j] * a, cs[j] * c
        base[j], from_below[j], from_above[j] = g, a, c


def far_kernel(sizes, maps, levels, prepared, *outputs):
    held = {}

    def store(b, q, value):
        held[b, q] = value

    extent_y = sizes[0]
    line_coefs(prepared[...], maps, sizes, 0, extent_y, store)
    groups = [tuple(held[b, q] for q in range(4)) for b in range(extent_y)]
    for (_, radix), coefs in zip(levels, outputs):
        groups = [
            functools.reduce(merge_coefs, groups[g : g + radix])
            for g in range(0, len(groups), radix)
        ]
        for number, group in enumerate(groups):
            for q in range(4):
                coefs[number, q] = group[q]


def double_coefs(below, above, scale, steps=None):
    size_z = below.shape[0]
    row = iota(below.shape, 0)
    stride, level = 1, 0
    while stride < size_z:
        low, high = row < stride, row >= size_z - stride
        low_a = jnp.where(low, 1.0, turn(below, stride))
        low_c = jnp.where(low, 0.0, turn(above, stride))
        high_a = jnp.where(high, 0.0, turn(below, -stride))
        high_c = jnp.where(high, 1.0, turn(above, -stride))
        inverse = 1.0 / (1.0 - below * low_c - above * high_a)
        below, above = below * inverse, above * inverse
        if steps is not None:
            factor = scale if level == 0 else 1.0
            steps[level, 0] = inverse * factor
            steps[level, 1] = jnp.where(low, 0.0, below * factor)
            steps[level, 2] = jnp.where(high, 0.0, above * factor)
        below, above = below * low_a, above * high_c
        stride, level = stride * 2, level + 1
    return below, above


def z_coef_kernel(sizes, maps, prepared, drift_z, steps, ends, pushes, packed, weights):
    extent_y, extent_z, size_x, size_y, size_z = sizes
    total_y, total_z = size_y * extent_y, size_z * extent_z
    y_start = lax.axis_index("gy") * size_y
    z_start = lax.axis_index("gz") * size_z
    params = prepared[...]
    d2 = params[DIFFUSION + 2 : DIFFUSION + 3]
    lane = iota((size_y, LANES), 1)
    divisors = []
    for i in range(size_x):
        plane = drift_z[i]
        factor = jnp.where(lane == ABOVE, d2 + plane, d2 - roll(plane, BELOW, 1))
        divisors.append(
            jnp.where((lane == ABOVE) | (lane == BELOW), 1.0 / factor, 0.0)
        )
    pushes[...] = pack_planes(divisors)
    x_bump, x_part = x_factors(params, maps, size_x)
    outer = only(outer_z_rows(params, maps, z_start, size_z, total_z), maps, 2)
    rows = []
    for j in range(size_y):
        position = iota((1, LANES), 0) + (y_start + j)
        bumps, part = y_factors(params, maps, position, total_y)
        rows.append((x_bump * bumps) * (x_part + part))
    outer = half_drift(jnp.concatenate(rows, axis=0), outer)
    outer = to_lines([outer[j * size_x : (j + 1) * size_x] for j in range(size_y)], size_x)
    inner = to_lines([drift_z[:, j, :] for j in range(size_y)], size_x)
    d2 = jnp.concatenate([d2] * (inner.shape[1] // LANES), axis=1)
    scale = 1.0 / (1.0 + 2.0 * d2)
    row = iota(inner.shape, 0)
    low, high = row == 0, row == size_z - 1
    before = jnp.where(low, outer[BELOW : BELOW + 1], turn(inner, 1))
    after = jnp.where(high, outer[ABOVE : ABOVE + 1], turn(inner, -1))
    below = jnp.where(low & (z_start == 0), 0.0, (d2 + before) * scale)
    above = jnp.where(high & (z_start + size_z == total_z), 0.0, (d2 - after) * scale)
    turned_below = jnp.where(low, 1.0, turn(above, 1))
    turned_above = jnp.where(high, 1.0, turn(below, -1))
    below, above = double_coefs(below, above, scale, steps)
    turned_below, turned_above = double_coefs(turned_below, turned_above, scale)
    weights[0] = turned_below * scale
    weights[1] = turned_above * scale
    ends[0] = below
    ends[1] = above
    packed[...] = jnp.concatenate(
        [
            jnp.zeros((2, inner.shape[1]), jnp.float32),
            below[:1],
            below[size_z - 1 :],
            above[:1],
            above[size_z - 1 :],
            jnp.zeros((2, inner.shape[1]), jnp.float32),
        ],
        axis=0,
    )


def gather_members(refs, own, count):
    held = [ref[...] for ref in refs]
    return [
        functools.reduce(
            lambda acc, s: jnp.where((own ^ s) == j, held[s], acc), range(1, count), held[0]
        )
        for j in range(count)
    ]


def join_message(first, last):
    size_x = first.shape[0] - ROWS
    extra = jnp.where(iota((ROWS, LANES), 0) == 0, first[size_x:], last[size_x:])
    return jnp.concatenate([first[:size_x], last[:size_x], extra], axis=0)


def split_message(message):
    size_x = (message.shape[0] - ROWS) // 2
    return (
        with_extra(message[:size_x], message[2 * size_x : 2 * size_x + 1]),
        with_extra(message[size_x : 2 * size_x], message[2 * size_x + 1 : 2 * size_x + 2]),
    )


def merge_kernel(stride, radix, local, facing, coefs, *refs):
    received, message = refs[:radix], refs[-1]
    digit = lax.rem(lax.div(lax.axis_index("gy"), stride), radix)
    first = 0 if local else lax.div(lax.axis_index("gy"), stride) - digit
    values = [split_message(m) for m in gather_members(received, digit, radix)]
    group = [tuple(coefs[first + j, q] for q in range(4)) for j in range(radix)]
    merged, total = group[0], values[0]
    for j in range(1, radix):
        total = merge_values(merged, group[j], total, values[j])
        merged = merge_coefs(merged, group[j])
    if facing:
        is_low = lax.axis_index("gy") < stride * radix
        message[...] = jnp.where(is_low, total[1], total[0])
    else:
        message[...] = join_message(*total)


def middle_kernel(levels, *refs):
    refs = list(refs)
    weights, pushes, packed, base, from_below, from_above = refs[:6]
    refs = refs[6:]
    inputs = []
    for stride, radix in levels:
        inputs.append((refs[0], refs[1 : 1 + radix]))
        refs = refs[1 + radix :]
    message, sources, seen = refs
    size_y, width = base.shape[:2]
    size_x = width - ROWS
    below = above = jnp.zeros((width, LANES), jnp.float32)
    for number in reversed(range(len(levels))):
        (stride, radix), (coefs, received) = levels[number], inputs[number]
        digit = lax.rem(lax.div(lax.axis_index("gy"), stride), radix)
        first = 0 if number == 0 else lax.div(lax.axis_index("gy"), stride) - digit
        members = gather_members(received, digit, radix)
        group = [tuple(coefs[first + j, q] for q in range(4)) for j in range(radix)]
        if members[0].shape[0] == width:
            c_last, a_first = group[0][3], group[1][0]
            inverse = 1.0 / (1.0 - c_last * a_first)
            below = jnp.where(digit == 0, 0.0, (members[0] + c_last * members[1]) * inverse)
            above = jnp.where(digit == 0, (members[1] + a_first * members[0]) * inverse, 0.0)
            continue
        values = [split_message(m) for m in members]
        lows, highs = chain(group, values, below, above)
        for j in range(radix):
            seen[j, 0] = lows[j]
            seen[j, 1] = highs[j]
        below, above = seen[digit, 0], seen[digit, 1]
    inner, outer = [], []
    for j in range(size_y):
        value = base[j] + from_below[j] * below + from_above[j] * above
        inner.append(value[:size_x])
        outer.append(value[size_x : size_x + 1])
    pushed = jnp.concatenate(outer, axis=0) * pushes[...]
    values = to_lines(inner, size_x)
    sources[...] = values
    message[...] = packed[...]
    message[0:1] = total_of(weights[0] * values) + lines_of(pushed, size_x, BELOW + 1)
    message[1:2] = total_of(weights[1] * values) + lines_of(pushed, size_x, 0)


def total_of(values):
    return jnp.sum(values, axis=0, keepdims=True)


def from_lines(values, size_x):
    rows = []
    for first in range(0, values.shape[1], LANES):
        tile = jnp.transpose(values[:, first : first + LANES])
        rows += [tile[q : q + size_x] for q in range(0, LANES, size_x)]
    return rows


def double_kernel(steps, sources, density, base):
    values = sources[...]
    stride, level = 1, 0
    while stride < values.shape[0]:
        values = (
            steps[level, 0] * values
            + steps[level, 1] * turn(values, stride)
            + steps[level, 2] * turn(values, -stride)
        )
        stride, level = stride * 2, level + 1
    for j, rows in enumerate(from_lines(values, density.shape[0])):
        base[j] = density[:, j, :] + rows


def merge_z(low, high):
    inverse = 1.0 / (1.0 - low[5] * high[2])
    onward, back = low[4] * inverse, high[3] * inverse
    return (
        low[0] + onward * (high[0] + high[2] * low[1]),
        high[1] + back * (low[1] + low[5] * high[0]),
        low[2] + onward * high[2] * low[3],
        back * low[3],
        onward * high[4],
        high[5] + back * low[5] * high[4],
    )


def unpack_ends(message):
    return tuple(message[s : s + 1] for s in range(6))


def merge_z_kernel(stride, radix, *refs):
    received, message = refs[:radix], refs[radix]
    digit = lax.rem(lax.div(lax.axis_index("gz"), stride), radix)
    members = [unpack_ends(m) for m in gather_members(received, digit, radix)]
    total = functools.reduce(merge_z, members)
    message[...] = jnp.concatenate(total + total[:2], axis=0)


def end_kernel(levels, base, ends, *refs):
    refs = list(refs)
    inputs = []
    for stride, radix in levels:
        inputs.append(refs[:radix])
        refs = refs[radix:]
    out, seen = refs
    below = above = jnp.zeros((1, ends.shape[2]), jnp.float32)
    for (stride, radix), received in zip(reversed(levels), reversed(inputs)):
        digit = lax.rem(lax.div(lax.axis_index("gz"), stride), radix)
        members = [unpack_ends(m) for m in gather_members(received, digit, radix)]
        lows, highs = chain(
            [(m[2], m[4], m[3], m[5]) for m in members],
            [(m[0], m[1]) for m in members],
            below,
            above,
        )
        for j in range(radix):
            seen[j, 0:1] = lows[j]
            seen[j, 1:2] = highs[j]
        below, above = seen[digit, 0:1], seen[digit, 1:2]
    values = ends[0] * below + ends[1] * above
    for j, rows in enumerate(from_lines(values, base.shape[1])):
        out[:, j, :] = base[j] + rows


def radices(extent):
    rounds, stride = [], 1
    while stride < extent:
        radix = 4 if (extent // stride) % 4 == 0 else 2
        rounds.append((stride, radix))
        stride *= radix
    return rounds


def exchange(message, axis, stride, radix):
    devices = range(lax.axis_size(axis))
    return [message] + [
        lax.ppermute(message, axis, [(i, i ^ (s * stride)) for i in devices])
        for s in range(1, radix)
    ]


def body(density, diffusion, centers, sharpness, affine, offsets):
    size_x, size_y, size_z = density.shape
    extent_y, extent_z = lax.axis_size("gy"), lax.axis_size("gz")
    sizes = (extent_y, extent_z, size_x, size_y, size_z)
    maps = centers.shape[0]
    width = size_x + ROWS
    wide = (size_y, width, LANES)
    narrow = (size_z, size_y * size_x)
    float32 = jnp.float32
    y_levels, z_levels = radices(extent_y), radices(extent_z)

    def shape(*dims):
        return jax.ShapeDtypeStruct(dims, float32)

    vmem = pl.BlockSpec(memory_space=pltpu.VMEM)
    hbm = pl.BlockSpec(memory_space=pltpu.HBM)

    def call(kernel, inputs, outputs, in_specs=None, scratch=(), flops=10**6):
        return pl.pallas_call(
            kernel,
            out_shape=outputs,
            in_specs=in_specs or [vmem] * len(inputs),
            out_specs=jax.tree.map(lambda _: vmem, outputs),
            scratch_shapes=list(scratch),
            compiler_params=pltpu.CompilerParams(vmem_limit_bytes=VMEM_LIMIT),
            cost_estimate=pl.CostEstimate(flops=flops, bytes_accessed=10**6, transcendentals=0),
        )(*inputs)

    raw = (
        density,
        diffusion.reshape(1, 3),
        centers.T,
        sharpness.reshape(1, maps),
        affine.transpose(1, 2, 0),
        offsets.T,
    )
    raw = tuple(pltpu.with_memory_space_constraint(array, pltpu.HBM) for array in raw)
    message, line_values, line_drifts, drift_z, prepared = call(
        functools.partial(start_kernel, extent_y, extent_z),
        raw,
        (
            shape(width + size_x, LANES),
            shape(*wide),
            shape(size_y + 2, width, LANES),
            shape(size_x, size_y, LANES),
            shape(PREPARED, LANES),
        ),
        [hbm] * len(raw),
        [
            pltpu.VMEM((size_x, 2 * size_y, LANES), float32),
            pltpu.VMEM((size_x, size_y, LANES), float32),
        ]
        + [pltpu.VMEM(array.shape, float32) for array in raw]
        + [pltpu.VMEM((PREPARED, LANES), float32), pltpu.SemaphoreType.DMA((len(raw),))],
    )
    stride, radix = y_levels[0]
    near, base, from_below, from_above = call(
        functools.partial(near_kernel, sizes, maps, stride, radix),
        [prepared, line_values, line_drifts],
        (shape(radix, 4, width, LANES), shape(*wide), shape(*wide), shape(*wide)),
    )
    far, count = [], extent_y
    for _, radix in y_levels[:-1]:
        count = count // radix
        far.append(shape(count, 4, width, LANES))
    if far:
        far = call(functools.partial(far_kernel, sizes, maps, y_levels[:-1]), [prepared], far)
    coefs = [near] + list(far)
    doublings = size_z.bit_length() - 1
    steps, ends, pushes, packed, weights = call(
        functools.partial(z_coef_kernel, sizes, maps),
        (prepared, drift_z),
        (
            shape(doublings, 3, *narrow),
            shape(2, *narrow),
            shape(size_y, LANES),
            shape(ROWS, size_y * size_x),
            shape(2, *narrow),
        ),
    )
    line_inputs = []
    for number, (stride, radix) in enumerate(y_levels):
        received = exchange(message, "gy", stride, radix)
        line_inputs += [coefs[number]] + received
        if number + 1 < len(y_levels):
            facing = number + 2 == len(y_levels) and y_levels[-1][1] == 2
            message = call(
                functools.partial(merge_kernel, stride, radix, number == 0, facing),
                [coefs[number]] + received + ([packed] if number == 0 else []),
                shape(width if facing else width + size_x, LANES),
            )
    message, sources = call(
        functools.partial(middle_kernel, y_levels),
        [weights, pushes, packed, base, from_below, from_above] + line_inputs,
        (shape(ROWS, size_y * size_x), shape(*narrow)),
        scratch=[pltpu.VMEM((4, 2, width, LANES), float32)],
    )
    base = call(double_kernel, [steps, sources, density], shape(size_y, size_x, size_z))
    end_inputs = []
    for number, (stride, radix) in enumerate(z_levels):
        received = exchange(message, "gz", stride, radix)
        end_inputs += received
        if number + 1 < len(z_levels):
            message = call(
                functools.partial(merge_z_kernel, stride, radix),
                received,
                shape(ROWS, size_y * size_x),
            )
    return call(
        functools.partial(end_kernel, z_levels),
        [base, ends] + end_inputs,
        shape(size_x, size_y, size_z),
        scratch=[pltpu.VMEM((4, ROWS, size_y * size_x), float32)],
    )


def solution(mesh):
    placed = (P(None, "gy", "gz"), P(), P(), P(), P(), P())
    return jax.shard_map(
        body, mesh=mesh, in_specs=placed, out_specs=P(None, "gy", "gz"), check_vma=False
    )
```

```python
import functools

import jax
import jax.numpy as jnp
from jax import lax
from jax.experimental import pallas as pl
from jax.experimental.pallas import tpu as pltpu
from jax.sharding import PartitionSpec as P

HALF_LIMIT = 600.0
LANES = 128
ROWS = 8
ABOVE, BELOW = 127, 31
VMEM_LIMIT = 48 * 1024 * 1024


def iota(shape, axis):
    return lax.broadcasted_iota(jnp.int32, shape, axis)


def coordinate(positions, line_total):
    return (2.0 * positions.astype(jnp.float32) + 1.0) * (1.0 / line_total) - 1.0


def roll(values, shift, axis):
    return pltpu.roll(values, shift % values.shape[axis], axis)


def matmul(left, right):
    low, high = split(left), split(right)
    columns = right.shape[0]
    both = lax.dot_general(
        jnp.concatenate(low, axis=1),
        jnp.concatenate([jnp.concatenate([part, part], axis=1) for part in high], axis=0),
        (((1,), (1,)), ((), ())),
        preferred_element_type=jnp.float32,
    )
    return both[:, :columns] + both[:, columns:]


def split(values):
    upper = values.astype(jnp.bfloat16)
    return upper, (values - upper.astype(jnp.float32)).astype(jnp.bfloat16)


def half_drift(left, right):
    return HALF_LIMIT * jnp.tanh(matmul(left, right))


SHARPNESS, CENTER, SLOPE, OFFSET, DIFFUSION, PREPARED = 0, 1, 4, 7, 8, 16


def component_of(maps):
    return iota((1, LANES), 1) // (2 * maps)


def first_term(maps):
    return (iota((1, LANES), 1) // maps) % 2 == 0


def bump(params, coord, axis):
    center = params[CENTER + axis : CENTER + axis + 1]
    return jnp.exp(-params[SHARPNESS : SHARPNESS + 1] * (coord - center) ** 2)


def slope(params, coord, axis):
    return coord * params[SLOPE + axis : SLOPE + axis + 1]


def x_factors(params, maps, size_x):
    coord = coordinate(iota((size_x, LANES), 0), size_x)
    return bump(params, coord, 0), jnp.where(first_term(maps), slope(params, coord, 0), 0.0)


def y_factors(params, maps, position, total_y):
    coord = coordinate(position, total_y)
    part = slope(params, coord, 1) + params[OFFSET : OFFSET + 1]
    return bump(params, coord, 1), jnp.where(
        first_term(maps), part, params[SLOPE + 2 : SLOPE + 3]
    )


def z_rows(params, maps, position, total_z):
    coord = coordinate(position, total_z)
    return bump(params, coord, 2) * jnp.where(first_term(maps), 1.0, coord)


def inner_z_rows(params, maps, z_start, size_z, total_z):
    return z_rows(params, maps, z_start + iota((size_z, LANES), 0), total_z)


def outer_positions(z_start, size_z):
    return jnp.where(iota((ROWS, LANES), 0) == 0, z_start - 1, z_start + size_z)


def outer_z_rows(params, maps, z_start, size_z, total_z):
    rows = z_rows(params, maps, outer_positions(z_start, size_z), total_z)
    return jnp.where(iota((size_z, LANES), 0) == BELOW, rows[:1], rows[1:2])


def only(rows, maps, component):
    return jnp.where(component_of(maps) == component, rows, 0.0)


def y_rows(params, maps, position, total_y):
    coord = coordinate(position, total_y)
    part = slope(params, coord, 1) + params[OFFSET : OFFSET + 1]
    return bump(params, coord, 1) * jnp.where(first_term(maps), part, 1.0)


def xz_rows(params, maps, size_x, z_start, size_z, total_z):
    x_coord = coordinate(iota((size_x, LANES), 0), size_x)
    z_coord = coordinate(outer_positions(z_start, size_z), total_z)
    x_bump, z_bump = bump(params, x_coord, 0), bump(params, z_coord, 2)
    x_part, z_part = slope(params, x_coord, 0), slope(params, z_coord, 2)
    rows = [
        (x_bump * z_bump[i : i + 1])
        * jnp.where(first_term(maps), 1.0, x_part + z_part[i : i + 1])
        for i in (1, 0)
    ]
    blank = jnp.zeros((BELOW + 1 - size_x, LANES), jnp.float32)
    rest = jnp.zeros((LANES - BELOW - 1 - size_x, LANES), jnp.float32)
    parts = [rows[0], blank, rows[1], rest] if size_x <= BELOW else [rows[0], rows[1], rest]
    return jnp.concatenate(parts, axis=0)


def with_extra(main, row):
    return jnp.concatenate([main, jnp.broadcast_to(row, (ROWS, LANES))], axis=0)


def pack_planes(planes):
    turned = [roll(plane, i + 1, 1) for i, plane in enumerate(planes)]
    while len(turned) > 1:
        turned = [sum(turned[i : i + 2]) for i in range(0, len(turned), 2)]
    return turned[0]


def lines_of(planes, size_x, first_lane):
    group = LANES // size_x
    place = iota((1, LANES), 1) // size_x
    turned = [roll(planes, q * size_x - first_lane, 1) for q in range(group)]
    rows = []
    for first in range(0, planes.shape[0], group):
        row = turned[0][first : first + 1]
        for q in range(1, group):
            row = jnp.where(place == q, turned[q][first + q : first + q + 1], row)
        rows.append(row)
    return jnp.concatenate(rows, axis=1)


def to_lines(rows, size_x):
    group = LANES // size_x
    return jnp.concatenate(
        [
            jnp.transpose(jnp.concatenate(rows[first : first + group], axis=0))
            for first in range(0, len(rows), group)
        ],
        axis=1,
    )


def turn(values, stride):
    stride = stride % values.shape[0]
    if stride % ROWS == 0:
        return jnp.concatenate([values[-stride:], values[:-stride]], axis=0)
    return roll(values, stride, 0)


def merge_coefs(low, high):
    inverse = 1.0 / (1.0 - low[3] * high[0])
    onward, back = low[1] * inverse, high[2] * inverse
    return (
        low[0] + onward * high[0] * low[2],
        onward * high[1],
        back * low[2],
        high[3] + back * low[3] * high[1],
    )


def merge_values(low, high, low_values, high_values):
    inverse = 1.0 / (1.0 - low[3] * high[0])
    return (
        low_values[0] + low[1] * inverse * (high_values[0] + high[0] * low_values[1]),
        high_values[1] + high[2] * inverse * (low_values[1] + low[3] * high_values[0]),
    )


def merge(low, high, low_values, high_values):
    return merge_coefs(low, high), merge_values(low, high, low_values, high_values)


def meet(low, high, below, above):
    (_, _, a_last, c_last), (_, r_last) = low
    (a_first, c_first, _, _), (r_first, _) = high
    inverse = 1.0 / (1.0 - c_last * a_first)
    upper = r_first + c_first * above
    left = (r_last + a_last * below + c_last * upper) * inverse
    return left, upper + a_first * left


def chain(coefs, values, below, above):
    count = len(coefs)
    if count == 4:
        halves = [merge(coefs[j], coefs[j + 1], values[j], values[j + 1]) for j in (0, 2)]
        left, right = meet(halves[0], halves[1], below, above)
        seen = [
            meet((coefs[j], values[j]), (coefs[j + 1], values[j + 1]), low, high)
            for j, low, high in ((0, below, right), (2, left, above))
        ]
        return [below, seen[0][0], left, seen[1][0]], [seen[0][1], right, seen[1][1], above]
    held, slope = below, None
    befores, firsts = [], []
    for j in range(count):
        a_first, c_first, a_last, c_last = coefs[j]
        r_first, r_last = values[j]
        befores.append((held, slope))
        if slope is None:
            first, first_slope = r_first + a_first * held, c_first
            held, slope = r_last + a_last * held, c_last
        else:
            inverse = 1.0 / (1.0 - a_first * slope)
            first = (r_first + a_first * held) * inverse
            first_slope = c_first * inverse
            held, slope = (
                r_last + a_last * (held + slope * first),
                c_last + a_last * slope * first_slope,
            )
        firsts.append((first, first_slope))
    seen_above = [None] * count
    seen_below = [None] * count
    upper = above
    for j in reversed(range(count)):
        seen_above[j] = upper
        upper = firsts[j][0] + firsts[j][1] * upper
        held, slope = befores[j]
        seen_below[j] = held if slope is None else held + slope * upper
    return seen_below, seen_above


def solve_x(up, down, source, pivot):
    size = len(source)
    half = size // 2
    low_g, low_c, high_g, high_c = {}, {}, {}, {}
    g = c = None
    for i in range(half):
        if i == 0:
            weight = 1.0 / pivot
            c = down[1] * weight
            g = source[0] * weight
        else:
            weight = 1.0 / (pivot - up[i - 1] * c)
            g = (source[i] + up[i - 1] * g) * weight
            c = down[i + 1] * weight
        low_g[i], low_c[i] = g, c
    for i in reversed(range(half, size)):
        if i == size - 1:
            weight = 1.0 / pivot
            c = up[i - 1] * weight
            g = source[i] * weight
        else:
            weight = 1.0 / (pivot - down[i + 1] * c)
            g = (source[i] + down[i + 1] * g) * weight
            c = up[i - 1] * weight
        high_g[i], high_c[i] = g, c
    out = [None] * size
    inverse = 1.0 / (1.0 - low_c[half - 1] * high_c[half])
    out[half - 1] = (low_g[half - 1] + low_c[half - 1] * high_g[half]) * inverse
    out[half] = high_g[half] + high_c[half] * out[half - 1]
    for i in reversed(range(half - 1)):
        out[i] = low_g[i] + low_c[i] * out[i + 1]
    for i in range(half + 1, size):
        out[i] = high_g[i] + high_c[i] * out[i - 1]
    return out


def start_kernel(
    extent_y,
    extent_z,
    density_hbm,
    diffusion_hbm,
    centers_hbm,
    sharpness_hbm,
    affine_hbm,
    offsets_hbm,
    message,
    line_values,
    line_drifts,
    drift_z_out,
    prepared,
    solved,
    drift_y_held,
    density,
    diffusion,
    centers,
    sharpness,
    affine,
    offsets,
    staged,
    semaphores,
):
    copies = [
        pltpu.make_async_copy(source, target, semaphores.at[number])
        for number, (source, target) in enumerate(
            [
                (diffusion_hbm, diffusion),
                (centers_hbm, centers),
                (sharpness_hbm, sharpness),
                (affine_hbm, affine),
                (offsets_hbm, offsets),
                (density_hbm, density),
            ]
        )
    ]
    for copy in copies:
        copy.start()
    size_x, size_y, size_z = density.shape
    total_y, total_z = size_y * extent_y, size_z * extent_z
    y_start = lax.axis_index("gy") * size_y
    z_start = lax.axis_index("gz") * size_z
    maps = centers.shape[1]
    for copy in copies[:-1]:
        copy.wait()

    staged[...] = jnp.zeros(staged.shape, jnp.float32)
    staged[0:1, :maps] = sharpness[...]
    staged[1:4, :maps] = centers[...]
    for c in range(3):
        staged[4 + 3 * c : 7 + 3 * c, :maps] = affine[c]
    staged[13:16, :maps] = offsets[...]
    rows = staged[...]
    width = maps
    while width < LANES:
        rows = rows + roll(rows, width, 1)
        width = 2 * width
    component = component_of(maps)
    rows = jnp.where(component < 3, rows, 0.0)

    def by_component(first, step):
        return jnp.where(
            component == 0,
            rows[first : first + 1],
            jnp.where(
                component == 1,
                rows[first + step : first + step + 1],
                rows[first + 2 * step : first + 2 * step + 1],
            ),
        )

    weights = [jnp.broadcast_to(diffusion[:, c : c + 1], (1, LANES)) for c in range(3)]
    params = jnp.concatenate(
        [rows[0:4]]
        + [by_component(4 + j, 3) for j in range(3)]
        + [by_component(13, 1)]
        + weights
        + [jnp.zeros((PREPARED - DIFFUSION - 3, LANES), jnp.float32)],
        axis=0,
    )
    prepared[...] = params
    d0, d1, d2 = weights

    x_bump, x_part = x_factors(params, maps, size_x)
    y_row = iota((size_y, LANES), 0)
    y_bump, y_part = y_factors(params, maps, y_start + y_row, total_y)
    out_bump, out_part = y_factors(
        params, maps, jnp.where(y_row == 0, y_start + size_y, y_start - 1), total_y
    )
    inner = inner_z_rows(params, maps, z_start, size_z, total_z)
    outer = outer_z_rows(params, maps, z_start, size_z, total_z)
    inner = [only(inner, maps, c) for c in range(3)]
    outer = only(outer, maps, 0)

    def rows_by_x(bumps, part):
        return jnp.concatenate(
            [(x_bump[i : i + 1] * bumps) * (x_part[i : i + 1] + part) for i in range(size_x)],
            axis=0,
        )

    right = jnp.concatenate([inner[0], outer, inner[1], inner[2]], axis=0)
    drifts = half_drift(rows_by_x(y_bump, y_part), right)
    out_drift = half_drift(rows_by_x(out_bump, out_part), inner[0])

    def block(number):
        columns = drifts[:, number * LANES : (number + 1) * LANES]
        return columns.reshape(size_x, size_y, LANES)

    drift_x, plane_drift, drift_y, drift_z = block(0), block(1), block(2), block(3)
    out_drift = out_drift.reshape(size_x, size_y, LANES)
    drift_y_held[...] = drift_y
    drift_z_out[...] = drift_z
    copies[-1].wait()
    rho = density[...]
    zero = jnp.zeros((1, size_y, LANES), jnp.float32)
    up, down = (d0 + drift_x) * rho, (d0 - drift_x) * rho
    total = (
        jnp.concatenate([zero, up[:-1]], axis=0)
        + jnp.concatenate([down[1:], zero], axis=0)
        - (2.0 * (d0 + d1 + d2)) * rho
    )
    sublane = iota((size_x, size_y, LANES), 1)
    lane = iota((size_x, size_y, LANES), 2)
    up, down = roll((d1 + drift_y) * rho, 1, 1), roll((d1 - drift_y) * rho, -1, 1)
    at_low, at_high = sublane == 0, sublane == size_y - 1
    row_source = jnp.where(at_low, up, jnp.where(at_high, down, 0.0))
    total = total + jnp.where(at_low, 0.0, up) + jnp.where(at_high, 0.0, down)
    up, down = (d2 + drift_z) * rho, (d2 - drift_z) * rho
    plane_source = jnp.where(
        lane == ABOVE, up, jnp.where(lane == BELOW, roll(down, BELOW, 2), 0.0)
    )
    up, down = roll(up, 1, 2), roll(down, -1, 2)
    at_low, at_high = lane == 0, lane == size_z - 1
    total = total + jnp.where(at_low, 0.0, up) + jnp.where(at_high, 0.0, down)

    source = jnp.concatenate([total, row_source, plane_source], axis=1)
    drift = jnp.concatenate([drift_x, out_drift, plane_drift], axis=1)
    answers = solve_x(d0 + drift, d0 - drift, source, 1.0 + 2.0 * d0)
    for i in range(size_x):
        solved[i] = answers[i][: 2 * size_y]
    planes = pack_planes([answer[2 * size_y :] for answer in answers])

    out_rows = [
        (x_bump * out_bump[j : j + 1]) * (x_part + out_part[j : j + 1])
        for j in (size_y - 1, 0)
    ]
    ends = half_drift(jnp.concatenate(out_rows, axis=0), inner[1])
    position = y_start - 1 + iota((2 * ROWS, LANES), 0)
    extra = half_drift(
        y_rows(params, maps, position, total_y),
        only(xz_rows(params, maps, size_x, z_start, size_z, total_z), maps, 1),
    )
    line_drift = (
        [ends[:size_x]]
        + [drift_y_held[:, j, :] for j in range(size_y)]
        + [ends[size_x:]]
    )
    line_drift = [with_extra(line_drift[j], extra[j : j + 1]) for j in range(size_y + 2)]
    values = [with_extra(solved[:, j, :], planes[j : j + 1]) for j in range(size_y)]
    for j in range(size_y):
        line_values[j] = values[j]
    for j in range(size_y + 2):
        line_drifts[j] = line_drift[j]
    inside = line_drift[1:-1]
    lines = solve_x([d1 + h for h in inside], [d1 - h for h in inside], values, 1.0 + 2.0 * d1)
    r_first, r_last = lines[0], lines[-1]
    pushed_up = solved[:, size_y, :] / (d1 + line_drift[size_y][:size_x])
    pushed_down = solved[:, 2 * size_y - 1, :] / (d1 - line_drift[1][:size_x])
    blank = jnp.zeros((1, LANES), jnp.float32)
    message[...] = join_message(
        r_first + with_extra(pushed_down, blank), r_last + with_extra(pushed_up, blank)
    )


def line_factors(line_drift, j, size_y, d1, y_start, total_y):
    lower, upper = d1 + line_drift[j], d1 - line_drift[j + 2]
    if j == 0:
        lower = jnp.where(y_start == 0, 0.0, lower)
    if j == size_y - 1:
        upper = jnp.where(y_start + size_y == total_y, 0.0, upper)
    return lower, upper


def line_coefs(params, maps, sizes, start, count, store):
    extent_y, extent_z, size_x, size_y, size_z = sizes
    total_y, total_z = size_y * extent_y, size_z * extent_z
    z_start = lax.axis_index("gz") * size_z
    d1 = params[DIFFUSION + 1 : DIFFUSION + 2]
    x_bump, x_part = x_factors(params, maps, size_x)
    inner = only(inner_z_rows(params, maps, z_start, size_z, total_z), maps, 1)
    planes = only(xz_rows(params, maps, size_x, z_start, size_z, total_z), maps, 1)
    whole = count == extent_y
    offsets = list(range(size_y)) if whole else list(range(-1, size_y + 1))
    left, left_extra = [], []
    for j in offsets:
        for b in range(count):
            position = iota((1, LANES), 0) + ((start + b) * size_y + j)
            bumps, part = y_factors(params, maps, position, total_y)
            left.append((x_bump * bumps) * (x_part + part))
        block = iota((max(count, ROWS), LANES), 0)
        left_extra.append(
            y_rows(params, maps, (start + block) * size_y + j, total_y)
        )
    depth = left_extra[0].shape[0]
    main = half_drift(jnp.concatenate(left, axis=0), inner)
    main = main.reshape(len(offsets), count, size_x, LANES)
    main = [main[j] for j in range(len(offsets))]
    extra = half_drift(jnp.concatenate(left_extra, axis=0), planes)
    extra = [extra[j * depth : (j + 1) * depth] for j in range(len(offsets))]
    if whole:
        main = (
            [jnp.concatenate([main[-1][:1], main[-1][:-1]], axis=0)]
            + main
            + [jnp.concatenate([main[0][1:], main[0][-1:]], axis=0)]
        )
        extra = [roll(extra[-1], 1, 0)] + extra + [roll(extra[0], -1, 0)]
    numbers = start + iota((depth, LANES), 0)
    pivot = 1.0 + 2.0 * d1
    at_start, at_end = numbers == 0, numbers == extent_y - 1

    def scan(drifts, starts, ends):
        a_first = c_first = a_last = c_last = None
        for j in range(size_y):
            lower, upper = d1 + drifts[j], d1 - drifts[j + 2]
            if j == 0:
                lower = starts(lower)
            if j == size_y - 1:
                upper = ends(upper)
            if j == 0:
                weight = 1.0 / pivot
                a_first, c_first = lower * weight, upper * weight
                a_last, c_last = a_first, c_first
            else:
                weight = 1.0 / (pivot - lower * c_last)
                step, c_last = lower * weight, upper * weight
                a_last = step * a_last
                a_first = a_first + c_first * a_last
                c_first = c_first * c_last
        return a_first, c_first, a_last, c_last

    def masked(values, number):
        return jnp.concatenate(
            [
                jnp.where(start + b == number, 0.0, values[b])[None]
                for b in range(count)
            ],
            axis=0,
        )

    main = scan(main, lambda v: masked(v, 0), lambda v: masked(v, extent_y - 1))
    extra = scan(
        extra,
        lambda v: jnp.where(at_start, 0.0, v),
        lambda v: jnp.where(at_end, 0.0, v),
    )
    for b in range(count):
        for q in range(4):
            store(b, q, with_extra(main[q][b], extra[q][b : b + 1]))


def near_kernel(
    sizes,
    maps,
    stride,
    radix,
    prepared,
    line_values,
    line_drifts,
    coefs,
    base,
    from_below,
    from_above,
):
    digit = lax.rem(lax.div(lax.axis_index("gy"), stride), radix)
    start = lax.div(lax.axis_index("gy"), stride) - digit
    params = prepared[...]

    def store(b, q, value):
        coefs[b, q] = value

    line_coefs(params, maps, sizes, start, radix, store)
    extent_y, _, _, size_y, _ = sizes
    d1 = params[DIFFUSION + 1 : DIFFUSION + 2]
    pivot = 1.0 + 2.0 * d1
    y_start = lax.axis_index("gy") * size_y
    g = a = c = None
    gs, as_, cs = [], [], []
    for j in range(size_y):
        lower, upper = line_factors(line_drifts, j, size_y, d1, y_start, size_y * extent_y)
        if j == 0:
            weight = 1.0 / pivot
            g, a = line_values[j] * weight, lower * weight
        else:
            weight = 1.0 / (pivot - lower * c)
            g, a = (line_values[j] + lower * g) * weight, lower * a * weight
        c = upper * weight
        gs.append(g)
        as_.append(a)
        cs.append(c)
    base[size_y - 1], from_below[size_y - 1], from_above[size_y - 1] = g, a, c
    for j in reversed(range(size_y - 1)):
        g, a, c = gs[j] + cs[j] * g, as_[j] + cs[j] * a, cs[j] * c
        base[j], from_below[j], from_above[j] = g, a, c


def far_kernel(sizes, maps, levels, prepared, *outputs):
    held = {}

    def store(b, q, value):
        held[b, q] = value

    extent_y = sizes[0]
    line_coefs(prepared[...], maps, sizes, 0, extent_y, store)
    groups = [tuple(held[b, q] for q in range(4)) for b in range(extent_y)]
    for (_, radix), coefs in zip(levels, outputs):
        groups = [
            functools.reduce(merge_coefs, groups[g : g + radix])
            for g in range(0, len(groups), radix)
        ]
        for number, group in enumerate(groups):
            for q in range(4):
                coefs[number, q] = group[q]


def double_coefs(below, above, scale, steps=None):
    size_z = below.shape[0]
    row = iota(below.shape, 0)
    stride, level = 1, 0
    while stride < size_z:
        low, high = row < stride, row >= size_z - stride
        low_a = jnp.where(low, 1.0, turn(below, stride))
        low_c = jnp.where(low, 0.0, turn(above, stride))
        high_a = jnp.where(high, 0.0, turn(below, -stride))
        high_c = jnp.where(high, 1.0, turn(above, -stride))
        inverse = 1.0 / (1.0 - below * low_c - above * high_a)
        below, above = below * inverse, above * inverse
        if steps is not None:
            factor = scale if level == 0 else 1.0
            steps[level, 0] = inverse * factor
            steps[level, 1] = jnp.where(low, 0.0, below * factor)
            steps[level, 2] = jnp.where(high, 0.0, above * factor)
        below, above = below * low_a, above * high_c
        stride, level = stride * 2, level + 1
    return below, above


def z_coef_kernel(sizes, maps, prepared, drift_z, steps, ends, pushes, packed, weights):
    extent_y, extent_z, size_x, size_y, size_z = sizes
    total_y, total_z = size_y * extent_y, size_z * extent_z
    y_start = lax.axis_index("gy") * size_y
    z_start = lax.axis_index("gz") * size_z
    params = prepared[...]
    d2 = params[DIFFUSION + 2 : DIFFUSION + 3]
    lane = iota((size_y, LANES), 1)
    divisors = []
    for i in range(size_x):
        plane = drift_z[i]
        factor = jnp.where(lane == ABOVE, d2 + plane, d2 - roll(plane, BELOW, 1))
        divisors.append(
            jnp.where((lane == ABOVE) | (lane == BELOW), 1.0 / factor, 0.0)
        )
    pushes[...] = pack_planes(divisors)
    x_bump, x_part = x_factors(params, maps, size_x)
    outer = only(outer_z_rows(params, maps, z_start, size_z, total_z), maps, 2)
    rows = []
    for j in range(size_y):
        position = iota((1, LANES), 0) + (y_start + j)
        bumps, part = y_factors(params, maps, position, total_y)
        rows.append((x_bump * bumps) * (x_part + part))
    outer = half_drift(jnp.concatenate(rows, axis=0), outer)
    outer = to_lines([outer[j * size_x : (j + 1) * size_x] for j in range(size_y)], size_x)
    inner = to_lines([drift_z[:, j, :] for j in range(size_y)], size_x)
    d2 = jnp.concatenate([d2] * (inner.shape[1] // LANES), axis=1)
    scale = 1.0 / (1.0 + 2.0 * d2)
    row = iota(inner.shape, 0)
    low, high = row == 0, row == size_z - 1
    before = jnp.where(low, outer[BELOW : BELOW + 1], turn(inner, 1))
    after = jnp.where(high, outer[ABOVE : ABOVE + 1], turn(inner, -1))
    below = jnp.where(low & (z_start == 0), 0.0, (d2 + before) * scale)
    above = jnp.where(high & (z_start + size_z == total_z), 0.0, (d2 - after) * scale)
    turned_below = jnp.where(low, 1.0, turn(above, 1))
    turned_above = jnp.where(high, 1.0, turn(below, -1))
    below, above = double_coefs(below, above, scale, steps)
    turned_below, turned_above = double_coefs(turned_below, turned_above, scale)
    weights[0] = turned_below * scale
    weights[1] = turned_above * scale
    ends[0] = below
    ends[1] = above
    packed[...] = jnp.concatenate(
        [
            jnp.zeros((2, inner.shape[1]), jnp.float32),
            below[:1],
            below[size_z - 1 :],
            above[:1],
            above[size_z - 1 :],
            jnp.zeros((2, inner.shape[1]), jnp.float32),
        ],
        axis=0,
    )


def gather_members(refs, own, count):
    held = [ref[...] for ref in refs]
    return [
        functools.reduce(
            lambda acc, s: jnp.where((own ^ s) == j, held[s], acc), range(1, count), held[0]
        )
        for j in range(count)
    ]


def join_message(first, last):
    size_x = first.shape[0] - ROWS
    extra = jnp.where(iota((ROWS, LANES), 0) == 0, first[size_x:], last[size_x:])
    return jnp.concatenate([first[:size_x], last[:size_x], extra], axis=0)


def split_message(message):
    size_x = (message.shape[0] - ROWS) // 2
    return (
        with_extra(message[:size_x], message[2 * size_x : 2 * size_x + 1]),
        with_extra(message[size_x : 2 * size_x], message[2 * size_x + 1 : 2 * size_x + 2]),
    )


def merge_kernel(stride, radix, local, facing, coefs, *refs):
    received, message = refs[:radix], refs[-1]
    digit = lax.rem(lax.div(lax.axis_index("gy"), stride), radix)
    first = 0 if local else lax.div(lax.axis_index("gy"), stride) - digit
    values = [split_message(m) for m in gather_members(received, digit, radix)]
    group = [tuple(coefs[first + j, q] for q in range(4)) for j in range(radix)]
    merged, total = group[0], values[0]
    for j in range(1, radix):
        total = merge_values(merged, group[j], total, values[j])
        merged = merge_coefs(merged, group[j])
    if facing:
        is_low = lax.axis_index("gy") < stride * radix
        message[...] = jnp.where(is_low, total[1], total[0])
    else:
        message[...] = join_message(*total)


def middle_kernel(levels, *refs):
    refs = list(refs)
    weights, pushes, packed, base, from_below, from_above = refs[:6]
    refs = refs[6:]
    inputs = []
    for stride, radix in levels:
        inputs.append((refs[0], refs[1 : 1 + radix]))
        refs = refs[1 + radix :]
    message, sources, seen = refs
    size_y, width = base.shape[:2]
    size_x = width - ROWS
    below = above = jnp.zeros((width, LANES), jnp.float32)
    for number in reversed(range(len(levels))):
        (stride, radix), (coefs, received) = levels[number], inputs[number]
        digit = lax.rem(lax.div(lax.axis_index("gy"), stride), radix)
        first = 0 if number == 0 else lax.div(lax.axis_index("gy"), stride) - digit
        members = gather_members(received, digit, radix)
        group = [tuple(coefs[first + j, q] for q in range(4)) for j in range(radix)]
        if members[0].shape[0] == width:
            c_last, a_first = group[0][3], group[1][0]
            inverse = 1.0 / (1.0 - c_last * a_first)
            below = jnp.where(digit == 0, 0.0, (members[0] + c_last * members[1]) * inverse)
            above = jnp.where(digit == 0, (members[1] + a_first * members[0]) * inverse, 0.0)
            continue
        values = [split_message(m) for m in members]
        lows, highs = chain(group, values, below, above)
        for j in range(radix):
            seen[j, 0] = lows[j]
            seen[j, 1] = highs[j]
        below, above = seen[digit, 0], seen[digit, 1]
    inner, outer = [], []
    for j in range(size_y):
        value = base[j] + from_below[j] * below + from_above[j] * above
        inner.append(value[:size_x])
        outer.append(value[size_x : size_x + 1])
    pushed = jnp.concatenate(outer, axis=0) * pushes[...]
    values = to_lines(inner, size_x)
    sources[...] = values
    message[...] = packed[...]
    message[0:1] = total_of(weights[0] * values) + lines_of(pushed, size_x, BELOW + 1)
    message[1:2] = total_of(weights[1] * values) + lines_of(pushed, size_x, 0)


def total_of(values):
    return jnp.sum(values, axis=0, keepdims=True)


def from_lines(values, size_x):
    rows = []
    for first in range(0, values.shape[1], LANES):
        tile = jnp.transpose(values[:, first : first + LANES])
        rows += [tile[q : q + size_x] for q in range(0, LANES, size_x)]
    return rows


def double_kernel(steps, sources, density, base):
    values = sources[...]
    stride, level = 1, 0
    while stride < values.shape[0]:
        values = (
            steps[level, 0] * values
            + steps[level, 1] * turn(values, stride)
            + steps[level, 2] * turn(values, -stride)
        )
        stride, level = stride * 2, level + 1
    for j, rows in enumerate(from_lines(values, density.shape[0])):
        base[j] = density[:, j, :] + rows


def merge_z(low, high):
    inverse = 1.0 / (1.0 - low[5] * high[2])
    onward, back = low[4] * inverse, high[3] * inverse
    return (
        low[0] + onward * (high[0] + high[2] * low[1]),
        high[1] + back * (low[1] + low[5] * high[0]),
        low[2] + onward * high[2] * low[3],
        back * low[3],
        onward * high[4],
        high[5] + back * low[5] * high[4],
    )


def unpack_ends(message):
    return tuple(message[s : s + 1] for s in range(6))


def merge_z_kernel(stride, radix, *refs):
    received, message = refs[:radix], refs[radix]
    digit = lax.rem(lax.div(lax.axis_index("gz"), stride), radix)
    members = [unpack_ends(m) for m in gather_members(received, digit, radix)]
    total = functools.reduce(merge_z, members)
    message[...] = jnp.concatenate(total + total[:2], axis=0)


def end_kernel(levels, base, ends, *refs):
    refs = list(refs)
    inputs = []
    for stride, radix in levels:
        inputs.append(refs[:radix])
        refs = refs[radix:]
    out, seen = refs
    below = above = jnp.zeros((1, ends.shape[2]), jnp.float32)
    for (stride, radix), received in zip(reversed(levels), reversed(inputs)):
        digit = lax.rem(lax.div(lax.axis_index("gz"), stride), radix)
        members = [unpack_ends(m) for m in gather_members(received, digit, radix)]
        lows, highs = chain(
            [(m[2], m[4], m[3], m[5]) for m in members],
            [(m[0], m[1]) for m in members],
            below,
            above,
        )
        for j in range(radix):
            seen[j, 0:1] = lows[j]
            seen[j, 1:2] = highs[j]
        below, above = seen[digit, 0:1], seen[digit, 1:2]
    values = ends[0] * below + ends[1] * above
    for j, rows in enumerate(from_lines(values, base.shape[1])):
        out[:, j, :] = base[j] + rows


def radices(extent):
    rounds, stride = [], 1
    while stride < extent:
        radix = 4 if (extent // stride) % 4 == 0 else 2
        rounds.append((stride, radix))
        stride *= radix
    return rounds


def exchange(message, axis, stride, radix):
    devices = range(lax.axis_size(axis))
    return [message] + [
        lax.ppermute(message, axis, [(i, i ^ (s * stride)) for i in devices])
        for s in range(1, radix)
    ]


def body(density, diffusion, centers, sharpness, affine, offsets):
    size_x, size_y, size_z = density.shape
    extent_y, extent_z = lax.axis_size("gy"), lax.axis_size("gz")
    sizes = (extent_y, extent_z, size_x, size_y, size_z)
    maps = centers.shape[0]
    width = size_x + ROWS
    wide = (size_y, width, LANES)
    narrow = (size_z, size_y * size_x)
    float32 = jnp.float32
    y_levels, z_levels = radices(extent_y), radices(extent_z)

    def shape(*dims):
        return jax.ShapeDtypeStruct(dims, float32)

    vmem = pl.BlockSpec(memory_space=pltpu.VMEM)
    hbm = pl.BlockSpec(memory_space=pltpu.HBM)

    def call(kernel, inputs, outputs, in_specs=None, scratch=(), flops=10**6):
        return pl.pallas_call(
            kernel,
            out_shape=outputs,
            in_specs=in_specs or [vmem] * len(inputs),
            out_specs=jax.tree.map(lambda _: vmem, outputs),
            scratch_shapes=list(scratch),
            compiler_params=pltpu.CompilerParams(vmem_limit_bytes=VMEM_LIMIT),
            cost_estimate=pl.CostEstimate(flops=flops, bytes_accessed=10**6, transcendentals=0),
        )(*inputs)

    raw = (
        density,
        diffusion.reshape(1, 3),
        centers.T,
        sharpness.reshape(1, maps),
        affine.transpose(1, 2, 0),
        offsets.T,
    )
    raw = tuple(pltpu.with_memory_space_constraint(array, pltpu.HBM) for array in raw)
    message, line_values, line_drifts, drift_z, prepared = call(
        functools.partial(start_kernel, extent_y, extent_z),
        raw,
        (
            shape(width + size_x, LANES),
            shape(*wide),
            shape(size_y + 2, width, LANES),
            shape(size_x, size_y, LANES),
            shape(PREPARED, LANES),
        ),
        [hbm] * len(raw),
        [
            pltpu.VMEM((size_x, 2 * size_y, LANES), float32),
            pltpu.VMEM((size_x, size_y, LANES), float32),
        ]
        + [pltpu.VMEM(array.shape, float32) for array in raw]
        + [pltpu.VMEM((PREPARED, LANES), float32), pltpu.SemaphoreType.DMA((len(raw),))],
    )
    stride, radix = y_levels[0]
    near, base, from_below, from_above = call(
        functools.partial(near_kernel, sizes, maps, stride, radix),
        [prepared, line_values, line_drifts],
        (shape(radix, 4, width, LANES), shape(*wide), shape(*wide), shape(*wide)),
    )
    far, count = [], extent_y
    for _, radix in y_levels[:-1]:
        count = count // radix
        far.append(shape(count, 4, width, LANES))
    if far:
        far = call(functools.partial(far_kernel, sizes, maps, y_levels[:-1]), [prepared], far)
    coefs = [near] + list(far)
    doublings = size_z.bit_length() - 1
    steps, ends, pushes, packed, weights = call(
        functools.partial(z_coef_kernel, sizes, maps),
        (prepared, drift_z),
        (
            shape(doublings, 3, *narrow),
            shape(2, *narrow),
            shape(size_y, LANES),
            shape(ROWS, size_y * size_x),
            shape(2, *narrow),
        ),
    )
    line_inputs = []
    for number, (stride, radix) in enumerate(y_levels):
        received = exchange(message, "gy", stride, radix)
        line_inputs += [coefs[number]] + received
        if number + 1 < len(y_levels):
            facing = number + 2 == len(y_levels) and y_levels[-1][1] == 2
            message = call(
                functools.partial(merge_kernel, stride, radix, number == 0, facing),
                [coefs[number]] + received + ([packed] if number == 0 else []),
                shape(width if facing else width + size_x, LANES),
            )
    message, sources = call(
        functools.partial(middle_kernel, y_levels),
        [weights, pushes, packed, base, from_below, from_above] + line_inputs,
        (shape(ROWS, size_y * size_x), shape(*narrow)),
        scratch=[pltpu.VMEM((4, 2, width, LANES), float32)],
    )
    base = call(double_kernel, [steps, sources, density], shape(size_y, size_x, size_z))
    end_inputs = []
    for number, (stride, radix) in enumerate(z_levels):
        received = exchange(message, "gz", stride, radix)
        end_inputs += received
        if number + 1 < len(z_levels):
            message = call(
                functools.partial(merge_z_kernel, stride, radix),
                received,
                shape(ROWS, size_y * size_x),
            )
    return call(
        functools.partial(end_kernel, z_levels),
        [base, ends] + end_inputs,
        shape(size_x, size_y, size_z),
        scratch=[pltpu.VMEM((4, ROWS, size_y * size_x), float32)],
    )


def solution(mesh):
    placed = (P(None, "gy", "gz"), P(), P(), P(), P(), P())
    return jax.shard_map(
        body, mesh=mesh, in_specs=placed, out_specs=P(None, "gy", "gz"), check_vma=False
    )
```

```python
import functools

import jax
import jax.numpy as jnp
from jax import lax
from jax.experimental import pallas as pl
from jax.experimental.pallas import tpu as pltpu
from jax.sharding import PartitionSpec as P

HALF_LIMIT = 600.0
LANES = 128
ROWS = 8
ABOVE, BELOW = 127, 31
VMEM_LIMIT = 48 * 1024 * 1024


def iota(shape, axis):
    return lax.broadcasted_iota(jnp.int32, shape, axis)


def coordinate(positions, line_total):
    return (2.0 * positions.astype(jnp.float32) + 1.0) * (1.0 / line_total) - 1.0


def roll(values, shift, axis):
    return pltpu.roll(values, shift % values.shape[axis], axis)


def matmul(left, right):
    low, high = split(left), split(right)
    columns = right.shape[0]
    both = lax.dot_general(
        jnp.concatenate(low, axis=1),
        jnp.concatenate([jnp.concatenate([part, part], axis=1) for part in high], axis=0),
        (((1,), (1,)), ((), ())),
        preferred_element_type=jnp.float32,
    )
    return both[:, :columns] + both[:, columns:]


def split(values):
    upper = values.astype(jnp.bfloat16)
    return upper, (values - upper.astype(jnp.float32)).astype(jnp.bfloat16)


def half_drift(left, right):
    return HALF_LIMIT * jnp.tanh(matmul(left, right))


SHARPNESS, CENTER, SLOPE, OFFSET, DIFFUSION, PREPARED = 0, 1, 4, 7, 8, 16


def component_of(maps):
    return iota((1, LANES), 1) // (2 * maps)


def first_term(maps):
    return (iota((1, LANES), 1) // maps) % 2 == 0


def bump(params, coord, axis):
    center = params[CENTER + axis : CENTER + axis + 1]
    return jnp.exp(-params[SHARPNESS : SHARPNESS + 1] * (coord - center) ** 2)


def slope(params, coord, axis):
    return coord * params[SLOPE + axis : SLOPE + axis + 1]


def x_factors(params, maps, size_x):
    coord = coordinate(iota((size_x, LANES), 0), size_x)
    return bump(params, coord, 0), jnp.where(first_term(maps), slope(params, coord, 0), 0.0)


def y_factors(params, maps, position, total_y):
    coord = coordinate(position, total_y)
    part = slope(params, coord, 1) + params[OFFSET : OFFSET + 1]
    return bump(params, coord, 1), jnp.where(
        first_term(maps), part, params[SLOPE + 2 : SLOPE + 3]
    )


def z_rows(params, maps, position, total_z):
    coord = coordinate(position, total_z)
    return bump(params, coord, 2) * jnp.where(first_term(maps), 1.0, coord)


def inner_z_rows(params, maps, z_start, size_z, total_z):
    return z_rows(params, maps, z_start + iota((size_z, LANES), 0), total_z)


def outer_positions(z_start, size_z):
    return jnp.where(iota((ROWS, LANES), 0) == 0, z_start - 1, z_start + size_z)


def outer_z_rows(params, maps, z_start, size_z, total_z):
    rows = z_rows(params, maps, outer_positions(z_start, size_z), total_z)
    return jnp.where(iota((size_z, LANES), 0) == BELOW, rows[:1], rows[1:2])


def only(rows, maps, component):
    return jnp.where(component_of(maps) == component, rows, 0.0)


def y_rows(params, maps, position, total_y):
    coord = coordinate(position, total_y)
    part = slope(params, coord, 1) + params[OFFSET : OFFSET + 1]
    return bump(params, coord, 1) * jnp.where(first_term(maps), part, 1.0)


def xz_rows(params, maps, size_x, z_start, size_z, total_z):
    x_coord = coordinate(iota((size_x, LANES), 0), size_x)
    z_coord = coordinate(outer_positions(z_start, size_z), total_z)
    x_bump, z_bump = bump(params, x_coord, 0), bump(params, z_coord, 2)
    x_part, z_part = slope(params, x_coord, 0), slope(params, z_coord, 2)
    rows = [
        (x_bump * z_bump[i : i + 1])
        * jnp.where(first_term(maps), 1.0, x_part + z_part[i : i + 1])
        for i in (1, 0)
    ]
    blank = jnp.zeros((BELOW + 1 - size_x, LANES), jnp.float32)
    rest = jnp.zeros((LANES - BELOW - 1 - size_x, LANES), jnp.float32)
    parts = [rows[0], blank, rows[1], rest] if size_x <= BELOW else [rows[0], rows[1], rest]
    return jnp.concatenate(parts, axis=0)


def with_extra(main, row):
    return jnp.concatenate([main, jnp.broadcast_to(row, (ROWS, LANES))], axis=0)


def pack_planes(planes):
    turned = [roll(plane, i + 1, 1) for i, plane in enumerate(planes)]
    while len(turned) > 1:
        turned = [sum(turned[i : i + 2]) for i in range(0, len(turned), 2)]
    return turned[0]


def lines_of(planes, size_x, first_lane):
    group = LANES // size_x
    place = iota((1, LANES), 1) // size_x
    turned = [roll(planes, q * size_x - first_lane, 1) for q in range(group)]
    rows = []
    for first in range(0, planes.shape[0], group):
        row = turned[0][first : first + 1]
        for q in range(1, group):
            row = jnp.where(place == q, turned[q][first + q : first + q + 1], row)
        rows.append(row)
    return jnp.concatenate(rows, axis=1)


def to_lines(rows, size_x):
    group = LANES // size_x
    return jnp.concatenate(
        [
            jnp.transpose(jnp.concatenate(rows[first : first + group], axis=0))
            for first in range(0, len(rows), group)
        ],
        axis=1,
    )


def turn(values, stride):
    stride = stride % values.shape[0]
    if stride % ROWS == 0:
        return jnp.concatenate([values[-stride:], values[:-stride]], axis=0)
    return roll(values, stride, 0)


def merge_coefs(low, high):
    inverse = 1.0 / (1.0 - low[3] * high[0])
    onward, back = low[1] * inverse, high[2] * inverse
    return (
        low[0] + onward * high[0] * low[2],
        onward * high[1],
        back * low[2],
        high[3] + back * low[3] * high[1],
    )


def merge_values(low, high, low_values, high_values):
    inverse = 1.0 / (1.0 - low[3] * high[0])
    return (
        low_values[0] + low[1] * inverse * (high_values[0] + high[0] * low_values[1]),
        high_values[1] + high[2] * inverse * (low_values[1] + low[3] * high_values[0]),
    )


def merge(low, high, low_values, high_values):
    return merge_coefs(low, high), merge_values(low, high, low_values, high_values)


def meet(low, high, below, above):
    (_, _, a_last, c_last), (_, r_last) = low
    (a_first, c_first, _, _), (r_first, _) = high
    inverse = 1.0 / (1.0 - c_last * a_first)
    upper = r_first + c_first * above
    left = (r_last + a_last * below + c_last * upper) * inverse
    return left, upper + a_first * left


def chain(coefs, values, below, above):
    count = len(coefs)
    if count == 4:
        halves = [merge(coefs[j], coefs[j + 1], values[j], values[j + 1]) for j in (0, 2)]
        left, right = meet(halves[0], halves[1], below, above)
        seen = [
            meet((coefs[j], values[j]), (coefs[j + 1], values[j + 1]), low, high)
            for j, low, high in ((0, below, right), (2, left, above))
        ]
        return [below, seen[0][0], left, seen[1][0]], [seen[0][1], right, seen[1][1], above]
    held, slope = below, None
    befores, firsts = [], []
    for j in range(count):
        a_first, c_first, a_last, c_last = coefs[j]
        r_first, r_last = values[j]
        befores.append((held, slope))
        if slope is None:
            first, first_slope = r_first + a_first * held, c_first
            held, slope = r_last + a_last * held, c_last
        else:
            inverse = 1.0 / (1.0 - a_first * slope)
            first = (r_first + a_first * held) * inverse
            first_slope = c_first * inverse
            held, slope = (
                r_last + a_last * (held + slope * first),
                c_last + a_last * slope * first_slope,
            )
        firsts.append((first, first_slope))
    seen_above = [None] * count
    seen_below = [None] * count
    upper = above
    for j in reversed(range(count)):
        seen_above[j] = upper
        upper = firsts[j][0] + firsts[j][1] * upper
        held, slope = befores[j]
        seen_below[j] = held if slope is None else held + slope * upper
    return seen_below, seen_above


def solve_x(up, down, source, pivot):
    size = source.shape[0]
    half = size // 2
    low_g, low_c, high_g, high_c = {}, {}, {}, {}
    g = c = None
    for i in range(half):
        if i == 0:
            weight = 1.0 / pivot
            c = down[1] * weight
            g = source[0] * weight
        else:
            weight = 1.0 / (pivot - up[i - 1] * c)
            g = (source[i] + up[i - 1] * g) * weight
            c = down[i + 1] * weight
        low_g[i], low_c[i] = g, c
    for i in reversed(range(half, size)):
        if i == size - 1:
            weight = 1.0 / pivot
            c = up[i - 1] * weight
            g = source[i] * weight
        else:
            weight = 1.0 / (pivot - down[i + 1] * c)
            g = (source[i] + down[i + 1] * g) * weight
            c = up[i - 1] * weight
        high_g[i], high_c[i] = g, c
    out = [None] * size
    inverse = 1.0 / (1.0 - low_c[half - 1] * high_c[half])
    out[half - 1] = (low_g[half - 1] + low_c[half - 1] * high_g[half]) * inverse
    out[half] = high_g[half] + high_c[half] * out[half - 1]
    for i in reversed(range(half - 1)):
        out[i] = low_g[i] + low_c[i] * out[i + 1]
    for i in range(half + 1, size):
        out[i] = high_g[i] + high_c[i] * out[i - 1]
    return out


def start_kernel(
    extent_y,
    extent_z,
    density_hbm,
    diffusion_hbm,
    centers_hbm,
    sharpness_hbm,
    affine_hbm,
    offsets_hbm,
    message,
    line_values,
    line_drifts,
    drift_z_out,
    prepared,
    solved,
    drift_y_held,
    density,
    diffusion,
    centers,
    sharpness,
    affine,
    offsets,
    staged,
    semaphores,
):
    copies = [
        pltpu.make_async_copy(source, target, semaphores.at[number])
        for number, (source, target) in enumerate(
            [
                (diffusion_hbm, diffusion),
                (centers_hbm, centers),
                (sharpness_hbm, sharpness),
                (affine_hbm, affine),
                (offsets_hbm, offsets),
                (density_hbm, density),
            ]
        )
    ]
    for copy in copies:
        copy.start()
    size_x, size_y, size_z = density.shape
    total_y, total_z = size_y * extent_y, size_z * extent_z
    y_start = lax.axis_index("gy") * size_y
    z_start = lax.axis_index("gz") * size_z
    maps = centers.shape[1]
    for copy in copies[:-1]:
        copy.wait()

    staged[...] = jnp.zeros(staged.shape, jnp.float32)
    staged[0:1, :maps] = sharpness[...]
    staged[1:4, :maps] = centers[...]
    for c in range(3):
        staged[4 + 3 * c : 7 + 3 * c, :maps] = affine[c]
    staged[13:16, :maps] = offsets[...]
    rows = staged[...]
    width = maps
    while width < LANES:
        rows = rows + roll(rows, width, 1)
        width = 2 * width
    component = component_of(maps)
    rows = jnp.where(component < 3, rows, 0.0)

    def by_component(first, step):
        return jnp.where(
            component == 0,
            rows[first : first + 1],
            jnp.where(
                component == 1,
                rows[first + step : first + step + 1],
                rows[first + 2 * step : first + 2 * step + 1],
            ),
        )

    weights = [jnp.broadcast_to(diffusion[:, c : c + 1], (1, LANES)) for c in range(3)]
    params = jnp.concatenate(
        [rows[0:4]]
        + [by_component(4 + j, 3) for j in range(3)]
        + [by_component(13, 1)]
        + weights
        + [jnp.zeros((PREPARED - DIFFUSION - 3, LANES), jnp.float32)],
        axis=0,
    )
    prepared[...] = params
    d0, d1, d2 = weights

    x_bump, x_part = x_factors(params, maps, size_x)
    y_row = iota((size_y, LANES), 0)
    y_bump, y_part = y_factors(params, maps, y_start + y_row, total_y)
    out_bump, out_part = y_factors(
        params, maps, jnp.where(y_row == 0, y_start + size_y, y_start - 1), total_y
    )
    inner = inner_z_rows(params, maps, z_start, size_z, total_z)
    outer = outer_z_rows(params, maps, z_start, size_z, total_z)
    inner = [only(inner, maps, c) for c in range(3)]
    outer = only(outer, maps, 0)

    def rows_by_x(bumps, part):
        return jnp.concatenate(
            [(x_bump[i : i + 1] * bumps) * (x_part[i : i + 1] + part) for i in range(size_x)],
            axis=0,
        )

    right = jnp.concatenate([inner[0], outer, inner[1], inner[2]], axis=0)
    drifts = half_drift(rows_by_x(y_bump, y_part), right)
    out_drift = half_drift(rows_by_x(out_bump, out_part), inner[0])

    def block(number):
        columns = drifts[:, number * LANES : (number + 1) * LANES]
        return columns.reshape(size_x, size_y, LANES)

    drift_x, plane_drift, drift_y, drift_z = block(0), block(1), block(2), block(3)
    out_drift = out_drift.reshape(size_x, size_y, LANES)
    drift_y_held[...] = drift_y
    drift_z_out[...] = drift_z
    copies[-1].wait()
    rho = density[...]
    zero = jnp.zeros((1, size_y, LANES), jnp.float32)
    up, down = (d0 + drift_x) * rho, (d0 - drift_x) * rho
    total = (
        jnp.concatenate([zero, up[:-1]], axis=0)
        + jnp.concatenate([down[1:], zero], axis=0)
        - (2.0 * (d0 + d1 + d2)) * rho
    )
    sublane = iota((size_x, size_y, LANES), 1)
    lane = iota((size_x, size_y, LANES), 2)
    up, down = roll((d1 + drift_y) * rho, 1, 1), roll((d1 - drift_y) * rho, -1, 1)
    at_low, at_high = sublane == 0, sublane == size_y - 1
    row_source = jnp.where(at_low, up, jnp.where(at_high, down, 0.0))
    total = total + jnp.where(at_low, 0.0, up) + jnp.where(at_high, 0.0, down)
    up, down = (d2 + drift_z) * rho, (d2 - drift_z) * rho
    plane_source = jnp.where(
        lane == ABOVE, up, jnp.where(lane == BELOW, roll(down, BELOW, 2), 0.0)
    )
    up, down = roll(up, 1, 2), roll(down, -1, 2)
    at_low, at_high = lane == 0, lane == size_z - 1
    total = total + jnp.where(at_low, 0.0, up) + jnp.where(at_high, 0.0, down)

    source = jnp.concatenate([total, row_source, plane_source], axis=1)
    drift = jnp.concatenate([drift_x, out_drift, plane_drift], axis=1)
    answers = solve_x(d0 + drift, d0 - drift, source, 1.0 + 2.0 * d0)
    for i in range(size_x):
        solved[i] = answers[i][: 2 * size_y]
    planes = pack_planes([answer[2 * size_y :] for answer in answers])

    out_rows = [
        (x_bump * out_bump[j : j + 1]) * (x_part + out_part[j : j + 1])
        for j in (size_y - 1, 0)
    ]
    ends = half_drift(jnp.concatenate(out_rows, axis=0), inner[1])
    position = y_start - 1 + iota((2 * ROWS, LANES), 0)
    extra = half_drift(
        y_rows(params, maps, position, total_y),
        only(xz_rows(params, maps, size_x, z_start, size_z, total_z), maps, 1),
    )
    line_drift = (
        [ends[:size_x]]
        + [drift_y_held[:, j, :] for j in range(size_y)]
        + [ends[size_x:]]
    )
    line_drift = [with_extra(line_drift[j], extra[j : j + 1]) for j in range(size_y + 2)]
    values = [with_extra(solved[:, j, :], planes[j : j + 1]) for j in range(size_y)]
    for j in range(size_y):
        line_values[j] = values[j]
    for j in range(size_y + 2):
        line_drifts[j] = line_drift[j]
    pivot = 1.0 + 2.0 * d1
    g = c = None
    gs, cs = [], []
    for j in range(size_y):
        lower, upper = line_factors(line_drift, j, size_y, d1, y_start, total_y)
        weight = 1.0 / (pivot if j == 0 else pivot - lower * c)
        g = (values[j] if j == 0 else values[j] + lower * g) * weight
        c = upper * weight
        gs.append(g)
        cs.append(c)
    r_first = r_last = g
    for j in reversed(range(size_y - 1)):
        r_first = gs[j] + cs[j] * r_first
    pushed_up = solved[:, size_y, :] / (d1 + line_drift[size_y][:size_x])
    pushed_down = solved[:, 2 * size_y - 1, :] / (d1 - line_drift[1][:size_x])
    blank = jnp.zeros((1, LANES), jnp.float32)
    message[...] = join_message(
        r_first + with_extra(pushed_down, blank), r_last + with_extra(pushed_up, blank)
    )


def line_factors(line_drift, j, size_y, d1, y_start, total_y):
    lower, upper = d1 + line_drift[j], d1 - line_drift[j + 2]
    if j == 0:
        lower = jnp.where(y_start == 0, 0.0, lower)
    if j == size_y - 1:
        upper = jnp.where(y_start + size_y == total_y, 0.0, upper)
    return lower, upper


def line_coefs(params, maps, sizes, start, count, store):
    extent_y, extent_z, size_x, size_y, size_z = sizes
    total_y, total_z = size_y * extent_y, size_z * extent_z
    z_start = lax.axis_index("gz") * size_z
    d1 = params[DIFFUSION + 1 : DIFFUSION + 2]
    x_bump, x_part = x_factors(params, maps, size_x)
    inner = only(inner_z_rows(params, maps, z_start, size_z, total_z), maps, 1)
    planes = only(xz_rows(params, maps, size_x, z_start, size_z, total_z), maps, 1)
    whole = count == extent_y
    offsets = list(range(size_y)) if whole else list(range(-1, size_y + 1))
    left, left_extra = [], []
    for j in offsets:
        for b in range(count):
            position = iota((1, LANES), 0) + ((start + b) * size_y + j)
            bumps, part = y_factors(params, maps, position, total_y)
            left.append((x_bump * bumps) * (x_part + part))
        block = iota((max(count, ROWS), LANES), 0)
        left_extra.append(
            y_rows(params, maps, (start + block) * size_y + j, total_y)
        )
    depth = left_extra[0].shape[0]
    main = half_drift(jnp.concatenate(left, axis=0), inner)
    main = main.reshape(len(offsets), count, size_x, LANES)
    main = [main[j] for j in range(len(offsets))]
    extra = half_drift(jnp.concatenate(left_extra, axis=0), planes)
    extra = [extra[j * depth : (j + 1) * depth] for j in range(len(offsets))]
    if whole:
        main = (
            [jnp.concatenate([main[-1][:1], main[-1][:-1]], axis=0)]
            + main
            + [jnp.concatenate([main[0][1:], main[0][-1:]], axis=0)]
        )
        extra = [roll(extra[-1], 1, 0)] + extra + [roll(extra[0], -1, 0)]
    numbers = start + iota((depth, LANES), 0)
    pivot = 1.0 + 2.0 * d1
    at_start, at_end = numbers == 0, numbers == extent_y - 1

    def scan(drifts, starts, ends):
        a_first = c_first = a_last = c_last = None
        for j in range(size_y):
            lower, upper = d1 + drifts[j], d1 - drifts[j + 2]
            if j == 0:
                lower = starts(lower)
            if j == size_y - 1:
                upper = ends(upper)
            if j == 0:
                weight = 1.0 / pivot
                a_first, c_first = lower * weight, upper * weight
                a_last, c_last = a_first, c_first
            else:
                weight = 1.0 / (pivot - lower * c_last)
                step, c_last = lower * weight, upper * weight
                a_last = step * a_last
                a_first = a_first + c_first * a_last
                c_first = c_first * c_last
        return a_first, c_first, a_last, c_last

    def masked(values, number):
        return jnp.concatenate(
            [
                jnp.where(start + b == number, 0.0, values[b])[None]
                for b in range(count)
            ],
            axis=0,
        )

    main = scan(main, lambda v: masked(v, 0), lambda v: masked(v, extent_y - 1))
    extra = scan(
        extra,
        lambda v: jnp.where(at_start, 0.0, v),
        lambda v: jnp.where(at_end, 0.0, v),
    )
    for b in range(count):
        for q in range(4):
            store(b, q, with_extra(main[q][b], extra[q][b : b + 1]))


def near_kernel(
    sizes,
    maps,
    stride,
    radix,
    prepared,
    line_values,
    line_drifts,
    coefs,
    base,
    from_below,
    from_above,
):
    digit = lax.rem(lax.div(lax.axis_index("gy"), stride), radix)
    start = lax.div(lax.axis_index("gy"), stride) - digit
    params = prepared[...]

    def store(b, q, value):
        coefs[b, q] = value

    line_coefs(params, maps, sizes, start, radix, store)
    extent_y, _, _, size_y, _ = sizes
    d1 = params[DIFFUSION + 1 : DIFFUSION + 2]
    pivot = 1.0 + 2.0 * d1
    y_start = lax.axis_index("gy") * size_y
    g = a = c = None
    gs, as_, cs = [], [], []
    for j in range(size_y):
        lower, upper = line_factors(line_drifts, j, size_y, d1, y_start, size_y * extent_y)
        if j == 0:
            weight = 1.0 / pivot
            g, a = line_values[j] * weight, lower * weight
        else:
            weight = 1.0 / (pivot - lower * c)
            g, a = (line_values[j] + lower * g) * weight, lower * a * weight
        c = upper * weight
        gs.append(g)
        as_.append(a)
        cs.append(c)
    base[size_y - 1], from_below[size_y - 1], from_above[size_y - 1] = g, a, c
    for j in reversed(range(size_y - 1)):
        g, a, c = gs[j] + cs[j] * g, as_[j] + cs[j] * a, cs[j] * c
        base[j], from_below[j], from_above[j] = g, a, c


def far_kernel(sizes, maps, levels, prepared, *outputs):
    held = {}

    def store(b, q, value):
        held[b, q] = value

    extent_y = sizes[0]
    line_coefs(prepared[...], maps, sizes, 0, extent_y, store)
    groups = [tuple(held[b, q] for q in range(4)) for b in range(extent_y)]
    for (_, radix), coefs in zip(levels, outputs):
        groups = [
            functools.reduce(merge_coefs, groups[g : g + radix])
            for g in range(0, len(groups), radix)
        ]
        for number, group in enumerate(groups):
            for q in range(4):
                coefs[number, q] = group[q]


def double_coefs(below, above, scale, steps=None):
    size_z = below.shape[0]
    row = iota(below.shape, 0)
    stride, level = 1, 0
    while stride < size_z:
        low, high = row < stride, row >= size_z - stride
        low_a = jnp.where(low, 1.0, turn(below, stride))
        low_c = jnp.where(low, 0.0, turn(above, stride))
        high_a = jnp.where(high, 0.0, turn(below, -stride))
        high_c = jnp.where(high, 1.0, turn(above, -stride))
        inverse = 1.0 / (1.0 - below * low_c - above * high_a)
        below, above = below * inverse, above * inverse
        if steps is not None:
            factor = scale if level == 0 else 1.0
            steps[level, 0] = inverse * factor
            steps[level, 1] = jnp.where(low, 0.0, below * factor)
            steps[level, 2] = jnp.where(high, 0.0, above * factor)
        below, above = below * low_a, above * high_c
        stride, level = stride * 2, level + 1
    return below, above


def z_coef_kernel(sizes, maps, prepared, drift_z, steps, ends, pushes, packed, weights):
    extent_y, extent_z, size_x, size_y, size_z = sizes
    total_y, total_z = size_y * extent_y, size_z * extent_z
    y_start = lax.axis_index("gy") * size_y
    z_start = lax.axis_index("gz") * size_z
    params = prepared[...]
    d2 = params[DIFFUSION + 2 : DIFFUSION + 3]
    lane = iota((size_y, LANES), 1)
    divisors = []
    for i in range(size_x):
        plane = drift_z[i]
        factor = jnp.where(lane == ABOVE, d2 + plane, d2 - roll(plane, BELOW, 1))
        divisors.append(
            jnp.where((lane == ABOVE) | (lane == BELOW), 1.0 / factor, 0.0)
        )
    pushes[...] = pack_planes(divisors)
    x_bump, x_part = x_factors(params, maps, size_x)
    outer = only(outer_z_rows(params, maps, z_start, size_z, total_z), maps, 2)
    rows = []
    for j in range(size_y):
        position = iota((1, LANES), 0) + (y_start + j)
        bumps, part = y_factors(params, maps, position, total_y)
        rows.append((x_bump * bumps) * (x_part + part))
    outer = half_drift(jnp.concatenate(rows, axis=0), outer)
    outer = to_lines([outer[j * size_x : (j + 1) * size_x] for j in range(size_y)], size_x)
    inner = to_lines([drift_z[:, j, :] for j in range(size_y)], size_x)
    d2 = jnp.concatenate([d2] * (inner.shape[1] // LANES), axis=1)
    scale = 1.0 / (1.0 + 2.0 * d2)
    row = iota(inner.shape, 0)
    low, high = row == 0, row == size_z - 1
    before = jnp.where(low, outer[BELOW : BELOW + 1], turn(inner, 1))
    after = jnp.where(high, outer[ABOVE : ABOVE + 1], turn(inner, -1))
    below = jnp.where(low & (z_start == 0), 0.0, (d2 + before) * scale)
    above = jnp.where(high & (z_start + size_z == total_z), 0.0, (d2 - after) * scale)
    turned_below = jnp.where(low, 1.0, turn(above, 1))
    turned_above = jnp.where(high, 1.0, turn(below, -1))
    below, above = double_coefs(below, above, scale, steps)
    turned_below, turned_above = double_coefs(turned_below, turned_above, scale)
    weights[0] = turned_below * scale
    weights[1] = turned_above * scale
    ends[0] = below
    ends[1] = above
    packed[...] = jnp.concatenate(
        [
            jnp.zeros((2, inner.shape[1]), jnp.float32),
            below[:1],
            below[size_z - 1 :],
            above[:1],
            above[size_z - 1 :],
            jnp.zeros((2, inner.shape[1]), jnp.float32),
        ],
        axis=0,
    )


def gather_members(refs, own, count):
    held = [ref[...] for ref in refs]
    return [
        functools.reduce(
            lambda acc, s: jnp.where((own ^ s) == j, held[s], acc), range(1, count), held[0]
        )
        for j in range(count)
    ]


def join_message(first, last):
    size_x = first.shape[0] - ROWS
    extra = jnp.where(iota((ROWS, LANES), 0) == 0, first[size_x:], last[size_x:])
    return jnp.concatenate([first[:size_x], last[:size_x], extra], axis=0)


def split_message(message):
    size_x = (message.shape[0] - ROWS) // 2
    return (
        with_extra(message[:size_x], message[2 * size_x : 2 * size_x + 1]),
        with_extra(message[size_x : 2 * size_x], message[2 * size_x + 1 : 2 * size_x + 2]),
    )


def merge_kernel(stride, radix, local, facing, coefs, *refs):
    received, message = refs[:radix], refs[-1]
    digit = lax.rem(lax.div(lax.axis_index("gy"), stride), radix)
    first = 0 if local else lax.div(lax.axis_index("gy"), stride) - digit
    values = [split_message(m) for m in gather_members(received, digit, radix)]
    group = [tuple(coefs[first + j, q] for q in range(4)) for j in range(radix)]
    while len(group) > 1:
        pairs = range(0, len(group), 2)
        values = [merge_values(group[j], group[j + 1], values[j], values[j + 1]) for j in pairs]
        group = [merge_coefs(group[j], group[j + 1]) for j in pairs]
    total = values[0]
    if facing:
        is_low = lax.axis_index("gy") < stride * radix
        message[...] = jnp.where(is_low, total[1], total[0])
    else:
        message[...] = join_message(*total)


def middle_kernel(levels, *refs):
    refs = list(refs)
    weights, pushes, packed, base, from_below, from_above = refs[:6]
    refs = refs[6:]
    inputs = []
    for stride, radix in levels:
        inputs.append((refs[0], refs[1 : 1 + radix]))
        refs = refs[1 + radix :]
    message, sources, seen = refs
    size_y, width = base.shape[:2]
    size_x = width - ROWS
    below = above = jnp.zeros((width, LANES), jnp.float32)
    for number in reversed(range(len(levels))):
        (stride, radix), (coefs, received) = levels[number], inputs[number]
        digit = lax.rem(lax.div(lax.axis_index("gy"), stride), radix)
        first = 0 if number == 0 else lax.div(lax.axis_index("gy"), stride) - digit
        members = gather_members(received, digit, radix)
        group = [tuple(coefs[first + j, q] for q in range(4)) for j in range(radix)]
        if members[0].shape[0] == width:
            c_last, a_first = group[0][3], group[1][0]
            inverse = 1.0 / (1.0 - c_last * a_first)
            below = jnp.where(digit == 0, 0.0, (members[0] + c_last * members[1]) * inverse)
            above = jnp.where(digit == 0, (members[1] + a_first * members[0]) * inverse, 0.0)
            continue
        values = [split_message(m) for m in members]
        lows, highs = chain(group, values, below, above)
        for j in range(radix):
            seen[j, 0] = lows[j]
            seen[j, 1] = highs[j]
        below, above = seen[digit, 0], seen[digit, 1]
    inner, outer = [], []
    for j in range(size_y):
        value = base[j] + from_below[j] * below + from_above[j] * above
        inner.append(value[:size_x])
        outer.append(value[size_x : size_x + 1])
    pushed = jnp.concatenate(outer, axis=0) * pushes[...]
    values = to_lines(inner, size_x)
    sources[...] = values
    message[...] = packed[...]
    message[0:1] = total_of(weights[0] * values) + lines_of(pushed, size_x, BELOW + 1)
    message[1:2] = total_of(weights[1] * values) + lines_of(pushed, size_x, 0)


def total_of(values):
    return jnp.sum(values, axis=0, keepdims=True)


def from_lines(values, size_x):
    rows = []
    for first in range(0, values.shape[1], LANES):
        tile = jnp.transpose(values[:, first : first + LANES])
        rows += [tile[q : q + size_x] for q in range(0, LANES, size_x)]
    return rows


def double_kernel(steps, sources, density, base):
    values = sources[...]
    stride, level = 1, 0
    while stride < values.shape[0]:
        values = (
            steps[level, 0] * values
            + steps[level, 1] * turn(values, stride)
            + steps[level, 2] * turn(values, -stride)
        )
        stride, level = stride * 2, level + 1
    for j, rows in enumerate(from_lines(values, density.shape[0])):
        base[j] = density[:, j, :] + rows


def merge_z(low, high):
    inverse = 1.0 / (1.0 - low[5] * high[2])
    onward, back = low[4] * inverse, high[3] * inverse
    return (
        low[0] + onward * (high[0] + high[2] * low[1]),
        high[1] + back * (low[1] + low[5] * high[0]),
        low[2] + onward * high[2] * low[3],
        back * low[3],
        onward * high[4],
        high[5] + back * low[5] * high[4],
    )


def unpack_ends(message):
    return tuple(message[s : s + 1] for s in range(6))


def merge_z_kernel(stride, radix, *refs):
    received, message = refs[:radix], refs[radix]
    digit = lax.rem(lax.div(lax.axis_index("gz"), stride), radix)
    members = [unpack_ends(m) for m in gather_members(received, digit, radix)]
    total = functools.reduce(merge_z, members)
    message[...] = jnp.concatenate(total + total[:2], axis=0)


def end_kernel(levels, base, ends, *refs):
    refs = list(refs)
    inputs = []
    for stride, radix in levels:
        inputs.append(refs[:radix])
        refs = refs[radix:]
    out, seen = refs
    below = above = jnp.zeros((1, ends.shape[2]), jnp.float32)
    for (stride, radix), received in zip(reversed(levels), reversed(inputs)):
        digit = lax.rem(lax.div(lax.axis_index("gz"), stride), radix)
        members = [unpack_ends(m) for m in gather_members(received, digit, radix)]
        lows, highs = chain(
            [(m[2], m[4], m[3], m[5]) for m in members],
            [(m[0], m[1]) for m in members],
            below,
            above,
        )
        for j in range(radix):
            seen[j, 0:1] = lows[j]
            seen[j, 1:2] = highs[j]
        below, above = seen[digit, 0:1], seen[digit, 1:2]
    values = ends[0] * below + ends[1] * above
    for j, rows in enumerate(from_lines(values, base.shape[1])):
        out[:, j, :] = base[j] + rows


def radices(extent):
    rounds, stride = [], 1
    while stride < extent:
        radix = 4 if (extent // stride) % 4 == 0 else 2
        rounds.append((stride, radix))
        stride *= radix
    return rounds


def exchange(message, axis, stride, radix):
    devices = range(lax.axis_size(axis))
    return [message] + [
        lax.ppermute(message, axis, [(i, i ^ (s * stride)) for i in devices])
        for s in range(1, radix)
    ]


def body(density, diffusion, centers, sharpness, affine, offsets):
    size_x, size_y, size_z = density.shape
    extent_y, extent_z = lax.axis_size("gy"), lax.axis_size("gz")
    sizes = (extent_y, extent_z, size_x, size_y, size_z)
    maps = centers.shape[0]
    width = size_x + ROWS
    wide = (size_y, width, LANES)
    narrow = (size_z, size_y * size_x)
    float32 = jnp.float32
    y_levels, z_levels = radices(extent_y), radices(extent_z)

    def shape(*dims):
        return jax.ShapeDtypeStruct(dims, float32)

    vmem = pl.BlockSpec(memory_space=pltpu.VMEM)
    hbm = pl.BlockSpec(memory_space=pltpu.HBM)

    def call(kernel, inputs, outputs, in_specs=None, scratch=(), flops=10**6):
        return pl.pallas_call(
            kernel,
            out_shape=outputs,
            in_specs=in_specs or [vmem] * len(inputs),
            out_specs=jax.tree.map(lambda _: vmem, outputs),
            scratch_shapes=list(scratch),
            compiler_params=pltpu.CompilerParams(vmem_limit_bytes=VMEM_LIMIT),
            cost_estimate=pl.CostEstimate(flops=flops, bytes_accessed=10**6, transcendentals=0),
        )(*inputs)

    raw = (
        density,
        diffusion.reshape(1, 3),
        centers.T,
        sharpness.reshape(1, maps),
        affine.transpose(1, 2, 0),
        offsets.T,
    )
    raw = tuple(pltpu.with_memory_space_constraint(array, pltpu.HBM) for array in raw)
    message, line_values, line_drifts, drift_z, prepared = call(
        functools.partial(start_kernel, extent_y, extent_z),
        raw,
        (
            shape(width + size_x, LANES),
            shape(*wide),
            shape(size_y + 2, width, LANES),
            shape(size_x, size_y, LANES),
            shape(PREPARED, LANES),
        ),
        [hbm] * len(raw),
        [
            pltpu.VMEM((size_x, 2 * size_y, LANES), float32),
            pltpu.VMEM((size_x, size_y, LANES), float32),
        ]
        + [pltpu.VMEM(array.shape, float32) for array in raw]
        + [pltpu.VMEM((PREPARED, LANES), float32), pltpu.SemaphoreType.DMA((len(raw),))],
    )
    stride, radix = y_levels[0]
    near, base, from_below, from_above = call(
        functools.partial(near_kernel, sizes, maps, stride, radix),
        [prepared, line_values, line_drifts],
        (shape(radix, 4, width, LANES), shape(*wide), shape(*wide), shape(*wide)),
    )
    far, count = [], extent_y
    for _, radix in y_levels[:-1]:
        count = count // radix
        far.append(shape(count, 4, width, LANES))
    if far:
        far = call(functools.partial(far_kernel, sizes, maps, y_levels[:-1]), [prepared], far)
    coefs = [near] + list(far)
    doublings = size_z.bit_length() - 1
    steps, ends, pushes, packed, weights = call(
        functools.partial(z_coef_kernel, sizes, maps),
        (prepared, drift_z),
        (
            shape(doublings, 3, *narrow),
            shape(2, *narrow),
            shape(size_y, LANES),
            shape(ROWS, size_y * size_x),
            shape(2, *narrow),
        ),
    )
    line_inputs = []
    for number, (stride, radix) in enumerate(y_levels):
        received = exchange(message, "gy", stride, radix)
        line_inputs += [coefs[number]] + received
        if number + 1 < len(y_levels):
            facing = number + 2 == len(y_levels) and y_levels[-1][1] == 2
            message = call(
                functools.partial(merge_kernel, stride, radix, number == 0, facing),
                [coefs[number]] + received + ([packed] + list(far) if number == 0 else []),
                shape(width if facing else width + size_x, LANES),
            )
    message, sources = call(
        functools.partial(middle_kernel, y_levels),
        [weights, pushes, packed, base, from_below, from_above] + line_inputs,
        (shape(ROWS, size_y * size_x), shape(*narrow)),
        scratch=[pltpu.VMEM((4, 2, width, LANES), float32)],
    )
    base = call(double_kernel, [steps, sources, density], shape(size_y, size_x, size_z))
    end_inputs = []
    for number, (stride, radix) in enumerate(z_levels):
        received = exchange(message, "gz", stride, radix)
        end_inputs += received
        if number + 1 < len(z_levels):
            message = call(
                functools.partial(merge_z_kernel, stride, radix),
                received,
                shape(ROWS, size_y * size_x),
            )
    return call(
        functools.partial(end_kernel, z_levels),
        [base, ends] + end_inputs,
        shape(size_x, size_y, size_z),
        scratch=[pltpu.VMEM((4, ROWS, size_y * size_x), float32)],
    )


def solution(mesh):
    placed = (P(None, "gy", "gz"), P(), P(), P(), P(), P())
    return jax.shard_map(
        body, mesh=mesh, in_specs=placed, out_specs=P(None, "gy", "gz"), check_vma=False
    )
```

```python
import functools

import jax
import jax.numpy as jnp
from jax import lax
from jax.experimental import pallas as pl
from jax.experimental.pallas import tpu as pltpu
from jax.sharding import PartitionSpec as P

HALF_LIMIT = 600.0
LANES = 128
ROWS = 8
ABOVE, BELOW = 127, 31
VMEM_LIMIT = 48 * 1024 * 1024


def iota(shape, axis):
    return lax.broadcasted_iota(jnp.int32, shape, axis)


def coordinate(positions, line_total):
    return (2.0 * positions.astype(jnp.float32) + 1.0) * (1.0 / line_total) - 1.0


def roll(values, shift, axis):
    return pltpu.roll(values, shift % values.shape[axis], axis)


def matmul(left, right):
    low, high = split(left), split(right)
    columns = right.shape[0]
    both = lax.dot_general(
        jnp.concatenate(low, axis=1),
        jnp.concatenate([jnp.concatenate([part, part], axis=1) for part in high], axis=0),
        (((1,), (1,)), ((), ())),
        preferred_element_type=jnp.float32,
    )
    return both[:, :columns] + both[:, columns:]


def split(values):
    upper = values.astype(jnp.bfloat16)
    return upper, (values - upper.astype(jnp.float32)).astype(jnp.bfloat16)


def half_drift(left, right):
    return HALF_LIMIT * jnp.tanh(matmul(left, right))


SHARPNESS, CENTER, SLOPE, OFFSET, DIFFUSION, PREPARED = 0, 1, 4, 7, 8, 16


def component_of(maps):
    return iota((1, LANES), 1) // (2 * maps)


def first_term(maps):
    return (iota((1, LANES), 1) // maps) % 2 == 0


def bump(params, coord, axis):
    center = params[CENTER + axis : CENTER + axis + 1]
    return jnp.exp(-params[SHARPNESS : SHARPNESS + 1] * (coord - center) ** 2)


def slope(params, coord, axis):
    return coord * params[SLOPE + axis : SLOPE + axis + 1]


def x_factors(params, maps, size_x):
    coord = coordinate(iota((size_x, LANES), 0), size_x)
    return bump(params, coord, 0), jnp.where(first_term(maps), slope(params, coord, 0), 0.0)


def y_factors(params, maps, position, total_y):
    coord = coordinate(position, total_y)
    part = slope(params, coord, 1) + params[OFFSET : OFFSET + 1]
    return bump(params, coord, 1), jnp.where(
        first_term(maps), part, params[SLOPE + 2 : SLOPE + 3]
    )


def z_rows(params, maps, position, total_z):
    coord = coordinate(position, total_z)
    return bump(params, coord, 2) * jnp.where(first_term(maps), 1.0, coord)


def inner_z_rows(params, maps, z_start, size_z, total_z):
    return z_rows(params, maps, z_start + iota((size_z, LANES), 0), total_z)


def outer_positions(z_start, size_z):
    return jnp.where(iota((ROWS, LANES), 0) == 0, z_start - 1, z_start + size_z)


def outer_z_rows(params, maps, z_start, size_z, total_z):
    rows = z_rows(params, maps, outer_positions(z_start, size_z), total_z)
    return jnp.where(iota((size_z, LANES), 0) == BELOW, rows[:1], rows[1:2])


def only(rows, maps, component):
    return jnp.where(component_of(maps) == component, rows, 0.0)


def y_rows(params, maps, position, total_y):
    coord = coordinate(position, total_y)
    part = slope(params, coord, 1) + params[OFFSET : OFFSET + 1]
    return bump(params, coord, 1) * jnp.where(first_term(maps), part, 1.0)


def xz_rows(params, maps, size_x, z_start, size_z, total_z):
    x_coord = coordinate(iota((size_x, LANES), 0), size_x)
    z_coord = coordinate(outer_positions(z_start, size_z), total_z)
    x_bump, z_bump = bump(params, x_coord, 0), bump(params, z_coord, 2)
    x_part, z_part = slope(params, x_coord, 0), slope(params, z_coord, 2)
    rows = [
        (x_bump * z_bump[i : i + 1])
        * jnp.where(first_term(maps), 1.0, x_part + z_part[i : i + 1])
        for i in (1, 0)
    ]
    blank = jnp.zeros((BELOW + 1 - size_x, LANES), jnp.float32)
    rest = jnp.zeros((LANES - BELOW - 1 - size_x, LANES), jnp.float32)
    parts = [rows[0], blank, rows[1], rest] if size_x <= BELOW else [rows[0], rows[1], rest]
    return jnp.concatenate(parts, axis=0)


def with_extra(main, row):
    return jnp.concatenate([main, jnp.broadcast_to(row, (ROWS, LANES))], axis=0)


def pack_planes(planes):
    turned = [roll(plane, i + 1, 1) for i, plane in enumerate(planes)]
    while len(turned) > 1:
        turned = [sum(turned[i : i + 2]) for i in range(0, len(turned), 2)]
    return turned[0]


def lines_of(planes, size_x, first_lane):
    group = LANES // size_x
    place = iota((1, LANES), 1) // size_x
    turned = [roll(planes, q * size_x - first_lane, 1) for q in range(group)]
    rows = []
    for first in range(0, planes.shape[0], group):
        row = turned[0][first : first + 1]
        for q in range(1, group):
            row = jnp.where(place == q, turned[q][first + q : first + q + 1], row)
        rows.append(row)
    return jnp.concatenate(rows, axis=1)


def to_lines(rows, size_x):
    group = LANES // size_x
    return jnp.concatenate(
        [
            jnp.transpose(jnp.concatenate(rows[first : first + group], axis=0))
            for first in range(0, len(rows), group)
        ],
        axis=1,
    )


def turn(values, stride):
    stride = stride % values.shape[0]
    if stride % ROWS == 0:
        return jnp.concatenate([values[-stride:], values[:-stride]], axis=0)
    return roll(values, stride, 0)


def merge_coefs(low, high):
    inverse = 1.0 / (1.0 - low[3] * high[0])
    onward, back = low[1] * inverse, high[2] * inverse
    return (
        low[0] + onward * high[0] * low[2],
        onward * high[1],
        back * low[2],
        high[3] + back * low[3] * high[1],
    )


def merge_values(low, high, low_values, high_values):
    inverse = 1.0 / (1.0 - low[3] * high[0])
    return (
        low_values[0] + low[1] * inverse * (high_values[0] + high[0] * low_values[1]),
        high_values[1] + high[2] * inverse * (low_values[1] + low[3] * high_values[0]),
    )


def merge(low, high, low_values, high_values):
    return merge_coefs(low, high), merge_values(low, high, low_values, high_values)


def meet(low, high, below, above):
    (_, _, a_last, c_last), (_, r_last) = low
    (a_first, c_first, _, _), (r_first, _) = high
    inverse = 1.0 / (1.0 - c_last * a_first)
    upper = r_first + c_first * above
    left = (r_last + a_last * below + c_last * upper) * inverse
    return left, upper + a_first * left


def chain(coefs, values, below, above):
    count = len(coefs)
    if count == 4:
        halves = [merge(coefs[j], coefs[j + 1], values[j], values[j + 1]) for j in (0, 2)]
        left, right = meet(halves[0], halves[1], below, above)
        seen = [
            meet((coefs[j], values[j]), (coefs[j + 1], values[j + 1]), low, high)
            for j, low, high in ((0, below, right), (2, left, above))
        ]
        return [below, seen[0][0], left, seen[1][0]], [seen[0][1], right, seen[1][1], above]
    held, slope = below, None
    befores, firsts = [], []
    for j in range(count):
        a_first, c_first, a_last, c_last = coefs[j]
        r_first, r_last = values[j]
        befores.append((held, slope))
        if slope is None:
            first, first_slope = r_first + a_first * held, c_first
            held, slope = r_last + a_last * held, c_last
        else:
            inverse = 1.0 / (1.0 - a_first * slope)
            first = (r_first + a_first * held) * inverse
            first_slope = c_first * inverse
            held, slope = (
                r_last + a_last * (held + slope * first),
                c_last + a_last * slope * first_slope,
            )
        firsts.append((first, first_slope))
    seen_above = [None] * count
    seen_below = [None] * count
    upper = above
    for j in reversed(range(count)):
        seen_above[j] = upper
        upper = firsts[j][0] + firsts[j][1] * upper
        held, slope = befores[j]
        seen_below[j] = held if slope is None else held + slope * upper
    return seen_below, seen_above


def solve_x(up, down, source, pivot):
    size = source.shape[0]
    half = size // 2
    low_g, low_c, high_g, high_c = {}, {}, {}, {}
    g = c = None
    for i in range(half):
        if i == 0:
            weight = 1.0 / pivot
            c = down[1] * weight
            g = source[0] * weight
        else:
            weight = 1.0 / (pivot - up[i - 1] * c)
            g = (source[i] + up[i - 1] * g) * weight
            c = down[i + 1] * weight
        low_g[i], low_c[i] = g, c
    for i in reversed(range(half, size)):
        if i == size - 1:
            weight = 1.0 / pivot
            c = up[i - 1] * weight
            g = source[i] * weight
        else:
            weight = 1.0 / (pivot - down[i + 1] * c)
            g = (source[i] + down[i + 1] * g) * weight
            c = up[i - 1] * weight
        high_g[i], high_c[i] = g, c
    out = [None] * size
    inverse = 1.0 / (1.0 - low_c[half - 1] * high_c[half])
    out[half - 1] = (low_g[half - 1] + low_c[half - 1] * high_g[half]) * inverse
    out[half] = high_g[half] + high_c[half] * out[half - 1]
    for i in reversed(range(half - 1)):
        out[i] = low_g[i] + low_c[i] * out[i + 1]
    for i in range(half + 1, size):
        out[i] = high_g[i] + high_c[i] * out[i - 1]
    return out


def start_kernel(
    extent_y,
    extent_z,
    density_hbm,
    diffusion_hbm,
    centers_hbm,
    sharpness_hbm,
    affine_hbm,
    offsets_hbm,
    message,
    line_values,
    line_drifts,
    drift_z_out,
    prepared,
    solved,
    drift_y_held,
    density,
    diffusion,
    centers,
    sharpness,
    affine,
    offsets,
    staged,
    semaphores,
):
    copies = [
        pltpu.make_async_copy(source, target, semaphores.at[number])
        for number, (source, target) in enumerate(
            [
                (diffusion_hbm, diffusion),
                (centers_hbm, centers),
                (sharpness_hbm, sharpness),
                (affine_hbm, affine),
                (offsets_hbm, offsets),
                (density_hbm, density),
            ]
        )
    ]
    for copy in copies:
        copy.start()
    size_x, size_y, size_z = density.shape
    total_y, total_z = size_y * extent_y, size_z * extent_z
    y_start = lax.axis_index("gy") * size_y
    z_start = lax.axis_index("gz") * size_z
    maps = centers.shape[1]
    for copy in copies[:-1]:
        copy.wait()

    staged[...] = jnp.zeros(staged.shape, jnp.float32)
    staged[0:1, :maps] = sharpness[...]
    staged[1:4, :maps] = centers[...]
    for c in range(3):
        staged[4 + 3 * c : 7 + 3 * c, :maps] = affine[c]
    staged[13:16, :maps] = offsets[...]
    rows = staged[...]
    width = maps
    while width < LANES:
        rows = rows + roll(rows, width, 1)
        width = 2 * width
    component = component_of(maps)
    rows = jnp.where(component < 3, rows, 0.0)

    def by_component(first, step):
        return jnp.where(
            component == 0,
            rows[first : first + 1],
            jnp.where(
                component == 1,
                rows[first + step : first + step + 1],
                rows[first + 2 * step : first + 2 * step + 1],
            ),
        )

    weights = [jnp.broadcast_to(diffusion[:, c : c + 1], (1, LANES)) for c in range(3)]
    params = jnp.concatenate(
        [rows[0:4]]
        + [by_component(4 + j, 3) for j in range(3)]
        + [by_component(13, 1)]
        + weights
        + [jnp.zeros((PREPARED - DIFFUSION - 3, LANES), jnp.float32)],
        axis=0,
    )
    prepared[...] = params
    d0, d1, d2 = weights

    x_bump, x_part = x_factors(params, maps, size_x)
    y_row = iota((size_y, LANES), 0)
    y_bump, y_part = y_factors(params, maps, y_start + y_row, total_y)
    out_bump, out_part = y_factors(
        params, maps, jnp.where(y_row == 0, y_start + size_y, y_start - 1), total_y
    )
    inner = inner_z_rows(params, maps, z_start, size_z, total_z)
    outer = outer_z_rows(params, maps, z_start, size_z, total_z)
    inner = [only(inner, maps, c) for c in range(3)]
    outer = only(outer, maps, 0)

    def rows_by_x(bumps, part):
        return jnp.concatenate(
            [(x_bump[i : i + 1] * bumps) * (x_part[i : i + 1] + part) for i in range(size_x)],
            axis=0,
        )

    right = jnp.concatenate([inner[0], outer, inner[1], inner[2]], axis=0)
    drifts = half_drift(rows_by_x(y_bump, y_part), right)
    out_drift = half_drift(rows_by_x(out_bump, out_part), inner[0])

    def block(number):
        columns = drifts[:, number * LANES : (number + 1) * LANES]
        return columns.reshape(size_x, size_y, LANES)

    drift_x, plane_drift, drift_y, drift_z = block(0), block(1), block(2), block(3)
    out_drift = out_drift.reshape(size_x, size_y, LANES)
    drift_y_held[...] = drift_y
    drift_z_out[...] = drift_z
    copies[-1].wait()
    rho = density[...]
    zero = jnp.zeros((1, size_y, LANES), jnp.float32)
    up, down = (d0 + drift_x) * rho, (d0 - drift_x) * rho
    total = (
        jnp.concatenate([zero, up[:-1]], axis=0)
        + jnp.concatenate([down[1:], zero], axis=0)
        - (2.0 * (d0 + d1 + d2)) * rho
    )
    sublane = iota((size_x, size_y, LANES), 1)
    lane = iota((size_x, size_y, LANES), 2)
    up, down = roll((d1 + drift_y) * rho, 1, 1), roll((d1 - drift_y) * rho, -1, 1)
    at_low, at_high = sublane == 0, sublane == size_y - 1
    row_source = jnp.where(at_low, up, jnp.where(at_high, down, 0.0))
    total = total + jnp.where(at_low, 0.0, up) + jnp.where(at_high, 0.0, down)
    up, down = (d2 + drift_z) * rho, (d2 - drift_z) * rho
    plane_source = jnp.where(
        lane == ABOVE, up, jnp.where(lane == BELOW, roll(down, BELOW, 2), 0.0)
    )
    up, down = roll(up, 1, 2), roll(down, -1, 2)
    at_low, at_high = lane == 0, lane == size_z - 1
    total = total + jnp.where(at_low, 0.0, up) + jnp.where(at_high, 0.0, down)

    source = jnp.concatenate([total, row_source, plane_source], axis=1)
    drift = jnp.concatenate([drift_x, out_drift, plane_drift], axis=1)
    answers = solve_x(d0 + drift, d0 - drift, source, 1.0 + 2.0 * d0)
    for i in range(size_x):
        solved[i] = answers[i][: 2 * size_y]
    planes = pack_planes([answer[2 * size_y :] for answer in answers])

    out_rows = [
        (x_bump * out_bump[j : j + 1]) * (x_part + out_part[j : j + 1])
        for j in (size_y - 1, 0)
    ]
    ends = half_drift(jnp.concatenate(out_rows, axis=0), inner[1])
    position = y_start - 1 + iota((2 * ROWS, LANES), 0)
    extra = half_drift(
        y_rows(params, maps, position, total_y),
        only(xz_rows(params, maps, size_x, z_start, size_z, total_z), maps, 1),
    )
    line_drift = (
        [ends[:size_x]]
        + [drift_y_held[:, j, :] for j in range(size_y)]
        + [ends[size_x:]]
    )
    line_drift = [with_extra(line_drift[j], extra[j : j + 1]) for j in range(size_y + 2)]
    values = [with_extra(solved[:, j, :], planes[j : j + 1]) for j in range(size_y)]
    for j in range(size_y):
        line_values[j] = values[j]
    for j in range(size_y + 2):
        line_drifts[j] = line_drift[j]
    pivot = 1.0 + 2.0 * d1
    g = c = None
    gs, cs = [], []
    for j in range(size_y):
        lower, upper = line_factors(line_drift, j, size_y, d1, y_start, total_y)
        weight = 1.0 / (pivot if j == 0 else pivot - lower * c)
        g = (values[j] if j == 0 else values[j] + lower * g) * weight
        c = upper * weight
        gs.append(g)
        cs.append(c)
    r_first = r_last = g
    for j in reversed(range(size_y - 1)):
        r_first = gs[j] + cs[j] * r_first
    pushed_up = solved[:, size_y, :] / (d1 + line_drift[size_y][:size_x])
    pushed_down = solved[:, 2 * size_y - 1, :] / (d1 - line_drift[1][:size_x])
    blank = jnp.zeros((1, LANES), jnp.float32)
    message[...] = join_message(
        r_first + with_extra(pushed_down, blank), r_last + with_extra(pushed_up, blank)
    )


def line_factors(line_drift, j, size_y, d1, y_start, total_y):
    lower, upper = d1 + line_drift[j], d1 - line_drift[j + 2]
    if j == 0:
        lower = jnp.where(y_start == 0, 0.0, lower)
    if j == size_y - 1:
        upper = jnp.where(y_start + size_y == total_y, 0.0, upper)
    return lower, upper


def line_coefs(params, maps, sizes, start, count, store):
    extent_y, extent_z, size_x, size_y, size_z = sizes
    total_y, total_z = size_y * extent_y, size_z * extent_z
    z_start = lax.axis_index("gz") * size_z
    d1 = params[DIFFUSION + 1 : DIFFUSION + 2]
    x_bump, x_part = x_factors(params, maps, size_x)
    inner = only(inner_z_rows(params, maps, z_start, size_z, total_z), maps, 1)
    planes = only(xz_rows(params, maps, size_x, z_start, size_z, total_z), maps, 1)
    whole = count == extent_y
    offsets = list(range(size_y)) if whole else list(range(-1, size_y + 1))
    left, left_extra = [], []
    for j in offsets:
        for b in range(count):
            position = iota((1, LANES), 0) + ((start + b) * size_y + j)
            bumps, part = y_factors(params, maps, position, total_y)
            left.append((x_bump * bumps) * (x_part + part))
        block = iota((max(count, ROWS), LANES), 0)
        left_extra.append(
            y_rows(params, maps, (start + block) * size_y + j, total_y)
        )
    depth = left_extra[0].shape[0]
    main = half_drift(jnp.concatenate(left, axis=0), inner)
    main = main.reshape(len(offsets), count, size_x, LANES)
    main = [main[j] for j in range(len(offsets))]
    extra = half_drift(jnp.concatenate(left_extra, axis=0), planes)
    extra = [extra[j * depth : (j + 1) * depth] for j in range(len(offsets))]
    if whole:
        main = (
            [jnp.concatenate([main[-1][:1], main[-1][:-1]], axis=0)]
            + main
            + [jnp.concatenate([main[0][1:], main[0][-1:]], axis=0)]
        )
        extra = [roll(extra[-1], 1, 0)] + extra + [roll(extra[0], -1, 0)]
    numbers = start + iota((depth, LANES), 0)
    pivot = 1.0 + 2.0 * d1
    at_start, at_end = numbers == 0, numbers == extent_y - 1

    def scan(drifts, starts, ends):
        a_first = c_first = a_last = c_last = None
        for j in range(size_y):
            lower, upper = d1 + drifts[j], d1 - drifts[j + 2]
            if j == 0:
                lower = starts(lower)
            if j == size_y - 1:
                upper = ends(upper)
            if j == 0:
                weight = 1.0 / pivot
                a_first, c_first = lower * weight, upper * weight
                a_last, c_last = a_first, c_first
            else:
                weight = 1.0 / (pivot - lower * c_last)
                step, c_last = lower * weight, upper * weight
                a_last = step * a_last
                a_first = a_first + c_first * a_last
                c_first = c_first * c_last
        return a_first, c_first, a_last, c_last

    def masked(values, number):
        return jnp.concatenate(
            [
                jnp.where(start + b == number, 0.0, values[b])[None]
                for b in range(count)
            ],
            axis=0,
        )

    main = scan(main, lambda v: masked(v, 0), lambda v: masked(v, extent_y - 1))
    extra = scan(
        extra,
        lambda v: jnp.where(at_start, 0.0, v),
        lambda v: jnp.where(at_end, 0.0, v),
    )
    for b in range(count):
        for q in range(4):
            store(b, q, with_extra(main[q][b], extra[q][b : b + 1]))


def near_kernel(
    sizes,
    maps,
    stride,
    radix,
    prepared,
    line_values,
    line_drifts,
    coefs,
    base,
    from_below,
    from_above,
):
    digit = lax.rem(lax.div(lax.axis_index("gy"), stride), radix)
    start = lax.div(lax.axis_index("gy"), stride) - digit
    params = prepared[...]

    def store(b, q, value):
        coefs[b, q] = value

    line_coefs(params, maps, sizes, start, radix, store)
    extent_y, _, _, size_y, _ = sizes
    d1 = params[DIFFUSION + 1 : DIFFUSION + 2]
    pivot = 1.0 + 2.0 * d1
    y_start = lax.axis_index("gy") * size_y
    g = a = c = None
    gs, as_, cs = [], [], []
    for j in range(size_y):
        lower, upper = line_factors(line_drifts, j, size_y, d1, y_start, size_y * extent_y)
        if j == 0:
            weight = 1.0 / pivot
            g, a = line_values[j] * weight, lower * weight
        else:
            weight = 1.0 / (pivot - lower * c)
            g, a = (line_values[j] + lower * g) * weight, lower * a * weight
        c = upper * weight
        gs.append(g)
        as_.append(a)
        cs.append(c)
    base[size_y - 1], from_below[size_y - 1], from_above[size_y - 1] = g, a, c
    for j in reversed(range(size_y - 1)):
        g, a, c = gs[j] + cs[j] * g, as_[j] + cs[j] * a, cs[j] * c
        base[j], from_below[j], from_above[j] = g, a, c


def far_kernel(sizes, maps, levels, prepared, *outputs):
    held = {}

    def store(b, q, value):
        held[b, q] = value

    extent_y = sizes[0]
    line_coefs(prepared[...], maps, sizes, 0, extent_y, store)
    groups = [tuple(held[b, q] for q in range(4)) for b in range(extent_y)]
    for (_, radix), coefs in zip(levels, outputs):
        groups = [
            functools.reduce(merge_coefs, groups[g : g + radix])
            for g in range(0, len(groups), radix)
        ]
        for number, group in enumerate(groups):
            for q in range(4):
                coefs[number, q] = group[q]


def double_coefs(below, above, scale, steps=None):
    size_z = below.shape[0]
    row = iota(below.shape, 0)
    stride, level = 1, 0
    while stride < size_z:
        low, high = row < stride, row >= size_z - stride
        low_a = jnp.where(low, 1.0, turn(below, stride))
        low_c = jnp.where(low, 0.0, turn(above, stride))
        high_a = jnp.where(high, 0.0, turn(below, -stride))
        high_c = jnp.where(high, 1.0, turn(above, -stride))
        inverse = 1.0 / (1.0 - below * low_c - above * high_a)
        below, above = below * inverse, above * inverse
        if steps is not None:
            factor = scale if level == 0 else 1.0
            steps[level, 0] = inverse * factor
            steps[level, 1] = jnp.where(low, 0.0, below * factor)
            steps[level, 2] = jnp.where(high, 0.0, above * factor)
        below, above = below * low_a, above * high_c
        stride, level = stride * 2, level + 1
    return below, above


def z_coef_kernel(sizes, maps, prepared, drift_z, steps, ends, pushes, packed, weights):
    extent_y, extent_z, size_x, size_y, size_z = sizes
    total_y, total_z = size_y * extent_y, size_z * extent_z
    y_start = lax.axis_index("gy") * size_y
    z_start = lax.axis_index("gz") * size_z
    params = prepared[...]
    d2 = params[DIFFUSION + 2 : DIFFUSION + 3]
    lane = iota((size_y, LANES), 1)
    divisors = []
    for i in range(size_x):
        plane = drift_z[i]
        factor = jnp.where(lane == ABOVE, d2 + plane, d2 - roll(plane, BELOW, 1))
        divisors.append(
            jnp.where((lane == ABOVE) | (lane == BELOW), 1.0 / factor, 0.0)
        )
    pushes[...] = pack_planes(divisors)
    x_bump, x_part = x_factors(params, maps, size_x)
    outer = only(outer_z_rows(params, maps, z_start, size_z, total_z), maps, 2)
    rows = []
    for j in range(size_y):
        position = iota((1, LANES), 0) + (y_start + j)
        bumps, part = y_factors(params, maps, position, total_y)
        rows.append((x_bump * bumps) * (x_part + part))
    outer = half_drift(jnp.concatenate(rows, axis=0), outer)
    outer = to_lines([outer[j * size_x : (j + 1) * size_x] for j in range(size_y)], size_x)
    inner = to_lines([drift_z[:, j, :] for j in range(size_y)], size_x)
    d2 = jnp.concatenate([d2] * (inner.shape[1] // LANES), axis=1)
    scale = 1.0 / (1.0 + 2.0 * d2)
    row = iota(inner.shape, 0)
    low, high = row == 0, row == size_z - 1
    before = jnp.where(low, outer[BELOW : BELOW + 1], turn(inner, 1))
    after = jnp.where(high, outer[ABOVE : ABOVE + 1], turn(inner, -1))
    below = jnp.where(low & (z_start == 0), 0.0, (d2 + before) * scale)
    above = jnp.where(high & (z_start + size_z == total_z), 0.0, (d2 - after) * scale)
    turned_below = jnp.where(low, 1.0, turn(above, 1))
    turned_above = jnp.where(high, 1.0, turn(below, -1))
    below, above = double_coefs(below, above, scale, steps)
    turned_below, turned_above = double_coefs(turned_below, turned_above, scale)
    weights[0] = turned_below * scale
    weights[1] = turned_above * scale
    ends[0] = below
    ends[1] = above
    packed[...] = jnp.concatenate(
        [
            jnp.zeros((2, inner.shape[1]), jnp.float32),
            below[:1],
            below[size_z - 1 :],
            above[:1],
            above[size_z - 1 :],
            jnp.zeros((2, inner.shape[1]), jnp.float32),
        ],
        axis=0,
    )


ORDER = {("gy", 2): (1,), ("gz", 2): (1,), ("gy", 4): (1, 3, 2), ("gz", 4): (1, 2, 3)}


def gather_members(refs, own, count, axis):
    held = {s: ref[...] for s, ref in zip((0,) + ORDER[axis, count], refs)}
    return [
        functools.reduce(
            lambda acc, s: jnp.where((own ^ s) == j, held[s], acc), range(1, count), held[0]
        )
        for j in range(count)
    ]


def join_message(first, last):
    size_x = first.shape[0] - ROWS
    extra = jnp.where(iota((ROWS, LANES), 0) == 0, first[size_x:], last[size_x:])
    return jnp.concatenate([first[:size_x], last[:size_x], extra], axis=0)


def split_message(message):
    size_x = (message.shape[0] - ROWS) // 2
    return (
        with_extra(message[:size_x], message[2 * size_x : 2 * size_x + 1]),
        with_extra(message[size_x : 2 * size_x], message[2 * size_x + 1 : 2 * size_x + 2]),
    )


def merge_kernel(stride, radix, local, facing, coefs, *refs):
    received, message = refs[:radix], refs[-1]
    digit = lax.rem(lax.div(lax.axis_index("gy"), stride), radix)
    first = 0 if local else lax.div(lax.axis_index("gy"), stride) - digit
    values = [split_message(m) for m in gather_members(received, digit, radix, "gy")]
    group = [tuple(coefs[first + j, q] for q in range(4)) for j in range(radix)]
    while len(group) > 1:
        pairs = range(0, len(group), 2)
        values = [merge_values(group[j], group[j + 1], values[j], values[j + 1]) for j in pairs]
        group = [merge_coefs(group[j], group[j + 1]) for j in pairs]
    total = values[0]
    if facing:
        is_low = lax.axis_index("gy") < stride * radix
        message[...] = jnp.where(is_low, total[1], total[0])
    else:
        message[...] = join_message(*total)


def middle_kernel(levels, *refs):
    refs = list(refs)
    weights, pushes, packed, base, from_below, from_above = refs[:6]
    refs = refs[6:]
    inputs = []
    for stride, radix in levels:
        inputs.append((refs[0], refs[1 : 1 + radix]))
        refs = refs[1 + radix :]
    message, sources, seen = refs
    size_y, width = base.shape[:2]
    size_x = width - ROWS
    below = above = jnp.zeros((width, LANES), jnp.float32)
    for number in reversed(range(len(levels))):
        (stride, radix), (coefs, received) = levels[number], inputs[number]
        digit = lax.rem(lax.div(lax.axis_index("gy"), stride), radix)
        first = 0 if number == 0 else lax.div(lax.axis_index("gy"), stride) - digit
        members = gather_members(received, digit, radix, "gy")
        group = [tuple(coefs[first + j, q] for q in range(4)) for j in range(radix)]
        if members[0].shape[0] == width:
            c_last, a_first = group[0][3], group[1][0]
            inverse = 1.0 / (1.0 - c_last * a_first)
            below = jnp.where(digit == 0, 0.0, (members[0] + c_last * members[1]) * inverse)
            above = jnp.where(digit == 0, (members[1] + a_first * members[0]) * inverse, 0.0)
            continue
        values = [split_message(m) for m in members]
        lows, highs = chain(group, values, below, above)
        for j in range(radix):
            seen[j, 0] = lows[j]
            seen[j, 1] = highs[j]
        below, above = seen[digit, 0], seen[digit, 1]
    inner, outer = [], []
    for j in range(size_y):
        value = base[j] + from_below[j] * below + from_above[j] * above
        inner.append(value[:size_x])
        outer.append(value[size_x : size_x + 1])
    pushed = jnp.concatenate(outer, axis=0) * pushes[...]
    values = to_lines(inner, size_x)
    sources[...] = values
    message[...] = packed[...]
    message[0:1] = total_of(weights[0] * values) + lines_of(pushed, size_x, BELOW + 1)
    message[1:2] = total_of(weights[1] * values) + lines_of(pushed, size_x, 0)


def total_of(values):
    return jnp.sum(values, axis=0, keepdims=True)


def from_lines(values, size_x):
    rows = []
    for first in range(0, values.shape[1], LANES):
        tile = jnp.transpose(values[:, first : first + LANES])
        rows += [tile[q : q + size_x] for q in range(0, LANES, size_x)]
    return rows


def double_kernel(steps, sources, density, base):
    values = sources[...]
    stride, level = 1, 0
    while stride < values.shape[0]:
        values = (
            steps[level, 0] * values
            + steps[level, 1] * turn(values, stride)
            + steps[level, 2] * turn(values, -stride)
        )
        stride, level = stride * 2, level + 1
    for j, rows in enumerate(from_lines(values, density.shape[0])):
        base[j] = density[:, j, :] + rows


def merge_z(low, high):
    inverse = 1.0 / (1.0 - low[5] * high[2])
    onward, back = low[4] * inverse, high[3] * inverse
    return (
        low[0] + onward * (high[0] + high[2] * low[1]),
        high[1] + back * (low[1] + low[5] * high[0]),
        low[2] + onward * high[2] * low[3],
        back * low[3],
        onward * high[4],
        high[5] + back * low[5] * high[4],
    )


def unpack_ends(message):
    return tuple(message[s : s + 1] for s in range(6))


def merge_z_kernel(stride, radix, *refs):
    received, message = refs[:radix], refs[radix]
    digit = lax.rem(lax.div(lax.axis_index("gz"), stride), radix)
    members = [unpack_ends(m) for m in gather_members(received, digit, radix, "gz")]
    total = functools.reduce(merge_z, members)
    message[...] = jnp.concatenate(total + total[:2], axis=0)


def end_kernel(levels, base, ends, *refs):
    refs = list(refs)
    inputs = []
    for stride, radix in levels:
        inputs.append(refs[:radix])
        refs = refs[radix:]
    out, seen = refs
    below = above = jnp.zeros((1, ends.shape[2]), jnp.float32)
    for (stride, radix), received in zip(reversed(levels), reversed(inputs)):
        digit = lax.rem(lax.div(lax.axis_index("gz"), stride), radix)
        members = [unpack_ends(m) for m in gather_members(received, digit, radix, "gz")]
        lows, highs = chain(
            [(m[2], m[4], m[3], m[5]) for m in members],
            [(m[0], m[1]) for m in members],
            below,
            above,
        )
        for j in range(radix):
            seen[j, 0:1] = lows[j]
            seen[j, 1:2] = highs[j]
        below, above = seen[digit, 0:1], seen[digit, 1:2]
    values = ends[0] * below + ends[1] * above
    for j, rows in enumerate(from_lines(values, base.shape[1])):
        out[:, j, :] = base[j] + rows


def radices(extent):
    rounds, stride = [], 1
    while stride < extent:
        radix = 4 if (extent // stride) % 4 == 0 else 2
        rounds.append((stride, radix))
        stride *= radix
    return rounds


def exchange(message, axis, stride, radix):
    devices = range(lax.axis_size(axis))
    return [message] + [
        lax.ppermute(message, axis, [(i, i ^ (s * stride)) for i in devices])
        for s in ORDER[axis, radix]
    ]


def body(density, diffusion, centers, sharpness, affine, offsets):
    size_x, size_y, size_z = density.shape
    extent_y, extent_z = lax.axis_size("gy"), lax.axis_size("gz")
    sizes = (extent_y, extent_z, size_x, size_y, size_z)
    maps = centers.shape[0]
    width = size_x + ROWS
    wide = (size_y, width, LANES)
    narrow = (size_z, size_y * size_x)
    float32 = jnp.float32
    y_levels, z_levels = radices(extent_y), radices(extent_z)

    def shape(*dims):
        return jax.ShapeDtypeStruct(dims, float32)

    vmem = pl.BlockSpec(memory_space=pltpu.VMEM)
    hbm = pl.BlockSpec(memory_space=pltpu.HBM)

    def call(kernel, inputs, outputs, in_specs=None, scratch=(), flops=10**6):
        return pl.pallas_call(
            kernel,
            out_shape=outputs,
            in_specs=in_specs or [vmem] * len(inputs),
            out_specs=jax.tree.map(lambda _: vmem, outputs),
            scratch_shapes=list(scratch),
            compiler_params=pltpu.CompilerParams(vmem_limit_bytes=VMEM_LIMIT),
            cost_estimate=pl.CostEstimate(flops=flops, bytes_accessed=10**6, transcendentals=0),
        )(*inputs)

    raw = (
        density,
        diffusion.reshape(1, 3),
        centers.T,
        sharpness.reshape(1, maps),
        affine.transpose(1, 2, 0),
        offsets.T,
    )
    raw = tuple(pltpu.with_memory_space_constraint(array, pltpu.HBM) for array in raw)
    message, line_values, line_drifts, drift_z, prepared = call(
        functools.partial(start_kernel, extent_y, extent_z),
        raw,
        (
            shape(width + size_x, LANES),
            shape(*wide),
            shape(size_y + 2, width, LANES),
            shape(size_x, size_y, LANES),
            shape(PREPARED, LANES),
        ),
        [hbm] * len(raw),
        [
            pltpu.VMEM((size_x, 2 * size_y, LANES), float32),
            pltpu.VMEM((size_x, size_y, LANES), float32),
        ]
        + [pltpu.VMEM(array.shape, float32) for array in raw]
        + [pltpu.VMEM((PREPARED, LANES), float32), pltpu.SemaphoreType.DMA((len(raw),))],
    )
    stride, radix = y_levels[0]
    near, base, from_below, from_above = call(
        functools.partial(near_kernel, sizes, maps, stride, radix),
        [prepared, line_values, line_drifts],
        (shape(radix, 4, width, LANES), shape(*wide), shape(*wide), shape(*wide)),
    )
    far, count = [], extent_y
    for _, radix in y_levels[:-1]:
        count = count // radix
        far.append(shape(count, 4, width, LANES))
    if far:
        far = call(functools.partial(far_kernel, sizes, maps, y_levels[:-1]), [prepared], far)
    coefs = [near] + list(far)
    doublings = size_z.bit_length() - 1
    steps, ends, pushes, packed, weights = call(
        functools.partial(z_coef_kernel, sizes, maps),
        (prepared, drift_z),
        (
            shape(doublings, 3, *narrow),
            shape(2, *narrow),
            shape(size_y, LANES),
            shape(ROWS, size_y * size_x),
            shape(2, *narrow),
        ),
    )
    line_inputs = []
    for number, (stride, radix) in enumerate(y_levels):
        received = exchange(message, "gy", stride, radix)
        line_inputs += [coefs[number]] + received
        if number + 1 < len(y_levels):
            facing = number + 2 == len(y_levels) and y_levels[-1][1] == 2
            message = call(
                functools.partial(merge_kernel, stride, radix, number == 0, facing),
                [coefs[number]] + received + ([packed] + list(far) if number == 0 else []),
                shape(width if facing else width + size_x, LANES),
            )
    message, sources = call(
        functools.partial(middle_kernel, y_levels),
        [weights, pushes, packed, base, from_below, from_above] + line_inputs,
        (shape(ROWS, size_y * size_x), shape(*narrow)),
        scratch=[pltpu.VMEM((4, 2, width, LANES), float32)],
    )
    base = call(double_kernel, [steps, sources, density], shape(size_y, size_x, size_z))
    end_inputs = []
    for number, (stride, radix) in enumerate(z_levels):
        received = exchange(message, "gz", stride, radix)
        end_inputs += received
        if number + 1 < len(z_levels):
            message = call(
                functools.partial(merge_z_kernel, stride, radix),
                received,
                shape(ROWS, size_y * size_x),
            )
    return call(
        functools.partial(end_kernel, z_levels),
        [base, ends] + end_inputs,
        shape(size_x, size_y, size_z),
        scratch=[pltpu.VMEM((4, ROWS, size_y * size_x), float32)],
    )


def solution(mesh):
    placed = (P(None, "gy", "gz"), P(), P(), P(), P(), P())
    return jax.shard_map(
        body, mesh=mesh, in_specs=placed, out_specs=P(None, "gy", "gz"), check_vma=False
    )
```
